32 devices in a mesh: dp: 16 (over z, y, core), seq: 2 (over x).
Axes of the slice: x: 2, y: 2, z: 4, core: 2. Of those that a mesh axis runs over, the one named last changes fastest.
Arguments:
- tokens: bfloat16 [32, 1024, 768], P('dp', 'seq'), may hold values from -6 to 6
- lengths: int32 [32], P('dp'), may hold values from 256 to 1024, as said below
- key_mask: int32 [32, 1024], P('dp', 'seq'), may hold values 0 or 1
- attn_gain: float32 [768], replicated, may hold values from 0.5 to 1.5
- attn_shift: float32 [768], replicated, may hold values from -3 to 3
- w_qkv: bfloat16 [768, 2304], replicated, may hold values from -0.3125 to 0.3125
- query_bias: float32 [768], replicated, may hold values from -3 to 3
- value_bias: float32 [768], replicated, may hold values from -3 to 3
- w_out: bfloat16 [768, 768], replicated, may hold values from -0.4375 to 0.4375
- out_bias: float32 [768], replicated, may hold values from -3 to 3
- ffn_gain: float32 [768], replicated, may hold values from 0.5 to 1.5
- ffn_shift: float32 [768], replicated, may hold values from -3 to 3
- w_in: bfloat16 [768, 3072], replicated, may hold values from -0.21875 to 0.21875
- in_bias: float32 [3072], replicated, may hold values from -3 to 3
- w_back: bfloat16 [3072, 768], replicated, may hold values from -0.21875 to 0.21875
- back_bias: float32 [768], replicated, may hold values from -3 to 3
- cotangent: bfloat16 [32, 1024, 768], P('dp', 'seq'), may hold values from -40 to 40
Outputs:
- layer_out: bfloat16 [32, 1024, 768], P('dp', 'seq')
- grad_tokens: float32 [32, 1024, 768], P('dp', 'seq')
- grad_attn_gain: float32 [768], P(('dp', 'seq'))
- grad_attn_shift: float32 [768], P(('dp', 'seq'))
- grad_w_qkv: float32 [768, 2304], P(('dp', 'seq'))
- grad_query_bias: float32 [768], P(('dp', 'seq'))
- grad_value_bias: float32 [768], P(('dp', 'seq'))
- grad_w_out: float32 [768, 768], P(('dp', 'seq'))
- grad_out_bias: float32 [768], P(('dp', 'seq'))
- grad_ffn_gain: float32 [768], P(('dp', 'seq'))
- grad_ffn_shift: float32 [768], P(('dp', 'seq'))
- grad_w_in: float32 [768, 3072], P(('dp', 'seq'))
- grad_in_bias: float32 [3072], P(('dp', 'seq'))
- grad_w_back: float32 [3072, 768], P(('dp', 'seq'))
- grad_back_bias: float32 [768], P(('dp', 'seq'))
The draws below stay inside these ranges and needn't reach their ends.
Inputs may be any that keep to these rules, and one draw needn't show every extreme that they name: `lengths`: in each aligned group of 2 sequences (those of one index of dp), one has length 1024.
All inputs are finite; a program needn't handle non-finite values. No bound on the sum of `key_mask` on one device may be relied on, other than what follows from the above.
Results may differ from the reference program's by a relative error of at most 0.023.
Values may be sent and summed in bfloat16 or wider, within the bound.
A program may use at most 256 MiB of HBM per device.

```python
import math
import jax
import jax.numpy as jnp
from jax import lax

D = 768
H = 12
HD = 64
FF = 3072
LEN = 1024
SEQ_DEV = 2
SEQUENCES = 32


def draw_lengths(key, part):
    key = jax.random.fold_in(key, 11)
    drawn = jax.random.randint(jax.random.fold_in(key, 1), (SEQUENCES,), LEN // 4, LEN + 1)
    groups = SEQUENCES // SEQ_DEV
    chosen = jax.random.randint(jax.random.fold_in(key, 2), (groups, 1), 0, SEQ_DEV)
    longest = (jnp.arange(SEQ_DEV, dtype=jnp.int32)[None, :] == chosen).reshape(SEQUENCES)
    return jnp.where(longest, LEN, drawn).astype(jnp.int32)


def draw_cotangent(key, part):
    key = jax.random.fold_in(key, 23)
    extent = (SEQUENCES, LEN, D)
    across = 1.0 + 2.0 * jnp.arange(SEQUENCES, dtype=jnp.float32) / max(SEQUENCES - 1, 1)
    along = 1.0 + jnp.arange(LEN, dtype=jnp.float32) / LEN
    rising = across[:, None, None] * along[None, :, None]
    sample = jax.random.normal(key, extent, jnp.float32)
    return (sample * rising * 0.5).astype(jnp.bfloat16)


def plant(values, own_key, low, high):
    shape = values.shape
    spot = [jax.random.randint(jax.random.fold_in(own_key, axis), (), 0, shape[axis]) for axis in range(len(shape))]
    values = values.at[tuple(spot)].set(low)
    longest = shape.index(max(shape))
    spot[longest] = (spot[longest] + 1) % shape[longest]
    return values.at[tuple(spot)].set(high)


def shard_levels(own_key, dims, shards, smallest, top_value):
    def one(dim, shards_of):
        draws = jax.random.uniform(jax.random.fold_in(jax.random.fold_in(own_key, 6), dim), (shards_of,), jnp.float32, smallest / len(shards), top_value / len(shards))
        return jnp.repeat(jnp.exp(draws), dims[dim] // shards_of).reshape((-1,) + (1,) * (len(dims) - dim - 1))

    factor_of = one(*shards[0])
    for cut in shards[1:]:
        factor_of = factor_of * one(*cut)
    return factor_of


def scatter_about(key, dims, width, limit, split=(), kind=jnp.bfloat16):
    loudness = shard_levels(key, dims, split, -0.22, 0.18) if split else 1.0
    values = jax.random.normal(key, dims, jnp.float32) * width * loudness
    return jnp.minimum(jnp.maximum(values, -limit), limit).astype(kind)


def setup_inputs(seed: int = 0) -> dict:
    key_of = jax.random.split(jax.random.key(seed), 18)
    tokens = scatter_about(key_of[0], (SEQUENCES, LEN, D), 1.0, 6.0, ((0, 16), (1, 2)))
    lengths = draw_lengths(jax.random.fold_in(key_of[17], 71), 0)
    key_mask = plant((jax.random.randint(key_of[2], (SEQUENCES, LEN), 0, 8) < 7).astype(jnp.int32), jax.random.fold_in(key_of[2], 1), 0, 1)
    attn_gain = jnp.clip(jax.random.uniform(key_of[3], (D,), jnp.float32, 0.5, 1.5), 0.5, 1.5)
    attn_shift = scatter_about(key_of[4], (D,), 0.5, 3.0, (), jnp.float32)
    w_qkv = scatter_about(key_of[5], (D, 3 * D), (D // 2) ** -0.5, 0.3125)
    query_bias = scatter_about(key_of[6], (D,), 0.5, 3.0, (), jnp.float32)
    value_bias = scatter_about(key_of[7], (D,), 0.5, 3.0, (), jnp.float32)
    w_out = scatter_about(key_of[8], (D, D), (D // 4) ** -0.5, 0.4375)
    out_bias = scatter_about(key_of[9], (D,), 0.5, 3.0, (), jnp.float32)
    ffn_gain = jnp.clip(jax.random.uniform(key_of[10], (D,), jnp.float32, 0.5, 1.5), 0.5, 1.5)
    ffn_shift = scatter_about(key_of[11], (D,), 0.5, 3.0, (), jnp.float32)
    w_in = scatter_about(key_of[12], (D, FF), D ** -0.5, 0.21875)
    in_bias = scatter_about(key_of[13], (FF,), 0.5, 3.0, (), jnp.float32)
    w_back = scatter_about(key_of[14], (FF, D), (FF // 4) ** -0.5, 0.21875)
    back_bias = scatter_about(key_of[15], (D,), 0.5, 3.0, (), jnp.float32)
    cotangent = draw_cotangent(jax.random.fold_in(key_of[17], 71), 0)
    return dict(tokens=tokens, lengths=lengths, key_mask=key_mask, attn_gain=attn_gain, attn_shift=attn_shift, w_qkv=w_qkv, query_bias=query_bias, value_bias=value_bias, w_out=w_out, out_bias=out_bias, ffn_gain=ffn_gain, ffn_shift=ffn_shift, w_in=w_in, in_bias=in_bias, w_back=w_back, back_bias=back_bias, cotangent=cotangent)


NEG_FILL = -1e+30
NORM_EPS = 1e-05
HIGHEST_PREC = lax.Precision.HIGHEST

@jax.custom_vjp
def low(v):
    return lax.optimization_barrier(v.astype(jnp.bfloat16)).astype(jnp.float32)

@jax.custom_vjp
def low_back(v):
    return v

def low_keep(v):
    return (low(v), None)

def low_pass(kept, grad):
    return (grad,)

def back_keep(v):
    return (v, None)

def back_low(kept, grad):
    return (low(grad),)
low.defvjp(low_keep, low_pass)
low_back.defvjp(back_keep, back_low)

def layer_norm(values, gain, shift):
    center = values - lax.optimization_barrier(jnp.mean(values, axis=-1, keepdims=True))
    spread = lax.optimization_barrier(jnp.mean(center * center, axis=-1, keepdims=True))
    return center * lax.rsqrt(spread + NORM_EPS) * gain + shift

def encoder_layer(inputs, seq_lengths, key_flags, params):
    attn_gain, attn_shift, w_qkv, query_bias, value_bias, w_out, out_bias, ffn_gain, ffn_shift, w_in, in_bias, w_back, back_bias = params
    group_size, seq_len, model_width = inputs.shape
    normed_attn = low(layer_norm(inputs, attn_gain, attn_shift))
    projected = jnp.einsum('gtd,de->gte', normed_attn, w_qkv, precision=HIGHEST_PREC)
    queries = low(low_back((projected[..., :model_width] + query_bias) * 0.125))
    key_heads = low(low_back(projected[..., model_width:2 * model_width]))
    value_heads = low(low_back(projected[..., 2 * model_width:] + value_bias))
    queries = queries.reshape(group_size, seq_len, H, HD)
    key_heads = key_heads.reshape(group_size, seq_len, H, HD)
    value_heads = value_heads.reshape(group_size, seq_len, H, HD)
    scores = low_back(jnp.einsum('gqhd,gkhd->gqhk', queries, key_heads, precision=HIGHEST_PREC))
    positions = jnp.arange(seq_len, dtype=jnp.int32)
    key_valid = (positions[None, :] < seq_lengths[:, None]) & (key_flags == 1)
    itself = positions[:, None] == positions[None, :]
    allowed = key_valid[:, None, None, :] | itself[None, :, None, :]
    row_max = lax.optimization_barrier(jnp.max(jnp.where(allowed, scores, NEG_FILL), axis=-1, keepdims=True))
    expo = jnp.exp(jnp.where(allowed, scores - row_max, NEG_FILL))
    probabilities = expo / lax.optimization_barrier(jnp.sum(expo, axis=-1, keepdims=True))
    attended = jnp.einsum('gqhk,gkhd->gqhd', low(probabilities), value_heads, precision=HIGHEST_PREC)
    context = low(low_back(attended.reshape(group_size, seq_len, model_width)))
    branch = low_back(jnp.einsum('gtd,de->gte', context, w_out, precision=HIGHEST_PREC) + out_bias)
    residual = inputs + branch
    normed_ffn = low(layer_norm(residual, ffn_gain, ffn_shift))
    pre_act = low_back(jnp.einsum('gtd,df->gtf', normed_ffn, w_in, precision=HIGHEST_PREC) + in_bias)
    activated = low(jax.nn.gelu(pre_act, approximate=True))
    return residual + jnp.einsum('gtf,fd->gtd', activated, w_back, precision=HIGHEST_PREC) + back_bias

def reference(tokens, lengths, key_mask, attn_gain, attn_shift, w_qkv, query_bias, value_bias, w_out, out_bias, ffn_gain, ffn_shift, w_in, in_bias, w_back, back_bias, cotangent):
    group_size = math.gcd(SEQUENCES, max(1, 2048 // LEN))
    batch_count = SEQUENCES // group_size
    weights = tuple((w.astype(jnp.float32) for w in (attn_gain, attn_shift, w_qkv, query_bias, value_bias, w_out, out_bias, ffn_gain, ffn_shift, w_in, in_bias, w_back, back_bias)))
    stacked = (tokens.reshape(batch_count, group_size, LEN, D), lengths.astype(jnp.int32).reshape(batch_count, group_size), key_mask.astype(jnp.int32).reshape(batch_count, group_size, LEN), cotangent.reshape(batch_count, group_size, LEN, D))

    def batch_step(totals, batch_item):
        inputs, seq_lengths, key_flags, cot_values = batch_item

        def run_layer(values, *params):
            return encoder_layer(values, seq_lengths, key_flags, params)
        layer_value, pullback = jax.vjp(run_layer, inputs.astype(jnp.float32), *weights)
        grads = pullback(cot_values.astype(jnp.float32))
        totals = tuple((a + b for a, b in zip(totals, grads[1:])))
        return (totals, (layer_value.astype(jnp.bfloat16), grads[0]))
    initial = tuple((jnp.zeros_like(w) for w in weights))
    totals, (outputs, input_grads) = lax.scan(batch_step, initial, stacked)
    return (outputs.reshape(SEQUENCES, LEN, D), input_grads.reshape(SEQUENCES, LEN, D), totals[0], totals[1], totals[2], totals[3], totals[4], totals[5], totals[6], totals[7], totals[8], totals[9], totals[10], totals[11], totals[12])
```

```python
import functools

import jax
import jax.numpy as jnp
from jax import lax
from jax.experimental import pallas as pl
from jax.experimental.pallas import tpu as pltpu
from jax.sharding import PartitionSpec as P

H = 12
HD = 64


NEG_FILL = -1e30
NORM_EPS = 1e-05

F32 = jnp.float32
BF16 = jnp.bfloat16
D = 768
FF = 3072
T = 1024
HALF = 512
PAIRS = 6
UNITS = 12
UW = 384
MESH = pl.DeviceIdType.MESH
VMEM_LIMIT = 60 * 1024 * 1024


def dot_nn(a, b):
    return lax.dot_general(a, b, (((1,), (0,)), ((), ())), preferred_element_type=F32)


def dot_nt(a, b):
    return lax.dot_general(a, b, (((1,), (1,)), ((), ())), preferred_element_type=F32)


def dot_tn(a, b):
    return lax.dot_general(a, b, (((0,), (0,)), ((), ())), preferred_element_type=F32)


def norm_parts(x):
    center = x - jnp.mean(x, axis=-1, keepdims=True)
    spread = jnp.mean(center * center, axis=-1, keepdims=True)
    rstd = lax.rsqrt(spread + NORM_EPS)
    return center * rstd, rstd


def norm_back(d_norm, n, rstd, gain):
    u = d_norm * gain
    mean_u = jnp.mean(u, axis=-1, keepdims=True)
    mean_un = jnp.mean(u * n, axis=-1, keepdims=True)
    return (u - mean_u - n * mean_un) * rstd


def fwd_kernel(
    len_ref, mask_ref, tok_ref, gain_ref, shift_ref, w_ref, qb_ref, vb_ref,
    nt_ref, q_ref, k_ref, v_ref, ctx_ref, lt_ref,
):
    @pl.loop(0, 4)
    def _(t):
        rows = pl.ds(pl.multiple_of(t * 256, 256), 256)
        n, _ = norm_parts(tok_ref[rows, :].astype(F32))
        normed = (n * gain_ref[...] + shift_ref[...]).astype(BF16)
        nt_ref[:, rows] = normed.T
        q_ref[rows, :] = ((dot_nn(normed, w_ref[:, :D]) + qb_ref[...]) * 0.125).astype(BF16)
        k_ref[rows, :] = dot_nn(normed, w_ref[:, D : 2 * D]).astype(BF16)
        v_ref[rows, :] = (dot_nn(normed, w_ref[:, 2 * D :]) + vb_ref[...]).astype(BF16)

    pos = lax.broadcasted_iota(jnp.int32, (1, T), 1)
    valid = (pos < len_ref[0]) & (mask_ref[...] == 1)
    bias = jnp.where(valid, 0.0, NEG_FILL).astype(F32)
    lane = lax.broadcasted_iota(jnp.int32, (1, 128), 1)
    eye = lax.broadcasted_iota(jnp.int32, (256, 256), 0) == lax.broadcasted_iota(
        jnp.int32, (256, 256), 1
    )

    @pl.loop(0, PAIRS)
    def _(p):
        cols = pl.ds(pl.multiple_of(p * 128, 128), 128)
        kp = k_ref[:, cols]
        vext = jnp.concatenate([v_ref[:, cols], jnp.ones((T, 128), BF16)], axis=1)
        kh = [jnp.where((lane < HD) == (h == 0), kp, jnp.zeros_like(kp)) for h in range(2)]
        for i in range(4):
            qi = q_ref[i * 256 : (i + 1) * 256, cols]
            outs = []
            for h in range(2):
                raw = dot_nt(qi, kh[h])
                pieces = []
                for j in range(4):
                    cut = slice(j * 256, (j + 1) * 256)
                    piece = raw[:, cut] + bias[:, cut]
                    if i == j:
                        piece = jnp.where(eye, raw[:, cut], piece)
                    pieces.append(piece)
                s = jnp.concatenate(pieces, axis=1)
                top = jnp.max(s, axis=1, keepdims=True)
                e = jnp.exp(s - top).astype(BF16)
                o = dot_nn(e, vext)
                total = o[:, 128:]
                outs.append(o[:, :128] / total)
                log_total = top + jnp.log(total)
                lt_ref[2 * p + h, :, i * 256 : (i + 1) * 256] = log_total.T[0:1, :]
            ctx_ref[i * 256 : (i + 1) * 256, cols] = jnp.where(lane < HD, outs[0], outs[1]).astype(BF16)


def blocks_of(top, bottom):
    return jnp.concatenate([top, bottom], axis=0).astype(BF16)


def place(index, first_x):
    z, y, c, x = index // 8, (index // 4) % 2, (index // 2) % 2, index % 2
    return c * 16 + z + 4 * (2 * y + x) + first_x * 4 * (x - y)


def ffn_kernel(
    tok_ref, cot_ref, ctx_ref, wo_ref, ob_ref, g_ref, s_ref, wi_ref, ib_ref, wb_ref, bb_ref,
    out_ref, dres_ref, datt_ref, grads_ref, vec_ref,
    nf_ref, act_ref, dpre_ref, dbr_ref, dn_ref, acc_ref,
):
    vec_ref[...] = jnp.zeros_like(vec_ref)

    @pl.loop(0, 4)
    def _(t):
        rows = pl.ds(pl.multiple_of(t * 256, 256), 256)
        ctx = ctx_ref[rows, :]
        res = tok_ref[rows, :].astype(F32) + dot_nn(ctx, wo_ref[...]) + ob_ref[...]
        n, rstd = norm_parts(res)
        normed = (n * g_ref[...] + s_ref[...]).astype(BF16)
        nf_ref[rows, :] = normed
        dy = cot_ref[rows, :]
        acc_ref[...] = res + bb_ref[...]
        dn_ref[...] = jnp.zeros_like(dn_ref)

        @pl.loop(0, 4)
        def _(c):
            cut = pl.ds(pl.multiple_of(c * 768, 768), 768)
            v = dot_nn(normed, wi_ref[:, cut]) + ib_ref[:, cut]
            wb = wb_ref[cut, :]
            d_act = dot_nt(dy, wb)
            sq = v * v
            th = jnp.tanh(v * (0.7978845608 + (0.7978845608 * 0.044715) * sq))
            half = 0.5 + 0.5 * th
            act = (v * half).astype(BF16)
            slope = half + v * (half * (1.0 - th)) * (
                0.7978845608 + (3 * 0.7978845608 * 0.044715) * sq
            )
            d_pre = (d_act * slope).astype(BF16)
            act_ref[rows, cut] = act
            dpre_ref[rows, cut] = d_pre
            acc_ref[...] += dot_nn(act, wb)
            dn_ref[...] += dot_nt(d_pre, wi_ref[:, cut])
            vec_ref[pl.ds(4 + c, 1), :] += jnp.sum(d_pre.astype(F32), axis=0, keepdims=True)

        out_ref[rows, :] = acc_ref[...].astype(BF16)
        d_normed = dn_ref[...]
        dyf = dy.astype(F32)
        d_res = dyf + norm_back(d_normed, n, rstd, g_ref[...])
        dres_ref[rows, :] = d_res
        d_branch = d_res.astype(BF16)
        dbr_ref[rows, :] = d_branch
        datt_ref[rows, :] = dot_nt(d_branch, wo_ref[...]).astype(BF16)
        vec_ref[0:1, :] += jnp.sum(dyf, axis=0, keepdims=True)
        vec_ref[1:2, :] += jnp.sum(d_normed * n, axis=0, keepdims=True)
        vec_ref[2:3, :] += jnp.sum(d_normed, axis=0, keepdims=True)
        vec_ref[3:4, :] += jnp.sum(d_branch.astype(F32), axis=0, keepdims=True)

    @pl.loop(0, 4)
    def _(u):
        cut = pl.ds(pl.multiple_of(u * 768, 768), 768)
        g = dot_tn(nf_ref[...], dpre_ref[:, cut])
        for r in range(32):
            rows = slice(r * 24, (r + 1) * 24)
            grads_ref[2 * u, place(r, 0)] = blocks_of(g[rows, :UW], g[rows, UW:])

    g = dot_tn(ctx_ref[...], dbr_ref[...])
    for r in range(32):
        rows = slice(r * 24, (r + 1) * 24)
        grads_ref[8, place(r, 0)] = blocks_of(g[rows, :UW], g[rows, UW:])

    @pl.loop(0, 4)
    def _(z):
        g = dot_tn(act_ref[:, pl.ds(pl.multiple_of(z * 768, 768), 768)], cot_ref[...])
        for r in range(8):
            for i in range(2):
                for j in range(2):
                    block = g[r * 96 + i * 48 : r * 96 + i * 48 + 48, j * UW : (j + 1) * UW]
                    grads_ref[4 * i + 2 * j + 1, place(r, 1) + z] = block.astype(BF16)


def bwd_kernel(
    len_ref, mask_ref, tok_ref, gain_ref, w_ref, nt_ref, q_ref, k_ref, v_ref, ctx_ref, lt_ref,
    datt_ref, dres_ref,
    dtok_ref, grads_ref, vec_ref,
    dproj_ref, dq_ref, gq_ref, delta_ref,
):
    lane = lax.broadcasted_iota(jnp.int32, (1, 128), 1)
    kpos = lax.broadcasted_iota(jnp.int32, (T, 1), 0)
    valid = (kpos < len_ref[0]) & (mask_ref[...] == 1)
    bias = jnp.where(valid, 0.0, NEG_FILL).astype(F32)
    eye = lax.broadcasted_iota(jnp.int32, (256, 256), 0) == lax.broadcasted_iota(
        jnp.int32, (256, 256), 1
    )
    head_of = lax.broadcasted_iota(jnp.int32, (8, 128), 1) // HD == lax.broadcasted_iota(
        jnp.int32, (8, 128), 0
    )
    pick = jnp.where(head_of, 1.0, 0.0).astype(F32)
    vec_ref[...] = jnp.zeros_like(vec_ref)

    @pl.loop(0, 3)
    def _(j):
        for half in range(2):
            p = 2 * j + half
            cols = pl.ds(pl.multiple_of(p * 128, 128), 128)
            qp, do = q_ref[:, cols], datt_ref[:, cols]
            prod = do.astype(F32) * ctx_ref[:, cols].astype(F32)
            delta = lax.dot_general(
                pick, prod, (((1,), (1,)), ((), ())),
                preferred_element_type=F32, precision=lax.Precision.HIGHEST,
            )
            delta_ref[...] = delta
            dq_ref[...] = jnp.zeros_like(dq_ref)
            for i in range(4):
                cut = slice(i * 256, (i + 1) * 256)
                kp, vp = k_ref[cut, cols], v_ref[cut, cols]
                dks, dvs = [], []
                for h in range(2):
                    mine = (lane < HD) == (h == 0)
                    kh = jnp.where(mine, kp, jnp.zeros_like(kp))
                    vh = jnp.where(mine, vp, jnp.zeros_like(vp))
                    raw = dot_nt(kh, qp)
                    pieces = []
                    for m in range(4):
                        piece = raw[:, m * 256 : (m + 1) * 256] + bias[cut]
                        if i == m:
                            piece = jnp.where(eye, raw[:, m * 256 : (m + 1) * 256], piece)
                        pieces.append(piece)
                    s = jnp.concatenate(pieces, axis=1)
                    e = jnp.exp(s - lt_ref[2 * p + h])
                    dvs.append(dot_nn(e.astype(BF16), do))
                    dp = dot_nt(vh, do)
                    ds = (e * (dp - delta_ref[h : h + 1, :])).astype(BF16)
                    dks.append(dot_nn(ds, qp))
                    dq_ref[...] += dot_tn(ds, kh)
                dproj_ref[3 * p + 1, cut] = jnp.where(lane < HD, dks[0], dks[1]).astype(BF16)
                dproj_ref[3 * p + 2, cut] = jnp.where(lane < HD, dvs[0], dvs[1]).astype(BF16)
            dproj_ref[3 * p] = dq_ref[...].astype(BF16) * jnp.asarray(0.125, BF16)
            d3 = jnp.concatenate([dproj_ref[3 * p + n] for n in range(3)], axis=1)
            vec_ref[0:1, cols] = jnp.sum(d3[:, :128].astype(F32), axis=0, keepdims=True)
            vec_ref[1:2, cols] = jnp.sum(d3[:, 256:].astype(F32), axis=0, keepdims=True)
            g = dot_nn(nt_ref[...], d3)
            if half == 0:
                gq_ref[...] = g
            else:
                for r in range(32):
                    rows = slice(r * 24, (r + 1) * 24)
                    grads_ref[j, place(r, (j + 1) % 2)] = blocks_of(gq_ref[rows, :], g[rows, :])

    @pl.loop(0, 4)
    def _(t):
        rows = pl.ds(pl.multiple_of(t * 256, 256), 256)
        dqs = jnp.concatenate([dproj_ref[3 * p, rows] for p in range(PAIRS)], axis=1)
        dks = jnp.concatenate([dproj_ref[3 * p + 1, rows] for p in range(PAIRS)], axis=1)
        dvs = jnp.concatenate([dproj_ref[3 * p + 2, rows] for p in range(PAIRS)], axis=1)
        d_normed = (
            dot_nt(dqs, w_ref[:, :D]) + dot_nt(dks, w_ref[:, D : 2 * D]) + dot_nt(dvs, w_ref[:, 2 * D :])
        )
        n, rstd = norm_parts(tok_ref[rows, :].astype(F32))
        dtok_ref[rows, :] = dres_ref[rows, :] + norm_back(d_normed, n, rstd, gain_ref[...])
        vec_ref[2:3, :] += jnp.sum(d_normed * n, axis=0, keepdims=True)
        vec_ref[3:4, :] += jnp.sum(d_normed, axis=0, keepdims=True)


def rs_kernel(
    gf_ref, gq_ref, vf_ref, vb_ref,
    gin_ref, gback_ref, gout_ref, gqkv_ref, vec_ref,
    r0, r1, r2, r3, vs, vr,
    s0, t0, s1, t1, s2, t2, s3, t3, sv, tv,
):
    dp, x = lax.axis_index("dp"), lax.axis_index("seq")
    z, y, c = dp // 4, (dp // 2) % 2, dp % 2
    over_c = (dp + 1 - 2 * c, x)
    over_x = (dp, 1 - x)
    over_y = (dp + 2 - 4 * y, x)
    over_z = [(lax.rem(z + d, 4) * 4 + y * 2 + c, x) for d in (1, 2, 3)]
    barrier = pltpu.get_barrier_semaphore()
    for to in (over_c, over_x, over_y, *over_z):
        pl.semaphore_signal(barrier, inc=1, device_id=to, device_id_type=MESH)
    pl.semaphore_wait(barrier, 6)

    def copy(src, dst, send, recv, to):
        return pltpu.make_async_remote_copy(
            src_ref=src, dst_ref=dst, send_sem=send, recv_sem=recv, device_id=to, device_id_type=MESH
        )

    def hop0(u, g, v):
        return copy(g.at[v, pl.ds((1 - c) * 16, 16)], r0.at[u], s0.at[u], t0.at[u], over_c)

    def axes(u):
        fx = u % 2
        first = (dp + (1 - fx) * (2 - 4 * y), x + fx * (1 - 2 * x))
        second = (dp + fx * (2 - 4 * y), x + (1 - fx) * (1 - 2 * x))
        return first, second, y + fx * (x - y), x + fx * (y - x)

    def hop1(u):
        first, _, a, _ = axes(u)
        return copy(r0.at[u, pl.ds((1 - a) * 8, 8)], r1.at[u], s1.at[u], t1.at[u], first)

    def hop2(u):
        _, second, _, b = axes(u)
        return copy(r1.at[u, pl.ds((1 - b) * 4, 4)], r2.at[u], s2.at[u], t2.at[u], second)

    def hop3(u, d):
        to = lax.rem(z + d + 1, 4)
        return copy(r2.at[u, to], r3.at[u, d], s3.at[u, d], t3.at[u, d], over_z[d])

    def vhop(n, to):
        src = vs.at[min(n, 3)]
        return copy(src, vr.at[n], sv.at[n], tv.at[n], to)

    hops = [over_c, over_x, over_y, *over_z]
    vs[0, :8] = vf_ref[...]
    vs[0, 8:] = vb_ref[...]
    vhop(0, hops[0]).start()

    @pl.loop(0, 9)
    def _(u):
        hop0(u, gf_ref, u).start()

    @pl.loop(0, 3)
    def _(u):
        hop0(u + 9, gq_ref, u).start()

    def one(u, g, v):
        hop0(u, g, v).wait_recv()

        @pl.loop(0, 16)
        def _(k):
            r0[u, k] = (r0[u, k].astype(F32) + g[v, c * 16 + k].astype(F32)).astype(BF16)

        hop1(u).start()

    @pl.loop(0, 9)
    def _(u):
        one(u, gf_ref, u)

    @pl.loop(0, 3)
    def _(u):
        one(u + 9, gq_ref, u)

    for n in range(2):
        vhop(n, hops[n]).wait_recv()
        vs[n + 1] = vs[n] + vr[n]
        vhop(n + 1, hops[n + 1]).start()

    @pl.loop(0, UNITS)
    def _(u):
        hop1(u).wait_recv()
        _, _, a, _ = axes(u)

        @pl.loop(0, 8)
        def _(k):
            r1[u, k] = (r1[u, k].astype(F32) + r0[u, a * 8 + k].astype(F32)).astype(BF16)

        hop2(u).start()

    vhop(2, hops[2]).wait_recv()
    vs[3] = vs[2] + vr[2]
    for d in range(3):
        vhop(3 + d, hops[3 + d]).start()

    @pl.loop(0, UNITS)
    def _(u):
        hop2(u).wait_recv()
        _, _, _, b = axes(u)

        @pl.loop(0, 4)
        def _(k):
            r2[u, k] = (r2[u, k].astype(F32) + r1[u, b * 4 + k].astype(F32)).astype(BF16)

        for d in range(3):
            hop3(u, d).start()

    for u in range(UNITS):
        total = r2[u, z].astype(F32)
        for d in range(3):
            hop3(u, d).wait_recv()
            total = total + r3[u, d].astype(F32)
        if u == 8:
            gout_ref[:, :UW] = total[:24]
            gout_ref[:, UW:] = total[24:]
        elif u > 8:
            for half in range(2):
                p = 2 * (u - 9) + half
                for n in range(3):
                    at = n * D + p * 128
                    gqkv_ref[:, at : at + 128] = total[half * 24 : half * 24 + 24, n * 128 : n * 128 + 128]
        elif u % 2 == 0:
            at = (u // 2) * 768
            gin_ref[:, at : at + UW] = total[:24]
            gin_ref[:, at + UW : at + 2 * UW] = total[24:]
        else:
            i, j = u // 4, (u // 2) % 2
            gback_ref[i * 48 : i * 48 + 48, j * UW : (j + 1) * UW] = total
    total = vs[3]
    for d in range(3):
        vhop(3 + d, hops[3 + d]).wait_recv()
        total = total + vr[3 + d]
    vec_ref[...] = total

    @pl.loop(0, 9)
    def _(u):
        hop0(u, gf_ref, u).wait_send()

    @pl.loop(0, 3)
    def _(u):
        hop0(u + 9, gq_ref, u).wait_send()

    @pl.loop(0, UNITS)
    def _(u):
        hop1(u).wait_send()
        hop2(u).wait_send()
        for d in range(3):
            hop3(u, d).wait_send()

    for n in range(6):
        vhop(n, hops[n]).wait_send()


VM = pl.BlockSpec(memory_space=pltpu.VMEM)
SM = pl.BlockSpec(memory_space=pltpu.SMEM)


def shape(dims, dtype):
    return jax.ShapeDtypeStruct(dims, dtype)


def call_fwd(length, mask, tok, gain, shift, w_qkv, qb, vb):
    low = shape((T, D), BF16)
    return pl.pallas_call(
        fwd_kernel,
        out_shape=(shape((D, T), BF16), low, low, low, low, shape((H, 1, T), F32)),
        in_specs=[SM] + [VM] * 7,
        out_specs=(VM,) * 6,
        compiler_params=pltpu.CompilerParams(vmem_limit_bytes=VMEM_LIMIT),
    )(length, mask, tok, gain, shift, w_qkv, qb, vb)


def call_ffn(*args):
    low = shape((T, D), BF16)
    return pl.pallas_call(
        ffn_kernel,
        out_shape=(
            low, shape((T, D), F32), low, shape((9, 32, 48, UW), BF16), shape((8, D), F32),
        ),
        in_specs=[VM] * 11,
        out_specs=(VM,) * 5,
        scratch_shapes=[
            pltpu.VMEM((T, D), BF16),
            pltpu.VMEM((T, FF), BF16),
            pltpu.VMEM((T, FF), BF16),
            pltpu.VMEM((T, D), BF16),
            pltpu.VMEM((256, D), F32),
            pltpu.VMEM((256, D), F32),
        ],
        compiler_params=pltpu.CompilerParams(vmem_limit_bytes=VMEM_LIMIT),
    )(*args)


def call_bwd(*args):
    return pl.pallas_call(
        bwd_kernel,
        out_shape=(shape((T, D), F32), shape((3, 32, 48, UW), BF16), shape((8, D), F32)),
        in_specs=[SM] + [VM] * 12,
        out_specs=(VM,) * 3,
        scratch_shapes=[
            pltpu.VMEM((18, T, 128), BF16),
            pltpu.VMEM((T, 128), F32),
            pltpu.VMEM((D, UW), F32),
            pltpu.VMEM((8, T), F32),
        ],
        compiler_params=pltpu.CompilerParams(vmem_limit_bytes=VMEM_LIMIT),
    )(*args)


def call_rs(gf, gq, vf, vb):
    dma = pltpu.SemaphoreType.DMA
    return pl.pallas_call(
        rs_kernel,
        out_shape=(
            shape((24, FF), F32), shape((96, D), F32), shape((24, D), F32), shape((24, 3 * D), F32),
            shape((16, D), F32),
        ),
        in_specs=[VM] * 4,
        out_specs=(VM,) * 5,
        scratch_shapes=[
            pltpu.VMEM((UNITS, 16, 48, UW), BF16),
            pltpu.VMEM((UNITS, 8, 48, UW), BF16),
            pltpu.VMEM((UNITS, 4, 48, UW), BF16),
            pltpu.VMEM((UNITS, 3, 48, UW), BF16),
            pltpu.VMEM((4, 16, D), F32),
            pltpu.VMEM((6, 16, D), F32),
            dma((UNITS,)), dma((UNITS,)), dma((UNITS,)), dma((UNITS,)), dma((UNITS,)), dma((UNITS,)),
            dma((UNITS, 3)), dma((UNITS, 3)), dma((6,)), dma((6,)),
        ],
        compiler_params=pltpu.CompilerParams(
            vmem_limit_bytes=VMEM_LIMIT, collective_id=0, has_side_effects=True
        ),
    )(gf, gq, vf, vb)


def whole_sequences(
    tokens, lengths, key_mask, attn_gain, attn_shift, w_qkv, query_bias, value_bias, w_out,
    out_bias, ffn_gain, ffn_shift, w_in, in_bias, w_back, back_bias, cotangent,
):
    x = lax.axis_index("seq")
    swap = [(0, 1), (1, 0)]

    def gather(rows):
        own = lax.dynamic_index_in_dim(rows, x, 0, keepdims=False)
        other = lax.dynamic_index_in_dim(rows, 1 - x, 0, keepdims=False)
        got = lax.ppermute(other, "seq", swap)
        return jnp.concatenate([jnp.where(x == 0, own, got), jnp.where(x == 0, got, own)], axis=0)

    def spread(rows):
        own = lax.dynamic_slice_in_dim(rows, x * HALF, HALF, 0)
        other = lax.dynamic_slice_in_dim(rows, (1 - x) * HALF, HALF, 0).astype(BF16)
        got = lax.ppermute(other, "seq", swap).astype(rows.dtype)
        return jnp.stack([jnp.where(x == 0, own, got), jnp.where(x == 0, got, own)], axis=0)

    def row(vector):
        return vector.reshape(1, -1)

    tok = gather(tokens)
    mask = gather(key_mask)
    length = lax.dynamic_slice_in_dim(lengths, x, 1)
    normed_t, q, k, v, ctx, log_total = call_fwd(
        length, row(mask), tok, row(attn_gain), row(attn_shift), w_qkv, row(query_bias), row(value_bias)
    )
    cotangent, _ = lax.optimization_barrier((cotangent, tok))
    cot = gather(cotangent)
    out, d_res, d_att, gf, vf = call_ffn(
        tok, cot, ctx, w_out, row(out_bias), row(ffn_gain), row(ffn_shift), w_in, row(in_bias),
        w_back, row(back_bias),
    )
    layer_out = spread(out)
    d_tok, gq, vb = call_bwd(
        length, mask.reshape(T, 1), tok, row(attn_gain), w_qkv, normed_t, q, k, v, ctx, log_total,
        d_att, d_res,
    )
    grad_tokens = spread(d_tok)
    g_in, g_back, g_out, g_qkv, vec = call_rs(gf, gq, vf, vb)
    rank = lax.axis_index("dp") * 2 + x
    mine = lax.dynamic_slice(vec, (0, rank * 24), (16, 24))
    ib = lax.dynamic_slice(vec, (4 + rank // 8, (rank % 8) * 96), (1, 96)).reshape(96)
    return (
        layer_out, grad_tokens, mine[10], mine[11], g_qkv, mine[8], mine[9], g_out, mine[3],
        mine[1], mine[2], g_in, ib, g_back, mine[0],
    )


def shifted(array, axis, by):
    devices = lax.axis_size(axis)
    return lax.ppermute(array, axis, [(i, (i + by) % devices) for i in range(devices)])


def layer_norm(values, gain, shift):
    center = values - jnp.mean(values, axis=-1, keepdims=True)
    spread = jnp.mean(center * center, axis=-1, keepdims=True)
    return center * lax.rsqrt(spread + NORM_EPS) * gain + shift


def partial_gelu(values):
    return jax.nn.gelu(values, approximate=True)


def outer_product(left, right):
    return lax.dot_general(
        left, right, (((0,), (0,)), ((), ())), preferred_element_type=jnp.float32
    )


def times_transposed(left, right):
    return lax.dot_general(
        left, right, (((1,), (1,)), ((), ())), preferred_element_type=jnp.float32
    )


def allowed_keys(lengths, flags_all, query_pos, first_key, key_count):
    key_pos = first_key + jnp.arange(key_count, dtype=jnp.int32)
    key_flags = lax.dynamic_slice_in_dim(flags_all, first_key, key_count, 1)
    key_valid = (key_pos[None, :] < lengths[:, None]) & (key_flags == 1)
    itself = key_pos[None, :] == query_pos[:, None]
    return key_valid[:, None, None, :] | itself[None, :, None, :]


def send_home(partial_grads):
    return shifted(partial_grads.astype(jnp.bfloat16), "seq", 1).astype(partial_grads.dtype)


def shards(
    tokens,
    lengths,
    key_mask,
    attn_gain,
    attn_shift,
    w_qkv,
    query_bias,
    value_bias,
    w_out,
    out_bias,
    ffn_gain,
    ffn_shift,
    w_in,
    in_bias,
    w_back,
    back_bias,
    cotangent,
):
    seq_count, span_dev, model_width = tokens.shape
    row_count = seq_count * span_dev
    members = lax.axis_size("seq")
    own_index = lax.axis_index("seq")
    query_pos = own_index * span_dev + jnp.arange(span_dev, dtype=jnp.int32)
    flags_all = lax.all_gather(key_mask, "seq", axis=1, tiled=True)
    inputs = tokens.astype(jnp.float32).reshape(row_count, model_width)
    normed_one, norm_pull_one = jax.vjp(layer_norm, inputs, attn_gain, attn_shift)
    normed_attn = normed_one.astype(jnp.bfloat16)
    projected = jnp.dot(normed_attn, w_qkv, preferred_element_type=jnp.float32)
    queries = ((projected[:, :model_width] + query_bias) * 0.125).astype(jnp.bfloat16)
    queries = queries.reshape(seq_count, span_dev, H, HD)
    keyval = jnp.concatenate(
        [projected[:, model_width : 2 * model_width], projected[:, 2 * model_width :] + value_bias],
        axis=1,
    ).astype(jnp.bfloat16)
    keyval = keyval.reshape(seq_count, span_dev, 2 * model_width)

    def split_block(block_kv):
        key_count = block_kv.shape[1]
        key_heads = block_kv[:, :, :model_width].reshape(seq_count, key_count, H, HD)
        value_heads = block_kv[:, :, model_width:].reshape(seq_count, key_count, H, HD)
        return (key_count, key_heads, value_heads)

    running_max = jnp.full((seq_count, span_dev, H), NEG_FILL, jnp.float32)
    key_count, key_heads, value_heads = split_block(
        lax.all_gather(keyval, "seq", axis=1, tiled=True)
    )
    scores = jnp.einsum("sqhd,skhd->sqhk", queries, key_heads, preferred_element_type=jnp.float32)
    allowed = allowed_keys(lengths, flags_all, query_pos, jnp.int32(0), key_count)
    new_max = jnp.maximum(running_max, jnp.max(jnp.where(allowed, scores, NEG_FILL), axis=-1))
    expo = jnp.exp(jnp.where(allowed, scores - new_max[..., None], NEG_FILL))
    running_sum = jnp.sum(expo, axis=-1)
    running_acc = jnp.einsum(
        "sqhk,skhd->sqhd",
        expo.astype(jnp.bfloat16),
        value_heads,
        preferred_element_type=jnp.float32,
    )
    attended = running_acc / running_sum[..., None]
    log_total = new_max + jnp.log(running_sum)
    context = attended.reshape(row_count, model_width).astype(jnp.bfloat16)
    residual = inputs + jnp.dot(context, w_out, preferred_element_type=jnp.float32) + out_bias
    normed_two, norm_pull_two = jax.vjp(layer_norm, residual, ffn_gain, ffn_shift)
    normed_ffn = normed_two.astype(jnp.bfloat16)
    pre_act = jnp.dot(normed_ffn, w_in, preferred_element_type=jnp.float32) + in_bias
    gelu_value, gelu_pull = jax.vjp(partial_gelu, pre_act)
    activated = gelu_value.astype(jnp.bfloat16)
    layer_out = (
        residual + jnp.dot(activated, w_back, preferred_element_type=jnp.float32) + back_bias
    )
    grad_rows = cotangent.reshape(row_count, model_width)
    grad_float = grad_rows.astype(jnp.float32)
    grad_back_bias = jnp.sum(grad_float, axis=0)
    grad_w_back = outer_product(activated, grad_rows)
    d_act = times_transposed(grad_rows, w_back)
    d_pre = gelu_pull(d_act)[0].astype(jnp.bfloat16)
    grad_in_bias = jnp.sum(d_pre.astype(jnp.float32), axis=0)
    grad_w_in = outer_product(normed_ffn, d_pre)
    d_normed = times_transposed(d_pre, w_in)
    d_res_part, grad_ffn_gain, grad_ffn_shift = norm_pull_two(d_normed)
    d_residual = grad_float + d_res_part
    d_branch = d_residual.astype(jnp.bfloat16)
    grad_out_bias = jnp.sum(d_branch.astype(jnp.float32), axis=0)
    grad_w_out = outer_product(context, d_branch)
    d_attended = (
        times_transposed(d_branch, w_out).astype(jnp.bfloat16).reshape(seq_count, span_dev, H, HD)
    )
    delta = jnp.sum(d_attended.astype(jnp.float32) * attended, axis=-1)

    def attend_back(block_kv, first_key):
        key_count, key_heads, value_heads = split_block(block_kv)
        scores = jnp.einsum(
            "sqhd,skhd->sqhk", queries, key_heads, preferred_element_type=jnp.float32
        )
        allowed = allowed_keys(lengths, flags_all, query_pos, first_key, key_count)
        weights_f = jnp.exp(jnp.where(allowed, scores - log_total[..., None], NEG_FILL))
        d_values = jnp.einsum(
            "sqhk,sqhd->skhd",
            weights_f.astype(jnp.bfloat16),
            d_attended,
            preferred_element_type=jnp.float32,
        )
        d_probs = jnp.einsum(
            "sqhd,skhd->sqhk", d_attended, value_heads, preferred_element_type=jnp.float32
        )
        d_scores = (weights_f * (d_probs - delta[..., None])).astype(jnp.bfloat16)
        d_query = jnp.einsum(
            "sqhk,skhd->sqhd", d_scores, key_heads, preferred_element_type=jnp.float32
        )
        d_keys = jnp.einsum(
            "sqhk,sqhd->skhd", d_scores, queries, preferred_element_type=jnp.float32
        )
        d_block = jnp.concatenate(
            [
                d_keys.reshape(seq_count, key_count, model_width),
                d_values.reshape(seq_count, key_count, model_width),
            ],
            axis=2,
        )
        return (d_query, d_block)

    zero_query = jnp.zeros((seq_count, span_dev, H, HD), jnp.float32)

    def turn(turn_index, state_now):
        current, d_current, d_query = state_now
        anchor = (own_index - turn_index) % members
        add_query, add_block = attend_back(current, anchor * span_dev)
        current = shifted(current, "seq", 1)
        return (current, send_home(d_current + add_block), d_query + add_query)

    start_back = (
        keyval,
        jnp.zeros((seq_count, span_dev, 2 * model_width), jnp.float32),
        zero_query,
    )
    current, d_current, d_query = lax.fori_loop(0, members - 1, turn, start_back)
    anchor = (own_index - (members - 1)) % members
    add_query, add_block = attend_back(current, anchor * span_dev)
    d_query = d_query + add_query
    d_keyval = send_home(d_current + add_block)
    d_query_low = d_query.reshape(row_count, model_width).astype(jnp.bfloat16)
    d_keyval_low = d_keyval.reshape(row_count, 2 * model_width).astype(jnp.bfloat16)
    query_scaled = d_query_low.astype(jnp.float32) * 0.125
    grad_query_bias = jnp.sum(query_scaled, axis=0)
    grad_value_bias = jnp.sum(d_keyval_low[:, model_width:].astype(jnp.float32), axis=0)
    d_projected = jnp.concatenate([query_scaled.astype(jnp.bfloat16), d_keyval_low], axis=1)
    grad_w_qkv = outer_product(normed_attn, d_projected)
    d_normed_attn = times_transposed(d_projected, w_qkv)
    d_in_part, grad_attn_gain, grad_attn_shift = norm_pull_one(d_normed_attn)
    grad_tokens = (d_residual + d_in_part).reshape(seq_count, span_dev, model_width)
    out_block = layer_out.astype(jnp.bfloat16).reshape(seq_count, span_dev, model_width)
    all_sums = (
        lax.psum_scatter(grad_attn_gain, ("dp", "seq"), scatter_dimension=0, tiled=True),
        lax.psum_scatter(grad_attn_shift, ("dp", "seq"), scatter_dimension=0, tiled=True),
        lax.psum_scatter(grad_w_qkv, ("dp", "seq"), scatter_dimension=0, tiled=True),
        lax.psum_scatter(grad_query_bias, ("dp", "seq"), scatter_dimension=0, tiled=True),
        lax.psum_scatter(grad_value_bias, ("dp", "seq"), scatter_dimension=0, tiled=True),
        lax.psum_scatter(grad_w_out, ("dp", "seq"), scatter_dimension=0, tiled=True),
        lax.psum_scatter(grad_out_bias, ("dp", "seq"), scatter_dimension=0, tiled=True),
        lax.psum_scatter(grad_ffn_gain, ("dp", "seq"), scatter_dimension=0, tiled=True),
        lax.psum_scatter(grad_ffn_shift, ("dp", "seq"), scatter_dimension=0, tiled=True),
        lax.psum_scatter(grad_w_in, ("dp", "seq"), scatter_dimension=0, tiled=True),
        lax.psum_scatter(grad_in_bias, ("dp", "seq"), scatter_dimension=0, tiled=True),
        lax.psum_scatter(grad_w_back, ("dp", "seq"), scatter_dimension=0, tiled=True),
        lax.psum_scatter(grad_back_bias, ("dp", "seq"), scatter_dimension=0, tiled=True),
    )
    return (
        out_block,
        grad_tokens,
        all_sums[0],
        all_sums[1],
        all_sums[2],
        all_sums[3],
        all_sums[4],
        all_sums[5],
        all_sums[6],
        all_sums[7],
        all_sums[8],
        all_sums[9],
        all_sums[10],
        all_sums[11],
        all_sums[12],
    )


def solution(mesh):
    sizes = dict(mesh.shape)
    whole = sizes == {"dp": 16, "seq": 2}
    return jax.shard_map(
        whole_sequences if whole else shards,
        mesh=mesh,
        in_specs=(
            P("dp", "seq", None),
            P("dp"),
            P("dp", "seq"),
            P(),
            P(),
            P(),
            P(),
            P(),
            P(),
            P(),
            P(),
            P(),
            P(),
            P(),
            P(),
            P(),
            P("dp", "seq", None),
        ),
        out_specs=(
            P("dp", "seq", None),
            P("dp", "seq", None),
            P(("dp", "seq")),
            P(("dp", "seq")),
            P(("dp", "seq"), None),
            P(("dp", "seq")),
            P(("dp", "seq")),
            P(("dp", "seq"), None),
            P(("dp", "seq")),
            P(("dp", "seq")),
            P(("dp", "seq")),
            P(("dp", "seq"), None),
            P(("dp", "seq")),
            P(("dp", "seq"), None),
            P(("dp", "seq")),
        ),
        check_vma=False,
    )
```

```python
import functools

import jax
import jax.numpy as jnp
from jax import lax
from jax.experimental import pallas as pl
from jax.experimental.pallas import tpu as pltpu
from jax.sharding import PartitionSpec as P

H = 12
HD = 64


NEG_FILL = -1e30
NORM_EPS = 1e-05

F32 = jnp.float32
BF16 = jnp.bfloat16
D = 768
FF = 3072
T = 1024
HALF = 512
PAIRS = 6
UW = 384
MESH = pl.DeviceIdType.MESH
VMEM_LIMIT = 60 * 1024 * 1024


def dot_nn(a, b):
    return lax.dot_general(a, b, (((1,), (0,)), ((), ())), preferred_element_type=F32)


def dot_nt(a, b):
    return lax.dot_general(a, b, (((1,), (1,)), ((), ())), preferred_element_type=F32)


def dot_tn(a, b):
    return lax.dot_general(a, b, (((0,), (0,)), ((), ())), preferred_element_type=F32)


def shape(dims, dtype):
    return jax.ShapeDtypeStruct(dims, dtype)


VM = pl.BlockSpec(memory_space=pltpu.VMEM)
SM = pl.BlockSpec(memory_space=pltpu.SMEM)
HB = pl.BlockSpec(memory_space=pl.ANY)
DMA = pltpu.SemaphoreType.DMA


def norm_parts(x):
    center = x - jnp.mean(x, axis=-1, keepdims=True)
    spread = jnp.mean(center * center, axis=-1, keepdims=True)
    rstd = lax.rsqrt(spread + NORM_EPS)
    return center * rstd, rstd


def norm_back(d_norm, n, rstd, gain):
    u = d_norm * gain
    mean_u = jnp.mean(u, axis=-1, keepdims=True)
    mean_un = jnp.mean(u * n, axis=-1, keepdims=True)
    return (u - mean_u - n * mean_un) * rstd


def fwd_kernel(
    len_ref, mask_ref, tok_ref, gain_ref, shift_ref, w_ref, qb_ref, vb_ref,
    nt_ref, q_ref, k_ref, v_ref, ctx_ref, lt_ref,
):
    @pl.loop(0, 4)
    def _(t):
        rows = pl.ds(pl.multiple_of(t * 256, 256), 256)
        n, _ = norm_parts(tok_ref[rows, :].astype(F32))
        normed = (n * gain_ref[...] + shift_ref[...]).astype(BF16)
        nt_ref[:, rows] = normed.T
        q_ref[rows, :] = ((dot_nn(normed, w_ref[:, :D]) + qb_ref[...]) * 0.125).astype(BF16)
        k_ref[rows, :] = dot_nn(normed, w_ref[:, D : 2 * D]).astype(BF16)
        v_ref[rows, :] = (dot_nn(normed, w_ref[:, 2 * D :]) + vb_ref[...]).astype(BF16)

    pos = lax.broadcasted_iota(jnp.int32, (1, T), 1)
    valid = (pos < len_ref[0]) & (mask_ref[...] == 1)
    bias = jnp.where(valid, 0.0, NEG_FILL).astype(F32)
    lane = lax.broadcasted_iota(jnp.int32, (1, 128), 1)
    eye = lax.broadcasted_iota(jnp.int32, (256, 256), 0) == lax.broadcasted_iota(
        jnp.int32, (256, 256), 1
    )

    @pl.loop(0, PAIRS)
    def _(p):
        cols = pl.ds(pl.multiple_of(p * 128, 128), 128)
        kp = k_ref[:, cols]
        vext = jnp.concatenate([v_ref[:, cols], jnp.ones((T, 128), BF16)], axis=1)
        kh = [jnp.where((lane < HD) == (h == 0), kp, jnp.zeros_like(kp)) for h in range(2)]
        for i in range(4):
            qi = q_ref[i * 256 : (i + 1) * 256, cols]
            outs = []
            for h in range(2):
                raw = dot_nt(qi, kh[h])
                pieces = []
                for j in range(4):
                    cut = slice(j * 256, (j + 1) * 256)
                    piece = raw[:, cut] + bias[:, cut]
                    if i == j:
                        piece = jnp.where(eye, raw[:, cut], piece)
                    pieces.append(piece)
                s = jnp.concatenate(pieces, axis=1)
                top = jnp.max(s, axis=1, keepdims=True)
                e = jnp.exp(s - top).astype(BF16)
                o = dot_nn(e, vext)
                total = o[:, 128:]
                outs.append(o[:, :128] / total)
                log_total = top + jnp.log(total)
                lt_ref[2 * p + h, :, i * 256 : (i + 1) * 256] = log_total.T[0:1, :]
            ctx_ref[i * 256 : (i + 1) * 256, cols] = jnp.where(lane < HD, outs[0], outs[1]).astype(BF16)


def blocks_of(top, bottom):
    return jnp.concatenate([top, bottom], axis=0).astype(BF16)


def place(index, first_x):
    z, y, c, x = index // 8, (index // 4) % 2, (index // 2) % 2, index % 2
    return c * 16 + z + 4 * (2 * y + x) + first_x * 4 * (x - y)


def reduction_scratch(units):
    sems = [DMA((units,)), DMA((units,)), DMA((units,)), DMA((units, 3))]
    return [pltpu.VMEM((units, n, 48, UW), BF16) for n in (16, 8, 4, 3)] + sems + sems


class Reduction:
    def __init__(self, units, x_first, own, parts, sums, held, sems):
        self.units, self.x_first = units, x_first
        self.own, self.parts, self.sums, self.held = own, parts, sums, held
        self.sends, self.recvs = sems[:4], sems[4:8]
        dp, x = lax.axis_index("dp"), lax.axis_index("seq")
        z, y, c = dp // 4, (dp // 2) % 2, dp % 2
        self.dp, self.x, self.y, self.z, self.c = dp, x, y, z, c
        self.over_c = (dp + 1 - 2 * c, x)
        self.over_x = (dp, 1 - x)
        self.over_y = (dp + 2 - 4 * y, x)
        self.over_z = [(lax.rem(z + d, 4) * 4 + y * 2 + c, x) for d in (1, 2, 3)]

    def barrier(self):
        sem = pltpu.get_barrier_semaphore()
        for to in (self.over_c, self.over_x, self.over_y, *self.over_z):
            pl.semaphore_signal(sem, inc=1, device_id=to, device_id_type=MESH)
        pl.semaphore_wait(sem, 6)

    def copy(self, src, dst, send, recv, to):
        return pltpu.make_async_remote_copy(
            src_ref=src, dst_ref=dst, send_sem=send, recv_sem=recv, device_id=to, device_id_type=MESH
        )

    def axes(self, u):
        fx, x, y, dp = self.x_first(u), self.x, self.y, self.dp
        first = (dp + (1 - fx) * (2 - 4 * y), x + fx * (1 - 2 * x))
        second = (dp + fx * (2 - 4 * y), x + (1 - fx) * (1 - 2 * x))
        return first, second, y + fx * (x - y), x + fx * (y - x)

    def hop0(self, u):
        src = self.parts(u).at[pl.ds((1 - self.c) * 16, 16)]
        return self.copy(src, self.held[0].at[u], self.sends[0].at[u], self.recvs[0].at[u], self.over_c)

    def hop1(self, u):
        first, _, a, _ = self.axes(u)
        src = self.held[0].at[u, pl.ds((1 - a) * 8, 8)]
        return self.copy(src, self.held[1].at[u], self.sends[1].at[u], self.recvs[1].at[u], first)

    def hop2(self, u):
        _, second, _, b = self.axes(u)
        src = self.held[1].at[u, pl.ds((1 - b) * 4, 4)]
        return self.copy(src, self.held[2].at[u], self.sends[2].at[u], self.recvs[2].at[u], second)

    def hop3(self, u, d):
        src = self.held[2].at[u, lax.rem(self.z + d + 1, 4)]
        return self.copy(
            src, self.held[3].at[u, d], self.sends[3].at[u, d], self.recvs[3].at[u, d], self.over_z[d]
        )

    def arrived(self, u):
        held = self.held[0].at[u]
        self.copy(held, held, self.sends[0].at[u], self.recvs[0].at[u], self.over_c).wait_recv()

    def start(self, u):
        self.hop0(u).start()

    def step1(self, u):
        self.arrived(u)
        _, _, a, _ = self.axes(u)
        held = self.held[0]

        def add(k):
            held[u, k] = (held[u, k].astype(F32) + self.own(u, k).astype(F32)).astype(BF16)

        @pl.loop(0, 8, unroll=2)
        def _(k):
            add((1 - a) * 8 + k)

        self.hop1(u).start()

        @pl.loop(0, 8, unroll=2)
        def _(k):
            add(a * 8 + k)

    def step2(self, u):
        self.hop1(u).wait_recv()
        _, _, a, b = self.axes(u)
        held, before = self.held[1], self.held[0]

        def add(k):
            held[u, k] = (held[u, k].astype(F32) + before[u, a * 8 + k].astype(F32)).astype(BF16)

        for k in range(4):
            add((1 - b) * 4 + k)
        self.hop2(u).start()
        for k in range(4):
            add(b * 4 + k)

    def step3(self, u):
        self.hop2(u).wait_recv()
        _, _, _, b = self.axes(u)
        held, before = self.held[2], self.held[1]
        for k in range(4):
            held[u, k] = (held[u, k].astype(F32) + before[u, b * 4 + k].astype(F32)).astype(BF16)
        for d in range(3):
            self.hop3(u, d).start()

    def finish(self, u):
        total = self.held[2][u, self.z].astype(F32)
        for d in range(3):
            self.hop3(u, d).wait_recv()
            total = total + self.held[3][u, d].astype(F32)
        self.sums[u] = total

    def drain(self):
        for u in range(self.units):
            self.hop0(u).wait_send()
            self.hop1(u).wait_send()
            self.hop2(u).wait_send()
            for d in range(3):
                self.hop3(u, d).wait_send()


def x_first_early(unit):
    return unit % 2


def x_first_late(unit):
    return (unit + 1) % 2


def ffn_kernel(
    tok_ref, cot_ref, ctx_ref, ob_ref, g_ref, s_ref, ib_ref, bb_ref, wo_hbm, wi_hbm, wb_hbm,
    lo_ref, logot_ref, dres_hbm, datt_hbm, grads_hbm, vec_ref, sums_ref,
    wo_ref, wi_ref, wb_ref, nf_ref, act_ref, dpre_ref, dbr_ref, res_ref, dn_ref, away_ref, datt_ref,
    parts_ref, grads_ref, sw, so, sx, tx, *reds,
):
    def parts(u):
        return parts_ref.at[u]

    def own_block(u, k):
        return parts_ref[u, red.c * 16 + k]

    red = Reduction(4, x_first_early, own_block, parts, sums_ref, reds[:4], reds[4:])
    x = red.x
    loads = [pltpu.make_async_copy(wo_hbm, wo_ref, sw.at[0])]
    for c in range(4):
        cut = pl.ds(c * 768, 768)
        loads.append(pltpu.make_async_copy(wi_hbm.at[:, cut], wi_ref.at[:, cut], sw.at[1 + 2 * c]))
        loads.append(pltpu.make_async_copy(wb_hbm.at[cut], wb_ref.at[cut], sw.at[2 + 2 * c]))
    for load in loads:
        load.start()
    red.barrier()
    vec_ref[...] = jnp.zeros_like(vec_ref)
    loads[0].wait()
    lo_copy = red.copy(away_ref, logot_ref, sx, tx, red.over_x)

    def rows_of(t):
        return pl.ds(pl.multiple_of(lax.rem((1 - x) * HALF + t * 256, T), 256), 256)

    @pl.loop(0, 4)
    def _(t):
        rows = rows_of(t)
        res = tok_ref[rows, :].astype(F32) + dot_nn(ctx_ref[rows, :], wo_ref[...]) + ob_ref[...]
        res_ref[rows, :] = res
        n, _ = norm_parts(res)
        normed = (n * g_ref[...] + s_ref[...]).astype(BF16)
        nf_ref[rows, :] = normed
        dn_ref[...] = res + bb_ref[...]
        for c in range(4):
            cut = slice(c * 768, (c + 1) * 768)

            @pl.when(t == 0)
            def _():
                loads[1 + 2 * c].wait()
                loads[2 + 2 * c].wait()

            v = dot_nn(normed, wi_ref[:, cut]) + ib_ref[:, cut]
            sq = v * v
            th = jnp.tanh(v * (0.7978845608 + (0.7978845608 * 0.044715) * sq))
            half = 0.5 + 0.5 * th
            act = (v * half).astype(BF16)
            slope = half + v * (half * (1.0 - th)) * (
                0.7978845608 + (3 * 0.7978845608 * 0.044715) * sq
            )
            act_ref[rows, cut] = act
            dpre_ref[rows, cut] = slope.astype(BF16)
            dn_ref[...] += dot_nn(act, wb_ref[cut, :])

        out = dn_ref[...].astype(BF16)

        @pl.when(t < 2)
        def _():
            away_ref[pl.ds(pl.multiple_of(t * 256, 256), 256)] = out

        @pl.when(t >= 2)
        def _():
            lo_ref[pl.ds(pl.multiple_of((t - 2) * 256, 256), 256)] = out

        @pl.when(t == 1)
        def _():
            lo_copy.start()

    @pl.loop(0, 4)
    def _(z):
        g = dot_tn(act_ref[:, pl.ds(pl.multiple_of(z * 768, 768), 768)], cot_ref[...])
        for r in range(8):
            for u in range(4):
                i, j = u // 2, u % 2
                block = g[r * 96 + i * 48 : r * 96 + i * 48 + 48, j * UW : (j + 1) * UW]
                parts_ref[u, place(r, x_first_early(u)) + z] = block.astype(BF16)

    for u in range(4):
        red.start(u)

    def tile_out(t, part):
        rows = rows_of(t)
        if part == 0:
            return pltpu.make_async_copy(res_ref.at[rows], dres_hbm.at[rows], so.at[2 * t])
        return pltpu.make_async_copy(datt_ref.at[rows], datt_hbm.at[rows], so.at[2 * t + 1])

    plan = {1: (1, 0), 2: (1, 1), 3: (1, 2), 4: (1, 3), 6: (2, 0), 8: (2, 1), 11: (2, 2), 13: (2, 3),
            14: (3, 0), 15: (3, 1)}

    @pl.loop(0, 4)
    def _(t):
        rows = rows_of(t)
        dy = cot_ref[rows, :]
        dn_ref[...] = jnp.zeros_like(dn_ref)
        for c in range(4):
            for at, (stage, u) in plan.items():
                if at % 4 == c:

                    @pl.when(t == at // 4)
                    def _():
                        (red.step1, red.step2, red.step3)[stage - 1](u)

            cut = slice(c * 768, (c + 1) * 768)
            d_act = dot_nt(dy, wb_ref[cut, :])
            d_pre = (d_act * dpre_ref[rows, cut].astype(F32)).astype(BF16)
            dpre_ref[rows, cut] = d_pre
            dn_ref[...] += dot_nt(d_pre, wi_ref[:, cut])
            vec_ref[4 + c : 5 + c, :] += jnp.sum(d_pre.astype(F32), axis=0, keepdims=True)

        n, rstd = norm_parts(res_ref[rows, :])
        d_normed = dn_ref[...]
        dyf = dy.astype(F32)
        d_res = dyf + norm_back(d_normed, n, rstd, g_ref[...])
        res_ref[rows, :] = d_res
        tile_out(t, 0).start()
        d_branch = d_res.astype(BF16)
        dbr_ref[rows, :] = d_branch
        datt_ref[rows, :] = dot_nt(d_branch, wo_ref[...]).astype(BF16)
        tile_out(t, 1).start()
        vec_ref[0:1, :] += jnp.sum(dyf, axis=0, keepdims=True)
        vec_ref[1:2, :] += jnp.sum(d_normed * n, axis=0, keepdims=True)
        vec_ref[2:3, :] += jnp.sum(d_normed, axis=0, keepdims=True)
        vec_ref[3:4, :] += jnp.sum(d_branch.astype(F32), axis=0, keepdims=True)

    def grads_out(u):
        return pltpu.make_async_copy(grads_ref.at[u], grads_hbm.at[u], so.at[8 + u])

    def unit(u, g):
        for r in range(32):
            rows = slice(r * 24, (r + 1) * 24)
            grads_ref[u, place(r, x_first_late(u))] = blocks_of(g[rows, :UW], g[rows, UW:])
        grads_out(u).start()

    @pl.loop(0, 4)
    def _(u):
        unit(u, dot_tn(nf_ref[...], dpre_ref[:, pl.ds(pl.multiple_of(u * 768, 768), 768)]))

        @pl.when(u == 2)
        def _():
            red.step3(2)

        @pl.when(u == 3)
        def _():
            red.step3(3)

    unit(4, dot_tn(ctx_ref[...], dbr_ref[...]))
    for u in range(4):
        red.finish(u)
    lo_copy.wait()
    red.drain()
    for t in range(4):
        tile_out(t, 0).wait()
        tile_out(t, 1).wait()
    for u in range(5):
        grads_out(u).wait()


def call_ffn(*args):
    return pl.pallas_call(
        ffn_kernel,
        out_shape=(
            shape((HALF, D), BF16), shape((HALF, D), BF16), shape((T, D), F32), shape((T, D), BF16),
            shape((5, 32, 48, UW), BF16), shape((8, D), F32), shape((4, 48, UW), F32),
        ),
        in_specs=[VM] * 8 + [HB] * 3,
        out_specs=(VM, VM, HB, HB, HB, VM, VM),
        scratch_shapes=[
            pltpu.VMEM((D, D), BF16),
            pltpu.VMEM((D, FF), BF16),
            pltpu.VMEM((FF, D), BF16),
            pltpu.VMEM((T, D), BF16),
            pltpu.VMEM((T, FF), BF16),
            pltpu.VMEM((T, FF), BF16),
            pltpu.VMEM((T, D), BF16),
            pltpu.VMEM((T, D), F32),
            pltpu.VMEM((256, D), F32),
            pltpu.VMEM((HALF, D), BF16),
            pltpu.VMEM((T, D), BF16),
            pltpu.VMEM((4, 32, 48, UW), BF16),
            pltpu.VMEM((5, 32, 48, UW), BF16),
            DMA((9,)), DMA((13,)), DMA, DMA, *reduction_scratch(4),
        ],
        compiler_params=pltpu.CompilerParams(
            vmem_limit_bytes=VMEM_LIMIT, collective_id=1, has_side_effects=True
        ),
    )(*args)


def bwd_kernel(
    len_ref, mask_ref, tok_ref, gain_ref, w_ref, nt_ref, q_ref, k_ref, v_ref, ctx_ref, lt_ref,
    datt_ref, dres_ref, vf_ref, gf_ref,
    dtok_ref, dgot_ref, sums_ref, vsum_ref,
    dproj_ref, dq_ref, gq_ref, delta_ref, own_ref, parts_ref, dsend_ref, vs_ref, vr_ref,
    sv, tv, sx, tx, so, *reds,
):
    def parts(u):
        return gf_ref.at[u] if u < 5 else parts_ref.at[u - 5]

    def own_block(u, k):
        return own_ref[u, k]

    red = Reduction(8, x_first_late, own_block, parts, sums_ref, reds[:4], reds[4:])
    x, c = red.x, red.c
    red.barrier()
    for u in range(5):
        red.start(u)
    fetch = pltpu.make_async_copy(gf_ref.at[:, pl.ds(c * 16, 16)], own_ref.at[pl.ds(0, 5)], so)
    fetch.start()

    there = pl.multiple_of((1 - x) * HALF, HALF)
    here = pl.multiple_of(x * HALF, HALF)

    def vhop(n, to):
        return red.copy(vs_ref.at[min(n, 3)], vr_ref.at[n], sv.at[n], tv.at[n], to)

    hops = [red.over_c, red.over_x, red.over_y, *red.over_z]

    lane = lax.broadcasted_iota(jnp.int32, (1, 128), 1)
    kpos = lax.broadcasted_iota(jnp.int32, (T, 1), 0)
    valid = (kpos < len_ref[0]) & (mask_ref[...] == 1)
    bias = jnp.where(valid, 0.0, NEG_FILL).astype(F32)
    eye = lax.broadcasted_iota(jnp.int32, (256, 256), 0) == lax.broadcasted_iota(
        jnp.int32, (256, 256), 1
    )
    head_of = lax.broadcasted_iota(jnp.int32, (8, 128), 1) // HD == lax.broadcasted_iota(
        jnp.int32, (8, 128), 0
    )
    pick = jnp.where(head_of, 1.0, 0.0).astype(F32)
    vs_ref[0, :8] = vf_ref[...]
    vs_ref[0, 8:] = jnp.zeros((8, D), F32)
    fetch.wait()

    def progress(j, k):
        if k % 2:
            one = 4 * j + (k - 1) // 2

            @pl.when(one < 6)
            def _():
                red.step1(one)

            three = 4 * j + (k - 11) // 2

            @pl.when((three >= 0) & (three < 6))
            def _():
                red.step3(three)
        else:
            two = 4 * j + k // 2 - 3

            @pl.when((two >= 0) & (two < 6))
            def _():
                red.step2(two)

            if k == 2:

                @pl.when(j == 2)
                def _():
                    red.step1(6)

    @pl.loop(0, 3)
    def _(j):
        for half in range(2):
            p = 2 * j + half
            cols = pl.ds(pl.multiple_of(p * 128, 128), 128)
            qp, do = q_ref[:, cols], datt_ref[:, cols]
            prod = do.astype(F32) * ctx_ref[:, cols].astype(F32)
            delta_ref[...] = lax.dot_general(
                pick, prod, (((1,), (1,)), ((), ())),
                preferred_element_type=F32, precision=lax.Precision.HIGHEST,
            )
            dq_ref[...] = jnp.zeros_like(dq_ref)
            for i in range(4):
                progress(j, half * 4 + i)
                cut = slice(i * 256, (i + 1) * 256)
                kp, vp = k_ref[cut, cols], v_ref[cut, cols]
                dks, dvs = [], []
                for h in range(2):
                    mine = (lane < HD) == (h == 0)
                    kh = jnp.where(mine, kp, jnp.zeros_like(kp))
                    vh = jnp.where(mine, vp, jnp.zeros_like(vp))
                    raw = dot_nt(kh, qp)
                    pieces = []
                    for m in range(4):
                        piece = raw[:, m * 256 : (m + 1) * 256] + bias[cut]
                        if i == m:
                            piece = jnp.where(eye, raw[:, m * 256 : (m + 1) * 256], piece)
                        pieces.append(piece)
                    s = jnp.concatenate(pieces, axis=1)
                    e = jnp.exp(s - lt_ref[2 * p + h])
                    dvs.append(dot_nn(e.astype(BF16), do))
                    dp = dot_nt(vh, do)
                    ds = (e * (dp - delta_ref[h : h + 1, :])).astype(BF16)
                    dks.append(dot_nn(ds, qp))
                    dq_ref[...] += dot_tn(ds, kh)
                dproj_ref[3 * p + 1, cut] = jnp.where(lane < HD, dks[0], dks[1]).astype(BF16)
                dproj_ref[3 * p + 2, cut] = jnp.where(lane < HD, dvs[0], dvs[1]).astype(BF16)
            dproj_ref[3 * p] = dq_ref[...].astype(BF16) * jnp.asarray(0.125, BF16)
            d3 = jnp.concatenate([dproj_ref[3 * p + n] for n in range(3)], axis=1)
            vs_ref[0, 8:9, cols] = jnp.sum(d3[:, :128].astype(F32), axis=0, keepdims=True)
            vs_ref[0, 9:10, cols] = jnp.sum(d3[:, 256:].astype(F32), axis=0, keepdims=True)
            g = dot_nn(nt_ref[...], d3)
            if half == 0:
                gq_ref[...] = g
            else:
                for r in range(32):
                    rows = slice(r * 24, (r + 1) * 24)
                    parts_ref[j, place(r, x_first_late(5 + j))] = blocks_of(gq_ref[rows, :], g[rows, :])
        own_ref[5 + j] = parts_ref[j, pl.ds(c * 16, 16)]
        for n in range(3):

            @pl.when(j == n)
            def _():
                red.start(5 + n)

    def tile(rows):
        dqs, dks, dvs = (
            jnp.concatenate([dproj_ref[3 * p + n, rows] for p in range(PAIRS)], axis=1) for n in range(3)
        )
        d_normed = (
            dot_nt(dqs, w_ref[:, :D]) + dot_nt(dks, w_ref[:, D : 2 * D]) + dot_nt(dvs, w_ref[:, 2 * D :])
        )
        n, rstd = norm_parts(tok_ref[rows, :].astype(F32))
        vs_ref[0, 10:11, :] += jnp.sum(d_normed * n, axis=0, keepdims=True)
        vs_ref[0, 11:12, :] += jnp.sum(d_normed, axis=0, keepdims=True)
        return dres_ref[rows, :] + norm_back(d_normed, n, rstd, gain_ref[...])

    def dcopy(t):
        rows = pl.ds(t * 256, 256)
        return red.copy(dsend_ref.at[rows], dgot_ref.at[rows], sx.at[t], tx.at[t], red.over_x)

    def away(t):
        dsend_ref[t * 256 : (t + 1) * 256] = tile(pl.ds(there + t * 256, 256)).astype(BF16)
        dcopy(t).start()

    def home(t):
        dtok_ref[t * 256 : (t + 1) * 256] = tile(pl.ds(here + t * 256, 256))

    away(0)
    red.step1(7)
    red.step2(6)
    away(1)
    home(0)
    home(1)
    vhop(0, hops[0]).start()
    red.step3(6)
    red.step2(7)
    vhop(0, hops[0]).wait_recv()
    vs_ref[1] = vs_ref[0] + vr_ref[0]
    vhop(1, hops[1]).start()
    for u in range(6):
        red.finish(u)
    red.step3(7)
    vhop(1, hops[1]).wait_recv()
    vs_ref[2] = vs_ref[1] + vr_ref[1]
    vhop(2, hops[2]).start()
    red.finish(6)
    vhop(2, hops[2]).wait_recv()
    vs_ref[3] = vs_ref[2] + vr_ref[2]
    for d in range(3):
        vhop(3 + d, hops[3 + d]).start()
    red.finish(7)
    total = vs_ref[3]
    for d in range(3):
        vhop(3 + d, hops[3 + d]).wait_recv()
        total = total + vr_ref[3 + d]
    vsum_ref[...] = total
    for t in range(2):
        dcopy(t).wait()
    for n in range(6):
        vhop(n, hops[n]).wait_send()
    red.drain()


def join_kernel(
    lo_ref, logot_ref, dtok_ref, dgot_ref, early_ref, late_ref, vec_ref,
    out_ref, gtok_ref, gin_ref, gback_ref, gout_ref, gqkv_ref, *rest,
):
    vouts, sem = rest[:9], rest[9]
    x = lax.axis_index("seq")
    copies = [
        pltpu.make_async_copy(lo_ref, out_ref.at[x], sem.at[0]),
        pltpu.make_async_copy(logot_ref, out_ref.at[1 - x], sem.at[1]),
        pltpu.make_async_copy(dtok_ref, gtok_ref.at[x], sem.at[2]),
    ]
    for copy in copies:
        copy.start()
    gtok_ref[1 - x] = dgot_ref[...].astype(F32)
    for u in range(4):
        gback_ref[u // 2 * 48 : u // 2 * 48 + 48, u % 2 * UW : (u % 2 + 1) * UW] = early_ref[u]
        gin_ref[:, u * D : u * D + UW] = late_ref[u, :24]
        gin_ref[:, u * D + UW : u * D + 2 * UW] = late_ref[u, 24:]
    gout_ref[:, :UW] = late_ref[4, :24]
    gout_ref[:, UW:] = late_ref[4, 24:]
    for p in range(PAIRS):
        part = late_ref[5 + p // 2, p % 2 * 24 : p % 2 * 24 + 24]
        for n in range(3):
            at = n * D + p * 128
            gqkv_ref[:, at : at + 128] = part[:, n * 128 : n * 128 + 128]
    rank = lax.axis_index("dp") * 2 + x
    mine = pltpu.roll(vec_ref[...], D - rank * 24, 1)
    for n, row in enumerate((10, 11, 8, 9, 3, 1, 2, 0)):
        vouts[n][...] = mine[row : row + 1, :24]
    z = rank // 8
    parts = pltpu.roll(vec_ref[4:8, :], D - (rank % 8) * 96, 1)
    chosen = parts[0:1, :96]
    for n in range(1, 4):
        chosen = jnp.where(z == n, parts[n : n + 1, :96], chosen)
    vouts[8][...] = chosen
    for copy in copies:
        copy.wait()


def call_bwd(*args):
    return pl.pallas_call(
        bwd_kernel,
        out_shape=(
            shape((HALF, D), F32), shape((HALF, D), BF16), shape((8, 48, UW), F32), shape((16, D), F32),
        ),
        in_specs=[SM] + [VM] * 13 + [HB],
        out_specs=(VM,) * 4,
        scratch_shapes=[
            pltpu.VMEM((18, T, 128), BF16),
            pltpu.VMEM((T, 128), F32),
            pltpu.VMEM((D, UW), F32),
            pltpu.VMEM((8, T), F32),
            pltpu.VMEM((8, 16, 48, UW), BF16),
            pltpu.VMEM((3, 32, 48, UW), BF16),
            pltpu.VMEM((HALF, D), BF16),
            pltpu.VMEM((4, 16, D), F32),
            pltpu.VMEM((6, 16, D), F32),
            DMA((6,)), DMA((6,)), DMA((2,)), DMA((2,)), DMA, *reduction_scratch(8),
        ],
        compiler_params=pltpu.CompilerParams(
            vmem_limit_bytes=VMEM_LIMIT, collective_id=0, has_side_effects=True
        ),
    )(*args)


def call_join(*args):
    return pl.pallas_call(
        join_kernel,
        out_shape=(
            shape((2, HALF, D), BF16), shape((2, HALF, D), F32), shape((24, FF), F32), shape((96, D), F32),
            shape((24, D), F32), shape((24, 3 * D), F32), *[shape((1, 24), F32)] * 8, shape((1, 96), F32),
        ),
        in_specs=[HB, HB, HB, VM, VM, VM, VM],
        out_specs=(VM,) * 15,
        scratch_shapes=[DMA((3,))],
        compiler_params=pltpu.CompilerParams(vmem_limit_bytes=VMEM_LIMIT),
    )(*args)


def call_fwd(length, mask, tok, gain, shift, w_qkv, qb, vb):
    low = shape((T, D), BF16)
    return pl.pallas_call(
        fwd_kernel,
        out_shape=(shape((D, T), BF16), low, low, low, low, shape((H, 1, T), F32)),
        in_specs=[SM] + [VM] * 7,
        out_specs=(VM,) * 6,
        compiler_params=pltpu.CompilerParams(vmem_limit_bytes=VMEM_LIMIT),
    )(length, mask, tok, gain, shift, w_qkv, qb, vb)

def whole_sequences(
    tokens, lengths, key_mask, attn_gain, attn_shift, w_qkv, query_bias, value_bias, w_out,
    out_bias, ffn_gain, ffn_shift, w_in, in_bias, w_back, back_bias, cotangent,
):
    x = lax.axis_index("seq")
    swap = [(0, 1), (1, 0)]

    def gather(rows):
        own = lax.dynamic_index_in_dim(rows, x, 0, keepdims=False)
        other = lax.dynamic_index_in_dim(rows, 1 - x, 0, keepdims=False)
        got = lax.ppermute(other, "seq", swap)
        return jnp.concatenate([jnp.where(x == 0, own, got), jnp.where(x == 0, got, own)], axis=0)

    def row(vector):
        return vector.reshape(1, -1)

    tok = gather(tokens)
    mask = gather(key_mask)
    length = lax.dynamic_slice_in_dim(lengths, x, 1)
    normed_t, q, k, v, ctx, log_total = call_fwd(
        length, row(mask), tok, row(attn_gain), row(attn_shift), w_qkv, row(query_bias), row(value_bias)
    )
    cotangent, _ = lax.optimization_barrier((cotangent, tok))
    cot = gather(cotangent)
    out, out_got, d_res, d_att, gf, vf, early = call_ffn(
        tok, cot, ctx, row(out_bias), row(ffn_gain), row(ffn_shift), row(in_bias), row(back_bias),
        w_out, w_in, w_back,
    )
    d_tok, d_got, late, vec = call_bwd(
        length, mask.reshape(T, 1), tok, row(attn_gain), w_qkv, normed_t, q, k, v, ctx, log_total,
        d_att, d_res, vf, gf,
    )
    (
        layer_out, grad_tokens, g_in, g_back, g_out, g_qkv, ag, ash, qb, vb, ob, fg, fs, bb, ib,
    ) = call_join(out, out_got, d_tok, d_got, early, late, vec)
    return (
        layer_out, grad_tokens, ag.reshape(24), ash.reshape(24), g_qkv, qb.reshape(24), vb.reshape(24),
        g_out, ob.reshape(24), fg.reshape(24), fs.reshape(24), g_in, ib.reshape(96), g_back,
        bb.reshape(24),
    )

def shifted(array, axis, by):
    devices = lax.axis_size(axis)
    return lax.ppermute(array, axis, [(i, (i + by) % devices) for i in range(devices)])


def layer_norm(values, gain, shift):
    center = values - jnp.mean(values, axis=-1, keepdims=True)
    spread = jnp.mean(center * center, axis=-1, keepdims=True)
    return center * lax.rsqrt(spread + NORM_EPS) * gain + shift


def partial_gelu(values):
    return jax.nn.gelu(values, approximate=True)


def outer_product(left, right):
    return lax.dot_general(
        left, right, (((0,), (0,)), ((), ())), preferred_element_type=jnp.float32
    )


def times_transposed(left, right):
    return lax.dot_general(
        left, right, (((1,), (1,)), ((), ())), preferred_element_type=jnp.float32
    )


def allowed_keys(lengths, flags_all, query_pos, first_key, key_count):
    key_pos = first_key + jnp.arange(key_count, dtype=jnp.int32)
    key_flags = lax.dynamic_slice_in_dim(flags_all, first_key, key_count, 1)
    key_valid = (key_pos[None, :] < lengths[:, None]) & (key_flags == 1)
    itself = key_pos[None, :] == query_pos[:, None]
    return key_valid[:, None, None, :] | itself[None, :, None, :]


def send_home(partial_grads):
    return shifted(partial_grads.astype(jnp.bfloat16), "seq", 1).astype(partial_grads.dtype)


def shards(
    tokens,
    lengths,
    key_mask,
    attn_gain,
    attn_shift,
    w_qkv,
    query_bias,
    value_bias,
    w_out,
    out_bias,
    ffn_gain,
    ffn_shift,
    w_in,
    in_bias,
    w_back,
    back_bias,
    cotangent,
):
    seq_count, span_dev, model_width = tokens.shape
    row_count = seq_count * span_dev
    members = lax.axis_size("seq")
    own_index = lax.axis_index("seq")
    query_pos = own_index * span_dev + jnp.arange(span_dev, dtype=jnp.int32)
    flags_all = lax.all_gather(key_mask, "seq", axis=1, tiled=True)
    inputs = tokens.astype(jnp.float32).reshape(row_count, model_width)
    normed_one, norm_pull_one = jax.vjp(layer_norm, inputs, attn_gain, attn_shift)
    normed_attn = normed_one.astype(jnp.bfloat16)
    projected = jnp.dot(normed_attn, w_qkv, preferred_element_type=jnp.float32)
    queries = ((projected[:, :model_width] + query_bias) * 0.125).astype(jnp.bfloat16)
    queries = queries.reshape(seq_count, span_dev, H, HD)
    keyval = jnp.concatenate(
        [projected[:, model_width : 2 * model_width], projected[:, 2 * model_width :] + value_bias],
        axis=1,
    ).astype(jnp.bfloat16)
    keyval = keyval.reshape(seq_count, span_dev, 2 * model_width)

    def split_block(block_kv):
        key_count = block_kv.shape[1]
        key_heads = block_kv[:, :, :model_width].reshape(seq_count, key_count, H, HD)
        value_heads = block_kv[:, :, model_width:].reshape(seq_count, key_count, H, HD)
        return (key_count, key_heads, value_heads)

    running_max = jnp.full((seq_count, span_dev, H), NEG_FILL, jnp.float32)
    key_count, key_heads, value_heads = split_block(
        lax.all_gather(keyval, "seq", axis=1, tiled=True)
    )
    scores = jnp.einsum("sqhd,skhd->sqhk", queries, key_heads, preferred_element_type=jnp.float32)
    allowed = allowed_keys(lengths, flags_all, query_pos, jnp.int32(0), key_count)
    new_max = jnp.maximum(running_max, jnp.max(jnp.where(allowed, scores, NEG_FILL), axis=-1))
    expo = jnp.exp(jnp.where(allowed, scores - new_max[..., None], NEG_FILL))
    running_sum = jnp.sum(expo, axis=-1)
    running_acc = jnp.einsum(
        "sqhk,skhd->sqhd",
        expo.astype(jnp.bfloat16),
        value_heads,
        preferred_element_type=jnp.float32,
    )
    attended = running_acc / running_sum[..., None]
    log_total = new_max + jnp.log(running_sum)
    context = attended.reshape(row_count, model_width).astype(jnp.bfloat16)
    residual = inputs + jnp.dot(context, w_out, preferred_element_type=jnp.float32) + out_bias
    normed_two, norm_pull_two = jax.vjp(layer_norm, residual, ffn_gain, ffn_shift)
    normed_ffn = normed_two.astype(jnp.bfloat16)
    pre_act = jnp.dot(normed_ffn, w_in, preferred_element_type=jnp.float32) + in_bias
    gelu_value, gelu_pull = jax.vjp(partial_gelu, pre_act)
    activated = gelu_value.astype(jnp.bfloat16)
    layer_out = (
        residual + jnp.dot(activated, w_back, preferred_element_type=jnp.float32) + back_bias
    )
    grad_rows = cotangent.reshape(row_count, model_width)
    grad_float = grad_rows.astype(jnp.float32)
    grad_back_bias = jnp.sum(grad_float, axis=0)
    grad_w_back = outer_product(activated, grad_rows)
    d_act = times_transposed(grad_rows, w_back)
    d_pre = gelu_pull(d_act)[0].astype(jnp.bfloat16)
    grad_in_bias = jnp.sum(d_pre.astype(jnp.float32), axis=0)
    grad_w_in = outer_product(normed_ffn, d_pre)
    d_normed = times_transposed(d_pre, w_in)
    d_res_part, grad_ffn_gain, grad_ffn_shift = norm_pull_two(d_normed)
    d_residual = grad_float + d_res_part
    d_branch = d_residual.astype(jnp.bfloat16)
    grad_out_bias = jnp.sum(d_branch.astype(jnp.float32), axis=0)
    grad_w_out = outer_product(context, d_branch)
    d_attended = (
        times_transposed(d_branch, w_out).astype(jnp.bfloat16).reshape(seq_count, span_dev, H, HD)
    )
    delta = jnp.sum(d_attended.astype(jnp.float32) * attended, axis=-1)

    def attend_back(block_kv, first_key):
        key_count, key_heads, value_heads = split_block(block_kv)
        scores = jnp.einsum(
            "sqhd,skhd->sqhk", queries, key_heads, preferred_element_type=jnp.float32
        )
        allowed = allowed_keys(lengths, flags_all, query_pos, first_key, key_count)
        weights_f = jnp.exp(jnp.where(allowed, scores - log_total[..., None], NEG_FILL))
        d_values = jnp.einsum(
            "sqhk,sqhd->skhd",
            weights_f.astype(jnp.bfloat16),
            d_attended,
            preferred_element_type=jnp.float32,
        )
        d_probs = jnp.einsum(
            "sqhd,skhd->sqhk", d_attended, value_heads, preferred_element_type=jnp.float32
        )
        d_scores = (weights_f * (d_probs - delta[..., None])).astype(jnp.bfloat16)
        d_query = jnp.einsum(
            "sqhk,skhd->sqhd", d_scores, key_heads, preferred_element_type=jnp.float32
        )
        d_keys = jnp.einsum(
            "sqhk,sqhd->skhd", d_scores, queries, preferred_element_type=jnp.float32
        )
        d_block = jnp.concatenate(
            [
                d_keys.reshape(seq_count, key_count, model_width),
                d_values.reshape(seq_count, key_count, model_width),
            ],
            axis=2,
        )
        return (d_query, d_block)

    zero_query = jnp.zeros((seq_count, span_dev, H, HD), jnp.float32)

    def turn(turn_index, state_now):
        current, d_current, d_query = state_now
        anchor = (own_index - turn_index) % members
        add_query, add_block = attend_back(current, anchor * span_dev)
        current = shifted(current, "seq", 1)
        return (current, send_home(d_current + add_block), d_query + add_query)

    start_back = (
        keyval,
        jnp.zeros((seq_count, span_dev, 2 * model_width), jnp.float32),
        zero_query,
    )
    current, d_current, d_query = lax.fori_loop(0, members - 1, turn, start_back)
    anchor = (own_index - (members - 1)) % members
    add_query, add_block = attend_back(current, anchor * span_dev)
    d_query = d_query + add_query
    d_keyval = send_home(d_current + add_block)
    d_query_low = d_query.reshape(row_count, model_width).astype(jnp.bfloat16)
    d_keyval_low = d_keyval.reshape(row_count, 2 * model_width).astype(jnp.bfloat16)
    query_scaled = d_query_low.astype(jnp.float32) * 0.125
    grad_query_bias = jnp.sum(query_scaled, axis=0)
    grad_value_bias = jnp.sum(d_keyval_low[:, model_width:].astype(jnp.float32), axis=0)
    d_projected = jnp.concatenate([query_scaled.astype(jnp.bfloat16), d_keyval_low], axis=1)
    grad_w_qkv = outer_product(normed_attn, d_projected)
    d_normed_attn = times_transposed(d_projected, w_qkv)
    d_in_part, grad_attn_gain, grad_attn_shift = norm_pull_one(d_normed_attn)
    grad_tokens = (d_residual + d_in_part).reshape(seq_count, span_dev, model_width)
    out_block = layer_out.astype(jnp.bfloat16).reshape(seq_count, span_dev, model_width)
    all_sums = (
        lax.psum_scatter(grad_attn_gain, ("dp", "seq"), scatter_dimension=0, tiled=True),
        lax.psum_scatter(grad_attn_shift, ("dp", "seq"), scatter_dimension=0, tiled=True),
        lax.psum_scatter(grad_w_qkv, ("dp", "seq"), scatter_dimension=0, tiled=True),
        lax.psum_scatter(grad_query_bias, ("dp", "seq"), scatter_dimension=0, tiled=True),
        lax.psum_scatter(grad_value_bias, ("dp", "seq"), scatter_dimension=0, tiled=True),
        lax.psum_scatter(grad_w_out, ("dp", "seq"), scatter_dimension=0, tiled=True),
        lax.psum_scatter(grad_out_bias, ("dp", "seq"), scatter_dimension=0, tiled=True),
        lax.psum_scatter(grad_ffn_gain, ("dp", "seq"), scatter_dimension=0, tiled=True),
        lax.psum_scatter(grad_ffn_shift, ("dp", "seq"), scatter_dimension=0, tiled=True),
        lax.psum_scatter(grad_w_in, ("dp", "seq"), scatter_dimension=0, tiled=True),
        lax.psum_scatter(grad_in_bias, ("dp", "seq"), scatter_dimension=0, tiled=True),
        lax.psum_scatter(grad_w_back, ("dp", "seq"), scatter_dimension=0, tiled=True),
        lax.psum_scatter(grad_back_bias, ("dp", "seq"), scatter_dimension=0, tiled=True),
    )
    return (
        out_block,
        grad_tokens,
        all_sums[0],
        all_sums[1],
        all_sums[2],
        all_sums[3],
        all_sums[4],
        all_sums[5],
        all_sums[6],
        all_sums[7],
        all_sums[8],
        all_sums[9],
        all_sums[10],
        all_sums[11],
        all_sums[12],
    )


def solution(mesh):
    sizes = dict(mesh.shape)
    whole = sizes == {"dp": 16, "seq": 2}
    return jax.shard_map(
        whole_sequences if whole else shards,
        mesh=mesh,
        in_specs=(
            P("dp", "seq", None),
            P("dp"),
            P("dp", "seq"),
            P(),
            P(),
            P(),
            P(),
            P(),
            P(),
            P(),
            P(),
            P(),
            P(),
            P(),
            P(),
            P(),
            P("dp", "seq", None),
        ),
        out_specs=(
            P("dp", "seq", None),
            P("dp", "seq", None),
            P(("dp", "seq")),
            P(("dp", "seq")),
            P(("dp", "seq"), None),
            P(("dp", "seq")),
            P(("dp", "seq")),
            P(("dp", "seq"), None),
            P(("dp", "seq")),
            P(("dp", "seq")),
            P(("dp", "seq")),
            P(("dp", "seq"), None),
            P(("dp", "seq")),
            P(("dp", "seq"), None),
            P(("dp", "seq")),
        ),
        check_vma=False,
    )
```

```python
import functools

import jax
import jax.numpy as jnp
from jax import lax
from jax.experimental import pallas as pl
from jax.experimental.pallas import tpu as pltpu
from jax.sharding import PartitionSpec as P

H = 12
HD = 64


NEG_FILL = -1e30
NORM_EPS = 1e-05

F32 = jnp.float32
BF16 = jnp.bfloat16
D = 768
FF = 3072
T = 1024
HALF = 512
PAIRS = 6
UW = 384
MESH = pl.DeviceIdType.MESH
VMEM_LIMIT = 60 * 1024 * 1024


def dot_nn(a, b):
    return lax.dot_general(a, b, (((1,), (0,)), ((), ())), preferred_element_type=F32)


def dot_nt(a, b):
    return lax.dot_general(a, b, (((1,), (1,)), ((), ())), preferred_element_type=F32)


def dot_tn(a, b):
    return lax.dot_general(a, b, (((0,), (0,)), ((), ())), preferred_element_type=F32)


def shape(dims, dtype):
    return jax.ShapeDtypeStruct(dims, dtype)


VM = pl.BlockSpec(memory_space=pltpu.VMEM)
SM = pl.BlockSpec(memory_space=pltpu.SMEM)
HB = pl.BlockSpec(memory_space=pl.ANY)
DMA = pltpu.SemaphoreType.DMA


def row(ref):
    return ref[...].reshape(1, -1)


def norm_parts(x):
    center = x - jnp.mean(x, axis=-1, keepdims=True)
    spread = jnp.mean(center * center, axis=-1, keepdims=True)
    rstd = lax.rsqrt(spread + NORM_EPS)
    return center * rstd, rstd


def norm_back(d_norm, n, rstd, gain):
    u = d_norm * gain
    mean_u = jnp.mean(u, axis=-1, keepdims=True)
    mean_un = jnp.mean(u * n, axis=-1, keepdims=True)
    return (u - mean_u - n * mean_un) * rstd


def blocks_of(top, bottom):
    return jnp.concatenate([top, bottom], axis=0).astype(BF16)


def place(index, first_x):
    z, y, c, x = index // 8, (index // 4) % 2, (index // 2) % 2, index % 2
    return c * 16 + z + 4 * (2 * y + x) + first_x * 4 * (x - y)


def reduction_scratch(units):
    sems = [DMA((units,)), DMA((units,)), DMA((units,)), DMA((units, 3))]
    return [pltpu.VMEM((units, n, 48, UW), BF16) for n in (16, 8, 4, 3)] + sems + sems


class Reduction:
    def __init__(self, units, x_first, own, parts, sums, held, sems):
        self.units, self.x_first = units, x_first
        self.own, self.parts, self.sums, self.held = own, parts, sums, held
        self.sends, self.recvs = sems[:4], sems[4:8]
        dp, x = lax.axis_index("dp"), lax.axis_index("seq")
        z, y, c = dp // 4, (dp // 2) % 2, dp % 2
        self.dp, self.x, self.y, self.z, self.c = dp, x, y, z, c
        self.over_c = (dp + 1 - 2 * c, x)
        self.over_x = (dp, 1 - x)
        self.over_y = (dp + 2 - 4 * y, x)
        self.over_z = [(lax.rem(z + d, 4) * 4 + y * 2 + c, x) for d in (1, 2, 3)]

    def barrier(self):
        sem = pltpu.get_barrier_semaphore()
        for to in (self.over_c, self.over_x, self.over_y, *self.over_z):
            pl.semaphore_signal(sem, inc=1, device_id=to, device_id_type=MESH)
        pl.semaphore_wait(sem, 6)

    def copy(self, src, dst, send, recv, to):
        return pltpu.make_async_remote_copy(
            src_ref=src, dst_ref=dst, send_sem=send, recv_sem=recv, device_id=to, device_id_type=MESH
        )

    def axes(self, u):
        fx, x, y, dp = self.x_first(u), self.x, self.y, self.dp
        first = (dp + (1 - fx) * (2 - 4 * y), x + fx * (1 - 2 * x))
        second = (dp + fx * (2 - 4 * y), x + (1 - fx) * (1 - 2 * x))
        return first, second, y + fx * (x - y), x + fx * (y - x)

    def hop0(self, u):
        src = self.parts(u).at[pl.ds((1 - self.c) * 16, 16)]
        return self.copy(src, self.held[0].at[u], self.sends[0].at[u], self.recvs[0].at[u], self.over_c)

    def hop1(self, u):
        first, _, a, _ = self.axes(u)
        src = self.held[0].at[u, pl.ds((1 - a) * 8, 8)]
        return self.copy(src, self.held[1].at[u], self.sends[1].at[u], self.recvs[1].at[u], first)

    def hop2(self, u):
        _, second, _, b = self.axes(u)
        src = self.held[1].at[u, pl.ds((1 - b) * 4, 4)]
        return self.copy(src, self.held[2].at[u], self.sends[2].at[u], self.recvs[2].at[u], second)

    def hop3(self, u, d):
        src = self.held[2].at[u, lax.rem(self.z + d + 1, 4)]
        return self.copy(
            src, self.held[3].at[u, d], self.sends[3].at[u, d], self.recvs[3].at[u, d], self.over_z[d]
        )

    def arrived(self, u):
        held = self.held[0].at[u]
        self.copy(held, held, self.sends[0].at[u], self.recvs[0].at[u], self.over_c).wait_recv()

    def start(self, u):
        self.hop0(u).start()

    def step1(self, u):
        self.arrived(u)
        _, _, a, _ = self.axes(u)
        held = self.held[0]

        def add(k):
            held[u, k] = (held[u, k].astype(F32) + self.own(u, k).astype(F32)).astype(BF16)

        @pl.loop(0, 8, unroll=2)
        def _(k):
            add((1 - a) * 8 + k)

        self.hop1(u).start()

        @pl.loop(0, 8, unroll=2)
        def _(k):
            add(a * 8 + k)

    def step2(self, u):
        self.hop1(u).wait_recv()
        _, _, a, b = self.axes(u)
        held, before = self.held[1], self.held[0]

        def add(k):
            held[u, k] = (held[u, k].astype(F32) + before[u, a * 8 + k].astype(F32)).astype(BF16)

        for k in range(4):
            add((1 - b) * 4 + k)
        self.hop2(u).start()
        for k in range(4):
            add(b * 4 + k)

    def step3(self, u):
        self.hop2(u).wait_recv()
        _, _, _, b = self.axes(u)
        held, before = self.held[2], self.held[1]
        for k in range(4):
            held[u, k] = (held[u, k].astype(F32) + before[u, b * 4 + k].astype(F32)).astype(BF16)
        for d in range(3):
            self.hop3(u, d).start()

    def finish(self, u):
        total = self.held[2][u, self.z].astype(F32)
        for d in range(3):
            self.hop3(u, d).wait_recv()
            total = total + self.held[3][u, d].astype(F32)
        self.sums[u] = total

    def drain(self):
        for u in range(self.units):
            self.hop0(u).wait_send()
            self.hop1(u).wait_send()
            self.hop2(u).wait_send()
            for d in range(3):
                self.hop3(u, d).wait_send()


def fwd_kernel(
    len_ref, mask_ref, gain_ref, shift_ref, qb_ref, vb_ref, tok_hbm, cot_hbm, w_hbm,
    nt_hbm, q_hbm, k_hbm, v_hbm, ctx_hbm, tok_out, cot_out, lt_ref, bias_ref,
    tok_ref, cot_ref, w_ref, nt_ref, q_ref, k_ref, v_ref, ctx_ref, mgot_ref,
    sl, so, sx, tx,
):
    dp, x = lax.axis_index("dp"), lax.axis_index("seq")
    here, there = pl.multiple_of(x * HALF, HALF), pl.multiple_of((1 - x) * HALF, HALF)
    load_w = pltpu.make_async_copy(w_hbm, w_ref, sl.at[0])
    load_tok = pltpu.make_async_copy(tok_hbm.at[x], tok_ref.at[pl.ds(here, HALF)], sl.at[1])
    load_cot = pltpu.make_async_copy(cot_hbm.at[x], cot_ref.at[pl.ds(here, HALF)], sl.at[2])
    load_tok.start()
    load_w.start()

    def swap(n):
        if n == 4:
            src, dst = mask_ref, mgot_ref
        else:
            side, buffer = (tok_hbm, tok_ref) if n < 4 else (cot_hbm, cot_ref)
            rows = 128 if n < 4 else 256
            at = (n if n < 4 else n - 5) * rows
            src = side.at[1 - x, pl.ds(at, rows)]
            dst = buffer.at[pl.ds(pl.multiple_of(here + at, rows), rows)]
        return pltpu.make_async_remote_copy(
            src_ref=src, dst_ref=dst, send_sem=sx.at[n], recv_sem=tx.at[n],
            device_id=(dp, 1 - x), device_id_type=MESH,
        )

    sem = pltpu.get_barrier_semaphore()
    pl.semaphore_signal(sem, inc=1, device_id=(dp, 1 - x), device_id_type=MESH)
    pl.semaphore_wait(sem, 1)
    swaps = [swap(n) for n in range(7)]
    for one in swaps:
        one.start()
    load_tok.wait()
    load_w.wait()
    load_cot.start()

    def project(first, count):
        rows = pl.ds(pl.multiple_of(first, count), count)
        n, _ = norm_parts(tok_ref[rows, :].astype(F32))
        normed = (n * row(gain_ref) + row(shift_ref)).astype(BF16)
        nt_ref[:, rows] = normed.T
        q_ref[rows, :] = ((dot_nn(normed, w_ref[:, :D]) + row(qb_ref)) * 0.125).astype(BF16)
        k_ref[rows, :] = dot_nn(normed, w_ref[:, D : 2 * D]).astype(BF16)
        v_ref[rows, :] = (dot_nn(normed, w_ref[:, 2 * D :]) + row(vb_ref)).astype(BF16)

    @pl.loop(0, 2)
    def _(t):
        project(here + t * 256, 256)

    for n in range(4):
        swaps[n].wait_recv()
        project(there + n * 128, 128)

    outs = [
        pltpu.make_async_copy(src, dst, so.at[n])
        for n, (src, dst) in enumerate(
            [(nt_ref, nt_hbm), (q_ref, q_hbm), (k_ref, k_hbm), (v_ref, v_hbm), (tok_ref, tok_out)]
        )
    ]
    for one in outs:
        one.start()
    swaps[4].wait_recv()
    pos = lax.broadcasted_iota(jnp.int32, (1, HALF), 1)
    for first, ref in ((here, mask_ref), (there, mgot_ref)):
        flags = jnp.where(x == 0, ref[0:1, :], ref[1:2, :])
        valid = (pos + first < len_ref[x]) & (flags == 1)
        bias_ref[:, pl.ds(first, HALF)] = jnp.where(valid, 0.0, NEG_FILL).astype(F32)
    bias = bias_ref[...]
    lane = lax.broadcasted_iota(jnp.int32, (1, 128), 1)
    eye = lax.broadcasted_iota(jnp.int32, (256, 256), 0) == lax.broadcasted_iota(
        jnp.int32, (256, 256), 1
    )

    def ctx_out(p):
        cols = pl.ds(pl.multiple_of(p * 128, 128), 128)
        return pltpu.make_async_copy(ctx_ref.at[:, cols], ctx_hbm.at[:, cols], so.at[5 + p])

    @pl.loop(0, PAIRS)
    def _(p):
        cols = pl.ds(pl.multiple_of(p * 128, 128), 128)
        kp = k_ref[:, cols]
        vext = jnp.concatenate([v_ref[:, cols], jnp.ones((T, 128), BF16)], axis=1)
        kh = [jnp.where((lane < HD) == (h == 0), kp, jnp.zeros_like(kp)) for h in range(2)]
        for i in range(4):
            qi = q_ref[i * 256 : (i + 1) * 256, cols]
            heads = []
            for h in range(2):
                raw = dot_nt(qi, kh[h])
                pieces = []
                for j in range(4):
                    cut = slice(j * 256, (j + 1) * 256)
                    piece = raw[:, cut] + bias[:, cut]
                    if i == j:
                        piece = jnp.where(eye, raw[:, cut], piece)
                    pieces.append(piece)
                s = jnp.concatenate(pieces, axis=1)
                top = jnp.max(s, axis=1, keepdims=True)
                e = jnp.exp(s - top).astype(BF16)
                o = dot_nn(e, vext)
                total = o[:, 128:]
                heads.append(o[:, :128] / total)
                log_total = top + jnp.log(total)
                lt_ref[2 * p + h, :, i * 256 : (i + 1) * 256] = log_total.T[0:1, :]
            ctx_ref[i * 256 : (i + 1) * 256, cols] = jnp.where(lane < HD, heads[0], heads[1]).astype(BF16)
        ctx_out(p).start()

    load_cot.wait()
    for n in (5, 6):
        swaps[n].wait_recv()
    last = pltpu.make_async_copy(cot_ref, cot_out, so.at[11])
    last.start()
    for one in swaps:
        one.wait_send()
    for one in outs:
        one.wait()
    for p in range(PAIRS):
        ctx_out(p).wait()
    last.wait()


def call_fwd(*args):
    low = shape((T, D), BF16)
    return pl.pallas_call(
        fwd_kernel,
        out_shape=(
            shape((D, T), BF16), low, low, low, low, low, low, shape((H, 1, T), F32), shape((1, T), F32),
        ),
        in_specs=[SM] + [VM] * 5 + [HB] * 3,
        out_specs=(HB,) * 7 + (VM, VM),
        scratch_shapes=[
            pltpu.VMEM((T, D), BF16),
            pltpu.VMEM((T, D), BF16),
            pltpu.VMEM((D, 3 * D), BF16),
            pltpu.VMEM((D, T), BF16),
            *[pltpu.VMEM((T, D), BF16)] * 4,
            pltpu.VMEM((2, HALF), jnp.int32),
            DMA((3,)), DMA((12,)), DMA((7,)), DMA((7,)),
        ],
        compiler_params=pltpu.CompilerParams(
            vmem_limit_bytes=VMEM_LIMIT, collective_id=2, has_side_effects=True
        ),
    )(*args)


def x_first_early(unit):
    return unit % 2


def x_first_late(unit):
    return (unit + 1) % 2


def ffn_kernel(
    tok_ref, cot_ref, ctx_ref, ob_ref, g_ref, s_ref, ib_ref, bb_ref, wo_hbm, wi_hbm, wb_hbm,
    lo_ref, logot_ref, dres_hbm, datt_hbm, grads_hbm, vec_ref, sums_ref,
    wo_ref, wi_ref, wb_ref, nf_ref, act_ref, dpre_ref, dbr_ref, res_ref, dn_ref, away_ref, datt_ref,
    parts_ref, grads_ref, sw, so, sx, tx, *reds,
):
    def parts(u):
        return parts_ref.at[u]

    def own_block(u, k):
        return parts_ref[u, red.c * 16 + k]

    red = Reduction(4, x_first_early, own_block, parts, sums_ref, reds[:4], reds[4:])
    x = red.x
    loads = [pltpu.make_async_copy(wo_hbm, wo_ref, sw.at[0])]
    for c in range(4):
        cut = pl.ds(c * 768, 768)
        loads.append(pltpu.make_async_copy(wi_hbm.at[:, cut], wi_ref.at[:, cut], sw.at[1 + 2 * c]))
        loads.append(pltpu.make_async_copy(wb_hbm.at[cut], wb_ref.at[cut], sw.at[2 + 2 * c]))
    for load in loads:
        load.start()
    red.barrier()
    vec_ref[...] = jnp.zeros_like(vec_ref)
    loads[0].wait()
    lo_copy = red.copy(away_ref, logot_ref, sx, tx, red.over_x)

    def rows_of(t):
        return pl.ds(pl.multiple_of(lax.rem((1 - x) * HALF + t * 256, T), 256), 256)

    def forward(t, loads_of):
        rows = rows_of(t)
        res = tok_ref[rows, :].astype(F32) + dot_nn(ctx_ref[rows, :], wo_ref[...]) + row(ob_ref)
        res_ref[rows, :] = res
        n, _ = norm_parts(res)
        normed = (n * row(g_ref) + row(s_ref)).astype(BF16)
        nf_ref[rows, :] = normed
        total = res + row(bb_ref)
        for c in range(4):
            cut = slice(c * 768, (c + 1) * 768)
            for load in loads_of(c):
                load.wait()
            v = dot_nn(normed, wi_ref[:, cut]) + row(ib_ref)[:, cut]
            sq = v * v
            th = jnp.tanh(v * (0.7978845608 + (0.7978845608 * 0.044715) * sq))
            half = 0.5 + 0.5 * th
            act = (v * half).astype(BF16)
            slope = half + v * (half * (1.0 - th)) * (
                0.7978845608 + (3 * 0.7978845608 * 0.044715) * sq
            )
            act_ref[rows, cut] = act
            dpre_ref[rows, cut] = slope.astype(BF16)
            total = total + dot_nn(act, wb_ref[cut, :])
        return total.astype(BF16)

    away_ref[0:256] = forward(0, lambda c: loads[1 + 2 * c : 3 + 2 * c])
    away_ref[256:512] = forward(1, lambda c: ())
    lo_copy.start()

    @pl.loop(0, 2)
    def _(t):
        lo_ref[pl.ds(pl.multiple_of(t * 256, 256), 256)] = forward(t + 2, lambda c: ())

    @pl.loop(0, 4)
    def _(z):
        g = dot_tn(act_ref[:, pl.ds(pl.multiple_of(z * 768, 768), 768)], cot_ref[...])
        for r in range(8):
            for u in range(4):
                i, j = u // 2, u % 2
                block = g[r * 96 + i * 48 : r * 96 + i * 48 + 48, j * UW : (j + 1) * UW]
                parts_ref[u, place(r, x_first_early(u)) + z] = block.astype(BF16)

    for u in range(4):
        red.start(u)

    def tile_out(t, part):
        rows = rows_of(t)
        if part == 0:
            return pltpu.make_async_copy(res_ref.at[rows], dres_hbm.at[rows], so.at[2 * t])
        return pltpu.make_async_copy(datt_ref.at[rows], datt_hbm.at[rows], so.at[2 * t + 1])

    plan = {2: (1, 0), 3: (1, 1), 4: (1, 2), 5: (1, 3), 10: (2, 1), 11: (2, 0), 15: (2, 3)}

    @pl.loop(0, 4)
    def _(t):
        rows = rows_of(t)
        dy = cot_ref[rows, :]
        dn_ref[...] = jnp.zeros_like(dn_ref)
        for c in range(4):
            for at, (stage, u) in plan.items():
                if at % 4 == c:

                    @pl.when(t == at // 4)
                    def _():
                        (red.step1, red.step2, red.step3)[stage - 1](u)

            cut = slice(c * 768, (c + 1) * 768)
            d_act = dot_nt(dy, wb_ref[cut, :])
            d_pre = (d_act * dpre_ref[rows, cut].astype(F32)).astype(BF16)
            dpre_ref[rows, cut] = d_pre
            dn_ref[...] += dot_nt(d_pre, wi_ref[:, cut])
            vec_ref[4 + c : 5 + c, :] += jnp.sum(d_pre.astype(F32), axis=0, keepdims=True)

        n, rstd = norm_parts(res_ref[rows, :])
        d_normed = dn_ref[...]
        dyf = dy.astype(F32)
        d_res = dyf + norm_back(d_normed, n, rstd, row(g_ref))
        res_ref[rows, :] = d_res
        tile_out(t, 0).start()
        d_branch = d_res.astype(BF16)
        dbr_ref[rows, :] = d_branch
        datt_ref[rows, :] = dot_nt(d_branch, wo_ref[...]).astype(BF16)
        tile_out(t, 1).start()
        vec_ref[0:1, :] += jnp.sum(dyf, axis=0, keepdims=True)
        vec_ref[1:2, :] += jnp.sum(d_normed * n, axis=0, keepdims=True)
        vec_ref[2:3, :] += jnp.sum(d_normed, axis=0, keepdims=True)
        vec_ref[3:4, :] += jnp.sum(d_branch.astype(F32), axis=0, keepdims=True)

    def grads_out(u):
        return pltpu.make_async_copy(grads_ref.at[u], grads_hbm.at[u], so.at[8 + u])

    def unit(u, g):
        for r in range(32):
            rows = slice(r * 24, (r + 1) * 24)
            grads_ref[u, place(r, x_first_late(u))] = blocks_of(g[rows, :UW], g[rows, UW:])
        grads_out(u).start()

    @pl.loop(0, 4)
    def _(u):
        unit(u, dot_tn(nf_ref[...], dpre_ref[:, pl.ds(pl.multiple_of(u * 768, 768), 768)]))

        @pl.when(u == 0)
        def _():
            red.step2(2)
            red.step3(1)

        @pl.when(u == 1)
        def _():
            red.step3(0)

        @pl.when(u == 3)
        def _():
            red.step3(3)
            red.step3(2)

    unit(4, dot_tn(ctx_ref[...], dbr_ref[...]))
    for u in range(4):
        red.finish(u)
    lo_copy.wait()
    red.drain()
    for t in range(4):
        tile_out(t, 0).wait()
        tile_out(t, 1).wait()
    for u in range(5):
        grads_out(u).wait()


def call_ffn(*args):
    return pl.pallas_call(
        ffn_kernel,
        out_shape=(
            shape((HALF, D), BF16), shape((HALF, D), BF16), shape((T, D), F32), shape((T, D), BF16),
            shape((5, 32, 48, UW), BF16), shape((8, D), F32), shape((4, 48, UW), F32),
        ),
        in_specs=[VM] * 8 + [HB] * 3,
        out_specs=(VM, VM, HB, HB, HB, VM, VM),
        scratch_shapes=[
            pltpu.VMEM((D, D), BF16),
            pltpu.VMEM((D, FF), BF16),
            pltpu.VMEM((FF, D), BF16),
            pltpu.VMEM((T, D), BF16),
            pltpu.VMEM((T, FF), BF16),
            pltpu.VMEM((T, FF), BF16),
            pltpu.VMEM((T, D), BF16),
            pltpu.VMEM((T, D), F32),
            pltpu.VMEM((256, D), F32),
            pltpu.VMEM((HALF, D), BF16),
            pltpu.VMEM((T, D), BF16),
            pltpu.VMEM((4, 32, 48, UW), BF16),
            pltpu.VMEM((5, 32, 48, UW), BF16),
            DMA((9,)), DMA((13,)), DMA, DMA, *reduction_scratch(4),
        ],
        compiler_params=pltpu.CompilerParams(
            vmem_limit_bytes=VMEM_LIMIT, collective_id=1, has_side_effects=True
        ),
    )(*args)


def bwd_kernel(
    bias_in, gain_ref, lt_ref, vf_ref,
    tok_hbm, w_hbm, nt_hbm, q_hbm, k_hbm, v_hbm, ctx_hbm, datt_hbm, dres_hbm, gf_ref,
    dtok_ref, dgot_ref, sums_ref, vsum_ref,
    tok_ref, w_ref, nt_ref, q_ref, k_ref, v_ref, ctx_ref, datt_ref, dres_ref, bias_ref,
    dproj_ref, dq_ref, gq_ref, delta_ref, own_ref, parts_ref, dsend_ref, vs_ref, vr_ref,
    sv, tv, sx, tx, so, sl, sp, *reds,
):
    def parts(u):
        return gf_ref.at[u] if u < 5 else parts_ref.at[u - 5]

    def own_block(u, k):
        return own_ref[u, k]

    red = Reduction(8, x_first_late, own_block, parts, sums_ref, reds[:4], reds[4:])
    x, c = red.x, red.c

    def load_pair(p):
        cols = pl.ds(pl.multiple_of(p * 128, 128), 128)
        sides = ((q_hbm, q_ref), (k_hbm, k_ref), (v_hbm, v_ref), (datt_hbm, datt_ref), (ctx_hbm, ctx_ref))
        return [
            pltpu.make_async_copy(src.at[:, cols], dst.at[:, cols], sp.at[n, p])
            for n, (src, dst) in enumerate(sides)
        ]

    for load in load_pair(0):
        load.start()
    red.barrier()
    for u in range(5):
        red.start(u)
    fetch = pltpu.make_async_copy(gf_ref.at[:, pl.ds(c * 16, 16)], own_ref.at[pl.ds(0, 5)], so)
    fetch.start()
    late_loads = [
        pltpu.make_async_copy(src, dst, sl.at[n])
        for n, (src, dst) in enumerate(
            [(nt_hbm, nt_ref), (w_hbm, w_ref), (tok_hbm, tok_ref), (dres_hbm, dres_ref)]
        )
    ]
    for load in load_pair(1):
        load.start()
    late_loads[0].start()
    for p in range(2, PAIRS):
        for load in load_pair(p):
            load.start()
    for load in late_loads[1:]:
        load.start()

    there = pl.multiple_of((1 - x) * HALF, HALF)
    here = pl.multiple_of(x * HALF, HALF)

    def vhop(n, to):
        return red.copy(vs_ref.at[min(n, 3)], vr_ref.at[n], sv.at[n], tv.at[n], to)

    hops = [red.over_c, red.over_x, red.over_y, *red.over_z]

    lane = lax.broadcasted_iota(jnp.int32, (1, 128), 1)
    bias_ref[...] = jnp.broadcast_to(bias_in[...], (128, T)).T
    eye = lax.broadcasted_iota(jnp.int32, (256, 256), 0) == lax.broadcasted_iota(
        jnp.int32, (256, 256), 1
    )
    head_of = lax.broadcasted_iota(jnp.int32, (8, 128), 1) // HD == lax.broadcasted_iota(
        jnp.int32, (8, 128), 0
    )
    pick = jnp.where(head_of, 1.0, 0.0).astype(F32)
    vs_ref[0, :8] = vf_ref[...]
    vs_ref[0, 8:] = jnp.zeros((8, D), F32)
    fetch.wait()
    for load in load_pair(0):
        load.wait()

    def progress(j, k):
        if k % 2:
            one = 4 * j + (k - 1) // 2

            @pl.when(one < 6)
            def _():
                red.step1(one)

            three = 4 * j + (k - 11) // 2

            @pl.when((three >= 0) & (three < 6))
            def _():
                red.step3(three)
        else:
            two = 4 * j + k // 2 - 3

            @pl.when((two >= 0) & (two < 6))
            def _():
                red.step2(two)

            if k in (2, 6):

                @pl.when(j == 2)
                def _():
                    (red.step1 if k == 2 else red.step2)(6)

    @pl.loop(0, 3)
    def _(j):
        for half in range(2):
            p = 2 * j + half
            cols = pl.ds(pl.multiple_of(p * 128, 128), 128)
            if half == 0:

                @pl.when(j > 0)
                def _():
                    for load in load_pair(2 * j):
                        load.wait()

            else:
                for load in load_pair(p):
                    load.wait()
            qp, do = q_ref[:, cols], datt_ref[:, cols]
            prod = do.astype(F32) * ctx_ref[:, cols].astype(F32)
            delta_ref[...] = lax.dot_general(
                pick, prod, (((1,), (1,)), ((), ())),
                preferred_element_type=F32, precision=lax.Precision.HIGHEST,
            )
            dq_ref[...] = jnp.zeros_like(dq_ref)
            for i in range(4):
                progress(j, half * 4 + i)
                cut = slice(i * 256, (i + 1) * 256)
                kp, vp = k_ref[cut, cols], v_ref[cut, cols]
                bias256 = jnp.concatenate([bias_ref[cut]] * 2, axis=1)
                dks, dvs = [], []
                for h in range(2):
                    mine = (lane < HD) == (h == 0)
                    kh = jnp.where(mine, kp, jnp.zeros_like(kp))
                    vh = jnp.where(mine, vp, jnp.zeros_like(vp))
                    raw = dot_nt(kh, qp)
                    pieces = []
                    for m in range(4):
                        piece = raw[:, m * 256 : (m + 1) * 256] + bias256
                        if i == m:
                            piece = jnp.where(eye, raw[:, m * 256 : (m + 1) * 256], piece)
                        pieces.append(piece)
                    s = jnp.concatenate(pieces, axis=1)
                    e = jnp.exp(s - lt_ref[2 * p + h])
                    dvs.append(dot_nn(e.astype(BF16), do))
                    dp = dot_nt(vh, do)
                    ds = (e * (dp - delta_ref[h : h + 1, :])).astype(BF16)
                    dks.append(dot_nn(ds, qp))
                    dq_ref[...] += dot_tn(ds, kh)
                dproj_ref[3 * p + 1, cut] = jnp.where(lane < HD, dks[0], dks[1]).astype(BF16)
                dproj_ref[3 * p + 2, cut] = jnp.where(lane < HD, dvs[0], dvs[1]).astype(BF16)
            dproj_ref[3 * p] = dq_ref[...].astype(BF16) * jnp.asarray(0.125, BF16)
            d3 = jnp.concatenate([dproj_ref[3 * p + n] for n in range(3)], axis=1)
            vs_ref[0, 8:9, cols] = jnp.sum(d3[:, :128].astype(F32), axis=0, keepdims=True)
            vs_ref[0, 9:10, cols] = jnp.sum(d3[:, 256:].astype(F32), axis=0, keepdims=True)
            if half == 0:

                @pl.when(j == 0)
                def _():
                    late_loads[0].wait()

            g = dot_nn(nt_ref[...], d3)
            if half == 0:
                gq_ref[...] = g
            else:
                for r in range(32):
                    rows = slice(r * 24, (r + 1) * 24)
                    parts_ref[j, place(r, x_first_late(5 + j))] = blocks_of(gq_ref[rows, :], g[rows, :])
        own_ref[5 + j] = parts_ref[j, pl.ds(c * 16, 16)]
        for n in range(3):

            @pl.when(j == n)
            def _():
                red.start(5 + n)

    def tile(rows):
        dqs, dks, dvs = (
            jnp.concatenate([dproj_ref[3 * p + n, rows] for p in range(PAIRS)], axis=1) for n in range(3)
        )
        d_normed = (
            dot_nt(dqs, w_ref[:, :D]) + dot_nt(dks, w_ref[:, D : 2 * D]) + dot_nt(dvs, w_ref[:, 2 * D :])
        )
        n, rstd = norm_parts(tok_ref[rows, :].astype(F32))
        vs_ref[0, 10:11, :] += jnp.sum(d_normed * n, axis=0, keepdims=True)
        vs_ref[0, 11:12, :] += jnp.sum(d_normed, axis=0, keepdims=True)
        return dres_ref[rows, :] + norm_back(d_normed, n, rstd, row(gain_ref))

    def dcopy(t):
        rows = pl.ds(t * 256, 256)
        return red.copy(dsend_ref.at[rows], dgot_ref.at[rows], sx.at[t], tx.at[t], red.over_x)

    def away(t):
        dsend_ref[t * 256 : (t + 1) * 256] = tile(pl.ds(there + t * 256, 256)).astype(BF16)
        dcopy(t).start()

    def home(t):
        dtok_ref[t * 256 : (t + 1) * 256] = tile(pl.ds(here + t * 256, 256))

    for load in late_loads[1:]:
        load.wait()
    away(0)
    red.step1(7)
    home(0)
    home(1)
    red.step3(6)
    red.step2(7)
    away(1)
    vhop(0, hops[0]).start()
    vhop(0, hops[0]).wait_recv()
    vs_ref[1] = vs_ref[0] + vr_ref[0]
    vhop(1, hops[1]).start()
    for u in range(6):
        red.finish(u)
    red.step3(7)
    vhop(1, hops[1]).wait_recv()
    vs_ref[2] = vs_ref[1] + vr_ref[1]
    vhop(2, hops[2]).start()
    red.finish(6)
    vhop(2, hops[2]).wait_recv()
    vs_ref[3] = vs_ref[2] + vr_ref[2]
    for d in range(3):
        vhop(3 + d, hops[3 + d]).start()
    red.finish(7)
    total = vs_ref[3]
    for d in range(3):
        vhop(3 + d, hops[3 + d]).wait_recv()
        total = total + vr_ref[3 + d]
    vsum_ref[...] = total
    for t in range(2):
        dcopy(t).wait()
    for n in range(6):
        vhop(n, hops[n]).wait_send()
    red.drain()


def join_kernel(
    lo_ref, logot_ref, dtok_ref, dgot_ref, early_ref, late_ref, vec_ref,
    out_ref, gtok_ref, gin_ref, gback_ref, gout_ref, gqkv_ref, *rest,
):
    vouts, sem = rest[:9], rest[9]
    x = lax.axis_index("seq")
    copies = [
        pltpu.make_async_copy(lo_ref, out_ref.at[x], sem.at[0]),
        pltpu.make_async_copy(logot_ref, out_ref.at[1 - x], sem.at[1]),
        pltpu.make_async_copy(dtok_ref, gtok_ref.at[x], sem.at[2]),
    ]
    for copy in copies:
        copy.start()
    gtok_ref[1 - x] = dgot_ref[...].astype(F32)
    for u in range(4):
        gback_ref[u // 2 * 48 : u // 2 * 48 + 48, u % 2 * UW : (u % 2 + 1) * UW] = early_ref[u]
        gin_ref[:, u * D : u * D + UW] = late_ref[u, :24]
        gin_ref[:, u * D + UW : u * D + 2 * UW] = late_ref[u, 24:]
    gout_ref[:, :UW] = late_ref[4, :24]
    gout_ref[:, UW:] = late_ref[4, 24:]
    for p in range(PAIRS):
        part = late_ref[5 + p // 2, p % 2 * 24 : p % 2 * 24 + 24]
        for n in range(3):
            at = n * D + p * 128
            gqkv_ref[:, at : at + 128] = part[:, n * 128 : n * 128 + 128]
    rank = lax.axis_index("dp") * 2 + x
    mine = pltpu.roll(vec_ref[...], D - rank * 24, 1)
    for n, row in enumerate((10, 11, 8, 9, 3, 1, 2, 0)):
        vouts[n][...] = mine[row : row + 1, :24]
    z = rank // 8
    parts = pltpu.roll(vec_ref[4:8, :], D - (rank % 8) * 96, 1)
    chosen = parts[0:1, :96]
    for n in range(1, 4):
        chosen = jnp.where(z == n, parts[n : n + 1, :96], chosen)
    vouts[8][...] = chosen
    for copy in copies:
        copy.wait()


def call_bwd(*args):
    return pl.pallas_call(
        bwd_kernel,
        out_shape=(
            shape((HALF, D), F32), shape((HALF, D), BF16), shape((8, 48, UW), F32), shape((16, D), F32),
        ),
        in_specs=[VM] * 4 + [HB] * 10,
        out_specs=(VM,) * 4,
        scratch_shapes=[
            pltpu.VMEM((T, D), BF16),
            pltpu.VMEM((D, 3 * D), BF16),
            pltpu.VMEM((D, T), BF16),
            *[pltpu.VMEM((T, D), BF16)] * 5,
            pltpu.VMEM((T, D), F32),
            pltpu.VMEM((T, 128), F32),
            pltpu.VMEM((18, T, 128), BF16),
            pltpu.VMEM((T, 128), F32),
            pltpu.VMEM((D, UW), F32),
            pltpu.VMEM((8, T), F32),
            pltpu.VMEM((8, 16, 48, UW), BF16),
            pltpu.VMEM((3, 32, 48, UW), BF16),
            pltpu.VMEM((HALF, D), BF16),
            pltpu.VMEM((4, 16, D), F32),
            pltpu.VMEM((6, 16, D), F32),
            DMA((6,)), DMA((6,)), DMA((2,)), DMA((2,)), DMA, DMA((4,)), DMA((5, PAIRS)),
            *reduction_scratch(8),
        ],
        compiler_params=pltpu.CompilerParams(
            vmem_limit_bytes=VMEM_LIMIT, collective_id=0, has_side_effects=True
        ),
    )(*args)


def call_join(*args):
    return pl.pallas_call(
        join_kernel,
        out_shape=(
            shape((2, HALF, D), BF16), shape((2, HALF, D), F32), shape((24, FF), F32), shape((96, D), F32),
            shape((24, D), F32), shape((24, 3 * D), F32), *[shape((1, 24), F32)] * 8, shape((1, 96), F32),
        ),
        in_specs=[HB, HB, HB, VM, VM, VM, VM],
        out_specs=(VM,) * 15,
        scratch_shapes=[DMA((3,))],
        compiler_params=pltpu.CompilerParams(vmem_limit_bytes=VMEM_LIMIT),
    )(*args)

def whole_sequences(
    tokens, lengths, key_mask, attn_gain, attn_shift, w_qkv, query_bias, value_bias, w_out,
    out_bias, ffn_gain, ffn_shift, w_in, in_bias, w_back, back_bias, cotangent,
):
    normed_t, q, k, v, ctx, tok, cot, log_total, bias = call_fwd(
        lengths, key_mask, attn_gain, attn_shift, query_bias, value_bias,
        tokens, cotangent, w_qkv,
    )
    out, out_got, d_res, d_att, gf, vf, early = call_ffn(
        tok, cot, ctx, out_bias, ffn_gain, ffn_shift, in_bias, back_bias,
        w_out, w_in, w_back,
    )
    d_tok, d_got, late, vec = call_bwd(
        bias, attn_gain, log_total, vf,
        tok, w_qkv, normed_t, q, k, v, ctx, d_att, d_res, gf,
    )
    (
        layer_out, grad_tokens, g_in, g_back, g_out, g_qkv, ag, ash, qb, vb, ob, fg, fs, bb, ib,
    ) = call_join(out, out_got, d_tok, d_got, early, late, vec)
    return (
        layer_out, grad_tokens, ag.reshape(24), ash.reshape(24), g_qkv, qb.reshape(24), vb.reshape(24),
        g_out, ob.reshape(24), fg.reshape(24), fs.reshape(24), g_in, ib.reshape(96), g_back,
        bb.reshape(24),
    )

def shifted(array, axis, by):
    devices = lax.axis_size(axis)
    return lax.ppermute(array, axis, [(i, (i + by) % devices) for i in range(devices)])


def layer_norm(values, gain, shift):
    center = values - jnp.mean(values, axis=-1, keepdims=True)
    spread = jnp.mean(center * center, axis=-1, keepdims=True)
    return center * lax.rsqrt(spread + NORM_EPS) * gain + shift


def partial_gelu(values):
    return jax.nn.gelu(values, approximate=True)


def outer_product(left, right):
    return lax.dot_general(
        left, right, (((0,), (0,)), ((), ())), preferred_element_type=jnp.float32
    )


def times_transposed(left, right):
    return lax.dot_general(
        left, right, (((1,), (1,)), ((), ())), preferred_element_type=jnp.float32
    )


def allowed_keys(lengths, flags_all, query_pos, first_key, key_count):
    key_pos = first_key + jnp.arange(key_count, dtype=jnp.int32)
    key_flags = lax.dynamic_slice_in_dim(flags_all, first_key, key_count, 1)
    key_valid = (key_pos[None, :] < lengths[:, None]) & (key_flags == 1)
    itself = key_pos[None, :] == query_pos[:, None]
    return key_valid[:, None, None, :] | itself[None, :, None, :]


def send_home(partial_grads):
    return shifted(partial_grads.astype(jnp.bfloat16), "seq", 1).astype(partial_grads.dtype)


def shards(
    tokens,
    lengths,
    key_mask,
    attn_gain,
    attn_shift,
    w_qkv,
    query_bias,
    value_bias,
    w_out,
    out_bias,
    ffn_gain,
    ffn_shift,
    w_in,
    in_bias,
    w_back,
    back_bias,
    cotangent,
):
    seq_count, span_dev, model_width = tokens.shape
    row_count = seq_count * span_dev
    members = lax.axis_size("seq")
    own_index = lax.axis_index("seq")
    query_pos = own_index * span_dev + jnp.arange(span_dev, dtype=jnp.int32)
    flags_all = lax.all_gather(key_mask, "seq", axis=1, tiled=True)
    inputs = tokens.astype(jnp.float32).reshape(row_count, model_width)
    normed_one, norm_pull_one = jax.vjp(layer_norm, inputs, attn_gain, attn_shift)
    normed_attn = normed_one.astype(jnp.bfloat16)
    projected = jnp.dot(normed_attn, w_qkv, preferred_element_type=jnp.float32)
    queries = ((projected[:, :model_width] + query_bias) * 0.125).astype(jnp.bfloat16)
    queries = queries.reshape(seq_count, span_dev, H, HD)
    keyval = jnp.concatenate(
        [projected[:, model_width : 2 * model_width], projected[:, 2 * model_width :] + value_bias],
        axis=1,
    ).astype(jnp.bfloat16)
    keyval = keyval.reshape(seq_count, span_dev, 2 * model_width)

    def split_block(block_kv):
        key_count = block_kv.shape[1]
        key_heads = block_kv[:, :, :model_width].reshape(seq_count, key_count, H, HD)
        value_heads = block_kv[:, :, model_width:].reshape(seq_count, key_count, H, HD)
        return (key_count, key_heads, value_heads)

    running_max = jnp.full((seq_count, span_dev, H), NEG_FILL, jnp.float32)
    key_count, key_heads, value_heads = split_block(
        lax.all_gather(keyval, "seq", axis=1, tiled=True)
    )
    scores = jnp.einsum("sqhd,skhd->sqhk", queries, key_heads, preferred_element_type=jnp.float32)
    allowed = allowed_keys(lengths, flags_all, query_pos, jnp.int32(0), key_count)
    new_max = jnp.maximum(running_max, jnp.max(jnp.where(allowed, scores, NEG_FILL), axis=-1))
    expo = jnp.exp(jnp.where(allowed, scores - new_max[..., None], NEG_FILL))
    running_sum = jnp.sum(expo, axis=-1)
    running_acc = jnp.einsum(
        "sqhk,skhd->sqhd",
        expo.astype(jnp.bfloat16),
        value_heads,
        preferred_element_type=jnp.float32,
    )
    attended = running_acc / running_sum[..., None]
    log_total = new_max + jnp.log(running_sum)
    context = attended.reshape(row_count, model_width).astype(jnp.bfloat16)
    residual = inputs + jnp.dot(context, w_out, preferred_element_type=jnp.float32) + out_bias
    normed_two, norm_pull_two = jax.vjp(layer_norm, residual, ffn_gain, ffn_shift)
    normed_ffn = normed_two.astype(jnp.bfloat16)
    pre_act = jnp.dot(normed_ffn, w_in, preferred_element_type=jnp.float32) + in_bias
    gelu_value, gelu_pull = jax.vjp(partial_gelu, pre_act)
    activated = gelu_value.astype(jnp.bfloat16)
    layer_out = (
        residual + jnp.dot(activated, w_back, preferred_element_type=jnp.float32) + back_bias
    )
    grad_rows = cotangent.reshape(row_count, model_width)
    grad_float = grad_rows.astype(jnp.float32)
    grad_back_bias = jnp.sum(grad_float, axis=0)
    grad_w_back = outer_product(activated, grad_rows)
    d_act = times_transposed(grad_rows, w_back)
    d_pre = gelu_pull(d_act)[0].astype(jnp.bfloat16)
    grad_in_bias = jnp.sum(d_pre.astype(jnp.float32), axis=0)
    grad_w_in = outer_product(normed_ffn, d_pre)
    d_normed = times_transposed(d_pre, w_in)
    d_res_part, grad_ffn_gain, grad_ffn_shift = norm_pull_two(d_normed)
    d_residual = grad_float + d_res_part
    d_branch = d_residual.astype(jnp.bfloat16)
    grad_out_bias = jnp.sum(d_branch.astype(jnp.float32), axis=0)
    grad_w_out = outer_product(context, d_branch)
    d_attended = (
        times_transposed(d_branch, w_out).astype(jnp.bfloat16).reshape(seq_count, span_dev, H, HD)
    )
    delta = jnp.sum(d_attended.astype(jnp.float32) * attended, axis=-1)

    def attend_back(block_kv, first_key):
        key_count, key_heads, value_heads = split_block(block_kv)
        scores = jnp.einsum(
            "sqhd,skhd->sqhk", queries, key_heads, preferred_element_type=jnp.float32
        )
        allowed = allowed_keys(lengths, flags_all, query_pos, first_key, key_count)
        weights_f = jnp.exp(jnp.where(allowed, scores - log_total[..., None], NEG_FILL))
        d_values = jnp.einsum(
            "sqhk,sqhd->skhd",
            weights_f.astype(jnp.bfloat16),
            d_attended,
            preferred_element_type=jnp.float32,
        )
        d_probs = jnp.einsum(
            "sqhd,skhd->sqhk", d_attended, value_heads, preferred_element_type=jnp.float32
        )
        d_scores = (weights_f * (d_probs - delta[..., None])).astype(jnp.bfloat16)
        d_query = jnp.einsum(
            "sqhk,skhd->sqhd", d_scores, key_heads, preferred_element_type=jnp.float32
        )
        d_keys = jnp.einsum(
            "sqhk,sqhd->skhd", d_scores, queries, preferred_element_type=jnp.float32
        )
        d_block = jnp.concatenate(
            [
                d_keys.reshape(seq_count, key_count, model_width),
                d_values.reshape(seq_count, key_count, model_width),
            ],
            axis=2,
        )
        return (d_query, d_block)

    zero_query = jnp.zeros((seq_count, span_dev, H, HD), jnp.float32)

    def turn(turn_index, state_now):
        current, d_current, d_query = state_now
        anchor = (own_index - turn_index) % members
        add_query, add_block = attend_back(current, anchor * span_dev)
        current = shifted(current, "seq", 1)
        return (current, send_home(d_current + add_block), d_query + add_query)

    start_back = (
        keyval,
        jnp.zeros((seq_count, span_dev, 2 * model_width), jnp.float32),
        zero_query,
    )
    current, d_current, d_query = lax.fori_loop(0, members - 1, turn, start_back)
    anchor = (own_index - (members - 1)) % members
    add_query, add_block = attend_back(current, anchor * span_dev)
    d_query = d_query + add_query
    d_keyval = send_home(d_current + add_block)
    d_query_low = d_query.reshape(row_count, model_width).astype(jnp.bfloat16)
    d_keyval_low = d_keyval.reshape(row_count, 2 * model_width).astype(jnp.bfloat16)
    query_scaled = d_query_low.astype(jnp.float32) * 0.125
    grad_query_bias = jnp.sum(query_scaled, axis=0)
    grad_value_bias = jnp.sum(d_keyval_low[:, model_width:].astype(jnp.float32), axis=0)
    d_projected = jnp.concatenate([query_scaled.astype(jnp.bfloat16), d_keyval_low], axis=1)
    grad_w_qkv = outer_product(normed_attn, d_projected)
    d_normed_attn = times_transposed(d_projected, w_qkv)
    d_in_part, grad_attn_gain, grad_attn_shift = norm_pull_one(d_normed_attn)
    grad_tokens = (d_residual + d_in_part).reshape(seq_count, span_dev, model_width)
    out_block = layer_out.astype(jnp.bfloat16).reshape(seq_count, span_dev, model_width)
    all_sums = (
        lax.psum_scatter(grad_attn_gain, ("dp", "seq"), scatter_dimension=0, tiled=True),
        lax.psum_scatter(grad_attn_shift, ("dp", "seq"), scatter_dimension=0, tiled=True),
        lax.psum_scatter(grad_w_qkv, ("dp", "seq"), scatter_dimension=0, tiled=True),
        lax.psum_scatter(grad_query_bias, ("dp", "seq"), scatter_dimension=0, tiled=True),
        lax.psum_scatter(grad_value_bias, ("dp", "seq"), scatter_dimension=0, tiled=True),
        lax.psum_scatter(grad_w_out, ("dp", "seq"), scatter_dimension=0, tiled=True),
        lax.psum_scatter(grad_out_bias, ("dp", "seq"), scatter_dimension=0, tiled=True),
        lax.psum_scatter(grad_ffn_gain, ("dp", "seq"), scatter_dimension=0, tiled=True),
        lax.psum_scatter(grad_ffn_shift, ("dp", "seq"), scatter_dimension=0, tiled=True),
        lax.psum_scatter(grad_w_in, ("dp", "seq"), scatter_dimension=0, tiled=True),
        lax.psum_scatter(grad_in_bias, ("dp", "seq"), scatter_dimension=0, tiled=True),
        lax.psum_scatter(grad_w_back, ("dp", "seq"), scatter_dimension=0, tiled=True),
        lax.psum_scatter(grad_back_bias, ("dp", "seq"), scatter_dimension=0, tiled=True),
    )
    return (
        out_block,
        grad_tokens,
        all_sums[0],
        all_sums[1],
        all_sums[2],
        all_sums[3],
        all_sums[4],
        all_sums[5],
        all_sums[6],
        all_sums[7],
        all_sums[8],
        all_sums[9],
        all_sums[10],
        all_sums[11],
        all_sums[12],
    )


def solution(mesh):
    sizes = dict(mesh.shape)
    whole = sizes == {"dp": 16, "seq": 2}
    return jax.shard_map(
        whole_sequences if whole else shards,
        mesh=mesh,
        in_specs=(
            P("dp", "seq", None),
            P("dp"),
            P("dp", "seq"),
            P(),
            P(),
            P(),
            P(),
            P(),
            P(),
            P(),
            P(),
            P(),
            P(),
            P(),
            P(),
            P(),
            P("dp", "seq", None),
        ),
        out_specs=(
            P("dp", "seq", None),
            P("dp", "seq", None),
            P(("dp", "seq")),
            P(("dp", "seq")),
            P(("dp", "seq"), None),
            P(("dp", "seq")),
            P(("dp", "seq")),
            P(("dp", "seq"), None),
            P(("dp", "seq")),
            P(("dp", "seq")),
            P(("dp", "seq")),
            P(("dp", "seq"), None),
            P(("dp", "seq")),
            P(("dp", "seq"), None),
            P(("dp", "seq")),
        ),
        check_vma=False,
    )
```

```python
import functools

import jax
import jax.numpy as jnp
from jax import lax
from jax.experimental import pallas as pl
from jax.experimental.pallas import tpu as pltpu
from jax.sharding import PartitionSpec as P

H = 12
HD = 64


NEG_FILL = -1e30
NORM_EPS = 1e-05

F32 = jnp.float32
BF16 = jnp.bfloat16
D = 768
FF = 3072
T = 1024
HALF = 512
PAIRS = 6
UW = 384
MESH = pl.DeviceIdType.MESH
VMEM_LIMIT = 62 * 1024 * 1024


def dot_nn(a, b):
    return lax.dot_general(a, b, (((1,), (0,)), ((), ())), preferred_element_type=F32)


def dot_nt(a, b):
    return lax.dot_general(a, b, (((1,), (1,)), ((), ())), preferred_element_type=F32)


def dot_tn(a, b):
    return lax.dot_general(a, b, (((0,), (0,)), ((), ())), preferred_element_type=F32)


def shape(dims, dtype):
    return jax.ShapeDtypeStruct(dims, dtype)


VM = pl.BlockSpec(memory_space=pltpu.VMEM)
SM = pl.BlockSpec(memory_space=pltpu.SMEM)
HB = pl.BlockSpec(memory_space=pl.ANY)
DMA = pltpu.SemaphoreType.DMA


def row(ref):
    return ref[...].reshape(1, -1)


def norm_parts(x):
    center = x - jnp.mean(x, axis=-1, keepdims=True)
    spread = jnp.mean(center * center, axis=-1, keepdims=True)
    rstd = lax.rsqrt(spread + NORM_EPS)
    return center * rstd, rstd


def norm_back(d_norm, n, rstd, gain):
    u = d_norm * gain
    mean_u = jnp.mean(u, axis=-1, keepdims=True)
    mean_un = jnp.mean(u * n, axis=-1, keepdims=True)
    return (u - mean_u - n * mean_un) * rstd


def blocks_of(top, bottom):
    return jnp.concatenate([top, bottom], axis=0).astype(BF16)


def place(index, first_x):
    z, y, c, x = index // 8, (index // 4) % 2, (index // 2) % 2, index % 2
    return c * 16 + z + 4 * (2 * y + x) + first_x * 4 * (x - y)


def reduction_scratch(units):
    sems = [DMA((units,)), DMA((units,)), DMA((units,)), DMA((units, 3))]
    return [pltpu.VMEM((units, n, 48, UW), BF16) for n in (16, 8, 4, 3)] + sems + sems


class Reduction:
    def __init__(self, units, own, parts, sums, held, sems):
        self.units = units
        self.own, self.parts, self.sums, self.held = own, parts, sums, held
        self.sends, self.recvs = sems[:4], sems[4:8]
        dp, x = lax.axis_index("dp"), lax.axis_index("seq")
        z, y, c = dp // 4, (dp // 2) % 2, dp % 2
        self.dp, self.x, self.y, self.z, self.c = dp, x, y, z, c
        self.over_c = (dp + 1 - 2 * c, x)
        self.over_x = (dp, 1 - x)
        self.over_y = (dp + 2 - 4 * y, x)
        self.over_z = [(lax.rem(z + d, 4) * 4 + y * 2 + c, x) for d in (1, 2, 3)]

    def barrier(self):
        sem = pltpu.get_barrier_semaphore()
        for to in (self.over_c, self.over_x, self.over_y, *self.over_z):
            pl.semaphore_signal(sem, inc=1, device_id=to, device_id_type=MESH)
        pl.semaphore_wait(sem, 6)

    def copy(self, src, dst, send, recv, to):
        return pltpu.make_async_remote_copy(
            src_ref=src, dst_ref=dst, send_sem=send, recv_sem=recv, device_id=to, device_id_type=MESH
        )

    def axes(self, u):
        fx, x, y, dp = x_first(u), self.x, self.y, self.dp
        first = (dp + (1 - fx) * (2 - 4 * y), x + fx * (1 - 2 * x))
        second = (dp + fx * (2 - 4 * y), x + (1 - fx) * (1 - 2 * x))
        return first, second, y + fx * (x - y), x + fx * (y - x)

    def hop0(self, u):
        src = self.parts(u).at[pl.ds((1 - self.c) * 16, 16)]
        return self.copy(src, self.held[0].at[u], self.sends[0].at[u], self.recvs[0].at[u], self.over_c)

    def hop1(self, u):
        first, _, a, _ = self.axes(u)
        src = self.held[0].at[u, pl.ds((1 - a) * 8, 8)]
        return self.copy(src, self.held[1].at[u], self.sends[1].at[u], self.recvs[1].at[u], first)

    def hop2(self, u):
        _, second, _, b = self.axes(u)
        src = self.held[1].at[u, pl.ds((1 - b) * 4, 4)]
        return self.copy(src, self.held[2].at[u], self.sends[2].at[u], self.recvs[2].at[u], second)

    def hop3(self, u, d):
        src = self.held[2].at[u, lax.rem(self.z + d + 1, 4)]
        return self.copy(
            src, self.held[3].at[u, d], self.sends[3].at[u, d], self.recvs[3].at[u, d], self.over_z[d]
        )

    def arrived(self, u):
        held = self.held[0].at[u]
        self.copy(held, held, self.sends[0].at[u], self.recvs[0].at[u], self.over_c).wait_recv()

    def start(self, u):
        self.hop0(u).start()

    def step1(self, u):
        self.arrived(u)
        _, _, a, _ = self.axes(u)
        held = self.held[0]

        def add(k):
            held[u, k] = (held[u, k].astype(F32) + self.own(u, k).astype(F32)).astype(BF16)

        @pl.loop(0, 8, unroll=2)
        def _(k):
            add((1 - a) * 8 + k)

        self.hop1(u).start()

        @pl.loop(0, 8, unroll=2)
        def _(k):
            add(a * 8 + k)

    def step2(self, u):
        self.hop1(u).wait_recv()
        _, _, a, b = self.axes(u)
        held, before = self.held[1], self.held[0]

        def add(k):
            held[u, k] = (held[u, k].astype(F32) + before[u, a * 8 + k].astype(F32)).astype(BF16)

        for k in range(4):
            add((1 - b) * 4 + k)
        self.hop2(u).start()
        for k in range(4):
            add(b * 4 + k)

    def step3(self, u):
        self.hop2(u).wait_recv()
        _, _, _, b = self.axes(u)
        held, before = self.held[2], self.held[1]
        for k in range(4):
            held[u, k] = (held[u, k].astype(F32) + before[u, b * 4 + k].astype(F32)).astype(BF16)
        for d in range(3):
            self.hop3(u, d).start()

    def finish(self, u):
        total = self.held[2][u, self.z].astype(F32)
        for d in range(3):
            self.hop3(u, d).wait_recv()
            total = total + self.held[3][u, d].astype(F32)
        self.sums[u] = total

    def drain(self):
        for u in range(self.units):
            self.hop0(u).wait_send()
            self.hop1(u).wait_send()
            self.hop2(u).wait_send()
            for d in range(3):
                self.hop3(u, d).wait_send()


def fwd_kernel(
    len_ref, mask_ref, gain_ref, shift_ref, qb_ref, vb_ref, tok_hbm, cot_hbm, w_hbm,
    nt_hbm, q_hbm, k_hbm, v_hbm, ctx_hbm, tok_out, cot_out, lt_ref, bias_ref,
    tok_ref, cot_ref, w_ref, nt_ref, q_ref, k_ref, v_ref, ctx_ref, mgot_ref,
    sl, so, sx, tx,
):
    dp, x = lax.axis_index("dp"), lax.axis_index("seq")
    here, there = 0, HALF
    load_w = pltpu.make_async_copy(w_hbm, w_ref, sl.at[0])
    load_tok = pltpu.make_async_copy(tok_hbm.at[x], tok_ref.at[pl.ds(here, HALF)], sl.at[1])
    load_cot = pltpu.make_async_copy(cot_hbm.at[x], cot_ref.at[pl.ds(here, HALF)], sl.at[2])
    load_tok.start()
    load_w.start()

    def swap(n):
        if n == 4:
            src, dst = mask_ref, mgot_ref
        else:
            side, buffer = (tok_hbm, tok_ref) if n < 4 else (cot_hbm, cot_ref)
            rows = 128 if n < 4 else 256
            at = (n if n < 4 else n - 5) * rows
            src = side.at[1 - x, pl.ds(at, rows)]
            dst = buffer.at[pl.ds(there + at, rows)]
        return pltpu.make_async_remote_copy(
            src_ref=src, dst_ref=dst, send_sem=sx.at[n], recv_sem=tx.at[n],
            device_id=(dp, 1 - x), device_id_type=MESH,
        )

    sem = pltpu.get_barrier_semaphore()
    pl.semaphore_signal(sem, inc=1, device_id=(dp, 1 - x), device_id_type=MESH)
    pl.semaphore_wait(sem, 1)
    swaps = [swap(n) for n in range(7)]
    for n in (4, 0, 1, 2, 3, 5, 6):
        swaps[n].start()
    load_tok.wait()
    load_w.wait()
    load_cot.start()

    def project(first, count):
        rows = pl.ds(pl.multiple_of(first, count), count)
        n, _ = norm_parts(tok_ref[rows, :].astype(F32))
        normed = (n * row(gain_ref) + row(shift_ref)).astype(BF16)
        nt_ref[:, rows] = normed.T
        q_ref[rows, :] = ((dot_nn(normed, w_ref[:, :D]) + row(qb_ref)) * 0.125).astype(BF16)
        k_ref[rows, :] = dot_nn(normed, w_ref[:, D : 2 * D]).astype(BF16)
        v_ref[rows, :] = (dot_nn(normed, w_ref[:, 2 * D :]) + row(vb_ref)).astype(BF16)

    @pl.loop(0, 2)
    def _(t):
        project(t * 256, 256)

    swaps[4].wait_recv()
    pos = lax.broadcasted_iota(jnp.int32, (1, HALF), 1)
    for first, ref in ((here, mask_ref), (there, mgot_ref)):
        flags = jnp.where(x == 0, ref[0:1, :], ref[1:2, :])
        at = jnp.where(x == 0, first, HALF - first)
        valid = (pos + at < len_ref[x]) & (flags == 1)
        half_bias = jnp.where(valid, 0.0, NEG_FILL).astype(F32)
        bias_ref[:, first : first + HALF] = half_bias
    lane = lax.broadcasted_iota(jnp.int32, (1, 128), 1)
    eye = lax.broadcasted_iota(jnp.int32, (256, 256), 0) == lax.broadcasted_iota(
        jnp.int32, (256, 256), 1
    )

    def attend(p):
        cols = pl.ds(pl.multiple_of(p * 128, 128), 128)
        kp, vp = k_ref[:, cols], v_ref[:, cols]
        vext = jnp.concatenate([vp, jnp.ones_like(vp)], axis=1)
        khs = [jnp.where((lane < HD) == (h == 0), kp, jnp.zeros_like(kp)) for h in range(2)]
        chains = [(a, h) for a in range(0, T, 256) for h in range(2)]

        def score(a, h):
            return dot_nt(q_ref[a : a + 256, cols], khs[h])

        def softmax(a, raw):
            pieces = []
            for b in range(0, T, 256):
                cut = raw[:, b : b + 256]
                piece = cut + bias_ref[:, b : b + 256]
                pieces.append(jnp.where(eye, cut, piece) if a == b else piece)
            s = jnp.concatenate(pieces, axis=1)
            top = jnp.max(s, axis=1, keepdims=True)
            return top, jnp.exp(s - top).astype(BF16)

        def finish(a, h, top, o):
            total = o[:, 128:]
            lt_ref[2 * p + h, :, a : a + 256] = (top + jnp.log(total)).T[0:1, :]
            return o[:, :128] / total

        outs = []
        raw = score(*chains[0])
        for n, (a, h) in enumerate(chains):
            ahead = score(*chains[n + 1]) if n + 1 < len(chains) else None
            top, e = softmax(a, raw)
            outs.append(finish(a, h, top, dot_nn(e, vext)))
            raw = ahead
            if h == 1:
                ctx_ref[a : a + 256, cols] = jnp.where(lane < HD, outs[-2], outs[-1]).astype(BF16)

    for n in range(4):
        swaps[n].wait_recv()
        project(there + n * 128, 128)

    outs = [
        pltpu.make_async_copy(src, dst, so.at[n])
        for n, (src, dst) in enumerate(
            [(nt_ref, nt_hbm), (q_ref, q_hbm), (k_ref, k_hbm), (v_ref, v_hbm), (tok_ref, tok_out)]
        )
    ]
    for one in outs:
        one.start()

    def ctx_out(p):
        cols = pl.ds(pl.multiple_of(p * 128, 128), 128)
        return pltpu.make_async_copy(ctx_ref.at[:, cols], ctx_hbm.at[:, cols], so.at[5 + p])

    @pl.loop(0, PAIRS)
    def _(p):
        attend(p)
        ctx_out(p).start()

    load_cot.wait()
    for n in (5, 6):
        swaps[n].wait_recv()
    last = pltpu.make_async_copy(cot_ref, cot_out, so.at[11])
    last.start()
    for one in swaps:
        one.wait_send()
    for one in outs:
        one.wait()
    for p in range(PAIRS):
        ctx_out(p).wait()
    last.wait()


def call_fwd(*args):
    low = shape((T, D), BF16)
    return pl.pallas_call(
        fwd_kernel,
        out_shape=(
            shape((D, T), BF16), low, low, low, low, low, low, shape((H, 1, T), F32), shape((1, T), F32),
        ),
        in_specs=[SM] + [VM] * 5 + [HB] * 3,
        out_specs=(HB,) * 7 + (VM, VM),
        scratch_shapes=[
            pltpu.VMEM((T, D), BF16),
            pltpu.VMEM((T, D), BF16),
            pltpu.VMEM((D, 3 * D), BF16),
            pltpu.VMEM((D, T), BF16),
            *[pltpu.VMEM((T, D), BF16)] * 4,
            pltpu.VMEM((2, HALF), jnp.int32),
            DMA((3,)), DMA((12,)), DMA((7,)), DMA((7,)),
        ],
        compiler_params=pltpu.CompilerParams(
            vmem_limit_bytes=VMEM_LIMIT, collective_id=2, has_side_effects=True
        ),
    )(*args)


def x_first(unit):
    return unit % 2


def ffn_kernel(
    tok_ref, ctx_ref, ob_ref, g_ref, s_ref, ib_ref, bb_ref, cot_hbm, wo_hbm, wi_hbm, wb_hbm,
    lo_ref, logot_ref, dres_hbm, datt_hbm, grads_hbm, vec_ref, sums_ref,
    wo_ref, wi_ref, wb_ref, nf_ref, act_ref, dpre_ref, dbr_ref, res_ref, dn_ref, away_ref, cot_ref,
    parts_ref, grads_ref, sw, so, sx, tx, *reds,
):
    def parts(u):
        return parts_ref.at[u]

    def own_block(u, k):
        return parts_ref[u, red.c * 16 + k]

    red = Reduction(3, own_block, parts, sums_ref, reds[:4], reds[4:])
    loads = [pltpu.make_async_copy(wo_hbm, wo_ref, sw.at[0])]
    for c in range(4):
        cut = pl.ds(c * 768, 768)
        loads.append(pltpu.make_async_copy(wi_hbm.at[:, cut], wi_ref.at[:, cut], sw.at[1 + 2 * c]))
        loads.append(pltpu.make_async_copy(wb_hbm.at[cut], wb_ref.at[cut], sw.at[2 + 2 * c]))
    loads.append(pltpu.make_async_copy(cot_hbm, cot_ref, sw.at[9]))
    for load in loads:
        load.start()
    red.barrier()
    vec_ref[...] = jnp.zeros_like(vec_ref)
    loads[0].wait()
    lo_copy = red.copy(away_ref, logot_ref, sx, tx, red.over_x)

    def grads_out(u):
        return pltpu.make_async_copy(grads_ref.at[u], grads_hbm.at[u], so.at[8 + u])

    def rows_of(t):
        return pl.ds(pl.multiple_of(HALF - t * HALF, HALF), HALF)

    def forward(t, loads_of):
        rows = rows_of(t)
        res = tok_ref[rows, :].astype(F32) + dot_nn(ctx_ref[rows, :], wo_ref[...]) + row(ob_ref)
        res_ref[rows, :] = res
        n, _ = norm_parts(res)
        normed = (n * row(g_ref) + row(s_ref)).astype(BF16)
        nf_ref[rows, :] = normed
        total = res + row(bb_ref)
        for c in range(4):
            cut = slice(c * 768, (c + 1) * 768)
            for load in loads_of(c):
                load.wait()
            v = dot_nn(normed, wi_ref[:, cut]) + row(ib_ref)[:, cut]
            sq = v * v
            th = jnp.tanh(v * (0.7978845608 + (0.7978845608 * 0.044715) * sq))
            half = 0.5 + 0.5 * th
            act = (v * half).astype(BF16)
            slope = half + v * (half * (1.0 - th)) * (
                0.7978845608 + (3 * 0.7978845608 * 0.044715) * sq
            )
            act_ref[rows, cut] = act
            dpre_ref[rows, cut] = slope.astype(BF16)
            total = total + dot_nn(act, wb_ref[cut, :])
        return total.astype(BF16)

    away_ref[...] = forward(0, lambda c: loads[1 + 2 * c : 3 + 2 * c])
    lo_copy.start()
    lo_ref[...] = forward(1, lambda c: ())

    loads[9].wait()

    @pl.loop(0, 4)
    def _(z):
        g = dot_tn(act_ref[:, pl.ds(pl.multiple_of(z * 768, 768), 768)], cot_ref[...])
        for r in range(8):
            for u in range(4):
                i, j = u // 2, u % 2
                block = g[r * 96 + i * 48 : r * 96 + i * 48 + 48, j * UW : (j + 1) * UW].astype(BF16)
                if u < 3:
                    parts_ref[u, place(r, x_first(u)) + z] = block
                else:
                    grads_ref[5, place(r, x_first(5)) + z] = block

    for u in range(3):
        red.start(u)
    grads_out(5).start()

    def tile_out(t, part):
        rows = rows_of(t)
        if part == 0:
            return pltpu.make_async_copy(res_ref.at[rows], dres_hbm.at[rows], so.at[2 * t])
        return pltpu.make_async_copy(cot_ref.at[rows], datt_hbm.at[rows], so.at[2 * t + 1])

    plan = {1: ((1, 0), (1, 1)), 2: ((1, 2),), 5: ((2, 1), (2, 0)), 7: ((2, 2),)}

    @pl.loop(0, 2)
    def _(t):
        rows = rows_of(t)
        dy = cot_ref[rows, :]
        dn_ref[...] = jnp.zeros_like(dn_ref)
        for c in range(4):
            for at, moves in plan.items():
                if at % 4 == c:

                    @pl.when(t == at // 4)
                    def _():
                        for stage, u in moves:
                            (red.step1, red.step2, red.step3)[stage - 1](u)

            cut = slice(c * 768, (c + 1) * 768)
            d_act = dot_nt(dy, wb_ref[cut, :])
            d_pre = (d_act * dpre_ref[rows, cut].astype(F32)).astype(BF16)
            dpre_ref[rows, cut] = d_pre
            dn_ref[...] += dot_nt(d_pre, wi_ref[:, cut])
            vec_ref[4 + c : 5 + c, :] += jnp.sum(d_pre.astype(F32), axis=0, keepdims=True)

        n, rstd = norm_parts(res_ref[rows, :])
        d_normed = dn_ref[...]
        dyf = dy.astype(F32)
        d_res = dyf + norm_back(d_normed, n, rstd, row(g_ref))
        res_ref[rows, :] = d_res
        tile_out(t, 0).start()
        d_branch = d_res.astype(BF16)
        dbr_ref[rows, :] = d_branch
        cot_ref[rows, :] = dot_nt(d_branch, wo_ref[...]).astype(BF16)
        tile_out(t, 1).start()
        vec_ref[0:1, :] += jnp.sum(dyf, axis=0, keepdims=True)
        vec_ref[1:2, :] += jnp.sum(d_normed * n, axis=0, keepdims=True)
        vec_ref[2:3, :] += jnp.sum(d_normed, axis=0, keepdims=True)
        vec_ref[3:4, :] += jnp.sum(d_branch.astype(F32), axis=0, keepdims=True)

    def unit(u, g):
        for r in range(32):
            rows = slice(r * 24, (r + 1) * 24)
            grads_ref[u, place(r, x_first(u))] = blocks_of(g[rows, :UW], g[rows, UW:])
        grads_out(u).start()

    @pl.loop(0, 4)
    def _(u):
        unit(u, dot_tn(nf_ref[...], dpre_ref[:, pl.ds(pl.multiple_of(u * 768, 768), 768)]))

        @pl.when(u == 0)
        def _():
            red.step3(1)
            red.step3(0)

        @pl.when(u == 2)
        def _():
            red.step3(2)

    unit(4, dot_tn(ctx_ref[...], dbr_ref[...]))
    for u in range(3):
        red.finish(u)
    lo_copy.wait()
    red.drain()
    for t in range(2):
        tile_out(t, 0).wait()
        tile_out(t, 1).wait()
    for u in range(6):
        grads_out(u).wait()


def call_ffn(*args):
    return pl.pallas_call(
        ffn_kernel,
        out_shape=(
            shape((HALF, D), BF16), shape((HALF, D), BF16), shape((T, D), F32), shape((T, D), BF16),
            shape((6, 32, 48, UW), BF16), shape((8, D), F32), shape((3, 48, UW), F32),
        ),
        in_specs=[VM] * 7 + [HB] * 4,
        out_specs=(VM, VM, HB, HB, HB, VM, VM),
        scratch_shapes=[
            pltpu.VMEM((D, D), BF16),
            pltpu.VMEM((D, FF), BF16),
            pltpu.VMEM((FF, D), BF16),
            pltpu.VMEM((T, D), BF16),
            pltpu.VMEM((T, FF), BF16),
            pltpu.VMEM((T, FF), BF16),
            pltpu.VMEM((T, D), BF16),
            pltpu.VMEM((T, D), F32),
            pltpu.VMEM((HALF, D), F32),
            pltpu.VMEM((HALF, D), BF16),
            pltpu.VMEM((T, D), BF16),
            pltpu.VMEM((3, 32, 48, UW), BF16),
            pltpu.VMEM((6, 32, 48, UW), BF16),
            DMA((10,)), DMA((14,)), DMA, DMA, *reduction_scratch(3),
        ],
        compiler_params=pltpu.CompilerParams(
            vmem_limit_bytes=VMEM_LIMIT, collective_id=1, has_side_effects=True
        ),
    )(*args)


def bwd_kernel(
    bias_in, gain_ref, lt_ref, vf_ref,
    tok_hbm, w_hbm, nt_hbm, q_hbm, k_hbm, v_hbm, ctx_hbm, datt_hbm, dres_hbm, gf_ref,
    dtok_ref, dgot_ref, sums_ref, vsum_ref,
    tok_ref, w_ref, nt_ref, q_ref, k_ref, v_ref, ctx_ref, datt_ref, dres_ref, bias_ref,
    dproj_ref, dqt_ref, gq_ref, delta_ref, own_ref, parts_ref, dsend_ref, vs_ref, vr_ref,
    sv, tv, sx, tx, so, sl, sp, *reds,
):
    def parts(u):
        return gf_ref.at[u] if u < 6 else parts_ref.at[u - 6]

    def own_block(u, k):
        return own_ref[u, k]

    red = Reduction(9, own_block, parts, sums_ref, reds[:4], reds[4:])
    c = red.c

    def load_pair(p):
        cols = pl.ds(pl.multiple_of(p * 128, 128), 128)
        sides = ((q_hbm, q_ref), (k_hbm, k_ref), (v_hbm, v_ref), (datt_hbm, datt_ref), (ctx_hbm, ctx_ref))
        return [
            pltpu.make_async_copy(src.at[:, cols], dst.at[:, cols], sp.at[n, p])
            for n, (src, dst) in enumerate(sides)
        ]

    for load in load_pair(0):
        load.start()
    red.barrier()
    for u in range(6):
        red.start(u)
    fetch = pltpu.make_async_copy(gf_ref.at[:, pl.ds(c * 16, 16)], own_ref.at[pl.ds(0, 6)], so)
    fetch.start()
    late_loads = [
        pltpu.make_async_copy(src, dst, sl.at[n])
        for n, (src, dst) in enumerate(
            [(nt_hbm, nt_ref), (w_hbm, w_ref), (tok_hbm, tok_ref), (dres_hbm, dres_ref)]
        )
    ]
    for load in load_pair(1):
        load.start()
    late_loads[0].start()
    for p in range(2, PAIRS):
        for load in load_pair(p):
            load.start()
    for load in late_loads[1:]:
        load.start()

    here, there = 0, HALF

    def vhop(n, to):
        return red.copy(vs_ref.at[min(n, 3)], vr_ref.at[n], sv.at[n], tv.at[n], to)

    hops = [red.over_c, red.over_x, red.over_y, *red.over_z]

    lane = lax.broadcasted_iota(jnp.int32, (1, 128), 1)
    bias_ref[...] = jnp.broadcast_to(bias_in[...], (128, T)).T
    eye = lax.broadcasted_iota(jnp.int32, (256, 256), 0) == lax.broadcasted_iota(
        jnp.int32, (256, 256), 1
    )
    head_of = lax.broadcasted_iota(jnp.int32, (8, 128), 1) // HD == lax.broadcasted_iota(
        jnp.int32, (8, 128), 0
    )
    pick = jnp.where(head_of, 1.0, 0.0).astype(F32)
    vs_ref[0, :8] = vf_ref[...]
    vs_ref[0, 8:] = jnp.zeros((8, D), F32)
    for load in load_pair(0):
        load.wait()

    def progress(j, k):
        if k == 3:

            @pl.when(j == 0)
            def _():
                fetch.wait()

        if k % 2:
            one = 4 * j + (k - 3) // 2

            @pl.when((one >= 0) & (one < 7))
            def _():
                red.step1(one)

            three = 4 * j + (k - 13) // 2

            @pl.when((three >= 0) & (three < 7))
            def _():
                red.step3(three)
        else:
            two = 4 * j + k // 2 - 4

            @pl.when((two >= 0) & (two < 7))
            def _():
                red.step2(two)

            if k in (2, 6):

                @pl.when(j == 2)
                def _():
                    (red.step1 if k == 2 else red.step2)(7)

    @pl.loop(0, 3)
    def _(j):
        for half in range(2):
            p = 2 * j + half
            cols = pl.ds(pl.multiple_of(p * 128, 128), 128)
            if half == 0:

                @pl.when(j > 0)
                def _():
                    for load in load_pair(2 * j):
                        load.wait()

            else:
                for load in load_pair(p):
                    load.wait()
            qp, do = q_ref[:, cols], datt_ref[:, cols]
            prod = do.astype(F32) * ctx_ref[:, cols].astype(F32)
            delta_ref[...] = lax.dot_general(
                pick, prod, (((1,), (1,)), ((), ())),
                preferred_element_type=F32, precision=lax.Precision.HIGHEST,
            )
            dqt_ref[...] = jnp.zeros_like(dqt_ref)
            zero = jnp.zeros_like(qp)
            q2 = jnp.concatenate([jnp.where(lane < HD, qp, zero), jnp.where(lane < HD, zero, qp)], axis=0)
            do2 = jnp.concatenate([jnp.where(lane < HD, do, zero), jnp.where(lane < HD, zero, do)], axis=0)
            for i in range(4):
                progress(j, half * 4 + i)
                cut = slice(i * 256, (i + 1) * 256)
                kp, vp = k_ref[cut, cols], v_ref[cut, cols]
                bias256 = jnp.concatenate([bias_ref[cut]] * 2, axis=1)
                khs, vhs, es, dss = [], [], [[], []], [[], []]
                for h in range(2):
                    mine = (lane < HD) == (h == 0)
                    khs.append(jnp.where(mine, kp, jnp.zeros_like(kp)))
                    vhs.append(jnp.where(mine, vp, jnp.zeros_like(vp)))
                for m in range(4):
                    qs = slice(m * 256, (m + 1) * 256)
                    for h in range(2):
                        raw = dot_nt(khs[h], qp[qs])
                        s = raw + bias256
                        if i == m:
                            s = jnp.where(eye, raw, s)
                        e = jnp.exp(s - lt_ref[2 * p + h, :, qs])
                        dp = dot_nt(vhs[h], do[qs])
                        dss[h].append((e * (dp - delta_ref[h : h + 1, qs])).astype(BF16))
                        es[h].append(e.astype(BF16))
                ds = [jnp.concatenate(d, axis=1) for d in dss]
                dqt_ref[...] += dot_nn(jnp.concatenate(khs, axis=0).T, jnp.concatenate(ds, axis=0))
                dproj_ref[3 * p + 1, cut] = dot_nn(jnp.concatenate(ds, axis=1), q2).astype(BF16)
                dproj_ref[3 * p + 2, cut] = dot_nn(jnp.concatenate(es[0] + es[1], axis=1), do2).astype(BF16)
            dproj_ref[3 * p] = dqt_ref[...].T.astype(BF16) * jnp.asarray(0.125, BF16)
            d3 = jnp.concatenate([dproj_ref[3 * p + n] for n in range(3)], axis=1)
            vs_ref[0, 8:9, cols] = jnp.sum(d3[:, :128].astype(F32), axis=0, keepdims=True)
            vs_ref[0, 9:10, cols] = jnp.sum(d3[:, 256:].astype(F32), axis=0, keepdims=True)
            if half == 0:

                @pl.when(j == 0)
                def _():
                    late_loads[0].wait()

            g = dot_nn(nt_ref[...], d3)
            if half == 0:
                gq_ref[...] = g
            else:
                for r in range(32):
                    rows = slice(r * 24, (r + 1) * 24)
                    parts_ref[j, place(r, x_first(6 + j))] = blocks_of(gq_ref[rows, :], g[rows, :])
        own_ref[6 + j] = parts_ref[j, pl.ds(c * 16, 16)]
        for n in range(3):

            @pl.when(j == n)
            def _():
                red.start(6 + n)

    def tile(rows):
        dqs, dks, dvs = (
            jnp.concatenate([dproj_ref[3 * p + n, rows] for p in range(PAIRS)], axis=1) for n in range(3)
        )
        d_normed = (
            dot_nt(dqs, w_ref[:, :D]) + dot_nt(dks, w_ref[:, D : 2 * D]) + dot_nt(dvs, w_ref[:, 2 * D :])
        )
        n, rstd = norm_parts(tok_ref[rows, :].astype(F32))
        vs_ref[0, 10:11, :] += jnp.sum(d_normed * n, axis=0, keepdims=True)
        vs_ref[0, 11:12, :] += jnp.sum(d_normed, axis=0, keepdims=True)
        return dres_ref[rows, :] + norm_back(d_normed, n, rstd, row(gain_ref))

    def dcopy(t):
        rows = pl.ds(t * 256, 256)
        return red.copy(dsend_ref.at[rows], dgot_ref.at[rows], sx.at[t], tx.at[t], red.over_x)

    def away(t):
        dsend_ref[t * 256 : (t + 1) * 256] = tile(pl.ds(there + t * 256, 256)).astype(BF16)

    def home(t):
        dtok_ref[t * 256 : (t + 1) * 256] = tile(pl.ds(here + t * 256, 256))

    def vstep(n):
        vhop(n, hops[n]).wait_recv()
        vs_ref[n + 1] = vs_ref[n] + vr_ref[n]

    for load in late_loads[1:]:
        load.wait()
    away(0)
    dcopy(0).start()
    red.step3(6)
    red.step1(8)
    away(1)
    home(0)
    home(1)
    vhop(0, hops[0]).start()
    red.step3(7)
    for u in range(7):
        red.finish(u)
    vstep(0)
    vhop(1, hops[1]).start()
    red.step2(8)
    dcopy(1).start()
    vstep(1)
    vhop(2, hops[2]).start()
    red.finish(7)
    red.step3(8)
    vstep(2)
    for d in range(3):
        vhop(3 + d, hops[3 + d]).start()
    red.finish(8)
    total = vs_ref[3]
    for d in range(3):
        vhop(3 + d, hops[3 + d]).wait_recv()
        total = total + vr_ref[3 + d]
    vsum_ref[...] = total
    for t in range(2):
        dcopy(t).wait()
    for n in range(6):
        vhop(n, hops[n]).wait_send()
    red.drain()


def join_kernel(
    lo_ref, logot_ref, dtok_ref, dgot_ref, early_ref, late_ref, vec_ref,
    out_ref, gtok_ref, gin_ref, gback_ref, gout_ref, gqkv_ref, *rest,
):
    vouts, sem = rest[:9], rest[9]
    x = lax.axis_index("seq")
    copies = [
        pltpu.make_async_copy(lo_ref, out_ref.at[x], sem.at[0]),
        pltpu.make_async_copy(logot_ref, out_ref.at[1 - x], sem.at[1]),
        pltpu.make_async_copy(dtok_ref, gtok_ref.at[x], sem.at[2]),
    ]
    for copy in copies:
        copy.start()
    gtok_ref[1 - x] = dgot_ref[...].astype(F32)
    for u in range(4):
        gback_ref[u // 2 * 48 : u // 2 * 48 + 48, u % 2 * UW : (u % 2 + 1) * UW] = (
            early_ref[u] if u < 3 else late_ref[5]
        )
        gin_ref[:, u * D : u * D + UW] = late_ref[u, :24]
        gin_ref[:, u * D + UW : u * D + 2 * UW] = late_ref[u, 24:]
    gout_ref[:, :UW] = late_ref[4, :24]
    gout_ref[:, UW:] = late_ref[4, 24:]
    for p in range(PAIRS):
        part = late_ref[6 + p // 2, p % 2 * 24 : p % 2 * 24 + 24]
        for n in range(3):
            at = n * D + p * 128
            gqkv_ref[:, at : at + 128] = part[:, n * 128 : n * 128 + 128]
    rank = lax.axis_index("dp") * 2 + x
    mine = pltpu.roll(vec_ref[...], D - rank * 24, 1)
    for n, row in enumerate((10, 11, 8, 9, 3, 1, 2, 0)):
        vouts[n][...] = mine[row : row + 1, :24]
    z = rank // 8
    parts = pltpu.roll(vec_ref[4:8, :], D - (rank % 8) * 96, 1)
    chosen = parts[0:1, :96]
    for n in range(1, 4):
        chosen = jnp.where(z == n, parts[n : n + 1, :96], chosen)
    vouts[8][...] = chosen
    for copy in copies:
        copy.wait()


def call_bwd(*args):
    return pl.pallas_call(
        bwd_kernel,
        out_shape=(
            shape((HALF, D), F32), shape((HALF, D), BF16), shape((9, 48, UW), F32), shape((16, D), F32),
        ),
        in_specs=[VM] * 4 + [HB] * 10,
        out_specs=(VM,) * 4,
        scratch_shapes=[
            pltpu.VMEM((T, D), BF16),
            pltpu.VMEM((D, 3 * D), BF16),
            pltpu.VMEM((D, T), BF16),
            *[pltpu.VMEM((T, D), BF16)] * 5,
            pltpu.VMEM((T, D), F32),
            pltpu.VMEM((T, 128), F32),
            pltpu.VMEM((18, T, 128), BF16),
            pltpu.VMEM((128, T), F32),
            pltpu.VMEM((D, UW), F32),
            pltpu.VMEM((8, T), F32),
            pltpu.VMEM((9, 16, 48, UW), BF16),
            pltpu.VMEM((3, 32, 48, UW), BF16),
            pltpu.VMEM((HALF, D), BF16),
            pltpu.VMEM((4, 16, D), F32),
            pltpu.VMEM((6, 16, D), F32),
            DMA((6,)), DMA((6,)), DMA((2,)), DMA((2,)), DMA, DMA((4,)), DMA((5, PAIRS)),
            *reduction_scratch(9),
        ],
        compiler_params=pltpu.CompilerParams(
            vmem_limit_bytes=VMEM_LIMIT, collective_id=0, has_side_effects=True
        ),
    )(*args)


def call_join(*args):
    return pl.pallas_call(
        join_kernel,
        out_shape=(
            shape((2, HALF, D), BF16), shape((2, HALF, D), F32), shape((24, FF), F32), shape((96, D), F32),
            shape((24, D), F32), shape((24, 3 * D), F32), *[shape((1, 24), F32)] * 8, shape((1, 96), F32),
        ),
        in_specs=[HB, HB, HB, VM, VM, VM, VM],
        out_specs=(VM,) * 15,
        scratch_shapes=[DMA((3,))],
        compiler_params=pltpu.CompilerParams(vmem_limit_bytes=VMEM_LIMIT),
    )(*args)

def whole_sequences(
    tokens, lengths, key_mask, attn_gain, attn_shift, w_qkv, query_bias, value_bias, w_out,
    out_bias, ffn_gain, ffn_shift, w_in, in_bias, w_back, back_bias, cotangent,
):
    normed_t, q, k, v, ctx, tok, cot, log_total, bias = call_fwd(
        lengths, key_mask, attn_gain, attn_shift, query_bias, value_bias,
        tokens, cotangent, w_qkv,
    )
    out, out_got, d_res, d_att, gf, vf, early = call_ffn(
        tok, ctx, out_bias, ffn_gain, ffn_shift, in_bias, back_bias, cot,
        w_out, w_in, w_back,
    )
    d_tok, d_got, late, vec = call_bwd(
        bias, attn_gain, log_total, vf,
        tok, w_qkv, normed_t, q, k, v, ctx, d_att, d_res, gf,
    )
    (
        layer_out, grad_tokens, g_in, g_back, g_out, g_qkv, ag, ash, qb, vb, ob, fg, fs, bb, ib,
    ) = call_join(out, out_got, d_tok, d_got, early, late, vec)
    return (
        layer_out, grad_tokens, ag.reshape(24), ash.reshape(24), g_qkv, qb.reshape(24), vb.reshape(24),
        g_out, ob.reshape(24), fg.reshape(24), fs.reshape(24), g_in, ib.reshape(96), g_back,
        bb.reshape(24),
    )

def shifted(array, axis, by):
    devices = lax.axis_size(axis)
    return lax.ppermute(array, axis, [(i, (i + by) % devices) for i in range(devices)])


def layer_norm(values, gain, shift):
    center = values - jnp.mean(values, axis=-1, keepdims=True)
    spread = jnp.mean(center * center, axis=-1, keepdims=True)
    return center * lax.rsqrt(spread + NORM_EPS) * gain + shift


def partial_gelu(values):
    return jax.nn.gelu(values, approximate=True)


def outer_product(left, right):
    return lax.dot_general(
        left, right, (((0,), (0,)), ((), ())), preferred_element_type=jnp.float32
    )


def times_transposed(left, right):
    return lax.dot_general(
        left, right, (((1,), (1,)), ((), ())), preferred_element_type=jnp.float32
    )


def allowed_keys(lengths, flags_all, query_pos, first_key, key_count):
    key_pos = first_key + jnp.arange(key_count, dtype=jnp.int32)
    key_flags = lax.dynamic_slice_in_dim(flags_all, first_key, key_count, 1)
    key_valid = (key_pos[None, :] < lengths[:, None]) & (key_flags == 1)
    itself = key_pos[None, :] == query_pos[:, None]
    return key_valid[:, None, None, :] | itself[None, :, None, :]


def send_home(partial_grads):
    return shifted(partial_grads.astype(jnp.bfloat16), "seq", 1).astype(partial_grads.dtype)


def shards(
    tokens,
    lengths,
    key_mask,
    attn_gain,
    attn_shift,
    w_qkv,
    query_bias,
    value_bias,
    w_out,
    out_bias,
    ffn_gain,
    ffn_shift,
    w_in,
    in_bias,
    w_back,
    back_bias,
    cotangent,
):
    seq_count, span_dev, model_width = tokens.shape
    row_count = seq_count * span_dev
    members = lax.axis_size("seq")
    own_index = lax.axis_index("seq")
    query_pos = own_index * span_dev + jnp.arange(span_dev, dtype=jnp.int32)
    flags_all = lax.all_gather(key_mask, "seq", axis=1, tiled=True)
    inputs = tokens.astype(jnp.float32).reshape(row_count, model_width)
    normed_one, norm_pull_one = jax.vjp(layer_norm, inputs, attn_gain, attn_shift)
    normed_attn = normed_one.astype(jnp.bfloat16)
    projected = jnp.dot(normed_attn, w_qkv, preferred_element_type=jnp.float32)
    queries = ((projected[:, :model_width] + query_bias) * 0.125).astype(jnp.bfloat16)
    queries = queries.reshape(seq_count, span_dev, H, HD)
    keyval = jnp.concatenate(
        [projected[:, model_width : 2 * model_width], projected[:, 2 * model_width :] + value_bias],
        axis=1,
    ).astype(jnp.bfloat16)
    keyval = keyval.reshape(seq_count, span_dev, 2 * model_width)

    def split_block(block_kv):
        key_count = block_kv.shape[1]
        key_heads = block_kv[:, :, :model_width].reshape(seq_count, key_count, H, HD)
        value_heads = block_kv[:, :, model_width:].reshape(seq_count, key_count, H, HD)
        return (key_count, key_heads, value_heads)

    running_max = jnp.full((seq_count, span_dev, H), NEG_FILL, jnp.float32)
    key_count, key_heads, value_heads = split_block(
        lax.all_gather(keyval, "seq", axis=1, tiled=True)
    )
    scores = jnp.einsum("sqhd,skhd->sqhk", queries, key_heads, preferred_element_type=jnp.float32)
    allowed = allowed_keys(lengths, flags_all, query_pos, jnp.int32(0), key_count)
    new_max = jnp.maximum(running_max, jnp.max(jnp.where(allowed, scores, NEG_FILL), axis=-1))
    expo = jnp.exp(jnp.where(allowed, scores - new_max[..., None], NEG_FILL))
    running_sum = jnp.sum(expo, axis=-1)
    running_acc = jnp.einsum(
        "sqhk,skhd->sqhd",
        expo.astype(jnp.bfloat16),
        value_heads,
        preferred_element_type=jnp.float32,
    )
    attended = running_acc / running_sum[..., None]
    log_total = new_max + jnp.log(running_sum)
    context = attended.reshape(row_count, model_width).astype(jnp.bfloat16)
    residual = inputs + jnp.dot(context, w_out, preferred_element_type=jnp.float32) + out_bias
    normed_two, norm_pull_two = jax.vjp(layer_norm, residual, ffn_gain, ffn_shift)
    normed_ffn = normed_two.astype(jnp.bfloat16)
    pre_act = jnp.dot(normed_ffn, w_in, preferred_element_type=jnp.float32) + in_bias
    gelu_value, gelu_pull = jax.vjp(partial_gelu, pre_act)
    activated = gelu_value.astype(jnp.bfloat16)
    layer_out = (
        residual + jnp.dot(activated, w_back, preferred_element_type=jnp.float32) + back_bias
    )
    grad_rows = cotangent.reshape(row_count, model_width)
    grad_float = grad_rows.astype(jnp.float32)
    grad_back_bias = jnp.sum(grad_float, axis=0)
    grad_w_back = outer_product(activated, grad_rows)
    d_act = times_transposed(grad_rows, w_back)
    d_pre = gelu_pull(d_act)[0].astype(jnp.bfloat16)
    grad_in_bias = jnp.sum(d_pre.astype(jnp.float32), axis=0)
    grad_w_in = outer_product(normed_ffn, d_pre)
    d_normed = times_transposed(d_pre, w_in)
    d_res_part, grad_ffn_gain, grad_ffn_shift = norm_pull_two(d_normed)
    d_residual = grad_float + d_res_part
    d_branch = d_residual.astype(jnp.bfloat16)
    grad_out_bias = jnp.sum(d_branch.astype(jnp.float32), axis=0)
    grad_w_out = outer_product(context, d_branch)
    d_attended = (
        times_transposed(d_branch, w_out).astype(jnp.bfloat16).reshape(seq_count, span_dev, H, HD)
    )
    delta = jnp.sum(d_attended.astype(jnp.float32) * attended, axis=-1)

    def attend_back(block_kv, first_key):
        key_count, key_heads, value_heads = split_block(block_kv)
        scores = jnp.einsum(
            "sqhd,skhd->sqhk", queries, key_heads, preferred_element_type=jnp.float32
        )
        allowed = allowed_keys(lengths, flags_all, query_pos, first_key, key_count)
        weights_f = jnp.exp(jnp.where(allowed, scores - log_total[..., None], NEG_FILL))
        d_values = jnp.einsum(
            "sqhk,sqhd->skhd",
            weights_f.astype(jnp.bfloat16),
            d_attended,
            preferred_element_type=jnp.float32,
        )
        d_probs = jnp.einsum(
            "sqhd,skhd->sqhk", d_attended, value_heads, preferred_element_type=jnp.float32
        )
        d_scores = (weights_f * (d_probs - delta[..., None])).astype(jnp.bfloat16)
        d_query = jnp.einsum(
            "sqhk,skhd->sqhd", d_scores, key_heads, preferred_element_type=jnp.float32
        )
        d_keys = jnp.einsum(
            "sqhk,sqhd->skhd", d_scores, queries, preferred_element_type=jnp.float32
        )
        d_block = jnp.concatenate(
            [
                d_keys.reshape(seq_count, key_count, model_width),
                d_values.reshape(seq_count, key_count, model_width),
            ],
            axis=2,
        )
        return (d_query, d_block)

    zero_query = jnp.zeros((seq_count, span_dev, H, HD), jnp.float32)

    def turn(turn_index, state_now):
        current, d_current, d_query = state_now
        anchor = (own_index - turn_index) % members
        add_query, add_block = attend_back(current, anchor * span_dev)
        current = shifted(current, "seq", 1)
        return (current, send_home(d_current + add_block), d_query + add_query)

    start_back = (
        keyval,
        jnp.zeros((seq_count, span_dev, 2 * model_width), jnp.float32),
        zero_query,
    )
    current, d_current, d_query = lax.fori_loop(0, members - 1, turn, start_back)
    anchor = (own_index - (members - 1)) % members
    add_query, add_block = attend_back(current, anchor * span_dev)
    d_query = d_query + add_query
    d_keyval = send_home(d_current + add_block)
    d_query_low = d_query.reshape(row_count, model_width).astype(jnp.bfloat16)
    d_keyval_low = d_keyval.reshape(row_count, 2 * model_width).astype(jnp.bfloat16)
    query_scaled = d_query_low.astype(jnp.float32) * 0.125
    grad_query_bias = jnp.sum(query_scaled, axis=0)
    grad_value_bias = jnp.sum(d_keyval_low[:, model_width:].astype(jnp.float32), axis=0)
    d_projected = jnp.concatenate([query_scaled.astype(jnp.bfloat16), d_keyval_low], axis=1)
    grad_w_qkv = outer_product(normed_attn, d_projected)
    d_normed_attn = times_transposed(d_projected, w_qkv)
    d_in_part, grad_attn_gain, grad_attn_shift = norm_pull_one(d_normed_attn)
    grad_tokens = (d_residual + d_in_part).reshape(seq_count, span_dev, model_width)
    out_block = layer_out.astype(jnp.bfloat16).reshape(seq_count, span_dev, model_width)
    all_sums = (
        lax.psum_scatter(grad_attn_gain, ("dp", "seq"), scatter_dimension=0, tiled=True),
        lax.psum_scatter(grad_attn_shift, ("dp", "seq"), scatter_dimension=0, tiled=True),
        lax.psum_scatter(grad_w_qkv, ("dp", "seq"), scatter_dimension=0, tiled=True),
        lax.psum_scatter(grad_query_bias, ("dp", "seq"), scatter_dimension=0, tiled=True),
        lax.psum_scatter(grad_value_bias, ("dp", "seq"), scatter_dimension=0, tiled=True),
        lax.psum_scatter(grad_w_out, ("dp", "seq"), scatter_dimension=0, tiled=True),
        lax.psum_scatter(grad_out_bias, ("dp", "seq"), scatter_dimension=0, tiled=True),
        lax.psum_scatter(grad_ffn_gain, ("dp", "seq"), scatter_dimension=0, tiled=True),
        lax.psum_scatter(grad_ffn_shift, ("dp", "seq"), scatter_dimension=0, tiled=True),
        lax.psum_scatter(grad_w_in, ("dp", "seq"), scatter_dimension=0, tiled=True),
        lax.psum_scatter(grad_in_bias, ("dp", "seq"), scatter_dimension=0, tiled=True),
        lax.psum_scatter(grad_w_back, ("dp", "seq"), scatter_dimension=0, tiled=True),
        lax.psum_scatter(grad_back_bias, ("dp", "seq"), scatter_dimension=0, tiled=True),
    )
    return (
        out_block,
        grad_tokens,
        all_sums[0],
        all_sums[1],
        all_sums[2],
        all_sums[3],
        all_sums[4],
        all_sums[5],
        all_sums[6],
        all_sums[7],
        all_sums[8],
        all_sums[9],
        all_sums[10],
        all_sums[11],
        all_sums[12],
    )


def solution(mesh):
    sizes = dict(mesh.shape)
    whole = sizes == {"dp": 16, "seq": 2}
    return jax.shard_map(
        whole_sequences if whole else shards,
        mesh=mesh,
        in_specs=(
            P("dp", "seq", None),
            P("dp"),
            P("dp", "seq"),
            P(),
            P(),
            P(),
            P(),
            P(),
            P(),
            P(),
            P(),
            P(),
            P(),
            P(),
            P(),
            P(),
            P("dp", "seq", None),
        ),
        out_specs=(
            P("dp", "seq", None),
            P("dp", "seq", None),
            P(("dp", "seq")),
            P(("dp", "seq")),
            P(("dp", "seq"), None),
            P(("dp", "seq")),
            P(("dp", "seq")),
            P(("dp", "seq"), None),
            P(("dp", "seq")),
            P(("dp", "seq")),
            P(("dp", "seq")),
            P(("dp", "seq"), None),
            P(("dp", "seq")),
            P(("dp", "seq"), None),
            P(("dp", "seq")),
        ),
        check_vma=False,
    )
```

```python
import functools

import jax
import jax.numpy as jnp
from jax import lax
from jax.experimental import pallas as pl
from jax.experimental.pallas import tpu as pltpu
from jax.sharding import PartitionSpec as P

H = 12
HD = 64


NEG_FILL = -1e30
NORM_EPS = 1e-05

F32 = jnp.float32
BF16 = jnp.bfloat16
D = 768
FF = 3072
T = 1024
HALF = 512
PAIRS = 6
UW = 384
MESH = pl.DeviceIdType.MESH
VMEM_LIMIT = 62 * 1024 * 1024


def dot_nn(a, b):
    return lax.dot_general(a, b, (((1,), (0,)), ((), ())), preferred_element_type=F32)


def dot_nt(a, b):
    return lax.dot_general(a, b, (((1,), (1,)), ((), ())), preferred_element_type=F32)


def dot_tn(a, b):
    return lax.dot_general(a, b, (((0,), (0,)), ((), ())), preferred_element_type=F32)


def shape(dims, dtype):
    return jax.ShapeDtypeStruct(dims, dtype)


VM = pl.BlockSpec(memory_space=pltpu.VMEM)
SM = pl.BlockSpec(memory_space=pltpu.SMEM)
HB = pl.BlockSpec(memory_space=pl.ANY)
DMA = pltpu.SemaphoreType.DMA


def row(ref):
    return ref[...].reshape(1, -1)


def norm_parts(x):
    center = x - jnp.mean(x, axis=-1, keepdims=True)
    spread = jnp.mean(center * center, axis=-1, keepdims=True)
    rstd = lax.rsqrt(spread + NORM_EPS)
    return center * rstd, rstd


def norm_back(d_norm, n, rstd, gain):
    u = d_norm * gain
    mean_u = jnp.mean(u, axis=-1, keepdims=True)
    mean_un = jnp.mean(u * n, axis=-1, keepdims=True)
    return (u - mean_u - n * mean_un) * rstd


def blocks_of(top, bottom):
    return jnp.concatenate([top, bottom], axis=0).astype(BF16)


def place(index, first_x):
    z, y, c, x = index // 8, (index // 4) % 2, (index // 2) % 2, index % 2
    return c * 16 + z + 4 * (2 * y + x) + first_x * 4 * (x - y)


def reduction_scratch(units):
    sems = [DMA((units,)), DMA((units,)), DMA((units,)), DMA((units, 3))]
    return [pltpu.VMEM((units, n, 48, UW), BF16) for n in (16, 8, 4, 3)] + sems + sems


class Reduction:
    def __init__(self, units, extra, own, parts, sums, held, sems):
        self.units, self.extra = units, extra
        self.own, self.parts, self.sums, self.held = own, parts, sums, held
        self.sends, self.recvs = sems[:4], sems[4:8]
        dp, x = lax.axis_index("dp"), lax.axis_index("seq")
        z, y, c = dp // 4, (dp // 2) % 2, dp % 2
        self.dp, self.x, self.y, self.z, self.c = dp, x, y, z, c
        self.over_c = (dp + 1 - 2 * c, x)
        self.over_x = (dp, 1 - x)
        self.over_y = (dp + 2 - 4 * y, x)
        self.over_z = [(lax.rem(z + d, 4) * 4 + y * 2 + c, x) for d in (1, 2, 3)]

    def barrier(self):
        sem = pltpu.get_barrier_semaphore()
        for to in (self.over_c, self.over_x, self.over_y, *self.over_z):
            pl.semaphore_signal(sem, inc=1, device_id=to, device_id_type=MESH)
        pl.semaphore_wait(sem, 6)

    def copy(self, src, dst, send, recv, to):
        return pltpu.make_async_remote_copy(
            src_ref=src, dst_ref=dst, send_sem=send, recv_sem=recv, device_id=to, device_id_type=MESH
        )

    def axes(self, u):
        fx, x, y, dp = x_first(u), self.x, self.y, self.dp
        first = (dp + (1 - fx) * (2 - 4 * y), x + fx * (1 - 2 * x))
        second = (dp + fx * (2 - 4 * y), x + (1 - fx) * (1 - 2 * x))
        return first, second, y + fx * (x - y), x + fx * (y - x)

    def hop0(self, u):
        src = self.parts(u).at[pl.ds((1 - self.c) * 16, 16)]
        return self.copy(src, self.held[0].at[u], self.sends[0].at[u], self.recvs[0].at[u], self.over_c)

    def hop1(self, u):
        first, _, a, _ = self.axes(u)
        src = self.held[0].at[u, pl.ds((1 - a) * 8, 8)]
        return self.copy(src, self.held[1].at[u], self.sends[1].at[u], self.recvs[1].at[u], first)

    def hop2(self, u):
        _, second, _, b = self.axes(u)
        src = self.held[1].at[u, pl.ds((1 - b) * 4, 4)]
        return self.copy(src, self.held[2].at[u], self.sends[2].at[u], self.recvs[2].at[u], second)

    def hop3(self, u, d):
        src = self.held[2].at[u, lax.rem(self.z + d + 1, 4)]
        return self.copy(
            src, self.held[3].at[u, d], self.sends[3].at[u, d], self.recvs[3].at[u, d], self.over_z[d]
        )

    def arrived(self, u):
        held = self.held[0].at[u]
        self.copy(held, held, self.sends[0].at[u], self.recvs[0].at[u], self.over_c).wait_recv()

    def start(self, u):
        self.hop0(u).start()

    def step1(self, u):
        self.arrived(u)
        _, _, a, _ = self.axes(u)
        held = self.held[0]

        def add(k):
            held[u, k] = (held[u, k].astype(F32) + self.own(u, k).astype(F32)).astype(BF16)

        @pl.loop(0, 8, unroll=2)
        def _(k):
            add((1 - a) * 8 + k)

        self.hop1(u).start()

        @pl.loop(0, 8, unroll=2)
        def _(k):
            add(a * 8 + k)

    def step2(self, u):
        self.hop1(u).wait_recv()
        _, _, a, b = self.axes(u)
        held, before = self.held[1], self.held[0]

        def add(k):
            held[u, k] = (held[u, k].astype(F32) + before[u, a * 8 + k].astype(F32)).astype(BF16)

        for k in range(4):
            add((1 - b) * 4 + k)
        self.hop2(u).start()
        for k in range(4):
            add(b * 4 + k)

    def step3(self, u):
        self.hop2(u).wait_recv()
        _, _, _, b = self.axes(u)
        held, before = self.held[2], self.held[1]
        for k in range(4):
            held[u, k] = (held[u, k].astype(F32) + before[u, b * 4 + k].astype(F32)).astype(BF16)
        for d in range(3):
            self.hop3(u, d).start()

    def finish(self, u):
        total = self.held[2][u, self.z].astype(F32)
        for d in range(3):
            self.hop3(u, d).wait_recv()
            total = total + self.held[3][u, d].astype(F32)
        self.sums[u] = total

    def last_hop(self, d):
        across, cross_send, cross_recv, sends, recvs = self.last
        u = self.units
        if d == 3:
            return self.copy(cross_send, cross_recv, sends.at[3], recvs.at[3], self.over_x)
        src = self.held[1].at[u, pl.ds(lax.rem(self.z + d + 1, 4) * 2, 2)]
        return self.copy(src, across.at[d], sends.at[d], recvs.at[d], self.over_z[d])

    def last_step2(self):
        u = self.units
        self.hop1(u).wait_recv()
        for k in range(8):
            self.held[1][u, k] = (
                self.held[1][u, k].astype(F32) + self.held[0][u, self.y * 8 + k].astype(F32)
            ).astype(BF16)
        for d in range(3):
            self.last_hop(d).start()

    def last_step3(self):
        across, cross_send = self.last[:2]
        for d in range(3):
            self.last_hop(d).wait_recv()
        totals = []
        for k in range(2):
            total = self.held[1][self.units, self.z * 2 + k].astype(F32)
            for d in range(3):
                total = total + across[d, k].astype(F32)
            totals.append(total)
        cross_send[...] = jnp.where(self.x == 0, totals[1], totals[0]).astype(BF16)
        self.last_hop(3).start()
        self.sums[self.units] = jnp.where(self.x == 0, totals[0], totals[1])

    def last_finish(self):
        self.last_hop(3).wait_recv()
        self.sums[self.units] = self.sums[self.units] + self.last[2][...].astype(F32)

    def drain(self):
        for u in range(self.units):
            self.hop0(u).wait_send()
            self.hop1(u).wait_send()
            self.hop2(u).wait_send()
            for d in range(3):
                self.hop3(u, d).wait_send()
        if self.extra:
            self.hop0(self.units).wait_send()
            self.hop1(self.units).wait_send()
            for d in range(4):
                self.last_hop(d).wait_send()


def fwd_kernel(
    len_ref, mask_ref, gain_ref, shift_ref, qb_ref, vb_ref, tok_hbm, cot_hbm, w_hbm,
    nt_hbm, q_hbm, k_hbm, v_hbm, ctx_hbm, tok_out, cot_out, lt_ref, bias_ref,
    tok_ref, cot_ref, w_ref, nt_ref, q_ref, k_ref, v_ref, ctx_ref, mgot_ref, part_ref, mx_ref, logs_ref,
    sl, so, sx, tx,
):
    dp, x = lax.axis_index("dp"), lax.axis_index("seq")
    here, there = 0, HALF
    load_w = pltpu.make_async_copy(w_hbm, w_ref, sl.at[0])
    load_tok = pltpu.make_async_copy(tok_hbm.at[x], tok_ref.at[pl.ds(here, HALF)], sl.at[1])
    load_cot = pltpu.make_async_copy(cot_hbm.at[x], cot_ref.at[pl.ds(here, HALF)], sl.at[2])
    load_tok.start()
    load_w.start()

    def swap(n):
        if n == 4:
            src, dst = mask_ref, mgot_ref
        else:
            side, buffer = (tok_hbm, tok_ref) if n < 4 else (cot_hbm, cot_ref)
            rows = 128 if n < 4 else 256
            at = (n if n < 4 else n - 5) * rows
            src = side.at[1 - x, pl.ds(at, rows)]
            dst = buffer.at[pl.ds(there + at, rows)]
        return pltpu.make_async_remote_copy(
            src_ref=src, dst_ref=dst, send_sem=sx.at[n], recv_sem=tx.at[n],
            device_id=(dp, 1 - x), device_id_type=MESH,
        )

    sem = pltpu.get_barrier_semaphore()
    pl.semaphore_signal(sem, inc=1, device_id=(dp, 1 - x), device_id_type=MESH)
    pl.semaphore_wait(sem, 1)
    swaps = [swap(n) for n in range(7)]
    for n in (4, 0, 1, 2, 3, 5, 6):
        swaps[n].start()
    load_tok.wait()
    load_w.wait()
    load_cot.start()

    def project(first, count):
        rows = pl.ds(pl.multiple_of(first, count), count)
        n, _ = norm_parts(tok_ref[rows, :].astype(F32))
        normed = (n * row(gain_ref) + row(shift_ref)).astype(BF16)
        nt_ref[:, rows] = normed.T
        q_ref[rows, :] = ((dot_nn(normed, w_ref[:, :D]) + row(qb_ref)) * 0.125).astype(BF16)
        k_ref[rows, :] = dot_nn(normed, w_ref[:, D : 2 * D]).astype(BF16)
        v_ref[rows, :] = (dot_nn(normed, w_ref[:, 2 * D :]) + row(vb_ref)).astype(BF16)

    @pl.loop(0, 2)
    def _(t):
        project(t * 256, 256)

    swaps[4].wait_recv()
    pos = lax.broadcasted_iota(jnp.int32, (1, HALF), 1)
    for first, ref in ((here, mask_ref), (there, mgot_ref)):
        flags = jnp.where(x == 0, ref[0:1, :], ref[1:2, :])
        at = jnp.where(x == 0, first, HALF - first)
        valid = (pos + at < len_ref[x]) & (flags == 1)
        half_bias = jnp.where(valid, 0.0, NEG_FILL).astype(F32)
        bias_ref[:, first : first + HALF] = half_bias
    lane = lax.broadcasted_iota(jnp.int32, (1, 128), 1)
    wide = lax.broadcasted_iota(jnp.int32, (256, 128), 1)
    logs_ref[...] = jnp.zeros_like(logs_ref)
    eye = lax.broadcasted_iota(jnp.int32, (256, 256), 0) == lax.broadcasted_iota(
        jnp.int32, (256, 256), 1
    )

    def attend(p, chains, spans, first):
        cols = pl.ds(pl.multiple_of(p * 128, 128), 128)
        keys, values = {}, {}
        for low, high in sorted(set(spans.values())):
            kp, vp = k_ref[low:high, cols], v_ref[low:high, cols]
            keys[low, high] = [jnp.where((lane < HD) == (h == 0), kp, jnp.zeros_like(kp)) for h in range(2)]
            values[low, high] = jnp.concatenate([vp, jnp.ones_like(vp)], axis=1)

        def score(a, h):
            return dot_nt(q_ref[a : a + 256, cols], keys[spans[a]][h])

        def softmax(a, raw, before):
            low, high = spans[a]
            pieces = []
            for b in range(low, high, 256):
                cut = raw[:, b - low : b - low + 256]
                piece = cut + bias_ref[:, b : b + 256]
                pieces.append(jnp.where(eye, cut, piece) if a == b else piece)
            s = jnp.concatenate(pieces, axis=1)
            top = jnp.max(s, axis=1, keepdims=True)
            if before is not None:
                top = jnp.maximum(top, before)
            return top, jnp.exp(s - top).astype(BF16)

        outs = []
        raw = score(*chains[0])
        for n, (a, h) in enumerate(chains):
            ahead = score(*chains[n + 1]) if n + 1 < len(chains) else None
            merge = not first and a < HALF
            before = mx_ref[2 * p + h, a : a + 256, 0:1] if merge else None
            top, e = softmax(a, raw, before)
            o = dot_nn(e, values[spans[a]])
            raw = ahead
            if first:
                part_ref[2 * p + h, a : a + 256] = o
                mx_ref[2 * p + h, a : a + 256] = jnp.broadcast_to(top, (256, 128))
                continue
            if merge:
                o = o + part_ref[2 * p + h, a : a + 256] * jnp.exp(before - top)
            total = o[:, 128:]
            logs_ref[a : a + 256] = jnp.where(wide == 2 * p + h, top + jnp.log(total), logs_ref[a : a + 256])
            outs.append(o[:, :128] / total)
            if h == 1:
                ctx_ref[a : a + 256, cols] = jnp.where(lane < HD, outs[-2], outs[-1]).astype(BF16)

    own = [(a, h) for a in (0, 256) for h in range(2)]
    other = [(a, h) for a in (512, 768) for h in range(2)]

    @pl.loop(0, PAIRS)
    def _(p):
        attend(p, own, {0: (0, HALF), 256: (0, HALF)}, True)

    for n in range(4):
        swaps[n].wait_recv()
        project(there + n * 128, 128)

    outs = [
        pltpu.make_async_copy(src, dst, so.at[n])
        for n, (src, dst) in enumerate(
            [(nt_ref, nt_hbm), (q_ref, q_hbm), (k_ref, k_hbm), (v_ref, v_hbm), (tok_ref, tok_out)]
        )
    ]
    for one in outs:
        one.start()

    def ctx_out(p):
        cols = pl.ds(pl.multiple_of(p * 128, 128), 128)
        return pltpu.make_async_copy(ctx_ref.at[:, cols], ctx_hbm.at[:, cols], so.at[5 + p])

    @pl.loop(0, PAIRS)
    def _(p):
        attend(p, own + other, {0: (HALF, T), 256: (HALF, T), 512: (0, T), 768: (0, T)}, False)
        ctx_out(p).start()

    logs = logs_ref[...].T
    for h in range(H):
        lt_ref[h] = logs[h : h + 1]
    load_cot.wait()
    for n in (5, 6):
        swaps[n].wait_recv()
    last = pltpu.make_async_copy(cot_ref, cot_out, so.at[11])
    last.start()
    for one in swaps:
        one.wait_send()
    for one in outs:
        one.wait()
    for p in range(PAIRS):
        ctx_out(p).wait()
    last.wait()


def call_fwd(*args):
    low = shape((T, D), BF16)
    return pl.pallas_call(
        fwd_kernel,
        out_shape=(
            shape((D, T), BF16), low, low, low, low, low, low, shape((H, 1, T), F32), shape((1, T), F32),
        ),
        in_specs=[SM] + [VM] * 5 + [HB] * 3,
        out_specs=(HB,) * 7 + (VM, VM),
        scratch_shapes=[
            pltpu.VMEM((T, D), BF16),
            pltpu.VMEM((T, D), BF16),
            pltpu.VMEM((D, 3 * D), BF16),
            pltpu.VMEM((D, T), BF16),
            *[pltpu.VMEM((T, D), BF16)] * 4,
            pltpu.VMEM((2, HALF), jnp.int32),
            pltpu.VMEM((H, HALF, 256), F32),
            pltpu.VMEM((H, HALF, 128), F32),
            pltpu.VMEM((T, 128), F32),
            DMA((3,)), DMA((12,)), DMA((7,)), DMA((7,)),
        ],
        compiler_params=pltpu.CompilerParams(
            vmem_limit_bytes=VMEM_LIMIT, collective_id=2, has_side_effects=True
        ),
    )(*args)


def x_first(unit):
    return (unit + 1) % 2


def ffn_kernel(
    tok_ref, ctx_ref, ob_ref, g_ref, s_ref, ib_ref, bb_ref, cot_hbm, wo_hbm, wi_hbm, wb_hbm,
    lo_ref, logot_ref, dres_hbm, datt_hbm, grads_hbm, vec_ref, sums_ref,
    wo_ref, wi_ref, wb_ref, nf_ref, act_ref, dpre_ref, dbr_ref, res_ref, dn_ref, away_ref, cot_ref,
    parts_ref, grads_ref, sw, so, sx, tx, *reds,
):
    def parts(u):
        return parts_ref.at[u]

    def own_block(u, k):
        return parts_ref[u, red.c * 16 + k]

    red = Reduction(2, 0, own_block, parts, sums_ref, reds[:4], reds[4:])
    loads = [pltpu.make_async_copy(wo_hbm, wo_ref, sw.at[0])]
    for c in range(4):
        cut = pl.ds(c * 768, 768)
        loads.append(pltpu.make_async_copy(wi_hbm.at[:, cut], wi_ref.at[:, cut], sw.at[1 + 2 * c]))
        loads.append(pltpu.make_async_copy(wb_hbm.at[cut], wb_ref.at[cut], sw.at[2 + 2 * c]))
    loads.append(pltpu.make_async_copy(cot_hbm, cot_ref, sw.at[9]))
    for load in loads:
        load.start()
    red.barrier()
    vec_ref[...] = jnp.zeros_like(vec_ref)
    loads[0].wait()
    lo_copy = red.copy(away_ref, logot_ref, sx, tx, red.over_x)

    def grads_out(u):
        return pltpu.make_async_copy(grads_ref.at[u], grads_hbm.at[u], so.at[8 + u])

    def rows_of(t):
        return pl.ds(pl.multiple_of(HALF - t * HALF, HALF), HALF)

    def forward(t, loads_of):
        rows = rows_of(t)
        res = tok_ref[rows, :].astype(F32) + dot_nn(ctx_ref[rows, :], wo_ref[...]) + row(ob_ref)
        res_ref[rows, :] = res
        n, _ = norm_parts(res)
        normed = (n * row(g_ref) + row(s_ref)).astype(BF16)
        nf_ref[rows, :] = normed
        total = res + row(bb_ref)
        for c in range(4):
            cut = slice(c * 768, (c + 1) * 768)
            for load in loads_of(c):
                load.wait()
            v = dot_nn(normed, wi_ref[:, cut]) + row(ib_ref)[:, cut]
            sq = v * v
            th = jnp.tanh(v * (0.7978845608 + (0.7978845608 * 0.044715) * sq))
            half = 0.5 + 0.5 * th
            act = (v * half).astype(BF16)
            slope = half + v * (half * (1.0 - th)) * (
                0.7978845608 + (3 * 0.7978845608 * 0.044715) * sq
            )
            act_ref[rows, cut] = act
            dpre_ref[rows, cut] = slope.astype(BF16)
            total = total + dot_nn(act, wb_ref[cut, :])
        return total.astype(BF16)

    away_ref[...] = forward(0, lambda c: loads[1 + 2 * c : 3 + 2 * c])
    lo_copy.start()
    lo_ref[...] = forward(1, lambda c: ())

    loads[9].wait()

    @pl.loop(0, 4)
    def _(z):
        g = dot_tn(act_ref[:, pl.ds(pl.multiple_of(z * 768, 768), 768)], cot_ref[...])
        for r in range(8):
            for u in range(4):
                i, j = u // 2, u % 2
                block = g[r * 96 + i * 48 : r * 96 + i * 48 + 48, j * UW : (j + 1) * UW].astype(BF16)
                if u < 2:
                    parts_ref[u, place(r, x_first(u)) + z] = block
                else:
                    grads_ref[3 + u, place(r, x_first(3 + u)) + z] = block

    for u in range(2):
        red.start(u)
    for u in (5, 6):
        grads_out(u).start()

    def tile_out(t, part):
        rows = rows_of(t)
        if part == 0:
            return pltpu.make_async_copy(res_ref.at[rows], dres_hbm.at[rows], so.at[2 * t])
        return pltpu.make_async_copy(cot_ref.at[rows], datt_hbm.at[rows], so.at[2 * t + 1])

    plan = {2: ((1, 0), (1, 1)), 6: ((2, 0), (2, 1))}

    @pl.loop(0, 2)
    def _(t):
        rows = rows_of(t)
        dy = cot_ref[rows, :]
        dn_ref[...] = jnp.zeros_like(dn_ref)
        for c in range(4):
            for at, moves in plan.items():
                if at % 4 == c:

                    @pl.when(t == at // 4)
                    def _():
                        for stage, u in moves:
                            (red.step1, red.step2, red.step3)[stage - 1](u)

            cut = slice(c * 768, (c + 1) * 768)
            d_act = dot_nt(dy, wb_ref[cut, :])
            d_pre = (d_act * dpre_ref[rows, cut].astype(F32)).astype(BF16)
            dpre_ref[rows, cut] = d_pre
            dn_ref[...] += dot_nt(d_pre, wi_ref[:, cut])
            vec_ref[4 + c : 5 + c, :] += jnp.sum(d_pre.astype(F32), axis=0, keepdims=True)

        n, rstd = norm_parts(res_ref[rows, :])
        d_normed = dn_ref[...]
        dyf = dy.astype(F32)
        d_res = dyf + norm_back(d_normed, n, rstd, row(g_ref))
        res_ref[rows, :] = d_res
        tile_out(t, 0).start()
        d_branch = d_res.astype(BF16)
        dbr_ref[rows, :] = d_branch
        cot_ref[rows, :] = dot_nt(d_branch, wo_ref[...]).astype(BF16)
        tile_out(t, 1).start()
        vec_ref[0:1, :] += jnp.sum(dyf, axis=0, keepdims=True)
        vec_ref[1:2, :] += jnp.sum(d_normed * n, axis=0, keepdims=True)
        vec_ref[2:3, :] += jnp.sum(d_normed, axis=0, keepdims=True)
        vec_ref[3:4, :] += jnp.sum(d_branch.astype(F32), axis=0, keepdims=True)

    def unit(u, g):
        for r in range(32):
            rows = slice(r * 24, (r + 1) * 24)
            grads_ref[u, place(r, x_first(u))] = blocks_of(g[rows, :UW], g[rows, UW:])
        grads_out(u).start()

    @pl.loop(0, 4)
    def _(u):
        unit(u, dot_tn(nf_ref[...], dpre_ref[:, pl.ds(pl.multiple_of(u * 768, 768), 768)]))

        @pl.when(u == 0)
        def _():
            red.step3(0)
            red.step3(1)

    unit(4, dot_tn(ctx_ref[...], dbr_ref[...]))
    for u in range(2):
        red.finish(u)
    lo_copy.wait()
    red.drain()
    for t in range(2):
        tile_out(t, 0).wait()
        tile_out(t, 1).wait()
    for u in range(7):
        grads_out(u).wait()


def call_ffn(*args):
    return pl.pallas_call(
        ffn_kernel,
        out_shape=(
            shape((HALF, D), BF16), shape((HALF, D), BF16), shape((T, D), F32), shape((T, D), BF16),
            shape((7, 32, 48, UW), BF16), shape((8, D), F32), shape((2, 48, UW), F32),
        ),
        in_specs=[VM] * 7 + [HB] * 4,
        out_specs=(VM, VM, HB, HB, HB, VM, VM),
        scratch_shapes=[
            pltpu.VMEM((D, D), BF16),
            pltpu.VMEM((D, FF), BF16),
            pltpu.VMEM((FF, D), BF16),
            pltpu.VMEM((T, D), BF16),
            pltpu.VMEM((T, FF), BF16),
            pltpu.VMEM((T, FF), BF16),
            pltpu.VMEM((T, D), BF16),
            pltpu.VMEM((T, D), F32),
            pltpu.VMEM((HALF, D), F32),
            pltpu.VMEM((HALF, D), BF16),
            pltpu.VMEM((T, D), BF16),
            pltpu.VMEM((2, 32, 48, UW), BF16),
            pltpu.VMEM((7, 32, 48, UW), BF16),
            DMA((10,)), DMA((15,)), DMA, DMA, *reduction_scratch(2),
        ],
        compiler_params=pltpu.CompilerParams(
            vmem_limit_bytes=VMEM_LIMIT, collective_id=1, has_side_effects=True
        ),
    )(*args)


def bwd_kernel(
    bias_in, gain_ref, lt_ref, vf_ref,
    tok_hbm, w_hbm, nt_hbm, q_hbm, k_hbm, v_hbm, ctx_hbm, datt_hbm, dres_hbm, gf_ref,
    dtok_hbm, dgot_hbm, sums_hbm, vsum_ref,
    tok_ref, w_ref, nt_ref, q_ref, k_ref, v_ref, ctx_ref, datt_ref, dres_ref, bias_ref,
    dproj_ref, dqt_ref, gq_ref, delta_ref, own_ref, parts_ref, dsend_ref, vs_ref, vr_ref, dtok_ref, dsend_got, sums_ref,
    sv, tv, sx, tx, so, sl, sp, across, cross_send, cross_recv, se, te, *reds,
):
    def parts(u):
        return gf_ref.at[u] if u < 7 else parts_ref.at[u - 7]

    def own_block(u, k):
        return own_ref[u, k]

    red = Reduction(9, 1, own_block, parts, sums_ref, reds[:4], reds[4:])
    red.last = (across, cross_send, cross_recv, se, te)
    c = red.c

    def load_pair(p):
        cols = pl.ds(pl.multiple_of(p * 128, 128), 128)
        sides = ((q_hbm, q_ref), (k_hbm, k_ref), (v_hbm, v_ref), (datt_hbm, datt_ref), (ctx_hbm, ctx_ref))
        return [
            pltpu.make_async_copy(src.at[:, cols], dst.at[:, cols], sp.at[n, p])
            for n, (src, dst) in enumerate(sides)
        ]

    for load in load_pair(0):
        load.start()
    red.barrier()
    for u in range(7):
        red.start(u)
    fetch = pltpu.make_async_copy(gf_ref.at[:, pl.ds(c * 16, 16)], own_ref.at[pl.ds(0, 7)], so)
    fetch.start()
    late_loads = [
        pltpu.make_async_copy(src, dst, sl.at[n])
        for n, (src, dst) in enumerate(
            [(nt_hbm, nt_ref), (w_hbm, w_ref), (tok_hbm, tok_ref), (dres_hbm, dres_ref)]
        )
    ]
    for load in load_pair(1):
        load.start()
    late_loads[0].start()
    for p in range(2, PAIRS):
        for load in load_pair(p):
            load.start()
    for load in late_loads[1:]:
        load.start()

    here, there = 0, HALF

    hops = [red.over_c, *red.over_z, red.over_y, red.over_x]

    def vhop(g, n):
        src = vs_ref.at[g, (0, 1, 1, 1, 2, 3)[n]]
        return red.copy(src, vr_ref.at[g, n], sv.at[g, n], tv.at[g, n], hops[n])

    def vstep(g, stage):
        came = ((), (0,), (1, 2, 3), (4,), (5,))[stage]
        if stage:
            total = vs_ref[g, stage - 1]
            for n in came:
                vhop(g, n).wait_recv()
                total = total + vr_ref[g, n]
            if stage == 4:
                vsum_ref[8 * g : 8 * g + 8] = total
            else:
                vs_ref[g, stage] = total
        for n in ((0,), (1, 2, 3), (4,), (5,), ())[stage]:
            vhop(g, n).start()

    lane = lax.broadcasted_iota(jnp.int32, (1, 128), 1)
    bias_ref[...] = jnp.broadcast_to(bias_in[...], (128, T)).T
    eye = lax.broadcasted_iota(jnp.int32, (256, 256), 0) == lax.broadcasted_iota(
        jnp.int32, (256, 256), 1
    )
    head_of = lax.broadcasted_iota(jnp.int32, (8, 128), 1) // HD == lax.broadcasted_iota(
        jnp.int32, (8, 128), 0
    )
    pick = jnp.where(head_of, 1.0, 0.0).astype(F32)
    vs_ref[0, 0] = vf_ref[...]
    vs_ref[1, 0] = jnp.zeros((8, D), F32)
    vstep(0, 0)
    for load in load_pair(0):
        load.wait()

    def progress(j, k):
        if k == 3:

            @pl.when(j == 0)
            def _():
                fetch.wait()

        if k == 7:
            for n in range(3):

                @pl.when(j == n)
                def _():
                    vstep(0, n + 1)

        if k % 2:
            one = 4 * j + (k - 3) // 2

            @pl.when((one >= 0) & (one < 9))
            def _():
                red.step1(one)

            three = 4 * j + (k - 13) // 2

            @pl.when(three >= 0)
            def _():
                red.step3(three)
        else:
            two = 4 * j + k // 2 - 4

            @pl.when(two >= 0)
            def _():
                red.step2(two)

    @pl.loop(0, 3)
    def _(j):
        for half in range(2):
            p = 2 * j + half
            cols = pl.ds(pl.multiple_of(p * 128, 128), 128)

            def lanes(at, p=p):
                return pl.ds(pl.multiple_of(at + p * 128, 128), 128)

            if half == 0:

                @pl.when(j > 0)
                def _():
                    for load in load_pair(2 * j):
                        load.wait()

            else:
                for load in load_pair(p):
                    load.wait()
            qp, do = q_ref[:, cols], datt_ref[:, cols]
            prod = do.astype(F32) * ctx_ref[:, cols].astype(F32)
            delta_ref[...] = lax.dot_general(
                pick, prod, (((1,), (1,)), ((), ())),
                preferred_element_type=F32, precision=lax.Precision.HIGHEST,
            )
            dqt_ref[...] = jnp.zeros_like(dqt_ref)
            zero = jnp.zeros_like(qp)
            q2 = jnp.concatenate([jnp.where(lane < HD, qp, zero), jnp.where(lane < HD, zero, qp)], axis=0)
            do2 = jnp.concatenate([jnp.where(lane < HD, do, zero), jnp.where(lane < HD, zero, do)], axis=0)
            for i in range(4):
                progress(j, half * 4 + i)
                cut = slice(i * 256, (i + 1) * 256)
                kp, vp = k_ref[cut, cols], v_ref[cut, cols]
                bias256 = jnp.concatenate([bias_ref[cut]] * 2, axis=1)
                khs, vhs, es, dss = [], [], [[], []], [[], []]
                for h in range(2):
                    mine = (lane < HD) == (h == 0)
                    khs.append(jnp.where(mine, kp, jnp.zeros_like(kp)))
                    vhs.append(jnp.where(mine, vp, jnp.zeros_like(vp)))
                for m in range(4):
                    qs = slice(m * 256, (m + 1) * 256)
                    for h in range(2):
                        raw = dot_nt(khs[h], qp[qs])
                        s = raw + bias256
                        if i == m:
                            s = jnp.where(eye, raw, s)
                        e = jnp.exp(s - lt_ref[2 * p + h, :, qs])
                        dp = dot_nt(vhs[h], do[qs])
                        dss[h].append((e * (dp - delta_ref[h : h + 1, qs])).astype(BF16))
                        es[h].append(e.astype(BF16))
                ds = [jnp.concatenate(d, axis=1) for d in dss]
                dqt_ref[...] += dot_nn(jnp.concatenate(khs, axis=0).T, jnp.concatenate(ds, axis=0))
                dproj_ref[cut, lanes(D)] = dot_nn(jnp.concatenate(ds, axis=1), q2).astype(BF16)
                dproj_ref[cut, lanes(2 * D)] = dot_nn(jnp.concatenate(es[0] + es[1], axis=1), do2).astype(BF16)
            dproj_ref[:, cols] = dqt_ref[...].T.astype(BF16) * jnp.asarray(0.125, BF16)
            d3 = jnp.concatenate([dproj_ref[:, lanes(n * D)] for n in range(3)], axis=1)
            vs_ref[1, 0, 0:1, cols] = jnp.sum(d3[:, :128].astype(F32), axis=0, keepdims=True)
            vs_ref[1, 0, 1:2, cols] = jnp.sum(d3[:, 256:].astype(F32), axis=0, keepdims=True)
            if half == 0:

                @pl.when(j == 0)
                def _():
                    late_loads[0].wait()

            g = dot_nn(nt_ref[...], d3)
            if half == 0:
                gq_ref[...] = g
            else:
                for r in range(32):
                    rows = slice(r * 24, (r + 1) * 24)
                    at = place(r, x_first(7 + j)) + j // 2 * (r // 8 - 3 * (r % 2))
                    parts_ref[j, at] = blocks_of(gq_ref[rows, :], g[rows, :])
        own_ref[7 + j] = parts_ref[j, pl.ds(c * 16, 16)]
        for n in range(3):

            @pl.when(j == n)
            def _():
                red.start(7 + n)

    def tile(rows):
        d_normed = dot_nt(dproj_ref[rows, :], w_ref[...])
        n, rstd = norm_parts(tok_ref[rows, :].astype(F32))
        vs_ref[1, 0, 2:3, :] += jnp.sum(d_normed * n, axis=0, keepdims=True)
        vs_ref[1, 0, 3:4, :] += jnp.sum(d_normed, axis=0, keepdims=True)
        return dres_ref[rows, :] + norm_back(d_normed, n, rstd, row(gain_ref))

    def dcopy(t):
        rows = pl.ds(t * 256, 256)
        return red.copy(dsend_ref.at[rows], dsend_got.at[rows], sx.at[t], tx.at[t], red.over_x)

    def away(t):
        dsend_ref[t * 256 : (t + 1) * 256] = tile(pl.ds(there + t * 256, 256)).astype(BF16)

    def home(t):
        dtok_ref[t * 256 : (t + 1) * 256] = tile(pl.ds(here + t * 256, 256))

    for load in late_loads[1:]:
        load.wait()
    red.step2(8)
    away(0)
    dcopy(0).start()
    red.step3(6)
    away(1)
    dcopy(1).start()
    red.step1(9)
    home(0)
    home(1)
    keep = pltpu.make_async_copy(dtok_ref, dtok_hbm, so)
    keep.start()
    vstep(1, 0)
    red.step3(7)
    for u in range(7):
        red.finish(u)
    vstep(1, 1)
    red.step3(8)
    red.last_step2()
    vstep(1, 2)
    red.finish(7)
    red.finish(8)
    vstep(0, 4)
    vstep(1, 3)
    early = pltpu.make_async_copy(sums_ref.at[pl.ds(0, 9)], sums_hbm.at[pl.ds(0, 9)], so)
    keep.wait()
    early.start()
    red.last_step3()
    vstep(1, 4)
    for t in range(2):
        dcopy(t).wait()
    got = pltpu.make_async_copy(dsend_got, dgot_hbm, sl.at[0])
    got.start()
    red.last_finish()
    early.wait()
    late = pltpu.make_async_copy(sums_ref.at[9], sums_hbm.at[9], so)
    late.start()
    for g in range(2):
        for n in range(6):
            vhop(g, n).wait_send()
    red.drain()
    got.wait()
    late.wait()


def join_kernel(
    lo_ref, logot_ref, dtok_ref, dgot_ref, early_ref, late_ref, vec_ref,
    out_ref, gtok_ref, gin_ref, gback_ref, gout_ref, gqkv_ref, *rest,
):
    vouts, sem = rest[:9], rest[9]
    x = lax.axis_index("seq")
    copies = [
        pltpu.make_async_copy(lo_ref, out_ref.at[x], sem.at[0]),
        pltpu.make_async_copy(logot_ref, out_ref.at[1 - x], sem.at[1]),
        pltpu.make_async_copy(dtok_ref, gtok_ref.at[x], sem.at[2]),
    ]
    for copy in copies:
        copy.start()
    gtok_ref[1 - x] = dgot_ref[...].astype(F32)
    for u in range(4):
        gback_ref[u // 2 * 48 : u // 2 * 48 + 48, u % 2 * UW : (u % 2 + 1) * UW] = (
            early_ref[u] if u < 2 else late_ref[3 + u]
        )
        gin_ref[:, u * D : u * D + UW] = late_ref[u, :24]
        gin_ref[:, u * D + UW : u * D + 2 * UW] = late_ref[u, 24:]
    gout_ref[:, :UW] = late_ref[4, :24]
    gout_ref[:, UW:] = late_ref[4, 24:]
    for p in range(PAIRS):
        part = late_ref[7 + p // 2, p % 2 * 24 : p % 2 * 24 + 24]
        for n in range(3):
            at = n * D + p * 128
            gqkv_ref[:, at : at + 128] = part[:, n * 128 : n * 128 + 128]
    rank = lax.axis_index("dp") * 2 + x
    mine = pltpu.roll(vec_ref[...], D - rank * 24, 1)
    for n, row in enumerate((10, 11, 8, 9, 3, 1, 2, 0)):
        vouts[n][...] = mine[row : row + 1, :24]
    z = rank // 8
    parts = pltpu.roll(vec_ref[4:8, :], D - (rank % 8) * 96, 1)
    chosen = parts[0:1, :96]
    for n in range(1, 4):
        chosen = jnp.where(z == n, parts[n : n + 1, :96], chosen)
    vouts[8][...] = chosen
    for copy in copies:
        copy.wait()


def call_bwd(*args):
    return pl.pallas_call(
        bwd_kernel,
        out_shape=(
            shape((HALF, D), F32), shape((HALF, D), BF16), shape((10, 48, UW), F32), shape((16, D), F32),
        ),
        in_specs=[VM] * 4 + [HB] * 10,
        out_specs=(HB, HB, HB, VM),
        scratch_shapes=[
            pltpu.VMEM((T, D), BF16),
            pltpu.VMEM((D, 3 * D), BF16),
            pltpu.VMEM((D, T), BF16),
            *[pltpu.VMEM((T, D), BF16)] * 5,
            pltpu.VMEM((T, D), F32),
            pltpu.VMEM((T, 128), F32),
            pltpu.VMEM((T, 3 * D), BF16),
            pltpu.VMEM((128, T), F32),
            pltpu.VMEM((D, UW), F32),
            pltpu.VMEM((8, T), F32),
            pltpu.VMEM((10, 16, 48, UW), BF16),
            pltpu.VMEM((3, 32, 48, UW), BF16),
            pltpu.VMEM((HALF, D), BF16),
            pltpu.VMEM((2, 4, 8, D), F32),
            pltpu.VMEM((2, 6, 8, D), F32),
            pltpu.VMEM((HALF, D), F32),
            pltpu.VMEM((HALF, D), BF16),
            pltpu.VMEM((10, 48, UW), F32),
            DMA((2, 6)), DMA((2, 6)), DMA((2,)), DMA((2,)), DMA, DMA((4,)), DMA((5, PAIRS)),
            pltpu.VMEM((3, 2, 48, UW), BF16),
            pltpu.VMEM((48, UW), BF16),
            pltpu.VMEM((48, UW), BF16),
            DMA((4,)), DMA((4,)), *reduction_scratch(10),
        ],
        compiler_params=pltpu.CompilerParams(
            vmem_limit_bytes=VMEM_LIMIT, collective_id=0, has_side_effects=True
        ),
    )(*args)


def call_join(*args):
    return pl.pallas_call(
        join_kernel,
        out_shape=(
            shape((2, HALF, D), BF16), shape((2, HALF, D), F32), shape((24, FF), F32), shape((96, D), F32),
            shape((24, D), F32), shape((24, 3 * D), F32), *[shape((1, 24), F32)] * 8, shape((1, 96), F32),
        ),
        in_specs=[HB, HB, HB, VM, VM, VM, VM],
        out_specs=(VM,) * 15,
        scratch_shapes=[DMA((3,))],
        compiler_params=pltpu.CompilerParams(vmem_limit_bytes=VMEM_LIMIT),
    )(*args)

def whole_sequences(
    tokens, lengths, key_mask, attn_gain, attn_shift, w_qkv, query_bias, value_bias, w_out,
    out_bias, ffn_gain, ffn_shift, w_in, in_bias, w_back, back_bias, cotangent,
):
    normed_t, q, k, v, ctx, tok, cot, log_total, bias = call_fwd(
        lengths, key_mask, attn_gain, attn_shift, query_bias, value_bias,
        tokens, cotangent, w_qkv,
    )
    out, out_got, d_res, d_att, gf, vf, early = call_ffn(
        tok, ctx, out_bias, ffn_gain, ffn_shift, in_bias, back_bias, cot,
        w_out, w_in, w_back,
    )
    d_tok, d_got, late, vec = call_bwd(
        bias, attn_gain, log_total, vf,
        tok, w_qkv, normed_t, q, k, v, ctx, d_att, d_res, gf,
    )
    (
        layer_out, grad_tokens, g_in, g_back, g_out, g_qkv, ag, ash, qb, vb, ob, fg, fs, bb, ib,
    ) = call_join(out, out_got, d_tok, d_got, early, late, vec)
    return (
        layer_out, grad_tokens, ag.reshape(24), ash.reshape(24), g_qkv, qb.reshape(24), vb.reshape(24),
        g_out, ob.reshape(24), fg.reshape(24), fs.reshape(24), g_in, ib.reshape(96), g_back,
        bb.reshape(24),
    )

def shifted(array, axis, by):
    devices = lax.axis_size(axis)
    return lax.ppermute(array, axis, [(i, (i + by) % devices) for i in range(devices)])


def layer_norm(values, gain, shift):
    center = values - jnp.mean(values, axis=-1, keepdims=True)
    spread = jnp.mean(center * center, axis=-1, keepdims=True)
    return center * lax.rsqrt(spread + NORM_EPS) * gain + shift


def partial_gelu(values):
    return jax.nn.gelu(values, approximate=True)


def outer_product(left, right):
    return lax.dot_general(
        left, right, (((0,), (0,)), ((), ())), preferred_element_type=jnp.float32
    )


def times_transposed(left, right):
    return lax.dot_general(
        left, right, (((1,), (1,)), ((), ())), preferred_element_type=jnp.float32
    )


def allowed_keys(lengths, flags_all, query_pos, first_key, key_count):
    key_pos = first_key + jnp.arange(key_count, dtype=jnp.int32)
    key_flags = lax.dynamic_slice_in_dim(flags_all, first_key, key_count, 1)
    key_valid = (key_pos[None, :] < lengths[:, None]) & (key_flags == 1)
    itself = key_pos[None, :] == query_pos[:, None]
    return key_valid[:, None, None, :] | itself[None, :, None, :]


def send_home(partial_grads):
    return shifted(partial_grads.astype(jnp.bfloat16), "seq", 1).astype(partial_grads.dtype)


def shards(
    tokens,
    lengths,
    key_mask,
    attn_gain,
    attn_shift,
    w_qkv,
    query_bias,
    value_bias,
    w_out,
    out_bias,
    ffn_gain,
    ffn_shift,
    w_in,
    in_bias,
    w_back,
    back_bias,
    cotangent,
):
    seq_count, span_dev, model_width = tokens.shape
    row_count = seq_count * span_dev
    members = lax.axis_size("seq")
    own_index = lax.axis_index("seq")
    query_pos = own_index * span_dev + jnp.arange(span_dev, dtype=jnp.int32)
    flags_all = lax.all_gather(key_mask, "seq", axis=1, tiled=True)
    inputs = tokens.astype(jnp.float32).reshape(row_count, model_width)
    normed_one, norm_pull_one = jax.vjp(layer_norm, inputs, attn_gain, attn_shift)
    normed_attn = normed_one.astype(jnp.bfloat16)
    projected = jnp.dot(normed_attn, w_qkv, preferred_element_type=jnp.float32)
    queries = ((projected[:, :model_width] + query_bias) * 0.125).astype(jnp.bfloat16)
    queries = queries.reshape(seq_count, span_dev, H, HD)
    keyval = jnp.concatenate(
        [projected[:, model_width : 2 * model_width], projected[:, 2 * model_width :] + value_bias],
        axis=1,
    ).astype(jnp.bfloat16)
    keyval = keyval.reshape(seq_count, span_dev, 2 * model_width)

    def split_block(block_kv):
        key_count = block_kv.shape[1]
        key_heads = block_kv[:, :, :model_width].reshape(seq_count, key_count, H, HD)
        value_heads = block_kv[:, :, model_width:].reshape(seq_count, key_count, H, HD)
        return (key_count, key_heads, value_heads)

    running_max = jnp.full((seq_count, span_dev, H), NEG_FILL, jnp.float32)
    key_count, key_heads, value_heads = split_block(
        lax.all_gather(keyval, "seq", axis=1, tiled=True)
    )
    scores = jnp.einsum("sqhd,skhd->sqhk", queries, key_heads, preferred_element_type=jnp.float32)
    allowed = allowed_keys(lengths, flags_all, query_pos, jnp.int32(0), key_count)
    new_max = jnp.maximum(running_max, jnp.max(jnp.where(allowed, scores, NEG_FILL), axis=-1))
    expo = jnp.exp(jnp.where(allowed, scores - new_max[..., None], NEG_FILL))
    running_sum = jnp.sum(expo, axis=-1)
    running_acc = jnp.einsum(
        "sqhk,skhd->sqhd",
        expo.astype(jnp.bfloat16),
        value_heads,
        preferred_element_type=jnp.float32,
    )
    attended = running_acc / running_sum[..., None]
    log_total = new_max + jnp.log(running_sum)
    context = attended.reshape(row_count, model_width).astype(jnp.bfloat16)
    residual = inputs + jnp.dot(context, w_out, preferred_element_type=jnp.float32) + out_bias
    normed_two, norm_pull_two = jax.vjp(layer_norm, residual, ffn_gain, ffn_shift)
    normed_ffn = normed_two.astype(jnp.bfloat16)
    pre_act = jnp.dot(normed_ffn, w_in, preferred_element_type=jnp.float32) + in_bias
    gelu_value, gelu_pull = jax.vjp(partial_gelu, pre_act)
    activated = gelu_value.astype(jnp.bfloat16)
    layer_out = (
        residual + jnp.dot(activated, w_back, preferred_element_type=jnp.float32) + back_bias
    )
    grad_rows = cotangent.reshape(row_count, model_width)
    grad_float = grad_rows.astype(jnp.float32)
    grad_back_bias = jnp.sum(grad_float, axis=0)
    grad_w_back = outer_product(activated, grad_rows)
    d_act = times_transposed(grad_rows, w_back)
    d_pre = gelu_pull(d_act)[0].astype(jnp.bfloat16)
    grad_in_bias = jnp.sum(d_pre.astype(jnp.float32), axis=0)
    grad_w_in = outer_product(normed_ffn, d_pre)
    d_normed = times_transposed(d_pre, w_in)
    d_res_part, grad_ffn_gain, grad_ffn_shift = norm_pull_two(d_normed)
    d_residual = grad_float + d_res_part
    d_branch = d_residual.astype(jnp.bfloat16)
    grad_out_bias = jnp.sum(d_branch.astype(jnp.float32), axis=0)
    grad_w_out = outer_product(context, d_branch)
    d_attended = (
        times_transposed(d_branch, w_out).astype(jnp.bfloat16).reshape(seq_count, span_dev, H, HD)
    )
    delta = jnp.sum(d_attended.astype(jnp.float32) * attended, axis=-1)

    def attend_back(block_kv, first_key):
        key_count, key_heads, value_heads = split_block(block_kv)
        scores = jnp.einsum(
            "sqhd,skhd->sqhk", queries, key_heads, preferred_element_type=jnp.float32
        )
        allowed = allowed_keys(lengths, flags_all, query_pos, first_key, key_count)
        weights_f = jnp.exp(jnp.where(allowed, scores - log_total[..., None], NEG_FILL))
        d_values = jnp.einsum(
            "sqhk,sqhd->skhd",
            weights_f.astype(jnp.bfloat16),
            d_attended,
            preferred_element_type=jnp.float32,
        )
        d_probs = jnp.einsum(
            "sqhd,skhd->sqhk", d_attended, value_heads, preferred_element_type=jnp.float32
        )
        d_scores = (weights_f * (d_probs - delta[..., None])).astype(jnp.bfloat16)
        d_query = jnp.einsum(
            "sqhk,skhd->sqhd", d_scores, key_heads, preferred_element_type=jnp.float32
        )
        d_keys = jnp.einsum(
            "sqhk,sqhd->skhd", d_scores, queries, preferred_element_type=jnp.float32
        )
        d_block = jnp.concatenate(
            [
                d_keys.reshape(seq_count, key_count, model_width),
                d_values.reshape(seq_count, key_count, model_width),
            ],
            axis=2,
        )
        return (d_query, d_block)

    zero_query = jnp.zeros((seq_count, span_dev, H, HD), jnp.float32)

    def turn(turn_index, state_now):
        current, d_current, d_query = state_now
        anchor = (own_index - turn_index) % members
        add_query, add_block = attend_back(current, anchor * span_dev)
        current = shifted(current, "seq", 1)
        return (current, send_home(d_current + add_block), d_query + add_query)

    start_back = (
        keyval,
        jnp.zeros((seq_count, span_dev, 2 * model_width), jnp.float32),
        zero_query,
    )
    current, d_current, d_query = lax.fori_loop(0, members - 1, turn, start_back)
    anchor = (own_index - (members - 1)) % members
    add_query, add_block = attend_back(current, anchor * span_dev)
    d_query = d_query + add_query
    d_keyval = send_home(d_current + add_block)
    d_query_low = d_query.reshape(row_count, model_width).astype(jnp.bfloat16)
    d_keyval_low = d_keyval.reshape(row_count, 2 * model_width).astype(jnp.bfloat16)
    query_scaled = d_query_low.astype(jnp.float32) * 0.125
    grad_query_bias = jnp.sum(query_scaled, axis=0)
    grad_value_bias = jnp.sum(d_keyval_low[:, model_width:].astype(jnp.float32), axis=0)
    d_projected = jnp.concatenate([query_scaled.astype(jnp.bfloat16), d_keyval_low], axis=1)
    grad_w_qkv = outer_product(normed_attn, d_projected)
    d_normed_attn = times_transposed(d_projected, w_qkv)
    d_in_part, grad_attn_gain, grad_attn_shift = norm_pull_one(d_normed_attn)
    grad_tokens = (d_residual + d_in_part).reshape(seq_count, span_dev, model_width)
    out_block = layer_out.astype(jnp.bfloat16).reshape(seq_count, span_dev, model_width)
    all_sums = (
        lax.psum_scatter(grad_attn_gain, ("dp", "seq"), scatter_dimension=0, tiled=True),
        lax.psum_scatter(grad_attn_shift, ("dp", "seq"), scatter_dimension=0, tiled=True),
        lax.psum_scatter(grad_w_qkv, ("dp", "seq"), scatter_dimension=0, tiled=True),
        lax.psum_scatter(grad_query_bias, ("dp", "seq"), scatter_dimension=0, tiled=True),
        lax.psum_scatter(grad_value_bias, ("dp", "seq"), scatter_dimension=0, tiled=True),
        lax.psum_scatter(grad_w_out, ("dp", "seq"), scatter_dimension=0, tiled=True),
        lax.psum_scatter(grad_out_bias, ("dp", "seq"), scatter_dimension=0, tiled=True),
        lax.psum_scatter(grad_ffn_gain, ("dp", "seq"), scatter_dimension=0, tiled=True),
        lax.psum_scatter(grad_ffn_shift, ("dp", "seq"), scatter_dimension=0, tiled=True),
        lax.psum_scatter(grad_w_in, ("dp", "seq"), scatter_dimension=0, tiled=True),
        lax.psum_scatter(grad_in_bias, ("dp", "seq"), scatter_dimension=0, tiled=True),
        lax.psum_scatter(grad_w_back, ("dp", "seq"), scatter_dimension=0, tiled=True),
        lax.psum_scatter(grad_back_bias, ("dp", "seq"), scatter_dimension=0, tiled=True),
    )
    return (
        out_block,
        grad_tokens,
        all_sums[0],
        all_sums[1],
        all_sums[2],
        all_sums[3],
        all_sums[4],
        all_sums[5],
        all_sums[6],
        all_sums[7],
        all_sums[8],
        all_sums[9],
        all_sums[10],
        all_sums[11],
        all_sums[12],
    )


def solution(mesh):
    sizes = dict(mesh.shape)
    whole = sizes == {"dp": 16, "seq": 2}
    return jax.shard_map(
        whole_sequences if whole else shards,
        mesh=mesh,
        in_specs=(
            P("dp", "seq", None),
            P("dp"),
            P("dp", "seq"),
            P(),
            P(),
            P(),
            P(),
            P(),
            P(),
            P(),
            P(),
            P(),
            P(),
            P(),
            P(),
            P(),
            P("dp", "seq", None),
        ),
        out_specs=(
            P("dp", "seq", None),
            P("dp", "seq", None),
            P(("dp", "seq")),
            P(("dp", "seq")),
            P(("dp", "seq"), None),
            P(("dp", "seq")),
            P(("dp", "seq")),
            P(("dp", "seq"), None),
            P(("dp", "seq")),
            P(("dp", "seq")),
            P(("dp", "seq")),
            P(("dp", "seq"), None),
            P(("dp", "seq")),
            P(("dp", "seq"), None),
            P(("dp", "seq")),
        ),
        check_vma=False,
    )
```

```python
import functools

import jax
import jax.numpy as jnp
from jax import lax
from jax.experimental import pallas as pl
from jax.experimental.pallas import tpu as pltpu
from jax.sharding import PartitionSpec as P

H = 12
HD = 64


NEG_FILL = -1e30
NORM_EPS = 1e-05

F32 = jnp.float32
BF16 = jnp.bfloat16
D = 768
FF = 3072
T = 1024
HALF = 512
PAIRS = 6
UW = 384
MESH = pl.DeviceIdType.MESH
VMEM_LIMIT = 62 * 1024 * 1024


def dot_nn(a, b):
    return lax.dot_general(a, b, (((1,), (0,)), ((), ())), preferred_element_type=F32)


def dot_nt(a, b):
    return lax.dot_general(a, b, (((1,), (1,)), ((), ())), preferred_element_type=F32)


def dot_tn(a, b):
    return lax.dot_general(a, b, (((0,), (0,)), ((), ())), preferred_element_type=F32)


def shape(dims, dtype):
    return jax.ShapeDtypeStruct(dims, dtype)


VM = pl.BlockSpec(memory_space=pltpu.VMEM)
SM = pl.BlockSpec(memory_space=pltpu.SMEM)
HB = pl.BlockSpec(memory_space=pl.ANY)
DMA = pltpu.SemaphoreType.DMA


def row(ref):
    return ref[...].reshape(1, -1)


def norm_parts(x):
    center = x - jnp.mean(x, axis=-1, keepdims=True)
    spread = jnp.mean(center * center, axis=-1, keepdims=True)
    rstd = lax.rsqrt(spread + NORM_EPS)
    return center * rstd, rstd


def norm_back(d_norm, n, rstd, gain):
    u = d_norm * gain
    mean_u = jnp.mean(u, axis=-1, keepdims=True)
    mean_un = jnp.mean(u * n, axis=-1, keepdims=True)
    return (u - mean_u - n * mean_un) * rstd


def blocks_of(top, bottom):
    return jnp.concatenate([top, bottom], axis=0).astype(BF16)


def place(index, first_x):
    z, y, c, x = index // 8, (index // 4) % 2, (index // 2) % 2, index % 2
    return c * 16 + z + 4 * (2 * y + x) + first_x * 4 * (x - y)


def reduction_scratch(units):
    sems = [DMA((units,)), DMA((units,)), DMA((units,)), DMA((units, 3))]
    return [pltpu.VMEM((units, n, 48, UW), BF16) for n in (16, 8, 4, 3)] + sems + sems


class Reduction:
    def __init__(self, units, extra, own, parts, sums, held, sems):
        self.units, self.extra = units, extra
        self.own, self.parts, self.sums, self.held = own, parts, sums, held
        self.sends, self.recvs = sems[:4], sems[4:8]
        dp, x = lax.axis_index("dp"), lax.axis_index("seq")
        z, y, c = dp // 4, (dp // 2) % 2, dp % 2
        self.dp, self.x, self.y, self.z, self.c = dp, x, y, z, c
        self.over_c = (dp + 1 - 2 * c, x)
        self.over_x = (dp, 1 - x)
        self.over_y = (dp + 2 - 4 * y, x)
        self.over_z = [(lax.rem(z + d, 4) * 4 + y * 2 + c, x) for d in (1, 2, 3)]

    def barrier(self):
        sem = pltpu.get_barrier_semaphore()
        for to in (self.over_c, self.over_x, self.over_y, *self.over_z):
            pl.semaphore_signal(sem, inc=1, device_id=to, device_id_type=MESH)
        pl.semaphore_wait(sem, 6)

    def copy(self, src, dst, send, recv, to):
        return pltpu.make_async_remote_copy(
            src_ref=src, dst_ref=dst, send_sem=send, recv_sem=recv, device_id=to, device_id_type=MESH
        )

    def axes(self, u):
        fx, x, y, dp = x_first(u), self.x, self.y, self.dp
        first = (dp + (1 - fx) * (2 - 4 * y), x + fx * (1 - 2 * x))
        second = (dp + fx * (2 - 4 * y), x + (1 - fx) * (1 - 2 * x))
        return first, second, y + fx * (x - y), x + fx * (y - x)

    def hop0(self, u):
        src = self.parts(u).at[pl.ds((1 - self.c) * 16, 16)]
        return self.copy(src, self.held[0].at[u], self.sends[0].at[u], self.recvs[0].at[u], self.over_c)

    def hop1(self, u):
        first, _, a, _ = self.axes(u)
        src = self.held[0].at[u, pl.ds((1 - a) * 8, 8)]
        return self.copy(src, self.held[1].at[u], self.sends[1].at[u], self.recvs[1].at[u], first)

    def hop2(self, u):
        _, second, _, b = self.axes(u)
        src = self.held[1].at[u, pl.ds((1 - b) * 4, 4)]
        return self.copy(src, self.held[2].at[u], self.sends[2].at[u], self.recvs[2].at[u], second)

    def hop3(self, u, d):
        src = self.held[2].at[u, lax.rem(self.z + d + 1, 4)]
        return self.copy(
            src, self.held[3].at[u, d], self.sends[3].at[u, d], self.recvs[3].at[u, d], self.over_z[d]
        )

    def arrived(self, u):
        held = self.held[0].at[u]
        self.copy(held, held, self.sends[0].at[u], self.recvs[0].at[u], self.over_c).wait_recv()

    def start(self, u):
        self.hop0(u).start()

    def step1(self, u):
        self.arrived(u)
        _, _, a, _ = self.axes(u)
        held = self.held[0]

        def add(k):
            held[u, k] = (held[u, k].astype(F32) + self.own(u, k).astype(F32)).astype(BF16)

        @pl.loop(0, 8, unroll=2)
        def _(k):
            add((1 - a) * 8 + k)

        self.hop1(u).start()

        @pl.loop(0, 8, unroll=2)
        def _(k):
            add(a * 8 + k)

    def step2(self, u):
        self.hop1(u).wait_recv()
        _, _, a, b = self.axes(u)
        held, before = self.held[1], self.held[0]

        def add(k):
            held[u, k] = (held[u, k].astype(F32) + before[u, a * 8 + k].astype(F32)).astype(BF16)

        for k in range(4):
            add((1 - b) * 4 + k)
        self.hop2(u).start()
        for k in range(4):
            add(b * 4 + k)

    def step3(self, u):
        self.hop2(u).wait_recv()
        _, _, _, b = self.axes(u)
        held, before = self.held[2], self.held[1]
        for k in range(4):
            held[u, k] = (held[u, k].astype(F32) + before[u, b * 4 + k].astype(F32)).astype(BF16)
        for d in range(3):
            self.hop3(u, d).start()

    def finish(self, u):
        total = self.held[2][u, self.z].astype(F32)
        for d in range(3):
            self.hop3(u, d).wait_recv()
            total = total + self.held[3][u, d].astype(F32)
        self.sums[u] = total

    def last_hop(self, d):
        across, cross_send, cross_recv, sends, recvs = self.last
        u = self.units
        if d == 3:
            return self.copy(cross_send, cross_recv, sends.at[3], recvs.at[3], self.over_x)
        src = self.held[1].at[u, pl.ds(lax.rem(self.z + d + 1, 4) * 2, 2)]
        return self.copy(src, across.at[d], sends.at[d], recvs.at[d], self.over_z[d])

    def last_step2(self):
        u = self.units
        self.hop1(u).wait_recv()
        for k in range(8):
            self.held[1][u, k] = (
                self.held[1][u, k].astype(F32) + self.held[0][u, self.y * 8 + k].astype(F32)
            ).astype(BF16)
        for d in range(3):
            self.last_hop(d).start()

    def last_step3(self):
        across, cross_send = self.last[:2]
        for d in range(3):
            self.last_hop(d).wait_recv()
        totals = []
        for k in range(2):
            total = self.held[1][self.units, self.z * 2 + k].astype(F32)
            for d in range(3):
                total = total + across[d, k].astype(F32)
            totals.append(total)
        cross_send[...] = jnp.where(self.x == 0, totals[1], totals[0]).astype(BF16)
        self.last_hop(3).start()
        self.sums[self.units] = jnp.where(self.x == 0, totals[0], totals[1])

    def last_finish(self):
        self.last_hop(3).wait_recv()
        self.sums[self.units] = self.sums[self.units] + self.last[2][...].astype(F32)

    def drain(self):
        for u in range(self.units):
            self.hop0(u).wait_send()
            self.hop1(u).wait_send()
            self.hop2(u).wait_send()
            for d in range(3):
                self.hop3(u, d).wait_send()
        if self.extra:
            self.hop0(self.units).wait_send()
            self.hop1(self.units).wait_send()
            for d in range(4):
                self.last_hop(d).wait_send()


def fwd_kernel(
    len_ref, mask_ref, gain_ref, shift_ref, qb_ref, vb_ref, tok_hbm, cot_hbm, w_hbm,
    nt_hbm, q_hbm, k_hbm, v_hbm, ctx_hbm, tok_out, cot_out, lt_ref, bias_ref,
    tok_ref, cot_ref, w_ref, nt_ref, q_ref, k_ref, v_ref, ctx_ref, mgot_ref, part_ref, mx_ref, logs_ref,
    sl, so, sx, tx,
):
    dp, x = lax.axis_index("dp"), lax.axis_index("seq")
    here, there = 0, HALF
    load_w = pltpu.make_async_copy(w_hbm, w_ref, sl.at[0])
    load_tok = pltpu.make_async_copy(tok_hbm.at[x], tok_ref.at[pl.ds(here, HALF)], sl.at[1])
    load_cot = pltpu.make_async_copy(cot_hbm.at[x], cot_ref.at[pl.ds(here, HALF)], sl.at[2])
    load_tok.start()
    load_w.start()

    def swap(n):
        if n == 4:
            src, dst = mask_ref, mgot_ref
        else:
            side, buffer = (tok_hbm, tok_ref) if n < 4 else (cot_hbm, cot_ref)
            rows = 128 if n < 4 else 256
            at = (n if n < 4 else n - 5) * rows
            src = side.at[1 - x, pl.ds(at, rows)]
            dst = buffer.at[pl.ds(there + at, rows)]
        return pltpu.make_async_remote_copy(
            src_ref=src, dst_ref=dst, send_sem=sx.at[n], recv_sem=tx.at[n],
            device_id=(dp, 1 - x), device_id_type=MESH,
        )

    sem = pltpu.get_barrier_semaphore()
    pl.semaphore_signal(sem, inc=1, device_id=(dp, 1 - x), device_id_type=MESH)
    pl.semaphore_wait(sem, 1)
    swaps = [swap(n) for n in range(7)]
    for n in (4, 0, 1, 2, 3, 5, 6):
        swaps[n].start()
    load_tok.wait()
    load_w.wait()
    load_cot.start()

    def project(first, count):
        rows = pl.ds(pl.multiple_of(first, count), count)
        n, _ = norm_parts(tok_ref[rows, :].astype(F32))
        normed = (n * row(gain_ref) + row(shift_ref)).astype(BF16)
        nt_ref[:, rows] = normed.T
        q_ref[rows, :] = ((dot_nn(normed, w_ref[:, :D]) + row(qb_ref)) * 0.125).astype(BF16)
        k_ref[rows, :] = dot_nn(normed, w_ref[:, D : 2 * D]).astype(BF16)
        v_ref[rows, :] = (dot_nn(normed, w_ref[:, 2 * D :]) + row(vb_ref)).astype(BF16)

    @pl.loop(0, 2)
    def _(t):
        project(t * 256, 256)

    swaps[4].wait_recv()
    pos = lax.broadcasted_iota(jnp.int32, (1, HALF), 1)
    for first, ref in ((here, mask_ref), (there, mgot_ref)):
        flags = jnp.where(x == 0, ref[0:1, :], ref[1:2, :])
        at = jnp.where(x == 0, first, HALF - first)
        valid = (pos + at < len_ref[x]) & (flags == 1)
        half_bias = jnp.where(valid, 0.0, NEG_FILL).astype(F32)
        bias_ref[:, first : first + HALF] = half_bias
    lane = lax.broadcasted_iota(jnp.int32, (1, 128), 1)
    wide = lax.broadcasted_iota(jnp.int32, (256, 128), 1)
    logs_ref[...] = jnp.zeros_like(logs_ref)
    eye = lax.broadcasted_iota(jnp.int32, (256, 256), 0) == lax.broadcasted_iota(
        jnp.int32, (256, 256), 1
    )

    def attend(p, chains, spans, first):
        cols = pl.ds(pl.multiple_of(p * 128, 128), 128)
        keys, values = {}, {}
        for low, high in sorted(set(spans.values())):
            kp, vp = k_ref[low:high, cols], v_ref[low:high, cols]
            keys[low, high] = [jnp.where((lane < HD) == (h == 0), kp, jnp.zeros_like(kp)) for h in range(2)]
            values[low, high] = jnp.concatenate([vp, jnp.ones_like(vp)], axis=1)

        def score(a, h):
            return dot_nt(q_ref[a : a + 256, cols], keys[spans[a]][h])

        def softmax(a, raw, before):
            low, high = spans[a]
            pieces = []
            for b in range(low, high, 256):
                cut = raw[:, b - low : b - low + 256]
                piece = cut + bias_ref[:, b : b + 256]
                pieces.append(jnp.where(eye, cut, piece) if a == b else piece)
            s = jnp.concatenate(pieces, axis=1)
            top = jnp.max(s, axis=1, keepdims=True)
            if before is not None:
                top = jnp.maximum(top, before)
            return top, jnp.exp(s - top).astype(BF16)

        outs = []
        raw = score(*chains[0])
        for n, (a, h) in enumerate(chains):
            ahead = score(*chains[n + 1]) if n + 1 < len(chains) else None
            merge = not first and a < HALF
            before = mx_ref[2 * p + h, a : a + 256, 0:1] if merge else None
            top, e = softmax(a, raw, before)
            o = dot_nn(e, values[spans[a]])
            raw = ahead
            if first:
                part_ref[2 * p + h, a : a + 256] = o
                mx_ref[2 * p + h, a : a + 256] = jnp.broadcast_to(top, (256, 128))
                continue
            if merge:
                o = o + part_ref[2 * p + h, a : a + 256] * jnp.exp(before - top)
            total = o[:, 128:]
            logs_ref[a : a + 256] = jnp.where(wide == 2 * p + h, top + jnp.log(total), logs_ref[a : a + 256])
            outs.append(o[:, :128] / total)
            if h == 1:
                ctx_ref[a : a + 256, cols] = jnp.where(lane < HD, outs[-2], outs[-1]).astype(BF16)

    own = [(a, h) for a in (0, 256) for h in range(2)]
    other = [(a, h) for a in (512, 768) for h in range(2)]

    @pl.loop(0, PAIRS)
    def _(p):
        attend(p, own, {0: (0, HALF), 256: (0, HALF)}, True)

    for n in range(4):
        swaps[n].wait_recv()
        project(there + n * 128, 128)

    outs = [
        pltpu.make_async_copy(src, dst, so.at[n])
        for n, (src, dst) in enumerate(
            [(nt_ref, nt_hbm), (q_ref, q_hbm), (k_ref, k_hbm), (v_ref, v_hbm), (tok_ref, tok_out)]
        )
    ]
    for one in outs:
        one.start()

    def ctx_out(p):
        cols = pl.ds(pl.multiple_of(p * 128, 128), 128)
        return pltpu.make_async_copy(ctx_ref.at[:, cols], ctx_hbm.at[:, cols], so.at[5 + p])

    @pl.loop(0, PAIRS)
    def _(p):
        attend(p, own + other, {0: (HALF, T), 256: (HALF, T), 512: (0, T), 768: (0, T)}, False)
        ctx_out(p).start()

    logs = logs_ref[...].T
    for h in range(H):
        lt_ref[h] = logs[h : h + 1]
    load_cot.wait()
    for n in (5, 6):
        swaps[n].wait_recv()
    last = pltpu.make_async_copy(cot_ref, cot_out, so.at[11])
    last.start()
    for one in swaps:
        one.wait_send()
    for one in outs:
        one.wait()
    for p in range(PAIRS):
        ctx_out(p).wait()
    last.wait()


def call_fwd(*args):
    low = shape((T, D), BF16)
    return pl.pallas_call(
        fwd_kernel,
        out_shape=(
            shape((D, T), BF16), low, low, low, low, low, low, shape((H, 1, T), F32), shape((1, T), F32),
        ),
        in_specs=[SM] + [VM] * 5 + [HB] * 3,
        out_specs=(HB,) * 7 + (VM, VM),
        scratch_shapes=[
            pltpu.VMEM((T, D), BF16),
            pltpu.VMEM((T, D), BF16),
            pltpu.VMEM((D, 3 * D), BF16),
            pltpu.VMEM((D, T), BF16),
            *[pltpu.VMEM((T, D), BF16)] * 4,
            pltpu.VMEM((2, HALF), jnp.int32),
            pltpu.VMEM((H, HALF, 256), F32),
            pltpu.VMEM((H, HALF, 128), F32),
            pltpu.VMEM((T, 128), F32),
            DMA((3,)), DMA((12,)), DMA((7,)), DMA((7,)),
        ],
        compiler_params=pltpu.CompilerParams(
            vmem_limit_bytes=VMEM_LIMIT, collective_id=2, has_side_effects=True
        ),
    )(*args)


def x_first(unit):
    return (unit + 1) % 2


def ffn_kernel(
    tok_ref, ctx_ref, ob_ref, g_ref, s_ref, ib_ref, bb_ref, cot_hbm, wo_hbm, wi_hbm, wb_hbm,
    lo_ref, logot_ref, dres_hbm, datt_hbm, grads_hbm, vec_ref, sums_ref,
    wo_ref, wi_ref, wb_ref, nf_ref, act_ref, dpre_ref, dbr_ref, res_ref, dn_ref, away_ref, cot_ref,
    parts_ref, grads_ref, sw, so, sx, tx, *reds,
):
    def parts(u):
        return parts_ref.at[u]

    def own_block(u, k):
        return parts_ref[u, red.c * 16 + k]

    red = Reduction(2, 0, own_block, parts, sums_ref, reds[:4], reds[4:])
    loads = [pltpu.make_async_copy(wo_hbm, wo_ref, sw.at[0])]
    for c in range(4):
        cut = pl.ds(c * 768, 768)
        loads.append(pltpu.make_async_copy(wi_hbm.at[:, cut], wi_ref.at[:, cut], sw.at[1 + 2 * c]))
        loads.append(pltpu.make_async_copy(wb_hbm.at[cut], wb_ref.at[cut], sw.at[2 + 2 * c]))
    loads.append(pltpu.make_async_copy(cot_hbm, cot_ref, sw.at[9]))
    for load in loads:
        load.start()
    red.barrier()
    vec_ref[...] = jnp.zeros_like(vec_ref)
    loads[0].wait()
    lo_copy = red.copy(away_ref, logot_ref, sx, tx, red.over_x)

    def grads_out(u):
        return pltpu.make_async_copy(grads_ref.at[u], grads_hbm.at[u], so.at[8 + u])

    def rows_of(t):
        return pl.ds(pl.multiple_of(HALF - t * HALF, HALF), HALF)

    def forward(t, loads_of):
        rows = rows_of(t)
        res = tok_ref[rows, :].astype(F32) + dot_nn(ctx_ref[rows, :], wo_ref[...]) + row(ob_ref)
        res_ref[rows, :] = res
        n, _ = norm_parts(res)
        normed = (n * row(g_ref) + row(s_ref)).astype(BF16)
        nf_ref[rows, :] = normed
        total = res + row(bb_ref)
        def pre(c):
            for load in loads_of(c):
                load.wait()
            cut = slice(c * 768, (c + 1) * 768)
            return dot_nn(normed, wi_ref[:, cut]) + row(ib_ref)[:, cut]

        v = pre(0)
        for c in range(4):
            cut = slice(c * 768, (c + 1) * 768)
            ahead = pre(c + 1) if c < 3 else None
            sq = v * v
            th = jnp.tanh(v * (0.7978845608 + (0.7978845608 * 0.044715) * sq))
            half = 0.5 + 0.5 * th
            act = (v * half).astype(BF16)
            slope = half + v * (half * (1.0 - th)) * (
                0.7978845608 + (3 * 0.7978845608 * 0.044715) * sq
            )
            act_ref[rows, cut] = act
            dpre_ref[rows, cut] = slope.astype(BF16)
            total = total + dot_nn(act, wb_ref[cut, :])
            v = ahead
        return total.astype(BF16)

    away_ref[...] = forward(0, lambda c: loads[1 + 2 * c : 3 + 2 * c])
    lo_copy.start()
    lo_ref[...] = forward(1, lambda c: ())

    loads[9].wait()

    @pl.loop(0, 4)
    def _(z):
        g = dot_tn(act_ref[:, pl.ds(pl.multiple_of(z * 768, 768), 768)], cot_ref[...])
        for r in range(8):
            for u in range(4):
                i, j = u // 2, u % 2
                block = g[r * 96 + i * 48 : r * 96 + i * 48 + 48, j * UW : (j + 1) * UW].astype(BF16)
                if u < 2:
                    parts_ref[u, place(r, x_first(u)) + z] = block
                else:
                    grads_ref[3 + u, place(r, x_first(3 + u)) + z] = block

    for u in range(2):
        red.start(u)
    for u in (5, 6):
        grads_out(u).start()

    def tile_out(t, part):
        rows = rows_of(t)
        if part == 0:
            return pltpu.make_async_copy(res_ref.at[rows], dres_hbm.at[rows], so.at[2 * t])
        return pltpu.make_async_copy(cot_ref.at[rows], datt_hbm.at[rows], so.at[2 * t + 1])

    plan = {2: ((1, 0), (1, 1)), 6: ((2, 0), (2, 1))}

    @pl.loop(0, 2)
    def _(t):
        rows = rows_of(t)
        dy = cot_ref[rows, :]
        dn_ref[...] = jnp.zeros_like(dn_ref)
        for c in range(4):
            for at, moves in plan.items():
                if at % 4 == c:

                    @pl.when(t == at // 4)
                    def _():
                        for stage, u in moves:
                            (red.step1, red.step2, red.step3)[stage - 1](u)

            cut = slice(c * 768, (c + 1) * 768)
            d_act = dot_nt(dy, wb_ref[cut, :])
            d_pre = (d_act * dpre_ref[rows, cut].astype(F32)).astype(BF16)
            dpre_ref[rows, cut] = d_pre
            dn_ref[...] += dot_nt(d_pre, wi_ref[:, cut])
            vec_ref[4 + c : 5 + c, :] += jnp.sum(d_pre.astype(F32), axis=0, keepdims=True)

        n, rstd = norm_parts(res_ref[rows, :])
        d_normed = dn_ref[...]
        dyf = dy.astype(F32)
        d_res = dyf + norm_back(d_normed, n, rstd, row(g_ref))
        res_ref[rows, :] = d_res
        tile_out(t, 0).start()
        d_branch = d_res.astype(BF16)
        dbr_ref[rows, :] = d_branch
        cot_ref[rows, :] = dot_nt(d_branch, wo_ref[...]).astype(BF16)
        tile_out(t, 1).start()
        vec_ref[0:1, :] += jnp.sum(dyf, axis=0, keepdims=True)
        vec_ref[1:2, :] += jnp.sum(d_normed * n, axis=0, keepdims=True)
        vec_ref[2:3, :] += jnp.sum(d_normed, axis=0, keepdims=True)
        vec_ref[3:4, :] += jnp.sum(d_branch.astype(F32), axis=0, keepdims=True)

    def unit(u, g):
        for r in range(32):
            rows = slice(r * 24, (r + 1) * 24)
            grads_ref[u, place(r, x_first(u))] = blocks_of(g[rows, :UW], g[rows, UW:])
        grads_out(u).start()

    @pl.loop(0, 4)
    def _(u):
        unit(u, dot_tn(nf_ref[...], dpre_ref[:, pl.ds(pl.multiple_of(u * 768, 768), 768)]))

        @pl.when(u == 0)
        def _():
            red.step3(0)
            red.step3(1)

    unit(4, dot_tn(ctx_ref[...], dbr_ref[...]))
    for u in range(2):
        red.finish(u)
    lo_copy.wait()
    red.drain()
    for t in range(2):
        tile_out(t, 0).wait()
        tile_out(t, 1).wait()
    for u in range(7):
        grads_out(u).wait()


def call_ffn(*args):
    return pl.pallas_call(
        ffn_kernel,
        out_shape=(
            shape((HALF, D), BF16), shape((HALF, D), BF16), shape((T, D), F32), shape((T, D), BF16),
            shape((7, 32, 48, UW), BF16), shape((8, D), F32), shape((2, 48, UW), F32),
        ),
        in_specs=[VM] * 7 + [HB] * 4,
        out_specs=(VM, VM, HB, HB, HB, VM, VM),
        scratch_shapes=[
            pltpu.VMEM((D, D), BF16),
            pltpu.VMEM((D, FF), BF16),
            pltpu.VMEM((FF, D), BF16),
            pltpu.VMEM((T, D), BF16),
            pltpu.VMEM((T, FF), BF16),
            pltpu.VMEM((T, FF), BF16),
            pltpu.VMEM((T, D), BF16),
            pltpu.VMEM((T, D), F32),
            pltpu.VMEM((HALF, D), F32),
            pltpu.VMEM((HALF, D), BF16),
            pltpu.VMEM((T, D), BF16),
            pltpu.VMEM((2, 32, 48, UW), BF16),
            pltpu.VMEM((7, 32, 48, UW), BF16),
            DMA((10,)), DMA((15,)), DMA, DMA, *reduction_scratch(2),
        ],
        compiler_params=pltpu.CompilerParams(
            vmem_limit_bytes=VMEM_LIMIT, collective_id=1, has_side_effects=True
        ),
    )(*args)


def bwd_kernel(
    bias_in, gain_ref, lt_ref, vf_ref,
    tok_hbm, w_hbm, nt_hbm, q_hbm, k_hbm, v_hbm, ctx_hbm, datt_hbm, dres_hbm, gf_ref,
    dtok_hbm, dgot_hbm, sums_hbm, vsum_ref,
    tok_ref, w_ref, nt_ref, q_ref, k_ref, v_ref, ctx_ref, datt_ref, dres_ref, bias_ref,
    dproj_ref, dqt_ref, gq_ref, delta_ref, own_ref, parts_ref, dsend_ref, vs_ref, vr_ref, dtok_ref, dsend_got, sums_ref,
    sv, tv, sx, tx, so, sl, sp, across, cross_send, cross_recv, se, te, *reds,
):
    def parts(u):
        return gf_ref.at[u] if u < 7 else parts_ref.at[u - 7]

    def own_block(u, k):
        return own_ref[u, k]

    red = Reduction(9, 1, own_block, parts, sums_ref, reds[:4], reds[4:])
    red.last = (across, cross_send, cross_recv, se, te)
    c = red.c

    def load_pair(p):
        cols = pl.ds(pl.multiple_of(p * 128, 128), 128)
        sides = ((q_hbm, q_ref), (k_hbm, k_ref), (v_hbm, v_ref), (datt_hbm, datt_ref), (ctx_hbm, ctx_ref))
        return [
            pltpu.make_async_copy(src.at[:, cols], dst.at[:, cols], sp.at[n, p])
            for n, (src, dst) in enumerate(sides)
        ]

    for load in load_pair(0):
        load.start()
    red.barrier()
    for u in range(7):
        red.start(u)
    fetch = pltpu.make_async_copy(gf_ref.at[:, pl.ds(c * 16, 16)], own_ref.at[pl.ds(0, 7)], so)
    fetch.start()
    late_loads = [
        pltpu.make_async_copy(src, dst, sl.at[n])
        for n, (src, dst) in enumerate(
            [(nt_hbm, nt_ref), (w_hbm, w_ref), (tok_hbm, tok_ref), (dres_hbm, dres_ref)]
        )
    ]
    for load in load_pair(1):
        load.start()
    late_loads[0].start()
    for p in range(2, PAIRS):
        for load in load_pair(p):
            load.start()
    for load in late_loads[1:]:
        load.start()

    here, there = 0, HALF

    hops = [red.over_c, *red.over_z, red.over_y, red.over_x]

    def vhop(g, n):
        src = vs_ref.at[g, (0, 1, 1, 1, 2, 3)[n]]
        return red.copy(src, vr_ref.at[g, n], sv.at[g, n], tv.at[g, n], hops[n])

    def vstep(g, stage):
        came = ((), (0,), (1, 2, 3), (4,), (5,))[stage]
        if stage:
            total = vs_ref[g, stage - 1]
            for n in came:
                vhop(g, n).wait_recv()
                total = total + vr_ref[g, n]
            if stage == 4:
                vsum_ref[8 * g : 8 * g + 8] = total
            else:
                vs_ref[g, stage] = total
        for n in ((0,), (1, 2, 3), (4,), (5,), ())[stage]:
            vhop(g, n).start()

    lane = lax.broadcasted_iota(jnp.int32, (1, 128), 1)
    bias_ref[...] = jnp.broadcast_to(bias_in[...], (128, T)).T
    eye = lax.broadcasted_iota(jnp.int32, (256, 256), 0) == lax.broadcasted_iota(
        jnp.int32, (256, 256), 1
    )
    head_of = lax.broadcasted_iota(jnp.int32, (8, 128), 1) // HD == lax.broadcasted_iota(
        jnp.int32, (8, 128), 0
    )
    pick = jnp.where(head_of, 1.0, 0.0).astype(F32)
    vs_ref[0, 0] = vf_ref[...]
    vs_ref[1, 0] = jnp.zeros((8, D), F32)
    vstep(0, 0)
    for load in load_pair(0):
        load.wait()

    def progress(j, k):
        if k == 3:

            @pl.when(j == 0)
            def _():
                fetch.wait()

        if k == 7:
            for n in range(3):

                @pl.when(j == n)
                def _():
                    vstep(0, n + 1)

        if k % 2:
            one = 4 * j + (k - 3) // 2

            @pl.when((one >= 0) & (one < 9))
            def _():
                red.step1(one)

            two = 4 * j + (k - 7) // 2

            @pl.when(two >= 0)
            def _():
                red.step2(two)

            three = 4 * j + (k - 11) // 2

            @pl.when(three >= 0)
            def _():
                red.step3(three)

    @pl.loop(0, 3)
    def _(j):
        for half in range(2):
            p = 2 * j + half
            cols = pl.ds(pl.multiple_of(p * 128, 128), 128)

            def lanes(at, p=p):
                return pl.ds(pl.multiple_of(at + p * 128, 128), 128)

            if half == 0:

                @pl.when(j > 0)
                def _():
                    for load in load_pair(2 * j):
                        load.wait()

            else:
                for load in load_pair(p):
                    load.wait()
            qp, do = q_ref[:, cols], datt_ref[:, cols]
            prod = do.astype(F32) * ctx_ref[:, cols].astype(F32)
            delta_ref[...] = lax.dot_general(
                pick, prod, (((1,), (1,)), ((), ())),
                preferred_element_type=F32, precision=lax.Precision.HIGHEST,
            )
            dqt_ref[...] = jnp.zeros_like(dqt_ref)
            zero = jnp.zeros_like(qp)
            q2 = jnp.concatenate([jnp.where(lane < HD, qp, zero), jnp.where(lane < HD, zero, qp)], axis=0)
            do2 = jnp.concatenate([jnp.where(lane < HD, do, zero), jnp.where(lane < HD, zero, do)], axis=0)
            for i in range(4):
                progress(j, half * 4 + i)
                cut = slice(i * 256, (i + 1) * 256)
                kp, vp = k_ref[cut, cols], v_ref[cut, cols]
                bias256 = jnp.concatenate([bias_ref[cut]] * 2, axis=1)
                khs, vhs, es, dss = [], [], [[], []], [[], []]
                for h in range(2):
                    mine = (lane < HD) == (h == 0)
                    khs.append(jnp.where(mine, kp, jnp.zeros_like(kp)))
                    vhs.append(jnp.where(mine, vp, jnp.zeros_like(vp)))
                for m in range(4):
                    qs = slice(m * 256, (m + 1) * 256)
                    for h in range(2):
                        raw = dot_nt(khs[h], qp[qs])
                        s = raw + bias256
                        if i == m:
                            s = jnp.where(eye, raw, s)
                        e = jnp.exp(s - lt_ref[2 * p + h, :, qs])
                        dp = dot_nt(vhs[h], do[qs])
                        dss[h].append((e * (dp - delta_ref[h : h + 1, qs])).astype(BF16))
                        es[h].append(e.astype(BF16))
                ds = [jnp.concatenate(d, axis=1) for d in dss]
                dqt_ref[...] += dot_nn(jnp.concatenate(khs, axis=0).T, jnp.concatenate(ds, axis=0))
                dproj_ref[cut, lanes(D)] = dot_nn(jnp.concatenate(ds, axis=1), q2).astype(BF16)
                dproj_ref[cut, lanes(2 * D)] = dot_nn(jnp.concatenate(es[0] + es[1], axis=1), do2).astype(BF16)
            dproj_ref[:, cols] = dqt_ref[...].T.astype(BF16) * jnp.asarray(0.125, BF16)
            d3 = jnp.concatenate([dproj_ref[:, lanes(n * D)] for n in range(3)], axis=1)
            vs_ref[1, 0, 0:1, cols] = jnp.sum(d3[:, :128].astype(F32), axis=0, keepdims=True)
            vs_ref[1, 0, 1:2, cols] = jnp.sum(d3[:, 256:].astype(F32), axis=0, keepdims=True)
            if half == 0:

                @pl.when(j == 0)
                def _():
                    late_loads[0].wait()

            g = dot_nn(nt_ref[...], d3)
            if half == 0:
                gq_ref[...] = g
            else:
                for r in range(32):
                    rows = slice(r * 24, (r + 1) * 24)
                    at = place(r, x_first(7 + j)) + j // 2 * (r // 8 - 3 * (r % 2))
                    parts_ref[j, at] = blocks_of(gq_ref[rows, :], g[rows, :])
        own_ref[7 + j] = parts_ref[j, pl.ds(c * 16, 16)]
        for n in range(3):

            @pl.when(j == n)
            def _():
                red.start(7 + n)

    def tile(rows):
        d_normed = dot_nt(dproj_ref[rows, :], w_ref[...])
        n, rstd = norm_parts(tok_ref[rows, :].astype(F32))
        vs_ref[1, 0, 2:3, :] += jnp.sum(d_normed * n, axis=0, keepdims=True)
        vs_ref[1, 0, 3:4, :] += jnp.sum(d_normed, axis=0, keepdims=True)
        return dres_ref[rows, :] + norm_back(d_normed, n, rstd, row(gain_ref))

    def dcopy(t):
        rows = pl.ds(t * 256, 256)
        return red.copy(dsend_ref.at[rows], dsend_got.at[rows], sx.at[t], tx.at[t], red.over_x)

    def away(t):
        dsend_ref[t * 256 : (t + 1) * 256] = tile(pl.ds(there + t * 256, 256)).astype(BF16)

    def home(t):
        dtok_ref[t * 256 : (t + 1) * 256] = tile(pl.ds(here + t * 256, 256))

    for load in late_loads[1:]:
        load.wait()
    red.step3(7)
    away(0)
    dcopy(0).start()
    red.step3(8)
    away(1)
    dcopy(1).start()
    red.step1(9)
    home(0)
    home(1)
    keep = pltpu.make_async_copy(dtok_ref, dtok_hbm, so)
    keep.start()
    vstep(1, 0)
    for u in range(7):
        red.finish(u)
    vstep(1, 1)
    red.last_step2()
    vstep(1, 2)
    red.finish(7)
    red.finish(8)
    vstep(0, 4)
    vstep(1, 3)
    early = pltpu.make_async_copy(sums_ref.at[pl.ds(0, 9)], sums_hbm.at[pl.ds(0, 9)], so)
    keep.wait()
    early.start()
    red.last_step3()
    vstep(1, 4)
    for t in range(2):
        dcopy(t).wait()
    got = pltpu.make_async_copy(dsend_got, dgot_hbm, sl.at[0])
    got.start()
    red.last_finish()
    early.wait()
    late = pltpu.make_async_copy(sums_ref.at[9], sums_hbm.at[9], so)
    late.start()
    for g in range(2):
        for n in range(6):
            vhop(g, n).wait_send()
    red.drain()
    got.wait()
    late.wait()


def join_kernel(
    lo_hbm, logot_hbm, dtok_hbm, dgot_hbm, early_ref, late_ref, vec_ref,
    out_hbm, gtok_hbm, gin_ref, gback_ref, gout_ref, gqkv_ref, *rest,
):
    vouts, (lo_ref, logot_ref, dtok_ref, dgot_ref, wide_ref, sem) = rest[:9], rest[9:]
    x = lax.axis_index("seq")
    pairs = ((lo_hbm, lo_ref), (logot_hbm, logot_ref), (dtok_hbm, dtok_ref), (dgot_hbm, dgot_ref))
    loads = [pltpu.make_async_copy(src, dst, sem.at[n]) for n, (src, dst) in enumerate(pairs)]
    stores = [
        pltpu.make_async_copy(lo_ref, out_hbm.at[x], sem.at[4]),
        pltpu.make_async_copy(logot_ref, out_hbm.at[1 - x], sem.at[5]),
        pltpu.make_async_copy(dtok_ref, gtok_hbm.at[x], sem.at[6]),
        pltpu.make_async_copy(wide_ref, gtok_hbm.at[1 - x], sem.at[7]),
    ]
    for n in (2, 3, 0, 1):
        loads[n].start()
    for n in (2, 3, 0, 1):
        loads[n].wait()
        if n == 3:
            wide_ref[...] = dgot_ref[...].astype(F32)
        stores[n].start()
    for u in range(4):
        gback_ref[u // 2 * 48 : u // 2 * 48 + 48, u % 2 * UW : (u % 2 + 1) * UW] = (
            early_ref[u] if u < 2 else late_ref[3 + u]
        )
        gin_ref[:, u * D : u * D + UW] = late_ref[u, :24]
        gin_ref[:, u * D + UW : u * D + 2 * UW] = late_ref[u, 24:]
    gout_ref[:, :UW] = late_ref[4, :24]
    gout_ref[:, UW:] = late_ref[4, 24:]
    for p in range(PAIRS):
        part = late_ref[7 + p // 2, p % 2 * 24 : p % 2 * 24 + 24]
        for n in range(3):
            at = n * D + p * 128
            gqkv_ref[:, at : at + 128] = part[:, n * 128 : n * 128 + 128]
    rank = lax.axis_index("dp") * 2 + x
    mine = pltpu.roll(vec_ref[...], D - rank * 24, 1)
    for n, row in enumerate((10, 11, 8, 9, 3, 1, 2, 0)):
        vouts[n][...] = mine[row : row + 1, :24]
    z = rank // 8
    parts = pltpu.roll(vec_ref[4:8, :], D - (rank % 8) * 96, 1)
    chosen = parts[0:1, :96]
    for n in range(1, 4):
        chosen = jnp.where(z == n, parts[n : n + 1, :96], chosen)
    vouts[8][...] = chosen
    for store in stores:
        store.wait()


def call_bwd(*args):
    return pl.pallas_call(
        bwd_kernel,
        out_shape=(
            shape((HALF, D), F32), shape((HALF, D), BF16), shape((10, 48, UW), F32), shape((16, D), F32),
        ),
        in_specs=[VM] * 4 + [HB] * 10,
        out_specs=(HB, HB, HB, VM),
        scratch_shapes=[
            pltpu.VMEM((T, D), BF16),
            pltpu.VMEM((D, 3 * D), BF16),
            pltpu.VMEM((D, T), BF16),
            *[pltpu.VMEM((T, D), BF16)] * 5,
            pltpu.VMEM((T, D), F32),
            pltpu.VMEM((T, 128), F32),
            pltpu.VMEM((T, 3 * D), BF16),
            pltpu.VMEM((128, T), F32),
            pltpu.VMEM((D, UW), F32),
            pltpu.VMEM((8, T), F32),
            pltpu.VMEM((10, 16, 48, UW), BF16),
            pltpu.VMEM((3, 32, 48, UW), BF16),
            pltpu.VMEM((HALF, D), BF16),
            pltpu.VMEM((2, 4, 8, D), F32),
            pltpu.VMEM((2, 6, 8, D), F32),
            pltpu.VMEM((HALF, D), F32),
            pltpu.VMEM((HALF, D), BF16),
            pltpu.VMEM((10, 48, UW), F32),
            DMA((2, 6)), DMA((2, 6)), DMA((2,)), DMA((2,)), DMA, DMA((4,)), DMA((5, PAIRS)),
            pltpu.VMEM((3, 2, 48, UW), BF16),
            pltpu.VMEM((48, UW), BF16),
            pltpu.VMEM((48, UW), BF16),
            DMA((4,)), DMA((4,)), *reduction_scratch(10),
        ],
        compiler_params=pltpu.CompilerParams(
            vmem_limit_bytes=VMEM_LIMIT, collective_id=0, has_side_effects=True
        ),
    )(*args)


def call_join(*args):
    return pl.pallas_call(
        join_kernel,
        out_shape=(
            shape((2, HALF, D), BF16), shape((2, HALF, D), F32), shape((24, FF), F32), shape((96, D), F32),
            shape((24, D), F32), shape((24, 3 * D), F32), *[shape((1, 24), F32)] * 8, shape((1, 96), F32),
        ),
        in_specs=[HB] * 4 + [VM] * 3,
        out_specs=(HB, HB, *[VM] * 13),
        scratch_shapes=[
            pltpu.VMEM((HALF, D), BF16),
            pltpu.VMEM((HALF, D), BF16),
            pltpu.VMEM((HALF, D), F32),
            pltpu.VMEM((HALF, D), BF16),
            pltpu.VMEM((HALF, D), F32),
            DMA((8,)),
        ],
        compiler_params=pltpu.CompilerParams(vmem_limit_bytes=VMEM_LIMIT),
    )(*args)

def whole_sequences(
    tokens, lengths, key_mask, attn_gain, attn_shift, w_qkv, query_bias, value_bias, w_out,
    out_bias, ffn_gain, ffn_shift, w_in, in_bias, w_back, back_bias, cotangent,
):
    normed_t, q, k, v, ctx, tok, cot, log_total, bias = call_fwd(
        lengths, key_mask, attn_gain, attn_shift, query_bias, value_bias,
        tokens, cotangent, w_qkv,
    )
    out, out_got, d_res, d_att, gf, vf, early = call_ffn(
        tok, ctx, out_bias, ffn_gain, ffn_shift, in_bias, back_bias, cot,
        w_out, w_in, w_back,
    )
    d_tok, d_got, late, vec = call_bwd(
        bias, attn_gain, log_total, vf,
        tok, w_qkv, normed_t, q, k, v, ctx, d_att, d_res, gf,
    )
    (
        layer_out, grad_tokens, g_in, g_back, g_out, g_qkv, ag, ash, qb, vb, ob, fg, fs, bb, ib,
    ) = call_join(out, out_got, d_tok, d_got, early, late, vec)
    return (
        layer_out, grad_tokens, ag.reshape(24), ash.reshape(24), g_qkv, qb.reshape(24), vb.reshape(24),
        g_out, ob.reshape(24), fg.reshape(24), fs.reshape(24), g_in, ib.reshape(96), g_back,
        bb.reshape(24),
    )

def shifted(array, axis, by):
    devices = lax.axis_size(axis)
    return lax.ppermute(array, axis, [(i, (i + by) % devices) for i in range(devices)])


def layer_norm(values, gain, shift):
    center = values - jnp.mean(values, axis=-1, keepdims=True)
    spread = jnp.mean(center * center, axis=-1, keepdims=True)
    return center * lax.rsqrt(spread + NORM_EPS) * gain + shift


def partial_gelu(values):
    return jax.nn.gelu(values, approximate=True)


def outer_product(left, right):
    return lax.dot_general(
        left, right, (((0,), (0,)), ((), ())), preferred_element_type=jnp.float32
    )


def times_transposed(left, right):
    return lax.dot_general(
        left, right, (((1,), (1,)), ((), ())), preferred_element_type=jnp.float32
    )


def allowed_keys(lengths, flags_all, query_pos, first_key, key_count):
    key_pos = first_key + jnp.arange(key_count, dtype=jnp.int32)
    key_flags = lax.dynamic_slice_in_dim(flags_all, first_key, key_count, 1)
    key_valid = (key_pos[None, :] < lengths[:, None]) & (key_flags == 1)
    itself = key_pos[None, :] == query_pos[:, None]
    return key_valid[:, None, None, :] | itself[None, :, None, :]


def send_home(partial_grads):
    return shifted(partial_grads.astype(jnp.bfloat16), "seq", 1).astype(partial_grads.dtype)


def shards(
    tokens,
    lengths,
    key_mask,
    attn_gain,
    attn_shift,
    w_qkv,
    query_bias,
    value_bias,
    w_out,
    out_bias,
    ffn_gain,
    ffn_shift,
    w_in,
    in_bias,
    w_back,
    back_bias,
    cotangent,
):
    seq_count, span_dev, model_width = tokens.shape
    row_count = seq_count * span_dev
    members = lax.axis_size("seq")
    own_index = lax.axis_index("seq")
    query_pos = own_index * span_dev + jnp.arange(span_dev, dtype=jnp.int32)
    flags_all = lax.all_gather(key_mask, "seq", axis=1, tiled=True)
    inputs = tokens.astype(jnp.float32).reshape(row_count, model_width)
    normed_one, norm_pull_one = jax.vjp(layer_norm, inputs, attn_gain, attn_shift)
    normed_attn = normed_one.astype(jnp.bfloat16)
    projected = jnp.dot(normed_attn, w_qkv, preferred_element_type=jnp.float32)
    queries = ((projected[:, :model_width] + query_bias) * 0.125).astype(jnp.bfloat16)
    queries = queries.reshape(seq_count, span_dev, H, HD)
    keyval = jnp.concatenate(
        [projected[:, model_width : 2 * model_width], projected[:, 2 * model_width :] + value_bias],
        axis=1,
    ).astype(jnp.bfloat16)
    keyval = keyval.reshape(seq_count, span_dev, 2 * model_width)

    def split_block(block_kv):
        key_count = block_kv.shape[1]
        key_heads = block_kv[:, :, :model_width].reshape(seq_count, key_count, H, HD)
        value_heads = block_kv[:, :, model_width:].reshape(seq_count, key_count, H, HD)
        return (key_count, key_heads, value_heads)

    running_max = jnp.full((seq_count, span_dev, H), NEG_FILL, jnp.float32)
    key_count, key_heads, value_heads = split_block(
        lax.all_gather(keyval, "seq", axis=1, tiled=True)
    )
    scores = jnp.einsum("sqhd,skhd->sqhk", queries, key_heads, preferred_element_type=jnp.float32)
    allowed = allowed_keys(lengths, flags_all, query_pos, jnp.int32(0), key_count)
    new_max = jnp.maximum(running_max, jnp.max(jnp.where(allowed, scores, NEG_FILL), axis=-1))
    expo = jnp.exp(jnp.where(allowed, scores - new_max[..., None], NEG_FILL))
    running_sum = jnp.sum(expo, axis=-1)
    running_acc = jnp.einsum(
        "sqhk,skhd->sqhd",
        expo.astype(jnp.bfloat16),
        value_heads,
        preferred_element_type=jnp.float32,
    )
    attended = running_acc / running_sum[..., None]
    log_total = new_max + jnp.log(running_sum)
    context = attended.reshape(row_count, model_width).astype(jnp.bfloat16)
    residual = inputs + jnp.dot(context, w_out, preferred_element_type=jnp.float32) + out_bias
    normed_two, norm_pull_two = jax.vjp(layer_norm, residual, ffn_gain, ffn_shift)
    normed_ffn = normed_two.astype(jnp.bfloat16)
    pre_act = jnp.dot(normed_ffn, w_in, preferred_element_type=jnp.float32) + in_bias
    gelu_value, gelu_pull = jax.vjp(partial_gelu, pre_act)
    activated = gelu_value.astype(jnp.bfloat16)
    layer_out = (
        residual + jnp.dot(activated, w_back, preferred_element_type=jnp.float32) + back_bias
    )
    grad_rows = cotangent.reshape(row_count, model_width)
    grad_float = grad_rows.astype(jnp.float32)
    grad_back_bias = jnp.sum(grad_float, axis=0)
    grad_w_back = outer_product(activated, grad_rows)
    d_act = times_transposed(grad_rows, w_back)
    d_pre = gelu_pull(d_act)[0].astype(jnp.bfloat16)
    grad_in_bias = jnp.sum(d_pre.astype(jnp.float32), axis=0)
    grad_w_in = outer_product(normed_ffn, d_pre)
    d_normed = times_transposed(d_pre, w_in)
    d_res_part, grad_ffn_gain, grad_ffn_shift = norm_pull_two(d_normed)
    d_residual = grad_float + d_res_part
    d_branch = d_residual.astype(jnp.bfloat16)
    grad_out_bias = jnp.sum(d_branch.astype(jnp.float32), axis=0)
    grad_w_out = outer_product(context, d_branch)
    d_attended = (
        times_transposed(d_branch, w_out).astype(jnp.bfloat16).reshape(seq_count, span_dev, H, HD)
    )
    delta = jnp.sum(d_attended.astype(jnp.float32) * attended, axis=-1)

    def attend_back(block_kv, first_key):
        key_count, key_heads, value_heads = split_block(block_kv)
        scores = jnp.einsum(
            "sqhd,skhd->sqhk", queries, key_heads, preferred_element_type=jnp.float32
        )
        allowed = allowed_keys(lengths, flags_all, query_pos, first_key, key_count)
        weights_f = jnp.exp(jnp.where(allowed, scores - log_total[..., None], NEG_FILL))
        d_values = jnp.einsum(
            "sqhk,sqhd->skhd",
            weights_f.astype(jnp.bfloat16),
            d_attended,
            preferred_element_type=jnp.float32,
        )
        d_probs = jnp.einsum(
            "sqhd,skhd->sqhk", d_attended, value_heads, preferred_element_type=jnp.float32
        )
        d_scores = (weights_f * (d_probs - delta[..., None])).astype(jnp.bfloat16)
        d_query = jnp.einsum(
            "sqhk,skhd->sqhd", d_scores, key_heads, preferred_element_type=jnp.float32
        )
        d_keys = jnp.einsum(
            "sqhk,sqhd->skhd", d_scores, queries, preferred_element_type=jnp.float32
        )
        d_block = jnp.concatenate(
            [
                d_keys.reshape(seq_count, key_count, model_width),
                d_values.reshape(seq_count, key_count, model_width),
            ],
            axis=2,
        )
        return (d_query, d_block)

    zero_query = jnp.zeros((seq_count, span_dev, H, HD), jnp.float32)

    def turn(turn_index, state_now):
        current, d_current, d_query = state_now
        anchor = (own_index - turn_index) % members
        add_query, add_block = attend_back(current, anchor * span_dev)
        current = shifted(current, "seq", 1)
        return (current, send_home(d_current + add_block), d_query + add_query)

    start_back = (
        keyval,
        jnp.zeros((seq_count, span_dev, 2 * model_width), jnp.float32),
        zero_query,
    )
    current, d_current, d_query = lax.fori_loop(0, members - 1, turn, start_back)
    anchor = (own_index - (members - 1)) % members
    add_query, add_block = attend_back(current, anchor * span_dev)
    d_query = d_query + add_query
    d_keyval = send_home(d_current + add_block)
    d_query_low = d_query.reshape(row_count, model_width).astype(jnp.bfloat16)
    d_keyval_low = d_keyval.reshape(row_count, 2 * model_width).astype(jnp.bfloat16)
    query_scaled = d_query_low.astype(jnp.float32) * 0.125
    grad_query_bias = jnp.sum(query_scaled, axis=0)
    grad_value_bias = jnp.sum(d_keyval_low[:, model_width:].astype(jnp.float32), axis=0)
    d_projected = jnp.concatenate([query_scaled.astype(jnp.bfloat16), d_keyval_low], axis=1)
    grad_w_qkv = outer_product(normed_attn, d_projected)
    d_normed_attn = times_transposed(d_projected, w_qkv)
    d_in_part, grad_attn_gain, grad_attn_shift = norm_pull_one(d_normed_attn)
    grad_tokens = (d_residual + d_in_part).reshape(seq_count, span_dev, model_width)
    out_block = layer_out.astype(jnp.bfloat16).reshape(seq_count, span_dev, model_width)
    all_sums = (
        lax.psum_scatter(grad_attn_gain, ("dp", "seq"), scatter_dimension=0, tiled=True),
        lax.psum_scatter(grad_attn_shift, ("dp", "seq"), scatter_dimension=0, tiled=True),
        lax.psum_scatter(grad_w_qkv, ("dp", "seq"), scatter_dimension=0, tiled=True),
        lax.psum_scatter(grad_query_bias, ("dp", "seq"), scatter_dimension=0, tiled=True),
        lax.psum_scatter(grad_value_bias, ("dp", "seq"), scatter_dimension=0, tiled=True),
        lax.psum_scatter(grad_w_out, ("dp", "seq"), scatter_dimension=0, tiled=True),
        lax.psum_scatter(grad_out_bias, ("dp", "seq"), scatter_dimension=0, tiled=True),
        lax.psum_scatter(grad_ffn_gain, ("dp", "seq"), scatter_dimension=0, tiled=True),
        lax.psum_scatter(grad_ffn_shift, ("dp", "seq"), scatter_dimension=0, tiled=True),
        lax.psum_scatter(grad_w_in, ("dp", "seq"), scatter_dimension=0, tiled=True),
        lax.psum_scatter(grad_in_bias, ("dp", "seq"), scatter_dimension=0, tiled=True),
        lax.psum_scatter(grad_w_back, ("dp", "seq"), scatter_dimension=0, tiled=True),
        lax.psum_scatter(grad_back_bias, ("dp", "seq"), scatter_dimension=0, tiled=True),
    )
    return (
        out_block,
        grad_tokens,
        all_sums[0],
        all_sums[1],
        all_sums[2],
        all_sums[3],
        all_sums[4],
        all_sums[5],
        all_sums[6],
        all_sums[7],
        all_sums[8],
        all_sums[9],
        all_sums[10],
        all_sums[11],
        all_sums[12],
    )


def solution(mesh):
    sizes = dict(mesh.shape)
    whole = sizes == {"dp": 16, "seq": 2}
    return jax.shard_map(
        whole_sequences if whole else shards,
        mesh=mesh,
        in_specs=(
            P("dp", "seq", None),
            P("dp"),
            P("dp", "seq"),
            P(),
            P(),
            P(),
            P(),
            P(),
            P(),
            P(),
            P(),
            P(),
            P(),
            P(),
            P(),
            P(),
            P("dp", "seq", None),
        ),
        out_specs=(
            P("dp", "seq", None),
            P("dp", "seq", None),
            P(("dp", "seq")),
            P(("dp", "seq")),
            P(("dp", "seq"), None),
            P(("dp", "seq")),
            P(("dp", "seq")),
            P(("dp", "seq"), None),
            P(("dp", "seq")),
            P(("dp", "seq")),
            P(("dp", "seq")),
            P(("dp", "seq"), None),
            P(("dp", "seq")),
            P(("dp", "seq"), None),
            P(("dp", "seq")),
        ),
        check_vma=False,
    )
```

```python
import functools

import jax
import jax.numpy as jnp
from jax import lax
from jax.experimental import pallas as pl
from jax.experimental.pallas import tpu as pltpu
from jax.sharding import PartitionSpec as P

H = 12
HD = 64


NEG_FILL = -1e30
NORM_EPS = 1e-05

F32 = jnp.float32
BF16 = jnp.bfloat16
D = 768
FF = 3072
T = 1024
HALF = 512
PAIRS = 6
UW = 384
MESH = pl.DeviceIdType.MESH
VMEM_LIMIT = 62 * 1024 * 1024


def dot_nn(a, b):
    return lax.dot_general(a, b, (((1,), (0,)), ((), ())), preferred_element_type=F32)


def dot_nt(a, b):
    return lax.dot_general(a, b, (((1,), (1,)), ((), ())), preferred_element_type=F32)


def dot_tn(a, b):
    return lax.dot_general(a, b, (((0,), (0,)), ((), ())), preferred_element_type=F32)


def shape(dims, dtype):
    return jax.ShapeDtypeStruct(dims, dtype)


VM = pl.BlockSpec(memory_space=pltpu.VMEM)
SM = pl.BlockSpec(memory_space=pltpu.SMEM)
HB = pl.BlockSpec(memory_space=pl.ANY)
DMA = pltpu.SemaphoreType.DMA


def row(ref):
    return ref[...].reshape(1, -1)


def norm_parts(x):
    center = x - jnp.mean(x, axis=-1, keepdims=True)
    spread = jnp.mean(center * center, axis=-1, keepdims=True)
    rstd = lax.rsqrt(spread + NORM_EPS)
    return center * rstd, rstd


def norm_back(d_norm, n, rstd, gain):
    u = d_norm * gain
    mean_u = jnp.mean(u, axis=-1, keepdims=True)
    mean_un = jnp.mean(u * n, axis=-1, keepdims=True)
    return (u - mean_u - n * mean_un) * rstd


def blocks_of(top, bottom):
    return jnp.concatenate([top, bottom], axis=0).astype(BF16)


def place(index, first_x):
    z, y, c, x = index // 8, (index // 4) % 2, (index // 2) % 2, index % 2
    return c * 16 + z + 4 * (2 * y + x) + first_x * 4 * (x - y)


def reduction_scratch(units):
    sems = [DMA((units,)), DMA((units,)), DMA((units,)), DMA((units, 3))]
    return [pltpu.VMEM((units, n, 48, UW), BF16) for n in (16, 8, 4, 3)] + sems + sems


class Reduction:
    def __init__(self, units, extra, own, parts, sums, held, sems):
        self.units, self.extra = units, extra
        self.own, self.parts, self.sums, self.held = own, parts, sums, held
        self.sends, self.recvs = sems[:4], sems[4:8]
        dp, x = lax.axis_index("dp"), lax.axis_index("seq")
        z, y, c = dp // 4, (dp // 2) % 2, dp % 2
        self.dp, self.x, self.y, self.z, self.c = dp, x, y, z, c
        self.over_c = (dp + 1 - 2 * c, x)
        self.over_x = (dp, 1 - x)
        self.over_y = (dp + 2 - 4 * y, x)
        self.over_z = [(lax.rem(z + d, 4) * 4 + y * 2 + c, x) for d in (1, 2, 3)]

    def barrier(self):
        sem = pltpu.get_barrier_semaphore()
        for to in (self.over_c, self.over_x, self.over_y, *self.over_z):
            pl.semaphore_signal(sem, inc=1, device_id=to, device_id_type=MESH)
        pl.semaphore_wait(sem, 6)

    def copy(self, src, dst, send, recv, to):
        return pltpu.make_async_remote_copy(
            src_ref=src, dst_ref=dst, send_sem=send, recv_sem=recv, device_id=to, device_id_type=MESH
        )

    def axes(self, u):
        fx, x, y, dp = x_first(u), self.x, self.y, self.dp
        first = (dp + (1 - fx) * (2 - 4 * y), x + fx * (1 - 2 * x))
        second = (dp + fx * (2 - 4 * y), x + (1 - fx) * (1 - 2 * x))
        return first, second, y + fx * (x - y), x + fx * (y - x)

    def hop0(self, u):
        src = self.parts(u).at[pl.ds((1 - self.c) * 16, 16)]
        return self.copy(src, self.held[0].at[u], self.sends[0].at[u], self.recvs[0].at[u], self.over_c)

    def hop1(self, u):
        first, _, a, _ = self.axes(u)
        src = self.held[0].at[u, pl.ds((1 - a) * 8, 8)]
        return self.copy(src, self.held[1].at[u], self.sends[1].at[u], self.recvs[1].at[u], first)

    def hop2(self, u):
        _, second, _, b = self.axes(u)
        src = self.held[1].at[u, pl.ds((1 - b) * 4, 4)]
        return self.copy(src, self.held[2].at[u], self.sends[2].at[u], self.recvs[2].at[u], second)

    def hop3(self, u, d):
        src = self.held[2].at[u, lax.rem(self.z + d + 1, 4)]
        return self.copy(
            src, self.held[3].at[u, d], self.sends[3].at[u, d], self.recvs[3].at[u, d], self.over_z[d]
        )

    def arrived(self, u):
        held = self.held[0].at[u]
        self.copy(held, held, self.sends[0].at[u], self.recvs[0].at[u], self.over_c).wait_recv()

    def start(self, u):
        self.hop0(u).start()

    def step1(self, u):
        self.arrived(u)
        _, _, a, _ = self.axes(u)
        held = self.held[0]

        def add(k):
            held[u, k] = (held[u, k].astype(F32) + self.own(u, k).astype(F32)).astype(BF16)

        @pl.loop(0, 8, unroll=2)
        def _(k):
            add((1 - a) * 8 + k)

        self.hop1(u).start()

        @pl.loop(0, 8, unroll=2)
        def _(k):
            add(a * 8 + k)

    def step2(self, u):
        self.hop1(u).wait_recv()
        _, _, a, b = self.axes(u)
        held, before = self.held[1], self.held[0]

        def add(k):
            held[u, k] = (held[u, k].astype(F32) + before[u, a * 8 + k].astype(F32)).astype(BF16)

        for k in range(4):
            add((1 - b) * 4 + k)
        self.hop2(u).start()
        for k in range(4):
            add(b * 4 + k)

    def step3(self, u):
        self.hop2(u).wait_recv()
        _, _, _, b = self.axes(u)
        held, before = self.held[2], self.held[1]
        for k in range(4):
            held[u, k] = (held[u, k].astype(F32) + before[u, b * 4 + k].astype(F32)).astype(BF16)
        for d in range(3):
            self.hop3(u, d).start()

    def finish(self, u):
        total = self.held[2][u, self.z].astype(F32)
        for d in range(3):
            self.hop3(u, d).wait_recv()
            total = total + self.held[3][u, d].astype(F32)
        self.sums[u] = total

    def last_hop(self, d):
        across, cross_send, cross_recv, sends, recvs = self.last
        u = self.units
        if d == 3:
            return self.copy(cross_send, cross_recv, sends.at[3], recvs.at[3], self.over_x)
        src = self.held[1].at[u, pl.ds(lax.rem(self.z + d + 1, 4) * 2, 2)]
        return self.copy(src, across.at[d], sends.at[d], recvs.at[d], self.over_z[d])

    def last_step2(self):
        u = self.units
        self.hop1(u).wait_recv()
        for k in range(8):
            self.held[1][u, k] = (
                self.held[1][u, k].astype(F32) + self.held[0][u, self.y * 8 + k].astype(F32)
            ).astype(BF16)
        for d in range(3):
            self.last_hop(d).start()

    def last_step3(self):
        across, cross_send = self.last[:2]
        for d in range(3):
            self.last_hop(d).wait_recv()
        totals = []
        for k in range(2):
            total = self.held[1][self.units, self.z * 2 + k].astype(F32)
            for d in range(3):
                total = total + across[d, k].astype(F32)
            totals.append(total)
        cross_send[...] = jnp.where(self.x == 0, totals[1], totals[0]).astype(BF16)
        self.last_hop(3).start()
        self.sums[self.units] = jnp.where(self.x == 0, totals[0], totals[1])

    def last_finish(self):
        self.last_hop(3).wait_recv()
        self.sums[self.units] = self.sums[self.units] + self.last[2][...].astype(F32)

    def drain(self):
        for u in range(self.units):
            self.hop0(u).wait_send()
            self.hop1(u).wait_send()
            self.hop2(u).wait_send()
            for d in range(3):
                self.hop3(u, d).wait_send()
        if self.extra:
            self.hop0(self.units).wait_send()
            self.hop1(self.units).wait_send()
            for d in range(4):
                self.last_hop(d).wait_send()


def fwd_kernel(
    len_ref, mask_ref, gain_ref, shift_ref, qb_ref, vb_ref, tok_hbm, cot_hbm, w_hbm,
    nt_hbm, q_hbm, k_hbm, v_hbm, ctx_hbm, tok_out, cot_out, lt_ref, bias_ref,
    tok_ref, cot_ref, w_ref, nt_ref, q_ref, k_ref, v_ref, ctx_ref, mgot_ref, part_ref, mx_ref, logs_ref,
    sl, so, sx, tx,
):
    dp, x = lax.axis_index("dp"), lax.axis_index("seq")
    here, there = 0, HALF
    load_w = pltpu.make_async_copy(w_hbm, w_ref, sl.at[0])
    load_tok = pltpu.make_async_copy(tok_hbm.at[x], tok_ref.at[pl.ds(here, HALF)], sl.at[1])
    load_cot = pltpu.make_async_copy(cot_hbm.at[x], cot_ref, sl.at[2])
    load_tok.start()
    load_w.start()

    def swap(n):
        if n == 4:
            src, dst = mask_ref, mgot_ref
        else:
            side, buffer = (tok_hbm, tok_ref) if n < 4 else (cot_hbm, cot_out)
            rows = 128 if n < 4 else 256
            at = (n if n < 4 else n - 5) * rows
            src = side.at[1 - x, pl.ds(at, rows)]
            dst = buffer.at[pl.ds(there + at, rows)]
        return pltpu.make_async_remote_copy(
            src_ref=src, dst_ref=dst, send_sem=sx.at[n], recv_sem=tx.at[n],
            device_id=(dp, 1 - x), device_id_type=MESH,
        )

    sem = pltpu.get_barrier_semaphore()
    pl.semaphore_signal(sem, inc=1, device_id=(dp, 1 - x), device_id_type=MESH)
    pl.semaphore_wait(sem, 1)
    swaps = [swap(n) for n in range(7)]
    for n in (4, 0, 1, 2, 3, 5, 6):
        swaps[n].start()
    load_tok.wait()
    load_w.wait()
    load_cot.start()

    def project(first, count):
        rows = pl.ds(pl.multiple_of(first, count), count)
        n, _ = norm_parts(tok_ref[rows, :].astype(F32))
        normed = (n * row(gain_ref) + row(shift_ref)).astype(BF16)
        nt_ref[:, rows] = normed.T
        q_ref[rows, :] = ((dot_nn(normed, w_ref[:, :D]) + row(qb_ref)) * 0.125).astype(BF16)
        k_ref[rows, :] = dot_nn(normed, w_ref[:, D : 2 * D]).astype(BF16)
        v_ref[rows, :] = (dot_nn(normed, w_ref[:, 2 * D :]) + row(vb_ref)).astype(BF16)

    @pl.loop(0, 2)
    def _(t):
        project(t * 256, 256)

    swaps[4].wait_recv()
    pos = lax.broadcasted_iota(jnp.int32, (1, HALF), 1)
    for first, ref in ((here, mask_ref), (there, mgot_ref)):
        flags = jnp.where(x == 0, ref[0:1, :], ref[1:2, :])
        at = jnp.where(x == 0, first, HALF - first)
        valid = (pos + at < len_ref[x]) & (flags == 1)
        half_bias = jnp.where(valid, 0.0, NEG_FILL).astype(F32)
        bias_ref[:, first : first + HALF] = half_bias
    lane = lax.broadcasted_iota(jnp.int32, (1, 128), 1)
    wide = lax.broadcasted_iota(jnp.int32, (256, 128), 1)
    logs_ref[...] = jnp.zeros_like(logs_ref)
    eye = lax.broadcasted_iota(jnp.int32, (256, 256), 0) == lax.broadcasted_iota(
        jnp.int32, (256, 256), 1
    )

    def attend(p, chains, spans, first):
        cols = pl.ds(pl.multiple_of(p * 128, 128), 128)
        keys, values = {}, {}
        for low, high in sorted(set(spans.values())):
            kp, vp = k_ref[low:high, cols], v_ref[low:high, cols]
            keys[low, high] = [jnp.where((lane < HD) == (h == 0), kp, jnp.zeros_like(kp)) for h in range(2)]
            values[low, high] = jnp.concatenate([vp, jnp.ones_like(vp)], axis=1)

        def score(a, h):
            return dot_nt(q_ref[a : a + 256, cols], keys[spans[a]][h])

        def softmax(a, raw, before):
            low, high = spans[a]
            pieces = []
            for b in range(low, high, 256):
                cut = raw[:, b - low : b - low + 256]
                piece = cut + bias_ref[:, b : b + 256]
                pieces.append(jnp.where(eye, cut, piece) if a == b else piece)
            s = jnp.concatenate(pieces, axis=1)
            top = jnp.max(s, axis=1, keepdims=True)
            if before is not None:
                top = jnp.maximum(top, before)
            return top, jnp.exp(s - top).astype(BF16)

        outs = []
        raw = score(*chains[0])
        for n, (a, h) in enumerate(chains):
            ahead = score(*chains[n + 1]) if n + 1 < len(chains) else None
            merge = not first and a < HALF
            before = mx_ref[2 * p + h, a : a + 256, 0:1] if merge else None
            top, e = softmax(a, raw, before)
            o = dot_nn(e, values[spans[a]])
            raw = ahead
            if first:
                part_ref[2 * p + h, a : a + 256] = o
                mx_ref[2 * p + h, a : a + 256] = jnp.broadcast_to(top, (256, 128))
                continue
            if merge:
                o = o + part_ref[2 * p + h, a : a + 256] * jnp.exp(before - top)
            total = o[:, 128:]
            logs_ref[a : a + 256] = jnp.where(wide == 2 * p + h, top + jnp.log(total), logs_ref[a : a + 256])
            outs.append(o[:, :128] / total)
            if h == 1:
                ctx_ref[a : a + 256, cols] = jnp.where(lane < HD, outs[-2], outs[-1]).astype(BF16)

    own = [(a, h) for a in (0, 256) for h in range(2)]
    other = [(a, h) for a in (512, 768) for h in range(2)]

    @pl.loop(0, PAIRS)
    def _(p):
        attend(p, own, {0: (0, HALF), 256: (0, HALF)}, True)

    for n in range(4):
        swaps[n].wait_recv()
        project(there + n * 128, 128)

    load_cot.wait()
    last = pltpu.make_async_copy(cot_ref, cot_out.at[pl.ds(here, HALF)], so.at[11])
    last.start()
    outs = [
        pltpu.make_async_copy(src, dst, so.at[n])
        for n, (src, dst) in enumerate(
            [(nt_ref, nt_hbm), (q_ref, q_hbm), (k_ref, k_hbm), (v_ref, v_hbm), (tok_ref, tok_out)]
        )
    ]
    for one in outs:
        one.start()

    def ctx_out(p):
        cols = pl.ds(pl.multiple_of(p * 128, 128), 128)
        return pltpu.make_async_copy(ctx_ref.at[:, cols], ctx_hbm.at[:, cols], so.at[5 + p])

    @pl.loop(0, PAIRS)
    def _(p):
        attend(p, own + other, {0: (HALF, T), 256: (HALF, T), 512: (0, T), 768: (0, T)}, False)
        ctx_out(p).start()

    logs = logs_ref[...].T
    for h in range(H):
        lt_ref[h] = logs[h : h + 1]
    for n in (5, 6):
        swaps[n].wait_recv()
    for one in swaps:
        one.wait_send()
    for one in outs:
        one.wait()
    for p in range(PAIRS):
        ctx_out(p).wait()
    last.wait()


def call_fwd(*args):
    low = shape((T, D), BF16)
    return pl.pallas_call(
        fwd_kernel,
        out_shape=(
            shape((D, T), BF16), low, low, low, low, low, low, shape((H, 1, T), F32), shape((1, T), F32),
        ),
        in_specs=[SM] + [VM] * 5 + [HB] * 3,
        out_specs=(HB,) * 7 + (VM, VM),
        scratch_shapes=[
            pltpu.VMEM((T, D), BF16),
            pltpu.VMEM((HALF, D), BF16),
            pltpu.VMEM((D, 3 * D), BF16),
            pltpu.VMEM((D, T), BF16),
            *[pltpu.VMEM((T, D), BF16)] * 4,
            pltpu.VMEM((2, HALF), jnp.int32),
            pltpu.VMEM((H, HALF, 256), F32),
            pltpu.VMEM((H, HALF, 128), F32),
            pltpu.VMEM((T, 128), F32),
            DMA((3,)), DMA((12,)), DMA((7,)), DMA((7,)),
        ],
        compiler_params=pltpu.CompilerParams(
            vmem_limit_bytes=VMEM_LIMIT, collective_id=2, has_side_effects=True
        ),
    )(*args)


def x_first(unit):
    return (unit + 1) % 2


def ffn_kernel(
    tok_ref, ctx_ref, ob_ref, g_ref, s_ref, ib_ref, bb_ref, cot_hbm, wo_hbm, wi_hbm, wb_hbm,
    lo_ref, logot_ref, dres_hbm, datt_hbm, grads_hbm, vec_ref, sums_ref,
    wo_ref, wi_ref, wb_ref, nf_ref, act_ref, dpre_ref, dbr_ref, res_ref, dn_ref, away_ref, cot_ref,
    parts_ref, grads_ref, sw, so, sx, tx, *reds,
):
    def parts(u):
        return parts_ref.at[u]

    def own_block(u, k):
        return parts_ref[u, red.c * 16 + k]

    red = Reduction(2, 0, own_block, parts, sums_ref, reds[:4], reds[4:])
    loads = [pltpu.make_async_copy(wo_hbm, wo_ref, sw.at[0])]
    for c in range(4):
        cut = pl.ds(c * 768, 768)
        loads.append(pltpu.make_async_copy(wi_hbm.at[:, cut], wi_ref.at[:, cut], sw.at[1 + 2 * c]))
        loads.append(pltpu.make_async_copy(wb_hbm.at[cut], wb_ref.at[cut], sw.at[2 + 2 * c]))
    loads.append(pltpu.make_async_copy(cot_hbm, cot_ref, sw.at[9]))
    for load in loads:
        load.start()
    red.barrier()
    vec_ref[...] = jnp.zeros_like(vec_ref)
    loads[0].wait()
    lo_copy = red.copy(away_ref, logot_ref, sx, tx, red.over_x)

    def grads_out(u):
        return pltpu.make_async_copy(grads_ref.at[u], grads_hbm.at[u], so.at[8 + u])

    def rows_of(t):
        return pl.ds(pl.multiple_of(HALF - t * HALF, HALF), HALF)

    def forward(t, loads_of):
        rows = rows_of(t)
        res = tok_ref[rows, :].astype(F32) + dot_nn(ctx_ref[rows, :], wo_ref[...]) + row(ob_ref)
        res_ref[rows, :] = res
        n, _ = norm_parts(res)
        normed = (n * row(g_ref) + row(s_ref)).astype(BF16)
        nf_ref[rows, :] = normed
        total = res + row(bb_ref)
        def pre(c):
            for load in loads_of(c):
                load.wait()
            cut = slice(c * 768, (c + 1) * 768)
            return dot_nn(normed, wi_ref[:, cut]) + row(ib_ref)[:, cut]

        v = pre(0)
        for c in range(4):
            cut = slice(c * 768, (c + 1) * 768)
            ahead = pre(c + 1) if c < 3 else None
            sq = v * v
            th = jnp.tanh(v * (0.7978845608 + (0.7978845608 * 0.044715) * sq))
            half = 0.5 + 0.5 * th
            act = (v * half).astype(BF16)
            slope = half + v * (half * (1.0 - th)) * (
                0.7978845608 + (3 * 0.7978845608 * 0.044715) * sq
            )
            act_ref[rows, cut] = act
            dpre_ref[rows, cut] = slope.astype(BF16)
            total = total + dot_nn(act, wb_ref[cut, :])
            v = ahead
        return total.astype(BF16)

    away_ref[...] = forward(0, lambda c: loads[1 + 2 * c : 3 + 2 * c])
    lo_copy.start()
    lo_ref[...] = forward(1, lambda c: ())

    loads[9].wait()

    @pl.loop(0, 4)
    def _(z):
        g = dot_tn(act_ref[:, pl.ds(pl.multiple_of(z * 768, 768), 768)], cot_ref[...])
        for r in range(8):
            for u in range(4):
                i, j = u // 2, u % 2
                block = g[r * 96 + i * 48 : r * 96 + i * 48 + 48, j * UW : (j + 1) * UW].astype(BF16)
                if u < 2:
                    parts_ref[u, place(r, x_first(u)) + z] = block
                else:
                    grads_ref[3 + u, place(r, x_first(3 + u)) + z] = block

    for u in range(2):
        red.start(u)
    for u in (5, 6):
        grads_out(u).start()

    def tile_out(t, part):
        rows = rows_of(t)
        if part == 0:
            return pltpu.make_async_copy(res_ref.at[rows], dres_hbm.at[rows], so.at[2 * t])
        return pltpu.make_async_copy(cot_ref.at[rows], datt_hbm.at[rows], so.at[2 * t + 1])

    plan = {2: ((1, 0), (1, 1)), 6: ((2, 0), (2, 1))}

    @pl.loop(0, 2)
    def _(t):
        rows = rows_of(t)
        dy = cot_ref[rows, :]
        dn_ref[...] = jnp.zeros_like(dn_ref)
        for c in range(4):
            for at, moves in plan.items():
                if at % 4 == c:

                    @pl.when(t == at // 4)
                    def _():
                        for stage, u in moves:
                            (red.step1, red.step2, red.step3)[stage - 1](u)

            cut = slice(c * 768, (c + 1) * 768)
            d_act = dot_nt(dy, wb_ref[cut, :])
            d_pre = (d_act * dpre_ref[rows, cut].astype(F32)).astype(BF16)
            dpre_ref[rows, cut] = d_pre
            dn_ref[...] += dot_nt(d_pre, wi_ref[:, cut])
            vec_ref[4 + c : 5 + c, :] += jnp.sum(d_pre.astype(F32), axis=0, keepdims=True)

        n, rstd = norm_parts(res_ref[rows, :])
        d_normed = dn_ref[...]
        dyf = dy.astype(F32)
        d_res = dyf + norm_back(d_normed, n, rstd, row(g_ref))
        res_ref[rows, :] = d_res
        tile_out(t, 0).start()
        d_branch = d_res.astype(BF16)
        dbr_ref[rows, :] = d_branch
        cot_ref[rows, :] = dot_nt(d_branch, wo_ref[...]).astype(BF16)
        tile_out(t, 1).start()
        vec_ref[0:1, :] += jnp.sum(dyf, axis=0, keepdims=True)
        vec_ref[1:2, :] += jnp.sum(d_normed * n, axis=0, keepdims=True)
        vec_ref[2:3, :] += jnp.sum(d_normed, axis=0, keepdims=True)
        vec_ref[3:4, :] += jnp.sum(d_branch.astype(F32), axis=0, keepdims=True)

    def unit(u, g):
        for r in range(32):
            rows = slice(r * 24, (r + 1) * 24)
            grads_ref[u, place(r, x_first(u))] = blocks_of(g[rows, :UW], g[rows, UW:])
        grads_out(u).start()

    @pl.loop(0, 4)
    def _(u):
        unit(u, dot_tn(nf_ref[...], dpre_ref[:, pl.ds(pl.multiple_of(u * 768, 768), 768)]))

        @pl.when(u == 0)
        def _():
            red.step3(0)
            red.step3(1)

    unit(4, dot_tn(ctx_ref[...], dbr_ref[...]))
    for u in range(2):
        red.finish(u)
    lo_copy.wait()
    red.drain()
    for t in range(2):
        tile_out(t, 0).wait()
        tile_out(t, 1).wait()
    for u in range(7):
        grads_out(u).wait()


def call_ffn(*args):
    return pl.pallas_call(
        ffn_kernel,
        out_shape=(
            shape((HALF, D), BF16), shape((HALF, D), BF16), shape((T, D), F32), shape((T, D), BF16),
            shape((7, 32, 48, UW), BF16), shape((8, D), F32), shape((2, 48, UW), F32),
        ),
        in_specs=[VM] * 7 + [HB] * 4,
        out_specs=(VM, VM, HB, HB, HB, VM, VM),
        scratch_shapes=[
            pltpu.VMEM((D, D), BF16),
            pltpu.VMEM((D, FF), BF16),
            pltpu.VMEM((FF, D), BF16),
            pltpu.VMEM((T, D), BF16),
            pltpu.VMEM((T, FF), BF16),
            pltpu.VMEM((T, FF), BF16),
            pltpu.VMEM((T, D), BF16),
            pltpu.VMEM((T, D), F32),
            pltpu.VMEM((HALF, D), F32),
            pltpu.VMEM((HALF, D), BF16),
            pltpu.VMEM((T, D), BF16),
            pltpu.VMEM((2, 32, 48, UW), BF16),
            pltpu.VMEM((7, 32, 48, UW), BF16),
            DMA((10,)), DMA((15,)), DMA, DMA, *reduction_scratch(2),
        ],
        compiler_params=pltpu.CompilerParams(
            vmem_limit_bytes=VMEM_LIMIT, collective_id=1, has_side_effects=True
        ),
    )(*args)


def bwd_kernel(
    bias_in, gain_ref, lt_ref, vf_ref,
    tok_hbm, w_hbm, nt_hbm, q_hbm, k_hbm, v_hbm, ctx_hbm, datt_hbm, dres_hbm, gf_ref,
    dtok_hbm, dgot_hbm, sums_hbm, vsum_ref,
    tok_ref, w_ref, nt_ref, q_ref, k_ref, v_ref, ctx_ref, datt_ref, dres_ref, bias_ref,
    dproj_ref, dqt_ref, gq_ref, delta_ref, own_ref, parts_ref, dsend_ref, vs_ref, vr_ref, dtok_ref, dsend_got, sums_ref,
    sv, tv, sx, tx, so, sl, sp, across, cross_send, cross_recv, se, te, *reds,
):
    def parts(u):
        return gf_ref.at[u] if u < 7 else parts_ref.at[u - 7]

    def own_block(u, k):
        return own_ref[u, k]

    red = Reduction(9, 1, own_block, parts, sums_ref, reds[:4], reds[4:])
    red.last = (across, cross_send, cross_recv, se, te)
    c = red.c

    def load_pair(p):
        cols = pl.ds(pl.multiple_of(p * 128, 128), 128)
        sides = ((q_hbm, q_ref), (k_hbm, k_ref), (v_hbm, v_ref), (datt_hbm, datt_ref), (ctx_hbm, ctx_ref))
        return [
            pltpu.make_async_copy(src.at[:, cols], dst.at[:, cols], sp.at[n, p])
            for n, (src, dst) in enumerate(sides)
        ]

    for load in load_pair(0):
        load.start()
    red.barrier()
    for u in range(7):
        red.start(u)
    fetch = pltpu.make_async_copy(gf_ref.at[:, pl.ds(c * 16, 16)], own_ref.at[pl.ds(0, 7)], so)
    fetch.start()
    late_loads = [
        pltpu.make_async_copy(src, dst, sl.at[n])
        for n, (src, dst) in enumerate(
            [(nt_hbm, nt_ref), (w_hbm, w_ref), (tok_hbm, tok_ref), (dres_hbm, dres_ref)]
        )
    ]
    for load in load_pair(1):
        load.start()
    late_loads[0].start()
    for p in range(2, PAIRS):
        for load in load_pair(p):
            load.start()
    for load in late_loads[1:]:
        load.start()

    here, there = 0, HALF

    hops = [red.over_c, *red.over_z, red.over_y, red.over_x]

    def vhop(g, n):
        src = vs_ref.at[g, (0, 1, 1, 1, 2, 3)[n]]
        return red.copy(src, vr_ref.at[g, n], sv.at[g, n], tv.at[g, n], hops[n])

    def vstep(g, stage):
        came = ((), (0,), (1, 2, 3), (4,), (5,))[stage]
        if stage:
            total = vs_ref[g, stage - 1]
            for n in came:
                vhop(g, n).wait_recv()
                total = total + vr_ref[g, n]
            if stage == 4:
                vsum_ref[8 * g : 8 * g + 8] = total
            else:
                vs_ref[g, stage] = total
        for n in ((0,), (1, 2, 3), (4,), (5,), ())[stage]:
            vhop(g, n).start()

    lane = lax.broadcasted_iota(jnp.int32, (1, 128), 1)
    bias_ref[...] = jnp.broadcast_to(bias_in[...], (128, T)).T
    eye = lax.broadcasted_iota(jnp.int32, (256, 256), 0) == lax.broadcasted_iota(
        jnp.int32, (256, 256), 1
    )
    head_of = lax.broadcasted_iota(jnp.int32, (8, 128), 1) // HD == lax.broadcasted_iota(
        jnp.int32, (8, 128), 0
    )
    pick = jnp.where(head_of, 1.0, 0.0).astype(F32)
    vs_ref[0, 0] = vf_ref[...]
    vs_ref[1, 0] = jnp.zeros((8, D), F32)
    vstep(0, 0)
    for load in load_pair(0):
        load.wait()

    def progress(j, k):
        if k == 3:

            @pl.when(j == 0)
            def _():
                fetch.wait()

        if k == 7:
            for n in range(3):

                @pl.when(j == n)
                def _():
                    vstep(0, n + 1)

        if k % 2:
            three = 4 * j + (k - 11) // 2

            @pl.when(three >= 0)
            def _():
                red.step3(three)

            two = 4 * j + (k - 7) // 2

            @pl.when(two >= 0)
            def _():
                red.step2(two)

            if k == 3:

                @pl.when(j == 0)
                def _():
                    red.step1(0)

            one = 4 * j + (k - 1) // 2

            @pl.when((one >= 1) & (one < 9))
            def _():
                red.step1(one)

    @pl.loop(0, 3)
    def _(j):
        for half in range(2):
            p = 2 * j + half
            cols = pl.ds(pl.multiple_of(p * 128, 128), 128)

            def lanes(at, p=p):
                return pl.ds(pl.multiple_of(at + p * 128, 128), 128)

            if half == 0:

                @pl.when(j > 0)
                def _():
                    for load in load_pair(2 * j):
                        load.wait()

            else:
                for load in load_pair(p):
                    load.wait()
            qp, do = q_ref[:, cols], datt_ref[:, cols]
            prod = do.astype(F32) * ctx_ref[:, cols].astype(F32)
            delta_ref[...] = lax.dot_general(
                pick, prod, (((1,), (1,)), ((), ())),
                preferred_element_type=F32, precision=lax.Precision.HIGHEST,
            )
            dqt_ref[...] = jnp.zeros_like(dqt_ref)
            zero = jnp.zeros_like(qp)
            q2 = jnp.concatenate([jnp.where(lane < HD, qp, zero), jnp.where(lane < HD, zero, qp)], axis=0)
            do2 = jnp.concatenate([jnp.where(lane < HD, do, zero), jnp.where(lane < HD, zero, do)], axis=0)
            for i in range(4):
                progress(j, half * 4 + i)
                cut = slice(i * 256, (i + 1) * 256)
                kp, vp = k_ref[cut, cols], v_ref[cut, cols]
                bias256 = jnp.concatenate([bias_ref[cut]] * 2, axis=1)
                khs, vhs, es, dss = [], [], [[], []], [[], []]
                for h in range(2):
                    mine = (lane < HD) == (h == 0)
                    khs.append(jnp.where(mine, kp, jnp.zeros_like(kp)))
                    vhs.append(jnp.where(mine, vp, jnp.zeros_like(vp)))
                for m in range(4):
                    qs = slice(m * 256, (m + 1) * 256)
                    for h in range(2):
                        raw = dot_nt(khs[h], qp[qs])
                        s = raw + bias256
                        if i == m:
                            s = jnp.where(eye, raw, s)
                        e = jnp.exp(s - lt_ref[2 * p + h, :, qs])
                        dp = dot_nt(vhs[h], do[qs])
                        dss[h].append((e * (dp - delta_ref[h : h + 1, qs])).astype(BF16))
                        es[h].append(e.astype(BF16))
                ds = [jnp.concatenate(d, axis=1) for d in dss]
                dqt_ref[...] += dot_nn(jnp.concatenate(khs, axis=0).T, jnp.concatenate(ds, axis=0))
                dproj_ref[cut, lanes(D)] = dot_nn(jnp.concatenate(ds, axis=1), q2).astype(BF16)
                dproj_ref[cut, lanes(2 * D)] = dot_nn(jnp.concatenate(es[0] + es[1], axis=1), do2).astype(BF16)
            dproj_ref[:, cols] = dqt_ref[...].T.astype(BF16) * jnp.asarray(0.125, BF16)
            d3 = jnp.concatenate([dproj_ref[:, lanes(n * D)] for n in range(3)], axis=1)
            vs_ref[1, 0, 0:1, cols] = jnp.sum(d3[:, :128].astype(F32), axis=0, keepdims=True)
            vs_ref[1, 0, 1:2, cols] = jnp.sum(d3[:, 256:].astype(F32), axis=0, keepdims=True)
            if half == 0:

                @pl.when(j == 0)
                def _():
                    late_loads[0].wait()

            g = dot_nn(nt_ref[...], d3)
            if half == 0:
                gq_ref[...] = g
            else:
                for r in range(32):
                    rows = slice(r * 24, (r + 1) * 24)
                    at = place(r, x_first(7 + j)) + j // 2 * (r // 8 - 3 * (r % 2))
                    parts_ref[j, at] = blocks_of(gq_ref[rows, :], g[rows, :])
        own_ref[7 + j] = parts_ref[j, pl.ds(c * 16, 16)]
        for n in range(3):

            @pl.when(j == n)
            def _():
                red.start(7 + n)

    def tile(rows):
        d_normed = dot_nt(dproj_ref[rows, :], w_ref[...])
        n, rstd = norm_parts(tok_ref[rows, :].astype(F32))
        vs_ref[1, 0, 2:3, :] += jnp.sum(d_normed * n, axis=0, keepdims=True)
        vs_ref[1, 0, 3:4, :] += jnp.sum(d_normed, axis=0, keepdims=True)
        return dres_ref[rows, :] + norm_back(d_normed, n, rstd, row(gain_ref))

    def dcopy(t):
        rows = pl.ds(t * 256, 256)
        return red.copy(dsend_ref.at[rows], dsend_got.at[rows], sx.at[t], tx.at[t], red.over_x)

    def away(t):
        dsend_ref[t * 256 : (t + 1) * 256] = tile(pl.ds(there + t * 256, 256)).astype(BF16)

    def home(t):
        dtok_ref[t * 256 : (t + 1) * 256] = tile(pl.ds(here + t * 256, 256))

    for load in late_loads[1:]:
        load.wait()
    red.step3(7)
    away(0)
    dcopy(0).start()
    red.step3(8)
    away(1)
    dcopy(1).start()
    red.step1(9)
    home(0)
    home(1)
    keep = pltpu.make_async_copy(dtok_ref, dtok_hbm, so)
    keep.start()
    vstep(1, 0)
    for u in range(7):
        red.finish(u)
    vstep(1, 1)
    red.last_step2()
    vstep(1, 2)
    red.finish(7)
    red.finish(8)
    vstep(0, 4)
    vstep(1, 3)
    early = pltpu.make_async_copy(sums_ref.at[pl.ds(0, 9)], sums_hbm.at[pl.ds(0, 9)], so)
    keep.wait()
    early.start()
    red.last_step3()
    vstep(1, 4)
    for t in range(2):
        dcopy(t).wait()
    got = pltpu.make_async_copy(dsend_got, dgot_hbm, sl.at[0])
    got.start()
    red.last_finish()
    early.wait()
    late = pltpu.make_async_copy(sums_ref.at[9], sums_hbm.at[9], so)
    late.start()
    for g in range(2):
        for n in range(6):
            vhop(g, n).wait_send()
    red.drain()
    got.wait()
    late.wait()


def join_kernel(
    lo_hbm, logot_hbm, dtok_hbm, dgot_hbm, early_ref, late_ref, vec_ref,
    out_hbm, gtok_hbm, gin_ref, gback_ref, gout_ref, gqkv_ref, *rest,
):
    vouts, (lo_ref, logot_ref, dtok_ref, dgot_ref, wide_ref, sem) = rest[:9], rest[9:]
    x = lax.axis_index("seq")
    pairs = ((lo_hbm, lo_ref), (logot_hbm, logot_ref), (dtok_hbm, dtok_ref), (dgot_hbm, dgot_ref))
    loads = [pltpu.make_async_copy(src, dst, sem.at[n]) for n, (src, dst) in enumerate(pairs)]
    stores = [
        pltpu.make_async_copy(lo_ref, out_hbm.at[x], sem.at[4]),
        pltpu.make_async_copy(logot_ref, out_hbm.at[1 - x], sem.at[5]),
        pltpu.make_async_copy(dtok_ref, gtok_hbm.at[x], sem.at[6]),
        pltpu.make_async_copy(wide_ref, gtok_hbm.at[1 - x], sem.at[7]),
    ]
    for n in (2, 3, 0, 1):
        loads[n].start()
    for n in (2, 3, 0, 1):
        loads[n].wait()
        if n == 3:
            wide_ref[...] = dgot_ref[...].astype(F32)
        stores[n].start()
    for u in range(4):
        gback_ref[u // 2 * 48 : u // 2 * 48 + 48, u % 2 * UW : (u % 2 + 1) * UW] = (
            early_ref[u] if u < 2 else late_ref[3 + u]
        )
        gin_ref[:, u * D : u * D + UW] = late_ref[u, :24]
        gin_ref[:, u * D + UW : u * D + 2 * UW] = late_ref[u, 24:]
    gout_ref[:, :UW] = late_ref[4, :24]
    gout_ref[:, UW:] = late_ref[4, 24:]
    for p in range(PAIRS):
        part = late_ref[7 + p // 2, p % 2 * 24 : p % 2 * 24 + 24]
        for n in range(3):
            at = n * D + p * 128
            gqkv_ref[:, at : at + 128] = part[:, n * 128 : n * 128 + 128]
    rank = lax.axis_index("dp") * 2 + x
    mine = pltpu.roll(vec_ref[...], D - rank * 24, 1)
    for n, row in enumerate((10, 11, 8, 9, 3, 1, 2, 0)):
        vouts[n][...] = mine[row : row + 1, :24]
    z = rank // 8
    parts = pltpu.roll(vec_ref[4:8, :], D - (rank % 8) * 96, 1)
    chosen = parts[0:1, :96]
    for n in range(1, 4):
        chosen = jnp.where(z == n, parts[n : n + 1, :96], chosen)
    vouts[8][...] = chosen
    for store in stores:
        store.wait()


def call_bwd(*args):
    return pl.pallas_call(
        bwd_kernel,
        out_shape=(
            shape((HALF, D), F32), shape((HALF, D), BF16), shape((10, 48, UW), F32), shape((16, D), F32),
        ),
        in_specs=[VM] * 4 + [HB] * 10,
        out_specs=(HB, HB, HB, VM),
        scratch_shapes=[
            pltpu.VMEM((T, D), BF16),
            pltpu.VMEM((D, 3 * D), BF16),
            pltpu.VMEM((D, T), BF16),
            *[pltpu.VMEM((T, D), BF16)] * 5,
            pltpu.VMEM((T, D), F32),
            pltpu.VMEM((T, 128), F32),
            pltpu.VMEM((T, 3 * D), BF16),
            pltpu.VMEM((128, T), F32),
            pltpu.VMEM((D, UW), F32),
            pltpu.VMEM((8, T), F32),
            pltpu.VMEM((10, 16, 48, UW), BF16),
            pltpu.VMEM((3, 32, 48, UW), BF16),
            pltpu.VMEM((HALF, D), BF16),
            pltpu.VMEM((2, 4, 8, D), F32),
            pltpu.VMEM((2, 6, 8, D), F32),
            pltpu.VMEM((HALF, D), F32),
            pltpu.VMEM((HALF, D), BF16),
            pltpu.VMEM((10, 48, UW), F32),
            DMA((2, 6)), DMA((2, 6)), DMA((2,)), DMA((2,)), DMA, DMA((4,)), DMA((5, PAIRS)),
            pltpu.VMEM((3, 2, 48, UW), BF16),
            pltpu.VMEM((48, UW), BF16),
            pltpu.VMEM((48, UW), BF16),
            DMA((4,)), DMA((4,)), *reduction_scratch(10),
        ],
        compiler_params=pltpu.CompilerParams(
            vmem_limit_bytes=VMEM_LIMIT, collective_id=0, has_side_effects=True
        ),
    )(*args)


def call_join(*args):
    return pl.pallas_call(
        join_kernel,
        out_shape=(
            shape((2, HALF, D), BF16), shape((2, HALF, D), F32), shape((24, FF), F32), shape((96, D), F32),
            shape((24, D), F32), shape((24, 3 * D), F32), *[shape((1, 24), F32)] * 8, shape((1, 96), F32),
        ),
        in_specs=[HB] * 4 + [VM] * 3,
        out_specs=(HB, HB, *[VM] * 13),
        scratch_shapes=[
            pltpu.VMEM((HALF, D), BF16),
            pltpu.VMEM((HALF, D), BF16),
            pltpu.VMEM((HALF, D), F32),
            pltpu.VMEM((HALF, D), BF16),
            pltpu.VMEM((HALF, D), F32),
            DMA((8,)),
        ],
        compiler_params=pltpu.CompilerParams(vmem_limit_bytes=VMEM_LIMIT),
    )(*args)

def whole_sequences(
    tokens, lengths, key_mask, attn_gain, attn_shift, w_qkv, query_bias, value_bias, w_out,
    out_bias, ffn_gain, ffn_shift, w_in, in_bias, w_back, back_bias, cotangent,
):
    normed_t, q, k, v, ctx, tok, cot, log_total, bias = call_fwd(
        lengths, key_mask, attn_gain, attn_shift, query_bias, value_bias,
        tokens, cotangent, w_qkv,
    )
    out, out_got, d_res, d_att, gf, vf, early = call_ffn(
        tok, ctx, out_bias, ffn_gain, ffn_shift, in_bias, back_bias, cot,
        w_out, w_in, w_back,
    )
    d_tok, d_got, late, vec = call_bwd(
        bias, attn_gain, log_total, vf,
        tok, w_qkv, normed_t, q, k, v, ctx, d_att, d_res, gf,
    )
    (
        layer_out, grad_tokens, g_in, g_back, g_out, g_qkv, ag, ash, qb, vb, ob, fg, fs, bb, ib,
    ) = call_join(out, out_got, d_tok, d_got, early, late, vec)
    return (
        layer_out, grad_tokens, ag.reshape(24), ash.reshape(24), g_qkv, qb.reshape(24), vb.reshape(24),
        g_out, ob.reshape(24), fg.reshape(24), fs.reshape(24), g_in, ib.reshape(96), g_back,
        bb.reshape(24),
    )

def shifted(array, axis, by):
    devices = lax.axis_size(axis)
    return lax.ppermute(array, axis, [(i, (i + by) % devices) for i in range(devices)])


def layer_norm(values, gain, shift):
    center = values - jnp.mean(values, axis=-1, keepdims=True)
    spread = jnp.mean(center * center, axis=-1, keepdims=True)
    return center * lax.rsqrt(spread + NORM_EPS) * gain + shift


def partial_gelu(values):
    return jax.nn.gelu(values, approximate=True)


def outer_product(left, right):
    return lax.dot_general(
        left, right, (((0,), (0,)), ((), ())), preferred_element_type=jnp.float32
    )


def times_transposed(left, right):
    return lax.dot_general(
        left, right, (((1,), (1,)), ((), ())), preferred_element_type=jnp.float32
    )


def allowed_keys(lengths, flags_all, query_pos, first_key, key_count):
    key_pos = first_key + jnp.arange(key_count, dtype=jnp.int32)
    key_flags = lax.dynamic_slice_in_dim(flags_all, first_key, key_count, 1)
    key_valid = (key_pos[None, :] < lengths[:, None]) & (key_flags == 1)
    itself = key_pos[None, :] == query_pos[:, None]
    return key_valid[:, None, None, :] | itself[None, :, None, :]


def send_home(partial_grads):
    return shifted(partial_grads.astype(jnp.bfloat16), "seq", 1).astype(partial_grads.dtype)


def shards(
    tokens,
    lengths,
    key_mask,
    attn_gain,
    attn_shift,
    w_qkv,
    query_bias,
    value_bias,
    w_out,
    out_bias,
    ffn_gain,
    ffn_shift,
    w_in,
    in_bias,
    w_back,
    back_bias,
    cotangent,
):
    seq_count, span_dev, model_width = tokens.shape
    row_count = seq_count * span_dev
    members = lax.axis_size("seq")
    own_index = lax.axis_index("seq")
    query_pos = own_index * span_dev + jnp.arange(span_dev, dtype=jnp.int32)
    flags_all = lax.all_gather(key_mask, "seq", axis=1, tiled=True)
    inputs = tokens.astype(jnp.float32).reshape(row_count, model_width)
    normed_one, norm_pull_one = jax.vjp(layer_norm, inputs, attn_gain, attn_shift)
    normed_attn = normed_one.astype(jnp.bfloat16)
    projected = jnp.dot(normed_attn, w_qkv, preferred_element_type=jnp.float32)
    queries = ((projected[:, :model_width] + query_bias) * 0.125).astype(jnp.bfloat16)
    queries = queries.reshape(seq_count, span_dev, H, HD)
    keyval = jnp.concatenate(
        [projected[:, model_width : 2 * model_width], projected[:, 2 * model_width :] + value_bias],
        axis=1,
    ).astype(jnp.bfloat16)
    keyval = keyval.reshape(seq_count, span_dev, 2 * model_width)

    def split_block(block_kv):
        key_count = block_kv.shape[1]
        key_heads = block_kv[:, :, :model_width].reshape(seq_count, key_count, H, HD)
        value_heads = block_kv[:, :, model_width:].reshape(seq_count, key_count, H, HD)
        return (key_count, key_heads, value_heads)

    running_max = jnp.full((seq_count, span_dev, H), NEG_FILL, jnp.float32)
    key_count, key_heads, value_heads = split_block(
        lax.all_gather(keyval, "seq", axis=1, tiled=True)
    )
    scores = jnp.einsum("sqhd,skhd->sqhk", queries, key_heads, preferred_element_type=jnp.float32)
    allowed = allowed_keys(lengths, flags_all, query_pos, jnp.int32(0), key_count)
    new_max = jnp.maximum(running_max, jnp.max(jnp.where(allowed, scores, NEG_FILL), axis=-1))
    expo = jnp.exp(jnp.where(allowed, scores - new_max[..., None], NEG_FILL))
    running_sum = jnp.sum(expo, axis=-1)
    running_acc = jnp.einsum(
        "sqhk,skhd->sqhd",
        expo.astype(jnp.bfloat16),
        value_heads,
        preferred_element_type=jnp.float32,
    )
    attended = running_acc / running_sum[..., None]
    log_total = new_max + jnp.log(running_sum)
    context = attended.reshape(row_count, model_width).astype(jnp.bfloat16)
    residual = inputs + jnp.dot(context, w_out, preferred_element_type=jnp.float32) + out_bias
    normed_two, norm_pull_two = jax.vjp(layer_norm, residual, ffn_gain, ffn_shift)
    normed_ffn = normed_two.astype(jnp.bfloat16)
    pre_act = jnp.dot(normed_ffn, w_in, preferred_element_type=jnp.float32) + in_bias
    gelu_value, gelu_pull = jax.vjp(partial_gelu, pre_act)
    activated = gelu_value.astype(jnp.bfloat16)
    layer_out = (
        residual + jnp.dot(activated, w_back, preferred_element_type=jnp.float32) + back_bias
    )
    grad_rows = cotangent.reshape(row_count, model_width)
    grad_float = grad_rows.astype(jnp.float32)
    grad_back_bias = jnp.sum(grad_float, axis=0)
    grad_w_back = outer_product(activated, grad_rows)
    d_act = times_transposed(grad_rows, w_back)
    d_pre = gelu_pull(d_act)[0].astype(jnp.bfloat16)
    grad_in_bias = jnp.sum(d_pre.astype(jnp.float32), axis=0)
    grad_w_in = outer_product(normed_ffn, d_pre)
    d_normed = times_transposed(d_pre, w_in)
    d_res_part, grad_ffn_gain, grad_ffn_shift = norm_pull_two(d_normed)
    d_residual = grad_float + d_res_part
    d_branch = d_residual.astype(jnp.bfloat16)
    grad_out_bias = jnp.sum(d_branch.astype(jnp.float32), axis=0)
    grad_w_out = outer_product(context, d_branch)
    d_attended = (
        times_transposed(d_branch, w_out).astype(jnp.bfloat16).reshape(seq_count, span_dev, H, HD)
    )
    delta = jnp.sum(d_attended.astype(jnp.float32) * attended, axis=-1)

    def attend_back(block_kv, first_key):
        key_count, key_heads, value_heads = split_block(block_kv)
        scores = jnp.einsum(
            "sqhd,skhd->sqhk", queries, key_heads, preferred_element_type=jnp.float32
        )
        allowed = allowed_keys(lengths, flags_all, query_pos, first_key, key_count)
        weights_f = jnp.exp(jnp.where(allowed, scores - log_total[..., None], NEG_FILL))
        d_values = jnp.einsum(
            "sqhk,sqhd->skhd",
            weights_f.astype(jnp.bfloat16),
            d_attended,
            preferred_element_type=jnp.float32,
        )
        d_probs = jnp.einsum(
            "sqhd,skhd->sqhk", d_attended, value_heads, preferred_element_type=jnp.float32
        )
        d_scores = (weights_f * (d_probs - delta[..., None])).astype(jnp.bfloat16)
        d_query = jnp.einsum(
            "sqhk,skhd->sqhd", d_scores, key_heads, preferred_element_type=jnp.float32
        )
        d_keys = jnp.einsum(
            "sqhk,sqhd->skhd", d_scores, queries, preferred_element_type=jnp.float32
        )
        d_block = jnp.concatenate(
            [
                d_keys.reshape(seq_count, key_count, model_width),
                d_values.reshape(seq_count, key_count, model_width),
            ],
            axis=2,
        )
        return (d_query, d_block)

    zero_query = jnp.zeros((seq_count, span_dev, H, HD), jnp.float32)

    def turn(turn_index, state_now):
        current, d_current, d_query = state_now
        anchor = (own_index - turn_index) % members
        add_query, add_block = attend_back(current, anchor * span_dev)
        current = shifted(current, "seq", 1)
        return (current, send_home(d_current + add_block), d_query + add_query)

    start_back = (
        keyval,
        jnp.zeros((seq_count, span_dev, 2 * model_width), jnp.float32),
        zero_query,
    )
    current, d_current, d_query = lax.fori_loop(0, members - 1, turn, start_back)
    anchor = (own_index - (members - 1)) % members
    add_query, add_block = attend_back(current, anchor * span_dev)
    d_query = d_query + add_query
    d_keyval = send_home(d_current + add_block)
    d_query_low = d_query.reshape(row_count, model_width).astype(jnp.bfloat16)
    d_keyval_low = d_keyval.reshape(row_count, 2 * model_width).astype(jnp.bfloat16)
    query_scaled = d_query_low.astype(jnp.float32) * 0.125
    grad_query_bias = jnp.sum(query_scaled, axis=0)
    grad_value_bias = jnp.sum(d_keyval_low[:, model_width:].astype(jnp.float32), axis=0)
    d_projected = jnp.concatenate([query_scaled.astype(jnp.bfloat16), d_keyval_low], axis=1)
    grad_w_qkv = outer_product(normed_attn, d_projected)
    d_normed_attn = times_transposed(d_projected, w_qkv)
    d_in_part, grad_attn_gain, grad_attn_shift = norm_pull_one(d_normed_attn)
    grad_tokens = (d_residual + d_in_part).reshape(seq_count, span_dev, model_width)
    out_block = layer_out.astype(jnp.bfloat16).reshape(seq_count, span_dev, model_width)
    all_sums = (
        lax.psum_scatter(grad_attn_gain, ("dp", "seq"), scatter_dimension=0, tiled=True),
        lax.psum_scatter(grad_attn_shift, ("dp", "seq"), scatter_dimension=0, tiled=True),
        lax.psum_scatter(grad_w_qkv, ("dp", "seq"), scatter_dimension=0, tiled=True),
        lax.psum_scatter(grad_query_bias, ("dp", "seq"), scatter_dimension=0, tiled=True),
        lax.psum_scatter(grad_value_bias, ("dp", "seq"), scatter_dimension=0, tiled=True),
        lax.psum_scatter(grad_w_out, ("dp", "seq"), scatter_dimension=0, tiled=True),
        lax.psum_scatter(grad_out_bias, ("dp", "seq"), scatter_dimension=0, tiled=True),
        lax.psum_scatter(grad_ffn_gain, ("dp", "seq"), scatter_dimension=0, tiled=True),
        lax.psum_scatter(grad_ffn_shift, ("dp", "seq"), scatter_dimension=0, tiled=True),
        lax.psum_scatter(grad_w_in, ("dp", "seq"), scatter_dimension=0, tiled=True),
        lax.psum_scatter(grad_in_bias, ("dp", "seq"), scatter_dimension=0, tiled=True),
        lax.psum_scatter(grad_w_back, ("dp", "seq"), scatter_dimension=0, tiled=True),
        lax.psum_scatter(grad_back_bias, ("dp", "seq"), scatter_dimension=0, tiled=True),
    )
    return (
        out_block,
        grad_tokens,
        all_sums[0],
        all_sums[1],
        all_sums[2],
        all_sums[3],
        all_sums[4],
        all_sums[5],
        all_sums[6],
        all_sums[7],
        all_sums[8],
        all_sums[9],
        all_sums[10],
        all_sums[11],
        all_sums[12],
    )


def solution(mesh):
    sizes = dict(mesh.shape)
    whole = sizes == {"dp": 16, "seq": 2}
    return jax.shard_map(
        whole_sequences if whole else shards,
        mesh=mesh,
        in_specs=(
            P("dp", "seq", None),
            P("dp"),
            P("dp", "seq"),
            P(),
            P(),
            P(),
            P(),
            P(),
            P(),
            P(),
            P(),
            P(),
            P(),
            P(),
            P(),
            P(),
            P("dp", "seq", None),
        ),
        out_specs=(
            P("dp", "seq", None),
            P("dp", "seq", None),
            P(("dp", "seq")),
            P(("dp", "seq")),
            P(("dp", "seq"), None),
            P(("dp", "seq")),
            P(("dp", "seq")),
            P(("dp", "seq"), None),
            P(("dp", "seq")),
            P(("dp", "seq")),
            P(("dp", "seq")),
            P(("dp", "seq"), None),
            P(("dp", "seq")),
            P(("dp", "seq"), None),
            P(("dp", "seq")),
        ),
        check_vma=False,
    )
```

```python
import functools

import jax
import jax.numpy as jnp
from jax import lax
from jax.experimental import pallas as pl
from jax.experimental.pallas import tpu as pltpu
from jax.sharding import PartitionSpec as P

H = 12
HD = 64


NEG_FILL = -1e30
NORM_EPS = 1e-05

F32 = jnp.float32
BF16 = jnp.bfloat16
D = 768
FF = 3072
T = 1024
HALF = 512
PAIRS = 6
UW = 384
MESH = pl.DeviceIdType.MESH
VMEM_LIMIT = 62 * 1024 * 1024


def dot_nn(a, b):
    return lax.dot_general(a, b, (((1,), (0,)), ((), ())), preferred_element_type=F32)


def dot_nt(a, b):
    return lax.dot_general(a, b, (((1,), (1,)), ((), ())), preferred_element_type=F32)


def dot_tn(a, b):
    return lax.dot_general(a, b, (((0,), (0,)), ((), ())), preferred_element_type=F32)


def shape(dims, dtype):
    return jax.ShapeDtypeStruct(dims, dtype)


VM = pl.BlockSpec(memory_space=pltpu.VMEM)
SM = pl.BlockSpec(memory_space=pltpu.SMEM)
HB = pl.BlockSpec(memory_space=pl.ANY)
DMA = pltpu.SemaphoreType.DMA


def row(ref):
    return ref[...].reshape(1, -1)


def norm_parts(x):
    center = x - jnp.mean(x, axis=-1, keepdims=True)
    spread = jnp.mean(center * center, axis=-1, keepdims=True)
    rstd = lax.rsqrt(spread + NORM_EPS)
    return center * rstd, rstd


def norm_back(d_norm, n, rstd, gain):
    u = d_norm * gain
    mean_u = jnp.mean(u, axis=-1, keepdims=True)
    mean_un = jnp.mean(u * n, axis=-1, keepdims=True)
    return (u - mean_u - n * mean_un) * rstd


def blocks_of(top, bottom):
    return jnp.concatenate([top, bottom], axis=0).astype(BF16)


def place(index, first_x):
    z, y, c, x = index // 8, (index // 4) % 2, (index // 2) % 2, index % 2
    return c * 16 + z + 4 * (2 * y + x) + first_x * 4 * (x - y)


def reduction_scratch(units):
    sems = [DMA((units,)), DMA((units,)), DMA((units,)), DMA((units, 3))]
    return [pltpu.VMEM((units, n, 48, UW), BF16) for n in (16, 8, 4, 3)] + sems + sems


class Reduction:
    def __init__(self, units, extra, own, parts, sums, held, sems):
        self.units, self.extra = units, extra
        self.own, self.parts, self.sums, self.held = own, parts, sums, held
        self.sends, self.recvs = sems[:4], sems[4:8]
        dp, x = lax.axis_index("dp"), lax.axis_index("seq")
        z, y, c = dp // 4, (dp // 2) % 2, dp % 2
        self.dp, self.x, self.y, self.z, self.c = dp, x, y, z, c
        self.over_c = (dp + 1 - 2 * c, x)
        self.over_x = (dp, 1 - x)
        self.over_y = (dp + 2 - 4 * y, x)
        self.over_z = [(lax.rem(z + d, 4) * 4 + y * 2 + c, x) for d in (1, 2, 3)]

    def barrier(self):
        sem = pltpu.get_barrier_semaphore()
        for to in (self.over_c, self.over_x, self.over_y, *self.over_z):
            pl.semaphore_signal(sem, inc=1, device_id=to, device_id_type=MESH)
        pl.semaphore_wait(sem, 6)

    def copy(self, src, dst, send, recv, to):
        return pltpu.make_async_remote_copy(
            src_ref=src, dst_ref=dst, send_sem=send, recv_sem=recv, device_id=to, device_id_type=MESH
        )

    def axes(self, u):
        fx, x, y, dp = x_first(u), self.x, self.y, self.dp
        first = (dp + (1 - fx) * (2 - 4 * y), x + fx * (1 - 2 * x))
        second = (dp + fx * (2 - 4 * y), x + (1 - fx) * (1 - 2 * x))
        return first, second, y + fx * (x - y), x + fx * (y - x)

    def hop0(self, u):
        src = self.parts(u).at[pl.ds((1 - self.c) * 16, 16)]
        return self.copy(src, self.held[0].at[u], self.sends[0].at[u], self.recvs[0].at[u], self.over_c)

    def hop1(self, u):
        first, _, a, _ = self.axes(u)
        src = self.held[0].at[u, pl.ds((1 - a) * 8, 8)]
        return self.copy(src, self.held[1].at[u], self.sends[1].at[u], self.recvs[1].at[u], first)

    def hop2(self, u):
        _, second, _, b = self.axes(u)
        src = self.held[1].at[u, pl.ds((1 - b) * 4, 4)]
        return self.copy(src, self.held[2].at[u], self.sends[2].at[u], self.recvs[2].at[u], second)

    def hop3(self, u, d):
        src = self.held[2].at[u, lax.rem(self.z + d + 1, 4)]
        return self.copy(
            src, self.held[3].at[u, d], self.sends[3].at[u, d], self.recvs[3].at[u, d], self.over_z[d]
        )

    def arrived(self, u):
        held = self.held[0].at[u]
        self.copy(held, held, self.sends[0].at[u], self.recvs[0].at[u], self.over_c).wait_recv()

    def start(self, u):
        self.hop0(u).start()

    def step1(self, u):
        self.arrived(u)
        _, _, a, _ = self.axes(u)
        held = self.held[0]

        def add(k):
            held[u, k] = (held[u, k].astype(F32) + self.own(u, k).astype(F32)).astype(BF16)

        @pl.loop(0, 8, unroll=2)
        def _(k):
            add((1 - a) * 8 + k)

        self.hop1(u).start()

        @pl.loop(0, 8, unroll=2)
        def _(k):
            add(a * 8 + k)

    def step2(self, u):
        self.hop1(u).wait_recv()
        _, _, a, b = self.axes(u)
        held, before = self.held[1], self.held[0]

        def add(k):
            held[u, k] = (held[u, k].astype(F32) + before[u, a * 8 + k].astype(F32)).astype(BF16)

        for k in range(4):
            add((1 - b) * 4 + k)
        self.hop2(u).start()
        for k in range(4):
            add(b * 4 + k)

    def step3(self, u):
        self.hop2(u).wait_recv()
        _, _, _, b = self.axes(u)
        held, before = self.held[2], self.held[1]
        for k in range(4):
            held[u, k] = (held[u, k].astype(F32) + before[u, b * 4 + k].astype(F32)).astype(BF16)
        for d in range(3):
            self.hop3(u, d).start()

    def finish(self, u):
        total = self.held[2][u, self.z].astype(F32)
        for d in range(3):
            self.hop3(u, d).wait_recv()
            total = total + self.held[3][u, d].astype(F32)
        self.sums[u] = total

    def last_hop(self, d):
        across, cross_send, cross_recv, sends, recvs = self.last
        u = self.units
        if d == 3:
            return self.copy(cross_send, cross_recv, sends.at[3], recvs.at[3], self.over_x)
        src = self.held[1].at[u, pl.ds(lax.rem(self.z + d + 1, 4) * 2, 2)]
        return self.copy(src, across.at[d], sends.at[d], recvs.at[d], self.over_z[d])

    def last_step2(self):
        u = self.units
        self.hop1(u).wait_recv()
        for k in range(8):
            self.held[1][u, k] = (
                self.held[1][u, k].astype(F32) + self.held[0][u, self.y * 8 + k].astype(F32)
            ).astype(BF16)
        for d in range(3):
            self.last_hop(d).start()

    def last_step3(self):
        across, cross_send = self.last[:2]
        for d in range(3):
            self.last_hop(d).wait_recv()
        totals = []
        for k in range(2):
            total = self.held[1][self.units, self.z * 2 + k].astype(F32)
            for d in range(3):
                total = total + across[d, k].astype(F32)
            totals.append(total)
        cross_send[...] = jnp.where(self.x == 0, totals[1], totals[0]).astype(BF16)
        self.last_hop(3).start()
        self.sums[self.units] = jnp.where(self.x == 0, totals[0], totals[1])

    def last_finish(self):
        self.last_hop(3).wait_recv()
        self.sums[self.units] = self.sums[self.units] + self.last[2][...].astype(F32)

    def drain(self):
        for u in range(self.units):
            self.hop0(u).wait_send()
            self.hop1(u).wait_send()
            self.hop2(u).wait_send()
            for d in range(3):
                self.hop3(u, d).wait_send()
        if self.extra:
            self.hop0(self.units).wait_send()
            self.hop1(self.units).wait_send()
            for d in range(4):
                self.last_hop(d).wait_send()


def fwd_kernel(
    len_ref, mask_ref, gain_ref, shift_ref, qb_ref, vb_ref, tok_hbm, cot_hbm, w_hbm,
    nt_hbm, q_hbm, k_hbm, v_hbm, ctx_hbm, tok_out, cot_out, lt_ref, bias_ref,
    tok_ref, cot_ref, w_ref, nt_ref, q_ref, k_ref, v_ref, ctx_ref, mgot_ref, part_ref, mx_ref, logs_ref,
    sl, so, sx, tx,
):
    dp, x = lax.axis_index("dp"), lax.axis_index("seq")
    here, there = 0, HALF
    load_w = pltpu.make_async_copy(w_hbm, w_ref, sl.at[0])
    load_tok = pltpu.make_async_copy(tok_hbm.at[x], tok_ref.at[pl.ds(here, HALF)], sl.at[1])
    load_cot = pltpu.make_async_copy(cot_hbm.at[x], cot_ref, sl.at[2])
    load_tok.start()
    load_w.start()

    def swap(n):
        if n == 4:
            src, dst = mask_ref, mgot_ref
        else:
            side, buffer = (tok_hbm, tok_ref) if n < 4 else (cot_hbm, cot_out)
            rows = 128 if n < 4 else 256
            at = (n if n < 4 else n - 5) * rows
            src = side.at[1 - x, pl.ds(at, rows)]
            dst = buffer.at[pl.ds(there + at, rows)]
        return pltpu.make_async_remote_copy(
            src_ref=src, dst_ref=dst, send_sem=sx.at[n], recv_sem=tx.at[n],
            device_id=(dp, 1 - x), device_id_type=MESH,
        )

    sem = pltpu.get_barrier_semaphore()
    pl.semaphore_signal(sem, inc=1, device_id=(dp, 1 - x), device_id_type=MESH)
    pl.semaphore_wait(sem, 1)
    swaps = [swap(n) for n in range(7)]
    for n in (4, 0, 1, 2, 3, 5, 6):
        swaps[n].start()
    load_tok.wait()
    load_w.wait()
    load_cot.start()

    def project(first, count):
        rows = pl.ds(pl.multiple_of(first, count), count)
        n, _ = norm_parts(tok_ref[rows, :].astype(F32))
        normed = (n * row(gain_ref) + row(shift_ref)).astype(BF16)
        nt_ref[:, rows] = normed.T
        q_ref[rows, :] = ((dot_nn(normed, w_ref[:, :D]) + row(qb_ref)) * 0.125).astype(BF16)
        k_ref[rows, :] = dot_nn(normed, w_ref[:, D : 2 * D]).astype(BF16)
        v_ref[rows, :] = (dot_nn(normed, w_ref[:, 2 * D :]) + row(vb_ref)).astype(BF16)

    @pl.loop(0, 2)
    def _(t):
        project(t * 256, 256)

    swaps[4].wait_recv()
    pos = lax.broadcasted_iota(jnp.int32, (1, HALF), 1)
    for first, ref in ((here, mask_ref), (there, mgot_ref)):
        flags = jnp.where(x == 0, ref[0:1, :], ref[1:2, :])
        at = jnp.where(x == 0, first, HALF - first)
        valid = (pos + at < len_ref[x]) & (flags == 1)
        half_bias = jnp.where(valid, 0.0, NEG_FILL).astype(F32)
        bias_ref[:, first : first + HALF] = half_bias
    lane = lax.broadcasted_iota(jnp.int32, (1, 128), 1)
    wide = lax.broadcasted_iota(jnp.int32, (256, 128), 1)
    logs_ref[...] = jnp.zeros_like(logs_ref)
    eye = lax.broadcasted_iota(jnp.int32, (256, 256), 0) == lax.broadcasted_iota(
        jnp.int32, (256, 256), 1
    )

    def attend(p, chains, spans, first):
        cols = pl.ds(pl.multiple_of(p * 128, 128), 128)
        keys, values = {}, {}
        for low, high in sorted(set(spans.values())):
            kp, vp = k_ref[low:high, cols], v_ref[low:high, cols]
            keys[low, high] = [jnp.where((lane < HD) == (h == 0), kp, jnp.zeros_like(kp)) for h in range(2)]
            values[low, high] = jnp.concatenate([vp, jnp.ones_like(vp)], axis=1)

        def score(a, h):
            return dot_nt(q_ref[a : a + 256, cols], keys[spans[a]][h])

        def softmax(a, raw, before):
            low, high = spans[a]
            pieces = []
            for b in range(low, high, 256):
                cut = raw[:, b - low : b - low + 256]
                piece = cut + bias_ref[:, b : b + 256]
                pieces.append(jnp.where(eye, cut, piece) if a == b else piece)
            s = jnp.concatenate(pieces, axis=1)
            top = jnp.max(s, axis=1, keepdims=True)
            if before is not None:
                top = jnp.maximum(top, before)
            return top, jnp.exp(s - top).astype(BF16)

        outs = []
        raw = score(*chains[0])
        for n, (a, h) in enumerate(chains):
            ahead = score(*chains[n + 1]) if n + 1 < len(chains) else None
            merge = not first and a < HALF
            before = mx_ref[2 * p + h, a : a + 256, 0:1] if merge else None
            top, e = softmax(a, raw, before)
            o = dot_nn(e, values[spans[a]])
            raw = ahead
            if first:
                part_ref[2 * p + h, a : a + 256] = o
                mx_ref[2 * p + h, a : a + 256] = jnp.broadcast_to(top, (256, 128))
                continue
            if merge:
                o = o + part_ref[2 * p + h, a : a + 256] * jnp.exp(before - top)
            total = o[:, 128:]
            logs_ref[a : a + 256] = jnp.where(wide == 2 * p + h, top + jnp.log(total), logs_ref[a : a + 256])
            outs.append(o[:, :128] / total)
            if h == 1:
                ctx_ref[a : a + 256, cols] = jnp.where(lane < HD, outs[-2], outs[-1]).astype(BF16)

    own = [(a, h) for a in (0, 256) for h in range(2)]
    other = [(a, h) for a in (512, 768) for h in range(2)]

    @pl.loop(0, PAIRS)
    def _(p):
        attend(p, own, {0: (0, HALF), 256: (0, HALF)}, True)

    for n in range(4):
        swaps[n].wait_recv()
        project(there + n * 128, 128)

    load_cot.wait()
    last = pltpu.make_async_copy(cot_ref, cot_out.at[pl.ds(here, HALF)], so.at[11])
    last.start()
    outs = [
        pltpu.make_async_copy(src, dst, so.at[n])
        for n, (src, dst) in enumerate(
            [(nt_ref, nt_hbm), (q_ref, q_hbm), (k_ref, k_hbm), (v_ref, v_hbm), (tok_ref, tok_out)]
        )
    ]
    for one in outs:
        one.start()

    def ctx_out(p):
        cols = pl.ds(pl.multiple_of(p * 128, 128), 128)
        return pltpu.make_async_copy(ctx_ref.at[:, cols], ctx_hbm.at[:, cols], so.at[5 + p])

    @pl.loop(0, PAIRS)
    def _(p):
        attend(p, own + other, {0: (HALF, T), 256: (HALF, T), 512: (0, T), 768: (0, T)}, False)
        ctx_out(p).start()

    logs = logs_ref[...].T
    for h in range(H):
        lt_ref[h] = logs[h : h + 1]
    for n in (5, 6):
        swaps[n].wait_recv()
    for one in swaps:
        one.wait_send()
    for one in outs:
        one.wait()
    for p in range(PAIRS):
        ctx_out(p).wait()
    last.wait()


def call_fwd(*args):
    low = shape((T, D), BF16)
    return pl.pallas_call(
        fwd_kernel,
        out_shape=(
            shape((D, T), BF16), low, low, low, low, low, low, shape((H, 1, T), F32), shape((1, T), F32),
        ),
        in_specs=[SM] + [VM] * 5 + [HB] * 3,
        out_specs=(HB,) * 7 + (VM, VM),
        scratch_shapes=[
            pltpu.VMEM((T, D), BF16),
            pltpu.VMEM((HALF, D), BF16),
            pltpu.VMEM((D, 3 * D), BF16),
            pltpu.VMEM((D, T), BF16),
            *[pltpu.VMEM((T, D), BF16)] * 4,
            pltpu.VMEM((2, HALF), jnp.int32),
            pltpu.VMEM((H, HALF, 256), F32),
            pltpu.VMEM((H, HALF, 128), F32),
            pltpu.VMEM((T, 128), F32),
            DMA((3,)), DMA((12,)), DMA((7,)), DMA((7,)),
        ],
        compiler_params=pltpu.CompilerParams(
            vmem_limit_bytes=VMEM_LIMIT, collective_id=2, has_side_effects=True
        ),
    )(*args)


def x_first(unit):
    return (unit + 1) % 2


def ffn_kernel(
    tok_ref, ctx_ref, ob_ref, g_ref, s_ref, ib_ref, bb_ref, cot_hbm, wo_hbm, wi_hbm, wb_hbm,
    lo_ref, logot_ref, dres_hbm, datt_hbm, grads_hbm, vec_ref, sums_ref,
    wo_ref, wi_ref, wb_ref, nf_ref, act_ref, dpre_ref, dbr_ref, res_ref, dn_ref, away_ref, cot_ref,
    parts_ref, grads_ref, sw, so, sx, tx, *reds,
):
    def parts(u):
        return parts_ref.at[u]

    def own_block(u, k):
        return parts_ref[u, red.c * 16 + k]

    red = Reduction(2, 0, own_block, parts, sums_ref, reds[:4], reds[4:])
    loads = [pltpu.make_async_copy(wo_hbm, wo_ref, sw.at[0])]
    for c in range(4):
        cut = pl.ds(c * 768, 768)
        loads.append(pltpu.make_async_copy(wi_hbm.at[:, cut], wi_ref.at[:, cut], sw.at[1 + 2 * c]))
        loads.append(pltpu.make_async_copy(wb_hbm.at[cut], wb_ref.at[cut], sw.at[2 + 2 * c]))
    loads.append(pltpu.make_async_copy(cot_hbm, cot_ref, sw.at[9]))
    for load in loads:
        load.start()
    red.barrier()
    vec_ref[...] = jnp.zeros_like(vec_ref)
    loads[0].wait()
    lo_copy = red.copy(away_ref, logot_ref, sx, tx, red.over_x)

    def grads_out(u):
        return pltpu.make_async_copy(grads_ref.at[u], grads_hbm.at[u], so.at[8 + u])

    def rows_of(t):
        return pl.ds(pl.multiple_of(HALF - t * HALF, HALF), HALF)

    def forward(t, loads_of):
        rows = rows_of(t)
        res = tok_ref[rows, :].astype(F32) + dot_nn(ctx_ref[rows, :], wo_ref[...]) + row(ob_ref)
        res_ref[rows, :] = res
        n, _ = norm_parts(res)
        normed = (n * row(g_ref) + row(s_ref)).astype(BF16)
        nf_ref[rows, :] = normed
        total = res + row(bb_ref)
        def pre(c):
            for load in loads_of(c):
                load.wait()
            cut = slice(c * 768, (c + 1) * 768)
            return dot_nn(normed, wi_ref[:, cut]) + row(ib_ref)[:, cut]

        v = pre(0)
        for c in range(4):
            cut = slice(c * 768, (c + 1) * 768)
            ahead = pre(c + 1) if c < 3 else None
            sq = v * v
            th = jnp.tanh(v * (0.7978845608 + (0.7978845608 * 0.044715) * sq))
            half = 0.5 + 0.5 * th
            act = (v * half).astype(BF16)
            slope = half + v * (half * (1.0 - th)) * (
                0.7978845608 + (3 * 0.7978845608 * 0.044715) * sq
            )
            act_ref[rows, cut] = act
            dpre_ref[rows, cut] = slope.astype(BF16)
            total = total + dot_nn(act, wb_ref[cut, :])
            v = ahead
        return total.astype(BF16)

    away_ref[...] = forward(0, lambda c: loads[1 + 2 * c : 3 + 2 * c])
    lo_copy.start()
    lo_ref[...] = forward(1, lambda c: ())

    loads[9].wait()

    @pl.loop(0, 4)
    def _(z):
        g = dot_tn(act_ref[:, pl.ds(pl.multiple_of(z * 768, 768), 768)], cot_ref[...])
        for r in range(8):
            for u in range(4):
                i, j = u // 2, u % 2
                block = g[r * 96 + i * 48 : r * 96 + i * 48 + 48, j * UW : (j + 1) * UW].astype(BF16)
                if u < 2:
                    parts_ref[u, place(r, x_first(u)) + z] = block
                else:
                    grads_ref[3 + u, place(r, x_first(3 + u)) + z] = block

    for u in range(2):
        red.start(u)
    for u in (5, 6):
        grads_out(u).start()

    def tile_out(t, part):
        rows = rows_of(t)
        if part == 0:
            return pltpu.make_async_copy(res_ref.at[rows], dres_hbm.at[rows], so.at[2 * t])
        return pltpu.make_async_copy(cot_ref.at[rows], datt_hbm.at[rows], so.at[2 * t + 1])

    plan = {2: ((1, 0), (1, 1)), 6: ((2, 0), (2, 1))}

    @pl.loop(0, 2)
    def _(t):
        rows = rows_of(t)
        dy = cot_ref[rows, :]
        dn_ref[...] = jnp.zeros_like(dn_ref)
        for c in range(4):
            for at, moves in plan.items():
                if at % 4 == c:

                    @pl.when(t == at // 4)
                    def _():
                        for stage, u in moves:
                            (red.step1, red.step2, red.step3)[stage - 1](u)

            cut = slice(c * 768, (c + 1) * 768)
            d_act = dot_nt(dy, wb_ref[cut, :])
            d_pre = (d_act * dpre_ref[rows, cut].astype(F32)).astype(BF16)
            dpre_ref[rows, cut] = d_pre
            dn_ref[...] += dot_nt(d_pre, wi_ref[:, cut])
            vec_ref[4 + c : 5 + c, :] += jnp.sum(d_pre.astype(F32), axis=0, keepdims=True)

        n, rstd = norm_parts(res_ref[rows, :])
        d_normed = dn_ref[...]
        dyf = dy.astype(F32)
        d_res = dyf + norm_back(d_normed, n, rstd, row(g_ref))
        res_ref[rows, :] = d_res
        tile_out(t, 0).start()
        d_branch = d_res.astype(BF16)
        dbr_ref[rows, :] = d_branch
        cot_ref[rows, :] = dot_nt(d_branch, wo_ref[...]).astype(BF16)
        tile_out(t, 1).start()
        vec_ref[0:1, :] += jnp.sum(dyf, axis=0, keepdims=True)
        vec_ref[1:2, :] += jnp.sum(d_normed * n, axis=0, keepdims=True)
        vec_ref[2:3, :] += jnp.sum(d_normed, axis=0, keepdims=True)
        vec_ref[3:4, :] += jnp.sum(d_branch.astype(F32), axis=0, keepdims=True)

    def unit(u, g):
        for r in range(32):
            rows = slice(r * 24, (r + 1) * 24)
            grads_ref[u, place(r, x_first(u))] = blocks_of(g[rows, :UW], g[rows, UW:])
        grads_out(u).start()

    @pl.loop(0, 4)
    def _(u):
        unit(u, dot_tn(nf_ref[...], dpre_ref[:, pl.ds(pl.multiple_of(u * 768, 768), 768)]))

        @pl.when(u == 0)
        def _():
            red.step3(0)
            red.step3(1)

    unit(4, dot_tn(ctx_ref[...], dbr_ref[...]))
    for u in range(2):
        red.finish(u)
    lo_copy.wait()
    red.drain()
    for t in range(2):
        tile_out(t, 0).wait()
        tile_out(t, 1).wait()
    for u in range(7):
        grads_out(u).wait()


def call_ffn(*args):
    return pl.pallas_call(
        ffn_kernel,
        out_shape=(
            shape((HALF, D), BF16), shape((HALF, D), BF16), shape((T, D), F32), shape((T, D), BF16),
            shape((7, 32, 48, UW), BF16), shape((8, D), F32), shape((2, 48, UW), F32),
        ),
        in_specs=[VM] * 7 + [HB] * 4,
        out_specs=(VM, VM, HB, HB, HB, VM, VM),
        scratch_shapes=[
            pltpu.VMEM((D, D), BF16),
            pltpu.VMEM((D, FF), BF16),
            pltpu.VMEM((FF, D), BF16),
            pltpu.VMEM((T, D), BF16),
            pltpu.VMEM((T, FF), BF16),
            pltpu.VMEM((T, FF), BF16),
            pltpu.VMEM((T, D), BF16),
            pltpu.VMEM((T, D), F32),
            pltpu.VMEM((HALF, D), F32),
            pltpu.VMEM((HALF, D), BF16),
            pltpu.VMEM((T, D), BF16),
            pltpu.VMEM((2, 32, 48, UW), BF16),
            pltpu.VMEM((7, 32, 48, UW), BF16),
            DMA((10,)), DMA((15,)), DMA, DMA, *reduction_scratch(2),
        ],
        compiler_params=pltpu.CompilerParams(
            vmem_limit_bytes=VMEM_LIMIT, collective_id=1, has_side_effects=True
        ),
    )(*args)


def bwd_kernel(
    bias_in, gain_ref, lt_ref, vf_ref,
    tok_hbm, w_hbm, nt_hbm, q_hbm, k_hbm, v_hbm, ctx_hbm, datt_hbm, dres_hbm, gf_ref,
    dtok_hbm, dgot_hbm, sums_hbm, vsum_ref,
    tok_ref, w_ref, nt_ref, q_ref, k_ref, v_ref, ctx_ref, datt_ref, dres_ref, bias_ref,
    dproj_ref, dqt_ref, gq_ref, delta_ref, own_ref, parts_ref, dsend_ref, vs_ref, vr_ref, dtok_ref, dsend_got, sums_ref,
    sv, tv, sx, tx, so, sl, sp, across, cross_send, cross_recv, se, te, *reds,
):
    def parts(u):
        return gf_ref.at[u] if u < 7 else parts_ref.at[u - 7]

    def own_block(u, k):
        return own_ref[u, k]

    red = Reduction(9, 1, own_block, parts, sums_ref, reds[:4], reds[4:])
    red.last = (across, cross_send, cross_recv, se, te)
    c = red.c

    def load_pair(p):
        cols = pl.ds(pl.multiple_of(p * 128, 128), 128)
        sides = ((q_hbm, q_ref), (k_hbm, k_ref), (v_hbm, v_ref), (datt_hbm, datt_ref), (ctx_hbm, ctx_ref))
        return [
            pltpu.make_async_copy(src.at[:, cols], dst.at[:, cols], sp.at[n, p])
            for n, (src, dst) in enumerate(sides)
        ]

    for load in load_pair(0):
        load.start()
    red.barrier()
    for u in range(7):
        red.start(u)
    fetch = pltpu.make_async_copy(gf_ref.at[:, pl.ds(c * 16, 16)], own_ref.at[pl.ds(0, 7)], so)
    fetch.start()
    late_loads = [
        pltpu.make_async_copy(src, dst, sl.at[n])
        for n, (src, dst) in enumerate(
            [(nt_hbm, nt_ref), (w_hbm, w_ref), (tok_hbm, tok_ref), (dres_hbm, dres_ref)]
        )
    ]
    for load in load_pair(1):
        load.start()
    late_loads[0].start()
    for p in range(2, PAIRS):
        for load in load_pair(p):
            load.start()
    for load in late_loads[1:]:
        load.start()

    here, there = 0, HALF

    hops = [red.over_c, *red.over_z, red.over_y, red.over_x]

    def vhop(g, n):
        src = vs_ref.at[g, (0, 1, 1, 1, 2, 3)[n]]
        return red.copy(src, vr_ref.at[g, n], sv.at[g, n], tv.at[g, n], hops[n])

    def vstep(g, stage):
        came = ((), (0,), (1, 2, 3), (4,), (5,))[stage]
        if stage:
            total = vs_ref[g, stage - 1]
            for n in came:
                vhop(g, n).wait_recv()
                total = total + vr_ref[g, n]
            if stage == 4:
                vsum_ref[8 * g : 8 * g + 8] = total
            else:
                vs_ref[g, stage] = total
        for n in ((0,), (1, 2, 3), (4,), (5,), ())[stage]:
            vhop(g, n).start()

    lane = lax.broadcasted_iota(jnp.int32, (1, 128), 1)
    bias_ref[...] = jnp.broadcast_to(bias_in[...], (128, T)).T
    eye = lax.broadcasted_iota(jnp.int32, (256, 256), 0) == lax.broadcasted_iota(
        jnp.int32, (256, 256), 1
    )
    head_of = lax.broadcasted_iota(jnp.int32, (8, 128), 1) // HD == lax.broadcasted_iota(
        jnp.int32, (8, 128), 0
    )
    pick = jnp.where(head_of, 1.0, 0.0).astype(F32)
    vs_ref[0, 0] = vf_ref[...]
    vs_ref[1, 0] = jnp.zeros((8, D), F32)
    vstep(0, 0)
    for load in load_pair(0):
        load.wait()

    def progress(j, k):
        if k == 3:

            @pl.when(j == 0)
            def _():
                fetch.wait()

        if k == 7:
            for n in range(3):

                @pl.when(j == n)
                def _():
                    vstep(0, n + 1)

        if k % 2:
            three = 4 * j + (k - 11) // 2

            @pl.when(three >= 0)
            def _():
                red.step3(three)

            two = 4 * j + (k - 7) // 2

            @pl.when(two >= 0)
            def _():
                red.step2(two)

            if k == 3:

                @pl.when(j == 0)
                def _():
                    red.step1(0)

            one = 4 * j + (k - 1) // 2

            @pl.when((one >= 1) & (one < 9))
            def _():
                red.step1(one)

    @pl.loop(0, 3)
    def _(j):
        for half in range(2):
            p = 2 * j + half
            cols = pl.ds(pl.multiple_of(p * 128, 128), 128)

            def lanes(at, p=p):
                return pl.ds(pl.multiple_of(at + p * 128, 128), 128)

            if half == 0:

                @pl.when(j > 0)
                def _():
                    for load in load_pair(2 * j):
                        load.wait()

            else:
                for load in load_pair(p):
                    load.wait()
            qp, do = q_ref[:, cols], datt_ref[:, cols]
            prod = do.astype(F32) * ctx_ref[:, cols].astype(F32)
            delta_ref[...] = lax.dot_general(
                pick, prod, (((1,), (1,)), ((), ())),
                preferred_element_type=F32, precision=lax.Precision.HIGHEST,
            )
            dqt_ref[...] = jnp.zeros_like(dqt_ref)
            zero = jnp.zeros_like(qp)
            q2 = jnp.concatenate([jnp.where(lane < HD, qp, zero), jnp.where(lane < HD, zero, qp)], axis=0)
            do2 = jnp.concatenate([jnp.where(lane < HD, do, zero), jnp.where(lane < HD, zero, do)], axis=0)
            for i in range(4):
                progress(j, half * 4 + i)
                cut = slice(i * 256, (i + 1) * 256)
                kp, vp = k_ref[cut, cols], v_ref[cut, cols]
                bias256 = jnp.concatenate([bias_ref[cut]] * 2, axis=1)
                khs, vhs, es, dss = [], [], [[], []], [[], []]
                for h in range(2):
                    mine = (lane < HD) == (h == 0)
                    khs.append(jnp.where(mine, kp, jnp.zeros_like(kp)))
                    vhs.append(jnp.where(mine, vp, jnp.zeros_like(vp)))
                for m in range(4):
                    qs = slice(m * 256, (m + 1) * 256)
                    for h in range(2):
                        raw = dot_nt(khs[h], qp[qs])
                        s = raw + bias256
                        if i == m:
                            s = jnp.where(eye, raw, s)
                        e = jnp.exp(s - lt_ref[2 * p + h, :, qs])
                        dp = dot_nt(vhs[h], do[qs])
                        dss[h].append((e * (dp - delta_ref[h : h + 1, qs])).astype(BF16))
                        es[h].append(e.astype(BF16))
                ds = [jnp.concatenate(d, axis=1) for d in dss]
                dqt_ref[...] += dot_nn(jnp.concatenate(khs, axis=0).T, jnp.concatenate(ds, axis=0))
                dproj_ref[cut, lanes(D)] = dot_nn(jnp.concatenate(ds, axis=1), q2).astype(BF16)
                dproj_ref[cut, lanes(2 * D)] = dot_nn(jnp.concatenate(es[0] + es[1], axis=1), do2).astype(BF16)
            dproj_ref[:, cols] = dqt_ref[...].T.astype(BF16) * jnp.asarray(0.125, BF16)
            d3 = jnp.concatenate([dproj_ref[:, lanes(n * D)] for n in range(3)], axis=1)
            vs_ref[1, 0, 0:1, cols] = jnp.sum(d3[:, :128].astype(F32), axis=0, keepdims=True)
            vs_ref[1, 0, 1:2, cols] = jnp.sum(d3[:, 256:].astype(F32), axis=0, keepdims=True)
            if half == 0:

                @pl.when(j == 0)
                def _():
                    late_loads[0].wait()

            g = dot_nn(nt_ref[...], d3)
            if half == 0:
                gq_ref[...] = g
            else:
                for r in range(32):
                    rows = slice(r * 24, (r + 1) * 24)
                    at = place(r, x_first(7 + j)) + j // 2 * (r // 8 - 3 * (r % 2))
                    parts_ref[j, at] = blocks_of(gq_ref[rows, :], g[rows, :])
        own_ref[7 + j] = parts_ref[j, pl.ds(c * 16, 16)]
        for n in range(3):

            @pl.when(j == n)
            def _():
                red.start(7 + n)

    def tile(rows):
        d_normed = dot_nt(dproj_ref[rows, :], w_ref[...])
        n, rstd = norm_parts(tok_ref[rows, :].astype(F32))
        vs_ref[1, 0, 2:3, :] += jnp.sum(d_normed * n, axis=0, keepdims=True)
        vs_ref[1, 0, 3:4, :] += jnp.sum(d_normed, axis=0, keepdims=True)
        return dres_ref[rows, :] + norm_back(d_normed, n, rstd, row(gain_ref))

    def dcopy(t):
        rows = pl.ds(t * 256, 256)
        return red.copy(dsend_ref.at[rows], dsend_got.at[rows], sx.at[t], tx.at[t], red.over_x)

    def away(t):
        dsend_ref[t * 256 : (t + 1) * 256] = tile(pl.ds(there + t * 256, 256)).astype(BF16)

    def home(t):
        dtok_ref[t * 256 : (t + 1) * 256] = tile(pl.ds(here + t * 256, 256))

    for load in late_loads[1:]:
        load.wait()
    away(0)
    dcopy(0).start()
    red.step3(7)
    away(1)
    dcopy(1).start()
    red.step1(9)
    red.step3(8)
    home(0)
    home(1)
    keep = pltpu.make_async_copy(dtok_ref, dtok_hbm, so)
    keep.start()
    vstep(1, 0)
    for u in range(7):
        red.finish(u)
    vstep(1, 1)
    red.last_step2()
    vstep(1, 2)
    red.finish(7)
    red.finish(8)
    vstep(0, 4)
    vstep(1, 3)
    early = pltpu.make_async_copy(sums_ref.at[pl.ds(0, 9)], sums_hbm.at[pl.ds(0, 9)], so)
    keep.wait()
    early.start()
    red.last_step3()
    vstep(1, 4)
    for t in range(2):
        dcopy(t).wait()
    got = pltpu.make_async_copy(dsend_got, dgot_hbm, sl.at[0])
    got.start()
    red.last_finish()
    early.wait()
    late = pltpu.make_async_copy(sums_ref.at[9], sums_hbm.at[9], so)
    late.start()
    for g in range(2):
        for n in range(6):
            vhop(g, n).wait_send()
    red.drain()
    got.wait()
    late.wait()


def join_kernel(
    lo_hbm, logot_hbm, dtok_hbm, dgot_hbm, early_ref, late_ref, vec_ref,
    out_hbm, gtok_hbm, gin_ref, gback_ref, gout_ref, gqkv_ref, *rest,
):
    vouts, (lo_ref, logot_ref, dtok_ref, dgot_ref, wide_ref, sem) = rest[:9], rest[9:]
    x = lax.axis_index("seq")
    pairs = ((lo_hbm, lo_ref), (logot_hbm, logot_ref), (dtok_hbm, dtok_ref), (dgot_hbm, dgot_ref))
    loads = [pltpu.make_async_copy(src, dst, sem.at[n]) for n, (src, dst) in enumerate(pairs)]
    stores = [
        pltpu.make_async_copy(lo_ref, out_hbm.at[x], sem.at[4]),
        pltpu.make_async_copy(logot_ref, out_hbm.at[1 - x], sem.at[5]),
        pltpu.make_async_copy(dtok_ref, gtok_hbm.at[x], sem.at[6]),
        pltpu.make_async_copy(wide_ref, gtok_hbm.at[1 - x], sem.at[7]),
    ]
    for n in (2, 3, 0, 1):
        loads[n].start()
    for n in (2, 3, 0, 1):
        loads[n].wait()
        if n == 3:
            wide_ref[...] = dgot_ref[...].astype(F32)
        stores[n].start()
    for u in range(4):
        gback_ref[u // 2 * 48 : u // 2 * 48 + 48, u % 2 * UW : (u % 2 + 1) * UW] = (
            early_ref[u] if u < 2 else late_ref[3 + u]
        )
        gin_ref[:, u * D : u * D + UW] = late_ref[u, :24]
        gin_ref[:, u * D + UW : u * D + 2 * UW] = late_ref[u, 24:]
    gout_ref[:, :UW] = late_ref[4, :24]
    gout_ref[:, UW:] = late_ref[4, 24:]
    for p in range(PAIRS):
        part = late_ref[7 + p // 2, p % 2 * 24 : p % 2 * 24 + 24]
        for n in range(3):
            at = n * D + p * 128
            gqkv_ref[:, at : at + 128] = part[:, n * 128 : n * 128 + 128]
    rank = lax.axis_index("dp") * 2 + x
    mine = pltpu.roll(vec_ref[...], D - rank * 24, 1)
    for n, row in enumerate((10, 11, 8, 9, 3, 1, 2, 0)):
        vouts[n][...] = mine[row : row + 1, :24]
    z = rank // 8
    parts = pltpu.roll(vec_ref[4:8, :], D - (rank % 8) * 96, 1)
    chosen = parts[0:1, :96]
    for n in range(1, 4):
        chosen = jnp.where(z == n, parts[n : n + 1, :96], chosen)
    vouts[8][...] = chosen
    for store in stores:
        store.wait()


def call_bwd(*args):
    return pl.pallas_call(
        bwd_kernel,
        out_shape=(
            shape((HALF, D), F32), shape((HALF, D), BF16), shape((10, 48, UW), F32), shape((16, D), F32),
        ),
        in_specs=[VM] * 4 + [HB] * 10,
        out_specs=(HB, HB, HB, VM),
        scratch_shapes=[
            pltpu.VMEM((T, D), BF16),
            pltpu.VMEM((D, 3 * D), BF16),
            pltpu.VMEM((D, T), BF16),
            *[pltpu.VMEM((T, D), BF16)] * 5,
            pltpu.VMEM((T, D), F32),
            pltpu.VMEM((T, 128), F32),
            pltpu.VMEM((T, 3 * D), BF16),
            pltpu.VMEM((128, T), F32),
            pltpu.VMEM((D, UW), F32),
            pltpu.VMEM((8, T), F32),
            pltpu.VMEM((10, 16, 48, UW), BF16),
            pltpu.VMEM((3, 32, 48, UW), BF16),
            pltpu.VMEM((HALF, D), BF16),
            pltpu.VMEM((2, 4, 8, D), F32),
            pltpu.VMEM((2, 6, 8, D), F32),
            pltpu.VMEM((HALF, D), F32),
            pltpu.VMEM((HALF, D), BF16),
            pltpu.VMEM((10, 48, UW), F32),
            DMA((2, 6)), DMA((2, 6)), DMA((2,)), DMA((2,)), DMA, DMA((4,)), DMA((5, PAIRS)),
            pltpu.VMEM((3, 2, 48, UW), BF16),
            pltpu.VMEM((48, UW), BF16),
            pltpu.VMEM((48, UW), BF16),
            DMA((4,)), DMA((4,)), *reduction_scratch(10),
        ],
        compiler_params=pltpu.CompilerParams(
            vmem_limit_bytes=VMEM_LIMIT, collective_id=0, has_side_effects=True
        ),
    )(*args)


def call_join(*args):
    return pl.pallas_call(
        join_kernel,
        out_shape=(
            shape((2, HALF, D), BF16), shape((2, HALF, D), F32), shape((24, FF), F32), shape((96, D), F32),
            shape((24, D), F32), shape((24, 3 * D), F32), *[shape((1, 24), F32)] * 8, shape((1, 96), F32),
        ),
        in_specs=[HB] * 4 + [VM] * 3,
        out_specs=(HB, HB, *[VM] * 13),
        scratch_shapes=[
            pltpu.VMEM((HALF, D), BF16),
            pltpu.VMEM((HALF, D), BF16),
            pltpu.VMEM((HALF, D), F32),
            pltpu.VMEM((HALF, D), BF16),
            pltpu.VMEM((HALF, D), F32),
            DMA((8,)),
        ],
        compiler_params=pltpu.CompilerParams(vmem_limit_bytes=VMEM_LIMIT),
    )(*args)

def whole_sequences(
    tokens, lengths, key_mask, attn_gain, attn_shift, w_qkv, query_bias, value_bias, w_out,
    out_bias, ffn_gain, ffn_shift, w_in, in_bias, w_back, back_bias, cotangent,
):
    normed_t, q, k, v, ctx, tok, cot, log_total, bias = call_fwd(
        lengths, key_mask, attn_gain, attn_shift, query_bias, value_bias,
        tokens, cotangent, w_qkv,
    )
    out, out_got, d_res, d_att, gf, vf, early = call_ffn(
        tok, ctx, out_bias, ffn_gain, ffn_shift, in_bias, back_bias, cot,
        w_out, w_in, w_back,
    )
    d_tok, d_got, late, vec = call_bwd(
        bias, attn_gain, log_total, vf,
        tok, w_qkv, normed_t, q, k, v, ctx, d_att, d_res, gf,
    )
    (
        layer_out, grad_tokens, g_in, g_back, g_out, g_qkv, ag, ash, qb, vb, ob, fg, fs, bb, ib,
    ) = call_join(out, out_got, d_tok, d_got, early, late, vec)
    return (
        layer_out, grad_tokens, ag.reshape(24), ash.reshape(24), g_qkv, qb.reshape(24), vb.reshape(24),
        g_out, ob.reshape(24), fg.reshape(24), fs.reshape(24), g_in, ib.reshape(96), g_back,
        bb.reshape(24),
    )

def shifted(array, axis, by):
    devices = lax.axis_size(axis)
    return lax.ppermute(array, axis, [(i, (i + by) % devices) for i in range(devices)])


def layer_norm(values, gain, shift):
    center = values - jnp.mean(values, axis=-1, keepdims=True)
    spread = jnp.mean(center * center, axis=-1, keepdims=True)
    return center * lax.rsqrt(spread + NORM_EPS) * gain + shift


def partial_gelu(values):
    return jax.nn.gelu(values, approximate=True)


def outer_product(left, right):
    return lax.dot_general(
        left, right, (((0,), (0,)), ((), ())), preferred_element_type=jnp.float32
    )


def times_transposed(left, right):
    return lax.dot_general(
        left, right, (((1,), (1,)), ((), ())), preferred_element_type=jnp.float32
    )


def allowed_keys(lengths, flags_all, query_pos, first_key, key_count):
    key_pos = first_key + jnp.arange(key_count, dtype=jnp.int32)
    key_flags = lax.dynamic_slice_in_dim(flags_all, first_key, key_count, 1)
    key_valid = (key_pos[None, :] < lengths[:, None]) & (key_flags == 1)
    itself = key_pos[None, :] == query_pos[:, None]
    return key_valid[:, None, None, :] | itself[None, :, None, :]


def send_home(partial_grads):
    return shifted(partial_grads.astype(jnp.bfloat16), "seq", 1).astype(partial_grads.dtype)


def shards(
    tokens,
    lengths,
    key_mask,
    attn_gain,
    attn_shift,
    w_qkv,
    query_bias,
    value_bias,
    w_out,
    out_bias,
    ffn_gain,
    ffn_shift,
    w_in,
    in_bias,
    w_back,
    back_bias,
    cotangent,
):
    seq_count, span_dev, model_width = tokens.shape
    row_count = seq_count * span_dev
    members = lax.axis_size("seq")
    own_index = lax.axis_index("seq")
    query_pos = own_index * span_dev + jnp.arange(span_dev, dtype=jnp.int32)
    flags_all = lax.all_gather(key_mask, "seq", axis=1, tiled=True)
    inputs = tokens.astype(jnp.float32).reshape(row_count, model_width)
    normed_one, norm_pull_one = jax.vjp(layer_norm, inputs, attn_gain, attn_shift)
    normed_attn = normed_one.astype(jnp.bfloat16)
    projected = jnp.dot(normed_attn, w_qkv, preferred_element_type=jnp.float32)
    queries = ((projected[:, :model_width] + query_bias) * 0.125).astype(jnp.bfloat16)
    queries = queries.reshape(seq_count, span_dev, H, HD)
    keyval = jnp.concatenate(
        [projected[:, model_width : 2 * model_width], projected[:, 2 * model_width :] + value_bias],
        axis=1,
    ).astype(jnp.bfloat16)
    keyval = keyval.reshape(seq_count, span_dev, 2 * model_width)

    def split_block(block_kv):
        key_count = block_kv.shape[1]
        key_heads = block_kv[:, :, :model_width].reshape(seq_count, key_count, H, HD)
        value_heads = block_kv[:, :, model_width:].reshape(seq_count, key_count, H, HD)
        return (key_count, key_heads, value_heads)

    running_max = jnp.full((seq_count, span_dev, H), NEG_FILL, jnp.float32)
    key_count, key_heads, value_heads = split_block(
        lax.all_gather(keyval, "seq", axis=1, tiled=True)
    )
    scores = jnp.einsum("sqhd,skhd->sqhk", queries, key_heads, preferred_element_type=jnp.float32)
    allowed = allowed_keys(lengths, flags_all, query_pos, jnp.int32(0), key_count)
    new_max = jnp.maximum(running_max, jnp.max(jnp.where(allowed, scores, NEG_FILL), axis=-1))
    expo = jnp.exp(jnp.where(allowed, scores - new_max[..., None], NEG_FILL))
    running_sum = jnp.sum(expo, axis=-1)
    running_acc = jnp.einsum(
        "sqhk,skhd->sqhd",
        expo.astype(jnp.bfloat16),
        value_heads,
        preferred_element_type=jnp.float32,
    )
    attended = running_acc / running_sum[..., None]
    log_total = new_max + jnp.log(running_sum)
    context = attended.reshape(row_count, model_width).astype(jnp.bfloat16)
    residual = inputs + jnp.dot(context, w_out, preferred_element_type=jnp.float32) + out_bias
    normed_two, norm_pull_two = jax.vjp(layer_norm, residual, ffn_gain, ffn_shift)
    normed_ffn = normed_two.astype(jnp.bfloat16)
    pre_act = jnp.dot(normed_ffn, w_in, preferred_element_type=jnp.float32) + in_bias
    gelu_value, gelu_pull = jax.vjp(partial_gelu, pre_act)
    activated = gelu_value.astype(jnp.bfloat16)
    layer_out = (
        residual + jnp.dot(activated, w_back, preferred_element_type=jnp.float32) + back_bias
    )
    grad_rows = cotangent.reshape(row_count, model_width)
    grad_float = grad_rows.astype(jnp.float32)
    grad_back_bias = jnp.sum(grad_float, axis=0)
    grad_w_back = outer_product(activated, grad_rows)
    d_act = times_transposed(grad_rows, w_back)
    d_pre = gelu_pull(d_act)[0].astype(jnp.bfloat16)
    grad_in_bias = jnp.sum(d_pre.astype(jnp.float32), axis=0)
    grad_w_in = outer_product(normed_ffn, d_pre)
    d_normed = times_transposed(d_pre, w_in)
    d_res_part, grad_ffn_gain, grad_ffn_shift = norm_pull_two(d_normed)
    d_residual = grad_float + d_res_part
    d_branch = d_residual.astype(jnp.bfloat16)
    grad_out_bias = jnp.sum(d_branch.astype(jnp.float32), axis=0)
    grad_w_out = outer_product(context, d_branch)
    d_attended = (
        times_transposed(d_branch, w_out).astype(jnp.bfloat16).reshape(seq_count, span_dev, H, HD)
    )
    delta = jnp.sum(d_attended.astype(jnp.float32) * attended, axis=-1)

    def attend_back(block_kv, first_key):
        key_count, key_heads, value_heads = split_block(block_kv)
        scores = jnp.einsum(
            "sqhd,skhd->sqhk", queries, key_heads, preferred_element_type=jnp.float32
        )
        allowed = allowed_keys(lengths, flags_all, query_pos, first_key, key_count)
        weights_f = jnp.exp(jnp.where(allowed, scores - log_total[..., None], NEG_FILL))
        d_values = jnp.einsum(
            "sqhk,sqhd->skhd",
            weights_f.astype(jnp.bfloat16),
            d_attended,
            preferred_element_type=jnp.float32,
        )
        d_probs = jnp.einsum(
            "sqhd,skhd->sqhk", d_attended, value_heads, preferred_element_type=jnp.float32
        )
        d_scores = (weights_f * (d_probs - delta[..., None])).astype(jnp.bfloat16)
        d_query = jnp.einsum(
            "sqhk,skhd->sqhd", d_scores, key_heads, preferred_element_type=jnp.float32
        )
        d_keys = jnp.einsum(
            "sqhk,sqhd->skhd", d_scores, queries, preferred_element_type=jnp.float32
        )
        d_block = jnp.concatenate(
            [
                d_keys.reshape(seq_count, key_count, model_width),
                d_values.reshape(seq_count, key_count, model_width),
            ],
            axis=2,
        )
        return (d_query, d_block)

    zero_query = jnp.zeros((seq_count, span_dev, H, HD), jnp.float32)

    def turn(turn_index, state_now):
        current, d_current, d_query = state_now
        anchor = (own_index - turn_index) % members
        add_query, add_block = attend_back(current, anchor * span_dev)
        current = shifted(current, "seq", 1)
        return (current, send_home(d_current + add_block), d_query + add_query)

    start_back = (
        keyval,
        jnp.zeros((seq_count, span_dev, 2 * model_width), jnp.float32),
        zero_query,
    )
    current, d_current, d_query = lax.fori_loop(0, members - 1, turn, start_back)
    anchor = (own_index - (members - 1)) % members
    add_query, add_block = attend_back(current, anchor * span_dev)
    d_query = d_query + add_query
    d_keyval = send_home(d_current + add_block)
    d_query_low = d_query.reshape(row_count, model_width).astype(jnp.bfloat16)
    d_keyval_low = d_keyval.reshape(row_count, 2 * model_width).astype(jnp.bfloat16)
    query_scaled = d_query_low.astype(jnp.float32) * 0.125
    grad_query_bias = jnp.sum(query_scaled, axis=0)
    grad_value_bias = jnp.sum(d_keyval_low[:, model_width:].astype(jnp.float32), axis=0)
    d_projected = jnp.concatenate([query_scaled.astype(jnp.bfloat16), d_keyval_low], axis=1)
    grad_w_qkv = outer_product(normed_attn, d_projected)
    d_normed_attn = times_transposed(d_projected, w_qkv)
    d_in_part, grad_attn_gain, grad_attn_shift = norm_pull_one(d_normed_attn)
    grad_tokens = (d_residual + d_in_part).reshape(seq_count, span_dev, model_width)
    out_block = layer_out.astype(jnp.bfloat16).reshape(seq_count, span_dev, model_width)
    all_sums = (
        lax.psum_scatter(grad_attn_gain, ("dp", "seq"), scatter_dimension=0, tiled=True),
        lax.psum_scatter(grad_attn_shift, ("dp", "seq"), scatter_dimension=0, tiled=True),
        lax.psum_scatter(grad_w_qkv, ("dp", "seq"), scatter_dimension=0, tiled=True),
        lax.psum_scatter(grad_query_bias, ("dp", "seq"), scatter_dimension=0, tiled=True),
        lax.psum_scatter(grad_value_bias, ("dp", "seq"), scatter_dimension=0, tiled=True),
        lax.psum_scatter(grad_w_out, ("dp", "seq"), scatter_dimension=0, tiled=True),
        lax.psum_scatter(grad_out_bias, ("dp", "seq"), scatter_dimension=0, tiled=True),
        lax.psum_scatter(grad_ffn_gain, ("dp", "seq"), scatter_dimension=0, tiled=True),
        lax.psum_scatter(grad_ffn_shift, ("dp", "seq"), scatter_dimension=0, tiled=True),
        lax.psum_scatter(grad_w_in, ("dp", "seq"), scatter_dimension=0, tiled=True),
        lax.psum_scatter(grad_in_bias, ("dp", "seq"), scatter_dimension=0, tiled=True),
        lax.psum_scatter(grad_w_back, ("dp", "seq"), scatter_dimension=0, tiled=True),
        lax.psum_scatter(grad_back_bias, ("dp", "seq"), scatter_dimension=0, tiled=True),
    )
    return (
        out_block,
        grad_tokens,
        all_sums[0],
        all_sums[1],
        all_sums[2],
        all_sums[3],
        all_sums[4],
        all_sums[5],
        all_sums[6],
        all_sums[7],
        all_sums[8],
        all_sums[9],
        all_sums[10],
        all_sums[11],
        all_sums[12],
    )


def solution(mesh):
    sizes = dict(mesh.shape)
    whole = sizes == {"dp": 16, "seq": 2}
    return jax.shard_map(
        whole_sequences if whole else shards,
        mesh=mesh,
        in_specs=(
            P("dp", "seq", None),
            P("dp"),
            P("dp", "seq"),
            P(),
            P(),
            P(),
            P(),
            P(),
            P(),
            P(),
            P(),
            P(),
            P(),
            P(),
            P(),
            P(),
            P("dp", "seq", None),
        ),
        out_specs=(
            P("dp", "seq", None),
            P("dp", "seq", None),
            P(("dp", "seq")),
            P(("dp", "seq")),
            P(("dp", "seq"), None),
            P(("dp", "seq")),
            P(("dp", "seq")),
            P(("dp", "seq"), None),
            P(("dp", "seq")),
            P(("dp", "seq")),
            P(("dp", "seq")),
            P(("dp", "seq"), None),
            P(("dp", "seq")),
            P(("dp", "seq"), None),
            P(("dp", "seq")),
        ),
        check_vma=False,
    )
```
